32 devices in a mesh: blk: 8 (over y, x, core), head: 4 (over z).
Axes of the slice: x: 2, y: 2, z: 4, core: 2. Of those that a mesh axis runs over, the one named last changes fastest.
Arguments:
- tokens: bfloat16 [4096, 2048], P(('blk', 'head')), may hold values from -6 to 6
- lengths: int32 [2], replicated, may hold values from 1024 to 2560, as said below
- block_order: int32 [32], replicated, may hold values from 0 to 31, each once
- bucket_of: int32 [257], replicated, may hold values from 0 to 31, as said below
- gain_attn: float32 [2048], P(('blk', 'head')), may hold values from 0.5 to 1.5
- w_query: bfloat16 [2048, 2048], P('blk', 'head'), may hold values from -0.015625 to 0.015625
- w_key: bfloat16 [2048, 2048], P('blk', 'head'), may hold values from -0.125 to 0.125
- w_value: bfloat16 [2048, 2048], P('blk', 'head'), may hold values from -0.125 to 0.125
- w_out: bfloat16 [2048, 2048], P('head', 'blk'), may hold values from -1.5 to 1.5
- bias_table: bfloat16 [32, 32], P('blk', 'head'), may hold values from -4 to 4
- gain_ffn: float32 [2048], P(('blk', 'head')), may hold values from 0.5 to 1.5
- w_gate: bfloat16 [2048, 5120], P('blk', 'head'), may hold values from -0.125 to 0.125
- w_up: bfloat16 [2048, 5120], P('blk', 'head'), may hold values from -0.125 to 0.125
- w_down: bfloat16 [5120, 2048], P('head', 'blk'), may hold values from -0.078125 to 0.078125
- cotangent: bfloat16 [4096, 2048], P(('blk', 'head')), may hold values from -6 to 6
Outputs:
- output: float32 [4096, 2048], P(('blk', 'head'))
- input_grad: float32 [4096, 2048], P(('blk', 'head'))
- grad_gain_attn: float32 [2048], P(('blk', 'head'))
- grad_w_query: float32 [2048, 2048], P('blk', 'head')
- grad_w_key: float32 [2048, 2048], P('blk', 'head')
- grad_w_value: float32 [2048, 2048], P('blk', 'head')
- grad_w_out: float32 [2048, 2048], P('head', 'blk')
- grad_bias_table: float32 [32, 32], P('blk', 'head')
- grad_gain_ffn: float32 [2048], P(('blk', 'head'))
- grad_w_gate: float32 [2048, 5120], P('blk', 'head')
- grad_w_up: float32 [2048, 5120], P('blk', 'head')
- grad_w_down: float32 [5120, 2048], P('head', 'blk')
The draws below stay inside these ranges and needn't reach their ends.
Inputs may be any that keep to these rules, and one draw needn't show every extreme that they name: lengths[n] is the length of sequence n in the packed order; they add up to 4096, and one of them has exactly 2560 tokens. Rows 128 * i to 128 * i + 127 of tokens and cotangent are the places 128 * block_order[i] onward of the packed order; every block appears once. bucket_of[r + 128] is the bucket of the relative position r (key's place minus query's) for -128 <= r <= 128; farther ones take the bucket of the nearer end. For r <= 0 it lies below 16, for r > 0 at or above; for |r| < 8 it is |r|, plus 32 // 2 when r > 0; it never falls as |r| grows on either side.
All inputs are finite; a program needn't handle non-finite values.
Results may differ from the reference program's by a relative error of at most 0.024.
Values may be sent and summed in bfloat16 or wider, within the bound.
No kernel may reach another device: no remote copies, remote signals or barrier semaphores. Data moves between devices by JAX's collectives and lax.ppermute only.
A program may use at most 192 MiB of HBM per device.

```python
import jax
import jax.numpy as jnp
from jax import lax

D = 2048
H = 32
HD = 64
FF = 5120
NB = 32
MAXDIST = 128
SPAN = 128
MINLEN = 1024
TOKENS = 4096
LONGEST = 2560
NSEQ = 2
NSPANS = 32


def draw_lengths(key, part):
    key = jax.random.fold_in(key, 5)
    pick_key, cut_key = jax.random.split(key)
    spare = TOKENS - LONGEST - (NSEQ - 1) * MINLEN
    cut_points = jnp.sort(jax.random.randint(cut_key, (max(NSEQ - 2, 0),), 0, spare + 1)).astype(jnp.int32)
    bounds = jnp.concatenate([jnp.zeros((1,), jnp.int32), cut_points, jnp.full((1,), spare, jnp.int32)])
    others = MINLEN + bounds[1:] - bounds[:-1]
    longest_at = jax.random.randint(pick_key, (), 0, NSEQ)
    seq_index = jnp.arange(NSEQ, dtype=jnp.int32)
    source_at = jnp.clip(seq_index - (seq_index > longest_at).astype(jnp.int32), 0, max(NSEQ - 2, 0))
    return jnp.where(seq_index == longest_at, LONGEST, others[source_at]).astype(jnp.int32)


def draw_bucket_of(key, part):
    key = jax.random.fold_in(key, 9)
    half_count = NB // 2
    exact_count = half_count // 2
    distance = jnp.arange(MAXDIST + 1, dtype=jnp.int32)
    candidates = jax.random.permutation(key, MAXDIST - exact_count).astype(jnp.int32) + exact_count + 1
    cut_points = candidates[:half_count - exact_count - 1]
    log_level = jnp.sum((distance[:, None] >= cut_points[None, :]).astype(jnp.int32), axis=1)
    magnitude = jnp.where(distance < exact_count, distance, exact_count + log_level)
    relative = jnp.arange(2 * MAXDIST + 1, dtype=jnp.int32) - MAXDIST
    return (jnp.where(relative > 0, half_count, 0) + magnitude[jnp.abs(relative)]).astype(jnp.int32)


def raised(array, key, source, target, blocks, factor):
    owner, partner = [(jnp.arange(array.shape[position]) // (array.shape[position] // blocks)).reshape([-1 if axis == position else 1 for axis in range(array.ndim)]) for position in (source, target)]
    chosen = jax.random.permutation(key, blocks)[partner]
    strong = (owner == chosen) | (owner == (partner + blocks // 2) % blocks)
    return jnp.where(strong, factor * array, array)


def level_of(key, dims, cuts, low, top_value):
    gain = 1.0
    for dim, blocks in cuts:
        draws = jax.random.uniform(jax.random.fold_in(jax.random.fold_in(key, 6), dim), (blocks,), jnp.float32, low / len(cuts), top_value / len(cuts))
        gain = gain * jnp.repeat(jnp.exp(draws), dims[dim] // blocks).reshape((-1,) + (1,) * (len(dims) - 1 - dim))
    return gain


def centred(stream_key, shape, width, most, cuts=(), kind=jnp.bfloat16):
    result = jax.random.normal(stream_key, shape, jnp.float32) * width
    if len(cuts) > 0:
        result = level_of(stream_key, shape, cuts, -0.22, 0.18) * result
    return jnp.clip(result, min=-most, max=most).astype(kind)


def noise_with(own_key, dims, deviation, most, cuts, heavy, held_as=jnp.bfloat16):
    drawn = deviation * jax.random.normal(own_key, dims, jnp.float32)
    if cuts:
        drawn = drawn * level_of(own_key, dims, cuts, -0.22, 0.18)
    return jnp.clip(raised(drawn, jax.random.fold_in(own_key, 3), *heavy), -most, most).astype(held_as)


def setup_inputs(seed: int = 0) -> dict:
    arg_keys = jax.random.split(jax.random.key(seed), 16)
    return {
        "tokens": centred(arg_keys[0], (TOKENS, D), 1.0, 6.0, ((0, 32),)),
        "lengths": draw_lengths(jax.random.fold_in(arg_keys[15], 71), 0),
        "block_order": jax.random.permutation(arg_keys[2], NSPANS).astype(jnp.int32),
        "bucket_of": draw_bucket_of(jax.random.fold_in(arg_keys[15], 71), 0),
        "gain_attn": jnp.clip(0.5 + 1.0 * jax.random.uniform(arg_keys[4], (D,), jnp.float32) ** level_of(arg_keys[4], (D,), ((0, 32),), -0.2, 0.2), 0.5, 1.5),
        "w_query": centred(arg_keys[5], (D, D), (D * HD) ** -0.5, 0.015625, ((0, 8), (1, 4))),
        "w_key": centred(arg_keys[6], (D, D), D ** -0.5, 0.125, ((0, 8), (1, 4))),
        "w_value": centred(arg_keys[7], (D, D), D ** -0.5, 0.125, ((0, 8), (1, 4))),
        "w_out": centred(arg_keys[8], (D, D), 16 ** -0.5, 1.5, ((0, 4), (1, 8))),
        "bias_table": centred(arg_keys[9], (NB, H), 1.0, 4.0, ((0, 8), (1, 4))),
        "gain_ffn": jnp.clip(0.5 + 1.0 * jax.random.uniform(arg_keys[10], (D,), jnp.float32) ** level_of(arg_keys[10], (D,), ((0, 32),), -0.2, 0.2), 0.5, 1.5),
        "w_gate": centred(arg_keys[11], (D, FF), D ** -0.5, 0.125, ((0, 8), (1, 4))),
        "w_up": centred(arg_keys[12], (D, FF), D ** -0.5, 0.125, ((0, 8), (1, 4))),
        "w_down": centred(arg_keys[13], (FF, D), FF ** -0.5, 0.078125, ((0, 4), (1, 8))),
        "cotangent": noise_with(arg_keys[14], (TOKENS, D), 1.0, 6.0, ((0, 32),), (0, 1, 32, 2.75)),
    }


norm_eps = 1e-06
masked_score = -1e+30

@jax.custom_vjp
def low(v):
    return lax.optimization_barrier(v.astype(jnp.bfloat16)).astype(jnp.float32)

@jax.custom_vjp
def low_back(v):
    return v

def low_keep(v):
    return (low(v), None)

def low_pass(kept, grad):
    return (grad,)

def back_keep(v):
    return (v, None)

def back_low(kept, grad):
    return (low(grad),)
low.defvjp(low_keep, low_pass)
low_back.defvjp(back_keep, back_low)

def product(left_side, right_side):
    return jnp.dot(left_side, right_side, precision=lax.Precision.HIGHEST, preferred_element_type=jnp.float32)

def rms_norm(values, gain_vec):
    inv_rms = lax.rsqrt(lax.optimization_barrier(jnp.mean(values * values, axis=-1, keepdims=True)) + norm_eps)
    return values * inv_rms * gain_vec

def segment_of(places, seq_ends):
    return lax.optimization_barrier(jnp.sum((places[:, None] >= seq_ends[None, :]).astype(jnp.int32), axis=1)).astype(jnp.int32)

def attend(query, key_rows, value_rows, bias_table, places, seq_ends, bucket_of):
    token_count = query.shape[0]
    block_size = min(256, token_count)
    segment = segment_of(places, seq_ends)
    rel_table = jnp.take(bias_table, bucket_of, axis=0).T
    key_heads = key_rows.reshape(token_count, H, HD)
    value_heads = value_rows.reshape(token_count, H, HD)

    def one_block(start):
        query_heads = lax.dynamic_slice_in_dim(query, start, block_size, 0).reshape(block_size, H, HD)
        query_place = lax.dynamic_slice_in_dim(places, start, block_size, 0)
        query_segment = lax.dynamic_slice_in_dim(segment, start, block_size, 0)
        scores = jnp.einsum('qhd,khd->hqk', query_heads, key_heads, precision=lax.Precision.HIGHEST)
        rel_index = jnp.clip(places[None, :] - query_place[:, None], -MAXDIST, MAXDIST) + MAXDIST
        scores = low_back(scores + jnp.take(rel_table, rel_index.astype(jnp.int32), axis=1))
        same_seq = query_segment[:, None] == segment[None, :]
        scores = jnp.where(same_seq[None], scores, masked_score)
        weights = jax.nn.softmax(scores, axis=-1)
        mixed_heads = jnp.einsum('hqk,khd->qhd', low(weights), value_heads, precision=lax.Precision.HIGHEST)
        return mixed_heads.reshape(block_size, H * HD)
    starts = jnp.arange(token_count // block_size, dtype=jnp.int32) * block_size
    return lax.map(jax.checkpoint(one_block), starts).reshape(token_count, H * HD)

def layer(tokens, gain_attn, w_query, w_key, w_value, w_out, bias_table, gain_ffn, w_gate, w_up, w_down, places, seq_ends, bucket_of):
    normed_one = low(rms_norm(tokens, gain_attn))
    query = low_back(low(product(normed_one, w_query)))
    key_rows = low_back(low(product(normed_one, w_key)))
    value_rows = low_back(low(product(normed_one, w_value)))
    mixed = low_back(low(attend(query, key_rows, value_rows, bias_table, places, seq_ends, bucket_of)))
    hidden_one = tokens + low_back(product(mixed, w_out))
    normed_two = low(rms_norm(hidden_one, gain_ffn))
    gate_pre = low_back(product(normed_two, w_gate))
    up_pre = low_back(product(normed_two, w_up))
    activated = low(jax.nn.gelu(gate_pre, approximate=True) * up_pre)
    return hidden_one + low_back(product(activated, w_down))

def reference(tokens, lengths, block_order, bucket_of, gain_attn, w_query, w_key, w_value, w_out, bias_table, gain_ffn, w_gate, w_up, w_down, cotangent):
    offsets = jnp.arange(SPAN, dtype=jnp.int32)
    places = (block_order[:, None] * SPAN + offsets[None, :]).reshape(-1).astype(jnp.int32)
    seq_ends = jnp.cumsum(lengths).astype(jnp.int32)
    floats = [item.astype(jnp.float32) for item in (tokens, gain_attn, w_query, w_key, w_value, w_out, bias_table, gain_ffn, w_gate, w_up, w_down)]

    def forward(*params):
        return layer(*params, places, seq_ends, bucket_of)
    output, pullback = jax.vjp(forward, *floats)
    gradients = pullback(cotangent.astype(jnp.float32))
    return (output, gradients[0], gradients[1], gradients[2], gradients[3], gradients[4], gradients[5], gradients[6], gradients[7], gradients[8], gradients[9], gradients[10])
```

```python
import functools

import jax
import jax.numpy as jnp
import numpy as np
from jax import lax
from jax.experimental import pallas as pl
from jax.experimental.pallas import tpu as pltpu
from jax.sharding import PartitionSpec as P

HD = 64
LANES = 2 * HD
MAXDIST = 128
SPAN = 128
BQ = 256
BK = 512
OFF = BK + 2 * SPAN
TABLE_ROWS = 2 * BK + BQ + 4 * SPAN
MID_BLOCKS = BQ // SPAN + 2
WIDE = 2 * BQ
EXTRA = 16
KT_ROWS = 80

norm_eps = 1e-06
masked_score = -1e30
f32 = jnp.float32
bf16 = jnp.bfloat16
MIB = 1 << 20


def rms_scale(values):
    return lax.rsqrt(jnp.mean(values * values, axis=-1, keepdims=True) + norm_eps)


def norm_back(d_normed, source, inv_rms, gain_vec):
    scaled = d_normed * gain_vec
    x_hat = source * inv_rms
    gain_part = jnp.sum(d_normed * x_hat, axis=0)
    d_source = inv_rms * (scaled - x_hat * jnp.mean(scaled * x_hat, axis=-1, keepdims=True))
    return (d_source, gain_part)


def dot_nn(left, right):
    return jnp.dot(left, right, preferred_element_type=f32)


def dot_nt(left, right):
    return lax.dot_general(left, right, (((1,), (1,)), ((), ())), preferred_element_type=f32)


def dot_tn(left, right):
    return lax.dot_general(left, right, (((0,), (0,)), ((), ())), preferred_element_type=f32)


def cyclic(count, by):
    return [(i, (i + by) % count) for i in range(count)]


def gather_slots(rows):
    count = lax.axis_size("head")
    if count != 4:
        return [rows] + [lax.ppermute(rows, "head", cyclic(count, s)) for s in range(1, count)]
    me = lax.axis_index("head")
    back_one = lax.ppermute(rows, "head", cyclic(4, 1))
    ahead_one = lax.ppermute(rows, "head", cyclic(4, 3))
    passed = jnp.where(me == 1, ahead_one, jnp.where(me == 2, back_one, rows))
    back_two = lax.ppermute(passed, "head", [(1, 0), (3, 1), (0, 2), (2, 3)])
    return [rows, back_one, back_two, ahead_one]


def sum_slots(parts):
    count = lax.axis_size("head")
    if count != 4:
        total = parts[0].astype(f32)
        for s in range(1, count):
            total = total + lax.ppermute(parts[s], "head", cyclic(count, count - s)).astype(f32)
        return total
    me = lax.axis_index("head")
    far = lax.ppermute(parts[2], "head", [(0, 1), (1, 3), (2, 0), (3, 2)])
    far_wide = far.astype(f32)
    to_back = jnp.where(me == 2, parts[1].astype(f32) + far_wide, parts[1].astype(f32)).astype(bf16)
    to_ahead = jnp.where(me == 1, parts[3].astype(f32) + far_wide, parts[3].astype(f32)).astype(bf16)
    from_ahead = lax.ppermute(to_back, "head", cyclic(4, 3))
    from_back = lax.ppermute(to_ahead, "head", cyclic(4, 1))
    mine = parts[0].astype(f32) + from_ahead.astype(f32) + from_back.astype(f32)
    return mine + jnp.where((me == 0) | (me == 3), far_wide, 0.0)


def is_power(count):
    return count & (count - 1) == 0


def gather_small(values):
    held = values[None]
    for axis in ("head", "blk"):
        count = lax.axis_size(axis)
        if not is_power(count):
            held = lax.all_gather(held, axis, axis=0, tiled=False)
        else:
            me = lax.axis_index(axis)
            held = held[None]
            bit = 1
            while bit < count:
                other = lax.ppermute(held, axis, [(i, i ^ bit) for i in range(count)])
                low = jnp.concatenate([held, other])
                high = jnp.concatenate([other, held])
                held = jnp.where((me // bit) % 2 == 0, low, high)
                bit *= 2
        if axis == "head":
            held = held.reshape(count, -1)
    return held


def scatter_small(values):
    for axis in ("blk", "head"):
        count = lax.axis_size(axis)
        if not is_power(count):
            values = lax.psum_scatter(values, axis, scatter_dimension=0, tiled=False)
            continue
        me = lax.axis_index(axis)
        bit = count // 2
        while bit >= 1:
            upper = (me // bit) % 2 == 1
            low, high = values[:bit], values[bit:]
            kept, sent = jnp.where(upper, high, low), jnp.where(upper, low, high)
            values = kept + lax.ppermute(sent, axis, [(i, i ^ bit) for i in range(count)])
            bit //= 2
        values = values[0]
    return values


def lane_low(shape):
    return lax.broadcasted_iota(jnp.int32, shape, 1) < HD


def swap_halves(tile):
    return pltpu.roll(tile, HD, 1)


def pair_up(first, second):
    low = lane_low(first.shape)
    return (
        jnp.where(low, first, swap_halves(second)),
        jnp.where(low, swap_halves(first), second),
    )


def project_kernel(slots, *refs):
    x_refs = refs[:slots]
    gain_ref, wq_ref, wk_ref, wv_ref, normed_ref, packed_ref = refs[slots:]
    rows = slots * SPAN

    @pl.when(pl.program_id(0) == 0)
    def _():
        for s in range(slots):
            wide = x_refs[s][...].astype(f32)
            normed = wide * rms_scale(wide) * gain_ref[...]
            normed_ref[s * SPAN : (s + 1) * SPAN, :] = normed.astype(bf16)

    normed = normed_ref[...]
    query = dot_nn(normed, wq_ref[...])
    key = dot_nn(normed, wk_ref[...])
    value = dot_nn(normed, wv_ref[...])
    half = rows // 2
    for pair in range(query.shape[1] // LANES):
        cols = slice(pair * LANES, (pair + 1) * LANES)
        both = pair_up(value[:, cols], key[:, cols])
        queries = pair_up(query[:half, cols], query[half:, cols])
        for member in range(2):
            packed_ref[2 * pair + member, :rows, :] = both[member].astype(bf16)
            packed_ref[2 * pair + member, rows:, :] = queries[member].astype(bf16)


def project(x_slots, gain, weights):
    slots = len(x_slots)
    rows, depth = slots * SPAN, x_slots[0].shape[1]
    width = weights.shape[1] // 3
    heads = width // HD
    tile = min(width, 256)
    steps = width // tile
    whole = pl.BlockSpec((SPAN, depth), lambda j: (0, 0))

    def columns(part):
        return pl.BlockSpec((depth, tile), lambda j: (0, part * steps + j))

    return pl.pallas_call(
        functools.partial(project_kernel, slots),
        grid=(steps,),
        in_specs=[whole] * slots
        + [pl.BlockSpec((1, depth), lambda j: (0, 0)), columns(0), columns(1), columns(2)],
        out_specs=[
            pl.BlockSpec((rows, depth), lambda j: (0, 0)),
            pl.BlockSpec((tile // HD, rows + rows // 2, LANES), lambda j: (j, 0, 0)),
        ],
        out_shape=[
            jax.ShapeDtypeStruct((rows, depth), bf16),
            jax.ShapeDtypeStruct((heads, rows + rows // 2, LANES), bf16),
        ],
        compiler_params=pltpu.CompilerParams(vmem_limit_bytes=40 * MIB),
        cost_estimate=pl.CostEstimate(
            flops=6 * rows * depth * width, bytes_accessed=6 * depth * width, transcendentals=0
        ),
        name="project",
    )(*x_slots, gain, weights, weights, weights)


def place_of(order_ref, info_ref, source, slot, slots):
    z = info_ref[0]
    return order_ref[source * slots + lax.rem(z - slot + slots, slots)]


def dyn(start, size, multiple):
    return pl.ds(pl.multiple_of(start, multiple), size)


def fill_table(bias_ref, table_ref):
    left = OFF - SPAN
    right = left + MID_BLOCKS * SPAN
    table_ref[:left, :] = jnp.broadcast_to(bias_ref[MID_BLOCKS : MID_BLOCKS + 1, :BQ], (left, BQ))
    table_ref[right:, :] = jnp.broadcast_to(
        bias_ref[MID_BLOCKS + 1 : MID_BLOCKS + 2, :BQ], (TABLE_ROWS - right, BQ)
    )
    for c in range(MID_BLOCKS):
        spread = jnp.broadcast_to(bias_ref[c : c + 1, :], (SPAN, WIDE))
        rolled = pltpu.roll(spread, 0, 1, stride=1, stride_axis=0)
        table_ref[left + c * SPAN : left + (c + 1) * SPAN, :] = rolled[:, :BQ]


def block_range(ends_ref, q0, total):
    count = ends_ref.shape[0]
    start, end, cut = jnp.int32(0), jnp.int32(total), jnp.bool_(False)
    for n in range(count):
        edge = ends_ref[n]
        start = jnp.where(edge <= q0, edge, start)
        cut = cut | ((edge > q0) & (edge < q0 + BQ))
    for n in range(count - 1, -1, -1):
        edge = ends_ref[n]
        end = jnp.where(edge >= q0 + BQ, edge, end)
    first = lax.div(start, BK)
    last = lax.div(end + BK - 1, BK)
    whole = jnp.logical_not(cut) & (lax.rem(start, BK) == 0) & (lax.rem(end, BK) == 0)
    near = jnp.clip(lax.div(jnp.maximum(q0 - SPAN, 0), BK), first, last)
    beyond = jnp.clip(lax.div(q0 + BQ + SPAN + BK - 1, BK), first, last)
    return first, near, beyond, last, whole


def same_sequence(ends_ref, k0, q0):
    key_place = k0 + lax.broadcasted_iota(jnp.int32, (BK, 1), 0)
    query_place = q0 + lax.broadcasted_iota(jnp.int32, (1, BQ), 1)
    key_seg = jnp.zeros((BK, 1), jnp.int32)
    query_seg = jnp.zeros((1, BQ), jnp.int32)
    for n in range(ends_ref.shape[0]):
        key_seg = key_seg + jnp.where(key_place >= ends_ref[n], 1, 0)
        query_seg = query_seg + jnp.where(query_place >= ends_ref[n], 1, 0)
    return key_seg == query_seg


def table_start(k0, q0):
    return pl.multiple_of(jnp.clip(k0 - q0, -(BK + 2 * SPAN), BQ + 2 * SPAN) + OFF, SPAN)


def sort_blocks(order_ref, info_ref, x_ref, slots, keep):
    sources = x_ref.shape[0]
    half = slots // 2
    high = jnp.logical_not(lane_low((SPAN, LANES)))
    for source in range(sources):
        for pair in range(half):
            packed = x_ref[
                source, (slots + pair) * SPAN : (slots + pair + 1) * SPAN, :
            ].astype(f32)
            queries = (swap_halves(packed), packed)
            for member in range(2):
                slot = pair + member * half
                place = place_of(order_ref, info_ref, source, slot, slots) * SPAN
                both = x_ref[source, slot * SPAN : (slot + 1) * SPAN, :]
                keep(place, both, jnp.where(high, queries[member], 0.0).astype(bf16))


def attend_kernel(
    slots, order_ref, ends_ref, info_ref, x_ref, bias_ref, mixed_ref, exact_ref, lse_ref,
    both_ref, query_ref, turned_ref, table_ref, held_ref,
):
    total = both_ref.shape[0]
    parted = info_ref.shape[0] > 3

    def keep(place, both, query):
        both_ref[dyn(place, SPAN, SPAN), :] = both
        query_ref[dyn(place, SPAN, SPAN), :] = query
        turned = both.astype(f32).T
        turned_ref[:, dyn(place, SPAN, SPAN)] = turned[:HD, :].astype(bf16)

    sort_blocks(order_ref, info_ref, x_ref, slots, keep)
    fill_table(bias_ref, table_ref)
    if parted:
        held_ref[...] = jnp.zeros_like(held_ref)
        exact_ref[...] = jnp.zeros_like(exact_ref)
        lse_ref[...] = jnp.zeros_like(lse_ref)
    left_bias = bias_ref[MID_BLOCKS : MID_BLOCKS + 1, :BQ]
    right_bias = bias_ref[MID_BLOCKS + 1 : MID_BLOCKS + 2, :BQ]
    start_state = (
        jnp.full((1, BQ), masked_score, f32),
        jnp.zeros((1, BQ), f32),
        jnp.zeros((HD, BQ), f32),
    )

    def one_block(block, unused):
        q0 = block * BQ
        first, near, beyond, last, whole = block_range(ends_ref, q0, total)
        query = query_ref[dyn(q0, BQ, BQ), :]

        def step(kind, tile, state):
            peak, mass, mix = state
            k0 = tile * BK
            scores = dot_nt(both_ref[dyn(k0, BK, BK), :], query)
            constant = 0.0
            if kind in ("near", "cut"):
                scores = scores + table_ref[pl.ds(table_start(k0, q0), BK), :]
            elif kind == "left":
                constant = left_bias
            else:
                constant = right_bias
            if kind == "cut":
                same = same_sequence(ends_ref, k0, q0)
                scores = jnp.where(same, scores, masked_score)
            new_peak = jnp.maximum(peak, jnp.max(scores, axis=0, keepdims=True) + constant)
            weights = jnp.exp(scores - (new_peak - constant))
            if kind == "cut":
                weights = jnp.where(same, weights, 0.0)
            rescale = jnp.exp(peak - new_peak)
            mass = mass * rescale + jnp.sum(weights, axis=0, keepdims=True)
            turned = turned_ref[:, dyn(k0, BK, BK)]
            mix = mix * rescale + dot_nn(turned, weights.astype(bf16))
            return (new_peak, mass, mix)

        def finish(state):
            peak, mass, mix = state
            exact = mix / mass
            exact_ref[:, dyn(q0, BQ, BQ)] = exact
            lse_ref[:, dyn(q0, BQ, BQ)] = peak + jnp.log(mass)
            padded = jnp.concatenate([exact, exact], axis=0)
            held_ref[dyn(q0, BQ, BQ), :] = padded.T

        @pl.when(whole)
        def _():
            state = lax.fori_loop(first, near, functools.partial(step, "left"), start_state)
            state = lax.fori_loop(near, beyond, functools.partial(step, "near"), state)
            finish(lax.fori_loop(beyond, last, functools.partial(step, "right"), state))

        @pl.when(jnp.logical_not(whole))
        def _():
            finish(lax.fori_loop(first, last, functools.partial(step, "cut"), start_state))

        return unused

    lax.fori_loop(info_ref[1], info_ref[2], one_block, 0)
    half = slots // 2
    low = lane_low((SPAN, LANES))
    for source in range(x_ref.shape[0]):
        for pair in range(half):
            places = [
                place_of(order_ref, info_ref, source, pair + m * half, slots) * SPAN
                for m in range(2)
            ]
            tiles = [held_ref[dyn(place, SPAN, SPAN), :] for place in places]
            mixed_ref[source, pair * SPAN : (pair + 1) * SPAN, :] = jnp.where(
                low, tiles[0], tiles[1]
            ).astype(bf16)


def vmem(shape, dtype):
    return pltpu.VMEM(shape, dtype)


def smem_spec():
    return pl.BlockSpec(memory_space=pltpu.SMEM)


def vmem_spec():
    return pl.BlockSpec(memory_space=pltpu.VMEM)


def attention_vmem(total):
    return int(min(58, 16 + 44 * (total / 16384)) * MIB)


def attend(order, ends, info, swapped, bias_rows, slots):
    sources = swapped.shape[0]
    total = sources * slots * SPAN
    return pl.pallas_call(
        functools.partial(attend_kernel, slots),
        in_specs=[smem_spec()] * 3 + [vmem_spec()] * 2,
        out_specs=[vmem_spec()] * 3,
        out_shape=[
            jax.ShapeDtypeStruct((sources, slots * SPAN // 2, LANES), bf16),
            jax.ShapeDtypeStruct((HD, total), f32),
            jax.ShapeDtypeStruct((1, total), f32),
        ],
        scratch_shapes=[
            vmem((total, LANES), bf16),
            vmem((total, LANES), bf16),
            vmem((HD, total), bf16),
            vmem((TABLE_ROWS, BQ), f32),
            vmem((total, LANES), f32),
        ],
        compiler_params=pltpu.CompilerParams(vmem_limit_bytes=attention_vmem(total)),
        cost_estimate=pl.CostEstimate(
            flops=total * total * 128, bytes_accessed=total * 2048, transcendentals=total * total // 2
        ),
        name="attend",
    )(order, ends, info, swapped, bias_rows)


def unroll_rows(tile):
    row = lax.broadcasted_iota(jnp.int32, tile.shape, 0)
    bit = 1
    while bit < tile.shape[0]:
        moved = pltpu.roll(tile, tile.shape[1] - bit, 1)
        tile = jnp.where((row // bit) % 2 == 1, moved, tile)
        bit *= 2
    return tile


def attend_back_kernel(
    slots, bucket_count, order_ref, ends_ref, info_ref, x_ref, mixed_ref, exact_ref, lse_ref,
    bias_ref, bucket_ref, grad_ref,
    both_ref, query_ref, back_ref, turned_ref, table_ref, d_table_ref, d_both_ref, d_query_ref,
    far_ref,
):
    total = both_ref.shape[0]
    sources = x_ref.shape[0]
    half = slots // 2
    low = lane_low((SPAN, LANES))

    def keep(place, both, query):
        both_ref[dyn(place, SPAN, SPAN), :] = both
        query_ref[dyn(place, SPAN, SPAN), :] = query
        turned = both.astype(f32).T
        turned_ref[:HD, dyn(place, SPAN, SPAN)] = turned[HD:, :].astype(bf16)

    sort_blocks(order_ref, info_ref, x_ref, slots, keep)
    for source in range(sources):
        for pair in range(half):
            packed = mixed_ref[source, pair * SPAN : (pair + 1) * SPAN, :].astype(f32)
            for member, tile in enumerate((packed, swap_halves(packed))):
                place = place_of(order_ref, info_ref, source, pair + member * half, slots) * SPAN
                back_ref[dyn(place, SPAN, SPAN), :] = jnp.where(low, tile, 0.0).astype(bf16)
    fill_table(bias_ref, table_ref)
    tail = lax.broadcasted_iota(jnp.int32, (KT_ROWS - HD, total), 0)
    turned_ref[HD:, :] = jnp.where(tail == 0, 1.0, 0.0).astype(bf16)
    d_table_ref[...] = jnp.zeros_like(d_table_ref)
    d_both_ref[...] = jnp.zeros_like(d_both_ref)
    far_ref[...] = jnp.zeros_like(far_ref)
    if info_ref.shape[0] > 3:
        d_query_ref[...] = jnp.zeros_like(d_query_ref)
    left_bias = bias_ref[MID_BLOCKS : MID_BLOCKS + 1, :BQ]
    right_bias = bias_ref[MID_BLOCKS + 1 : MID_BLOCKS + 2, :BQ]

    def one_block(block, unused):
        q0 = block * BQ
        first, near, beyond, last, whole = block_range(ends_ref, q0, total)
        query = query_ref[dyn(q0, BQ, BQ), :]
        back = back_ref[dyn(q0, BQ, BQ), :]
        lse = lse_ref[:, dyn(q0, BQ, BQ)]
        turned_back = back.astype(f32).T[:HD, :]
        delta = jnp.sum(turned_back * exact_ref[:, dyn(q0, BQ, BQ)], axis=0, keepdims=True)

        def step(kind, tile, d_turned):
            k0 = tile * BK
            keys = dyn(k0, BK, BK)
            both = both_ref[keys, :]
            scores = dot_nt(both, query)
            if kind in ("near", "cut"):
                rows = pl.ds(table_start(k0, q0), BK)
                weights = jnp.exp(scores + table_ref[rows, :] - lse)
            elif kind == "left":
                weights = jnp.exp(scores - (lse - left_bias))
            else:
                weights = jnp.exp(scores - (lse - right_bias))
            if kind == "cut":
                weights = jnp.where(same_sequence(ends_ref, k0, q0), weights, 0.0)
            d_probs = dot_nt(both, back)
            d_scores = (weights * (d_probs - delta)).astype(bf16)
            if kind in ("near", "cut"):
                d_table_ref[rows, :] = d_table_ref[rows, :] + d_scores.astype(f32)
            d_both_ref[keys, :] = (
                d_both_ref[keys, :] + dot_nn(weights.astype(bf16), back) + dot_nn(d_scores, query)
            )
            return d_turned + dot_nn(turned_ref[:, keys], d_scores)

        def finish(d_turned):
            top = d_turned[:HD, :]
            d_query_ref[dyn(q0, BQ, BQ), :] = jnp.concatenate([top, top], axis=0).T

        zero = jnp.zeros((KT_ROWS, BQ), f32)

        @pl.when(whole)
        def _():
            at_left = lax.fori_loop(first, near, functools.partial(step, "left"), zero)
            far_ref[0:1, :] = far_ref[0:1, :] + at_left[HD : HD + 1, :]
            at_near = lax.fori_loop(near, beyond, functools.partial(step, "near"), at_left)
            at_right = lax.fori_loop(beyond, last, functools.partial(step, "right"), zero)
            far_ref[1:2, :] = far_ref[1:2, :] + at_right[HD : HD + 1, :]
            finish(at_near + at_right)

        @pl.when(jnp.logical_not(whole))
        def _():
            finish(lax.fori_loop(first, last, functools.partial(step, "cut"), zero))

        return unused

    lax.fori_loop(info_ref[1], info_ref[2], one_block, 0)

    left = OFF - SPAN
    right = left + MID_BLOCKS * SPAN
    sums = []
    for c in range(MID_BLOCKS):
        tile = d_table_ref[left + c * SPAN : left + (c + 1) * SPAN, :]
        wide = jnp.concatenate([tile, jnp.zeros((SPAN, WIDE - BQ), f32)], axis=1)
        sums.append(jnp.sum(unroll_rows(wide), axis=0, keepdims=True))
    lefts = far_ref[0:1, :] + jnp.sum(d_table_ref[:left, :], axis=0, keepdims=True)
    rights = far_ref[1:2, :] + jnp.sum(d_table_ref[right:, :], axis=0, keepdims=True)
    blank = jnp.zeros((1, WIDE - BQ), f32)
    sums.append(jnp.concatenate([lefts, blank], axis=1))
    sums.append(jnp.concatenate([rights, blank], axis=1))
    sums = jnp.concatenate(sums, axis=0)
    buckets = bucket_ref[: MID_BLOCKS + 2, :]
    per_source = bucket_count // sources
    lane = lax.broadcasted_iota(jnp.int32, (1, LANES), 1)
    row = lax.broadcasted_iota(jnp.int32, (EXTRA, LANES), 0)
    for source in range(sources):
        line = jnp.zeros((1, LANES), f32)
        for j in range(per_source):
            picked = jnp.where(buckets == source * per_source + j, sums, 0.0)
            one = jnp.sum(jnp.sum(picked, axis=0, keepdims=True), axis=1, keepdims=True)
            line = jnp.where(lane == j, one, line)
        upper = line.astype(bf16).astype(f32)
        rest = line - upper
        grad_ref[source, 3 * half * SPAN :, :] = jnp.where(
            row == 0, upper, jnp.where(row == 1, rest, 0.0)
        ).astype(bf16)

    for source in range(sources):
        for pair in range(half):
            tiles = []
            for member in range(2):
                slot = pair + member * half
                place = place_of(order_ref, info_ref, source, slot, slots) * SPAN
                grad_ref[source, slot * SPAN : (slot + 1) * SPAN, :] = d_both_ref[
                    dyn(place, SPAN, SPAN), :
                ].astype(bf16)
                tiles.append(d_query_ref[dyn(place, SPAN, SPAN), :])
            grad_ref[source, (slots + pair) * SPAN : (slots + pair + 1) * SPAN, :] = jnp.where(
                low, tiles[0], tiles[1]
            ).astype(bf16)


def attend_back(
    order, ends, info, swapped, mixed_grad, exact, lse, bias_rows, bucket_rows, slots, bucket_count
):
    sources = swapped.shape[0]
    total = sources * slots * SPAN
    return pl.pallas_call(
        functools.partial(attend_back_kernel, slots, bucket_count),
        in_specs=[smem_spec()] * 3 + [vmem_spec()] * 6,
        out_specs=vmem_spec(),
        out_shape=jax.ShapeDtypeStruct((sources, slots * SPAN * 3 // 2 + EXTRA, LANES), bf16),
        scratch_shapes=[
            vmem((total, LANES), bf16),
            vmem((total, LANES), bf16),
            vmem((total, LANES), bf16),
            vmem((KT_ROWS, total), bf16),
            vmem((TABLE_ROWS, BQ), f32),
            vmem((TABLE_ROWS, BQ), f32),
            vmem((total, LANES), f32),
            vmem((total, LANES), f32),
            vmem((8, BQ), f32),
        ],
        compiler_params=pltpu.CompilerParams(vmem_limit_bytes=attention_vmem(total)),
        cost_estimate=pl.CostEstimate(
            flops=total * total * 320, bytes_accessed=total * 3072, transcendentals=total * total // 2
        ),
        name="attend_back",
    )(order, ends, info, swapped, mixed_grad, exact, lse, bias_rows, bucket_rows)


def out_kernel(slots, packed_ref, weight_ref, mix_ref, part_ref):
    heads = packed_ref.shape[0]
    half = slots * SPAN // 2

    @pl.when(pl.program_id(0) == 0)
    def _():
        for pair in range(heads // 2):
            first = packed_ref[2 * pair].astype(f32)
            second = packed_ref[2 * pair + 1].astype(f32)
            top, bottom = pair_up(first, second)
            cols = slice(pair * LANES, (pair + 1) * LANES)
            mix_ref[:half, cols] = top.astype(bf16)
            mix_ref[half:, cols] = bottom.astype(bf16)

    part = dot_nn(mix_ref[...], weight_ref[...]).astype(bf16)
    for s in range(slots):
        part_ref[s] = part[s * SPAN : (s + 1) * SPAN]


def out_project(packed, weight, slots):
    heads = packed.shape[0]
    rows, width, depth = slots * SPAN, heads * HD, weight.shape[1]
    tile = 512
    return pl.pallas_call(
        functools.partial(out_kernel, slots),
        grid=(depth // tile,),
        in_specs=[
            pl.BlockSpec(packed.shape, lambda j: (0, 0, 0)),
            pl.BlockSpec((width, tile), lambda j: (0, j)),
        ],
        out_specs=[
            pl.BlockSpec((rows, width), lambda j: (0, 0)),
            pl.BlockSpec((slots, SPAN, tile), lambda j: (0, 0, j)),
        ],
        out_shape=[
            jax.ShapeDtypeStruct((rows, width), bf16),
            jax.ShapeDtypeStruct((slots, SPAN, depth), bf16),
        ],
        compiler_params=pltpu.CompilerParams(vmem_limit_bytes=32 * MIB),
        cost_estimate=pl.CostEstimate(
            flops=2 * rows * depth * width, bytes_accessed=4 * depth * width, transcendentals=0
        ),
        name="out_project",
    )(packed, weight)


def feed_kernel(slots, *refs):
    normed_refs, grad_refs = refs[:slots], refs[slots : 2 * slots]
    both_ref, down_ref, rows_ref, rows_grad_ref, active_ref, d_both_ref = refs[2 * slots :]

    @pl.when(pl.program_id(0) == 0)
    def _():
        for s in range(slots):
            rows_ref[s * SPAN : (s + 1) * SPAN, :] = normed_refs[s][...]
            rows_grad_ref[s * SPAN : (s + 1) * SPAN, :] = grad_refs[s][...]

    tile = down_ref.shape[0]
    pre = dot_nn(rows_ref[...], both_ref[...])
    d_hidden = dot_nt(rows_grad_ref[...], down_ref[...])
    gate, up = pre[:, :tile], pre[:, tile:]
    scale, cubic = 0.7978845608028654, 0.044715
    square = gate * gate
    bent = jnp.tanh(scale * (gate + cubic * square * gate))
    half = 0.5 * (1.0 + bent)
    gelu = gate * half
    slope = half + 0.5 * gate * (1.0 - bent * bent) * (scale * (1.0 + 3.0 * cubic * square))
    active_ref[...] = (gelu * up).astype(bf16)
    d_both_ref[:, :tile] = (d_hidden * up * slope).astype(bf16)
    d_both_ref[:, tile:] = (d_hidden * gelu).astype(bf16)


def feed_tile(width):
    return 256 if width % 256 == 0 else 128


def feed(normed_slots, grad_slots, both, down):
    slots = len(normed_slots)
    rows, depth, width = slots * SPAN, both.shape[0], down.shape[0]
    tile = feed_tile(width)
    whole = pl.BlockSpec((SPAN, depth), lambda j: (0, 0))
    rows_spec = pl.BlockSpec((rows, depth), lambda j: (0, 0))
    return pl.pallas_call(
        functools.partial(feed_kernel, slots),
        grid=(width // tile,),
        in_specs=[whole] * (2 * slots)
        + [
            pl.BlockSpec((depth, 2 * tile), lambda j: (0, j)),
            pl.BlockSpec((tile, depth), lambda j: (j, 0)),
        ],
        out_specs=[
            rows_spec,
            rows_spec,
            pl.BlockSpec((rows, tile), lambda j: (0, j)),
            pl.BlockSpec((rows, 2 * tile), lambda j: (0, j)),
        ],
        out_shape=[
            jax.ShapeDtypeStruct((rows, depth), bf16),
            jax.ShapeDtypeStruct((rows, depth), bf16),
            jax.ShapeDtypeStruct((rows, width), bf16),
            jax.ShapeDtypeStruct((rows, 2 * width), bf16),
        ],
        compiler_params=pltpu.CompilerParams(vmem_limit_bytes=56 * MIB),
        cost_estimate=pl.CostEstimate(
            flops=6 * rows * depth * width,
            bytes_accessed=6 * depth * width,
            transcendentals=rows * width,
        ),
        name="feed",
    )(*normed_slots, *grad_slots, both, down)


def mix_back_kernel(slots, *refs):
    grad_refs = refs[:slots]
    weight_ref, rows_ref, packed_ref = refs[slots:]
    half = slots * SPAN // 2

    @pl.when(pl.program_id(0) == 0)
    def _():
        for s in range(slots):
            rows_ref[s * SPAN : (s + 1) * SPAN, :] = grad_refs[s][...]

    mixed = dot_nt(rows_ref[...], weight_ref[...])
    for pair in range(mixed.shape[1] // LANES):
        cols = slice(pair * LANES, (pair + 1) * LANES)
        both = pair_up(mixed[:half, cols], mixed[half:, cols])
        for member in range(2):
            packed_ref[2 * pair + member] = both[member].astype(bf16)


def mix_back(grad_slots, weight):
    slots = len(grad_slots)
    width, depth = weight.shape
    rows = slots * SPAN
    tile = min(width, 256)
    whole = pl.BlockSpec((SPAN, depth), lambda j: (0, 0))
    return pl.pallas_call(
        functools.partial(mix_back_kernel, slots),
        grid=(width // tile,),
        in_specs=[whole] * slots + [pl.BlockSpec((tile, depth), lambda j: (j, 0))],
        out_specs=[
            pl.BlockSpec((rows, depth), lambda j: (0, 0)),
            pl.BlockSpec((tile // HD, rows // 2, LANES), lambda j: (j, 0, 0)),
        ],
        out_shape=[
            jax.ShapeDtypeStruct((rows, depth), bf16),
            jax.ShapeDtypeStruct((width // HD, rows // 2, LANES), bf16),
        ],
        compiler_params=pltpu.CompilerParams(vmem_limit_bytes=32 * MIB),
        cost_estimate=pl.CostEstimate(
            flops=2 * rows * depth * width, bytes_accessed=4 * depth * width, transcendentals=0
        ),
        name="mix_back",
    )(*grad_slots, weight)


def project_back_kernel(slots, packed_ref, weight_ref, grads_ref, part_ref):
    heads = packed_ref.shape[0]
    rows = slots * SPAN
    half = rows // 2
    width = heads * HD

    @pl.when(pl.program_id(0) == 0)
    def _():
        for pair in range(heads // 2):
            start = pair * LANES
            tiles = [packed_ref[2 * pair + m].astype(f32) for m in range(2)]
            value, key = pair_up(tiles[0][:rows], tiles[1][:rows])
            top, bottom = pair_up(tiles[0][rows : rows + half], tiles[1][rows : rows + half])
            grads_ref[:half, start : start + LANES] = top.astype(bf16)
            grads_ref[half:, start : start + LANES] = bottom.astype(bf16)
            grads_ref[:, width + start : width + start + LANES] = key.astype(bf16)
            grads_ref[:, 2 * width + start : 2 * width + start + LANES] = value.astype(bf16)

    part = dot_nt(grads_ref[...], weight_ref[...]).astype(bf16)
    for s in range(slots):
        part_ref[s] = part[s * SPAN : (s + 1) * SPAN]


def project_back(packed, weights, slots):
    heads = packed.shape[0]
    depth, width = weights.shape
    rows = slots * SPAN
    tile = 512
    return pl.pallas_call(
        functools.partial(project_back_kernel, slots),
        grid=(depth // tile,),
        in_specs=[
            pl.BlockSpec(packed.shape, lambda j: (0, 0, 0)),
            pl.BlockSpec((tile, width), lambda j: (j, 0)),
        ],
        out_specs=[
            pl.BlockSpec((rows, width), lambda j: (0, 0)),
            pl.BlockSpec((slots, SPAN, tile), lambda j: (0, 0, j)),
        ],
        out_shape=[
            jax.ShapeDtypeStruct((rows, width), bf16),
            jax.ShapeDtypeStruct((slots, SPAN, depth), bf16),
        ],
        compiler_params=pltpu.CompilerParams(vmem_limit_bytes=40 * MIB),
        cost_estimate=pl.CostEstimate(
            flops=2 * rows * depth * width, bytes_accessed=2 * depth * width, transcendentals=0
        ),
        name="project_back",
    )(packed, weights)


def bucket_lines(bucket_of):
    count = bucket_of.shape[0]
    turned = bucket_of[::-1]
    pad = 5 * WIDE // 4
    padded = jnp.concatenate(
        [
            jnp.broadcast_to(turned[:1], (pad,)),
            turned,
            jnp.broadcast_to(turned[-1:], (pad,)),
        ]
    )
    zero_at = pad + count // 2
    keep = BQ + HD
    rows = []
    for c in range(MID_BLOCKS):
        base = zero_at - (c - 1) * SPAN
        rows.append(
            jnp.concatenate([padded[base : base + keep], padded[base - (WIDE - keep) : base]])
        )
    rows.append(jnp.broadcast_to(bucket_of[:1], (WIDE,)))
    rows.append(jnp.broadcast_to(bucket_of[-1:], (WIDE,)))
    spare = 8 * ((MID_BLOCKS + 2 + 7) // 8) - (MID_BLOCKS + 2)
    return jnp.concatenate([jnp.stack(rows), jnp.full((spare, WIDE), -1, bucket_of.dtype)])


def interleave(first, second, tile):
    rows = first.shape[0]
    return jnp.concatenate(
        [first.reshape(rows, -1, 1, tile), second.reshape(rows, -1, 1, tile)], axis=2
    ).reshape(rows, -1)


def on_device(
    tokens,
    lengths,
    block_order,
    bucket_of,
    gain_attn,
    w_query,
    w_key,
    w_value,
    w_out,
    bias_table,
    gain_ffn,
    w_gate,
    w_up,
    w_down,
    cotangent,
):
    blk_count, slots = lax.axis_size("blk"), lax.axis_size("head")
    blk_spot, head_spot = lax.axis_index("blk"), lax.axis_index("head")
    depth = tokens.shape[1]
    width = w_query.shape[1]
    heads = width // HD
    shares = blk_count // heads
    table_rows, table_heads = bias_table.shape
    bucket_count = table_rows * blk_count
    total = blk_count * slots * SPAN
    gain_size = gain_attn.shape[0]
    tile = feed_tile(w_gate.shape[1])

    token_slots = gather_slots(tokens)
    small = gather_small(
        jnp.concatenate([gain_attn, gain_ffn, bias_table.astype(f32).reshape(-1)])
    )
    full_qkv = lax.all_gather(
        jnp.concatenate([w_query, w_key, w_value], axis=1), "blk", axis=0, tiled=True
    )
    full_out = lax.all_gather(w_out, "blk", axis=1, tiled=True)
    full_both = lax.all_gather(interleave(w_gate, w_up, tile), "blk", axis=0, tiled=True)
    full_down = lax.all_gather(w_down, "blk", axis=1, tiled=True)
    gain_one = small[:, :, :gain_size].reshape(1, depth)
    gain_two = small[:, :, gain_size : 2 * gain_size].reshape(1, depth)

    tables = lax.dynamic_index_in_dim(small, head_spot, 1, False)[:, 2 * gain_size :]
    tables = tables.reshape(bucket_count, table_heads)
    my_head = blk_spot // shares
    my_bias = lax.dynamic_index_in_dim(tables, my_head, 1, False)
    bucket_rows = bucket_lines(bucket_of)
    bias_rows = jnp.sum(
        jnp.where(
            bucket_rows[None] == jnp.arange(bucket_count, dtype=jnp.int32)[:, None, None],
            my_bias[:, None, None],
            0.0,
        ),
        axis=0,
    )
    ends = jnp.cumsum(lengths).astype(jnp.int32)
    per_share = total // BQ // shares
    start = (blk_spot % shares) * per_share
    info = [head_spot, start, start + per_share] + ([start] if shares > 1 else [])
    info = jnp.stack([jnp.asarray(item, jnp.int32) for item in info])

    def swap(values):
        return lax.all_to_all(values, "blk", 0, 0, tiled=True)

    def to_heads(values):
        return swap(values if shares == 1 else jnp.repeat(values, shares, axis=0))

    def to_rows(values):
        values = swap(values)
        if shares == 1:
            return values
        values = values.reshape((heads, shares) + values.shape[1:])
        return jnp.sum(values.astype(f32), axis=1).astype(bf16)

    normed_one, packed = project(token_slots, gain_one, full_qkv)
    swapped = to_heads(packed)
    mixed, exact, lse = attend(block_order, ends, info, swapped, bias_rows, slots)
    attn_mix, out_parts = out_project(to_rows(mixed), full_out, slots)
    tokens_wide = tokens.astype(f32)
    hidden_one = tokens_wide + sum_slots([out_parts[s] for s in range(slots)])
    rstd_two = rms_scale(hidden_one)
    normed_two = (hidden_one * rstd_two * gain_two).astype(bf16)

    grad_slots = gather_slots(cotangent)
    normed_slots = gather_slots(normed_two)
    rows_two, rows_grad, active, d_both = feed(normed_slots, grad_slots, full_both, full_down)
    d_parts = dot_nt(d_both, full_both).astype(bf16)
    d_normed_two = sum_slots([d_parts[s * SPAN : (s + 1) * SPAN] for s in range(slots)])
    down_parts = dot_nn(active, full_down).astype(bf16)
    output = hidden_one + sum_slots([down_parts[s * SPAN : (s + 1) * SPAN] for s in range(slots)])
    grad_both = lax.psum_scatter(
        dot_tn(rows_two, d_both).astype(bf16), "blk", scatter_dimension=0, tiled=True
    )
    grad_down = lax.psum_scatter(
        dot_tn(active, rows_grad).astype(bf16), "blk", scatter_dimension=1, tiled=True
    )
    d_source_two, gain_part_two = norm_back(d_normed_two, hidden_one, rstd_two, gain_two)
    d_hidden_one = cotangent.astype(f32) + d_source_two

    attn_slots = gather_slots(d_hidden_one.astype(bf16))
    rows_attn, mix_grads = mix_back(attn_slots, full_out)
    grad_out = lax.psum_scatter(
        dot_tn(attn_mix, rows_attn).astype(bf16), "blk", scatter_dimension=1, tiled=True
    )
    grads = attend_back(
        block_order, ends, info, swapped, to_heads(mix_grads), exact, lse, bias_rows, bucket_rows,
        slots, bucket_count,
    )
    grads = swap(grads)
    extra = grads[:, -EXTRA : -EXTRA + 2, :table_rows].astype(f32).sum(axis=1)
    grad_table = extra.reshape(heads, shares, table_rows).sum(axis=1).T
    if shares > 1:
        grads = grads.reshape((heads, shares) + grads.shape[1:])
        grads = jnp.sum(grads.astype(f32), axis=1).astype(bf16)
    d_qkv, d_parts_one = project_back(grads, full_qkv, slots)
    grad_qkv = lax.psum_scatter(
        dot_tn(normed_one, d_qkv).astype(bf16), "blk", scatter_dimension=0, tiled=True
    )
    d_normed_one = sum_slots([d_parts_one[s] for s in range(slots)])
    d_source_one, gain_part_one = norm_back(
        d_normed_one, tokens_wide, rms_scale(tokens_wide), gain_one
    )
    input_grad = d_hidden_one + d_source_one
    gain_parts = jnp.stack(
        [part.reshape(blk_count, slots, gain_size) for part in (gain_part_one, gain_part_two)],
        axis=2,
    )
    gain_sums = scatter_small(gain_parts)
    grad_qkv = grad_qkv.astype(f32)
    grad_both = grad_both.astype(f32).reshape(grad_both.shape[0], -1, 2, tile)
    return (
        output,
        input_grad,
        gain_sums[0],
        grad_qkv[:, :width],
        grad_qkv[:, width : 2 * width],
        grad_qkv[:, 2 * width :],
        grad_out.astype(f32),
        grad_table,
        gain_sums[1],
        grad_both[:, :, 0].reshape(w_gate.shape),
        grad_both[:, :, 1].reshape(w_up.shape),
        grad_down.astype(f32),
    )


def solution(mesh):
    rows, spread = P(("blk", "head"), None), P(("blk", "head"))
    inward, outward = P("blk", "head"), P("head", "blk")
    in_specs = (
        rows, P(), P(), P(), spread, inward, inward, inward, outward, inward, spread,
        inward, inward, outward, rows,
    )
    out_specs = (
        rows, rows, spread, inward, inward, inward, outward, inward, spread,
        inward, inward, outward,
    )
    return jax.shard_map(
        on_device, mesh=mesh, in_specs=in_specs, out_specs=out_specs, check_vma=False
    )
```

```python
import functools

import jax
import jax.numpy as jnp
import numpy as np
from jax import lax
from jax.experimental import pallas as pl
from jax.experimental.pallas import tpu as pltpu
from jax.sharding import PartitionSpec as P

HD = 64
LANES = 2 * HD
MAXDIST = 128
SPAN = 128
BQ = 256
BK = 512
OFF = BK + 2 * SPAN
TABLE_ROWS = 2 * BK + BQ + 4 * SPAN
MID_BLOCKS = BQ // SPAN + 2
WIDE = 2 * BQ
EXTRA = 16
KT_ROWS = 80

norm_eps = 1e-06
masked_score = -1e30
f32 = jnp.float32
bf16 = jnp.bfloat16
MIB = 1 << 20


def rms_scale(values):
    return lax.rsqrt(jnp.mean(values * values, axis=-1, keepdims=True) + norm_eps)


def norm_back(d_normed, source, inv_rms, gain_vec):
    scaled = d_normed * gain_vec
    x_hat = source * inv_rms
    gain_part = jnp.sum(d_normed * x_hat, axis=0)
    d_source = inv_rms * (scaled - x_hat * jnp.mean(scaled * x_hat, axis=-1, keepdims=True))
    return (d_source, gain_part)


def dot_nn(left, right):
    return jnp.dot(left, right, preferred_element_type=f32)


def dot_nt(left, right):
    return lax.dot_general(left, right, (((1,), (1,)), ((), ())), preferred_element_type=f32)


def dot_tn(left, right):
    return lax.dot_general(left, right, (((0,), (0,)), ((), ())), preferred_element_type=f32)


def cyclic(count, by):
    return [(i, (i + by) % count) for i in range(count)]


def together(*values):
    return lax.optimization_barrier(values)


def gather_near(rows):
    count = lax.axis_size("head")
    if count != 4:
        return [rows] + [lax.ppermute(rows, "head", cyclic(count, s)) for s in range(1, count)]
    return [rows, lax.ppermute(rows, "head", cyclic(4, 1)), lax.ppermute(rows, "head", cyclic(4, 3))]


def gather_far(near):
    if lax.axis_size("head") != 4:
        return near
    rows, back_one, ahead_one = near
    me = lax.axis_index("head")
    passed = jnp.where(me == 1, ahead_one, jnp.where(me == 2, back_one, rows))
    back_two = lax.ppermute(passed, "head", [(1, 0), (3, 1), (0, 2), (2, 3)])
    return [rows, back_one, back_two, ahead_one]


def sum_far(parts):
    count = lax.axis_size("head")
    if count != 4:
        return []
    return [lax.ppermute(parts[2], "head", [(0, 1), (1, 3), (2, 0), (3, 2)])]


def sum_near(parts, far):
    count = lax.axis_size("head")
    if count != 4:
        return [parts[0]] + [
            lax.ppermute(parts[s], "head", cyclic(count, count - s)) for s in range(1, count)
        ]
    me = lax.axis_index("head")
    wide = far[0].astype(f32)
    to_back = jnp.where(me == 2, parts[1].astype(f32) + wide, parts[1].astype(f32)).astype(bf16)
    to_ahead = jnp.where(me == 1, parts[3].astype(f32) + wide, parts[3].astype(f32)).astype(bf16)
    from_ahead = lax.ppermute(to_back, "head", cyclic(4, 3))
    from_back = lax.ppermute(to_ahead, "head", cyclic(4, 1))
    return [parts[0], from_ahead, from_back, far[0]]


def sum_terms(terms):
    total = terms[0].astype(f32) + terms[1].astype(f32) + terms[2].astype(f32)
    if lax.axis_size("head") != 4:
        for term in terms[3:]:
            total = total + term.astype(f32)
        return total
    me = lax.axis_index("head")
    return total + jnp.where((me == 0) | (me == 3), terms[3].astype(f32), 0.0)


def is_power(count):
    return count & (count - 1) == 0


def gather_small(values):
    held = values[None]
    for axis in ("head", "blk"):
        count = lax.axis_size(axis)
        if not is_power(count):
            held = lax.all_gather(held, axis, axis=0, tiled=False)
        else:
            me = lax.axis_index(axis)
            held = held[None]
            bit = 1
            while bit < count:
                other = lax.ppermute(held, axis, [(i, i ^ bit) for i in range(count)])
                low = jnp.concatenate([held, other])
                high = jnp.concatenate([other, held])
                held = jnp.where((me // bit) % 2 == 0, low, high)
                bit *= 2
        if axis == "head":
            held = held.reshape(count, -1)
    return held


def scatter_blk(values):
    return jnp.sum(lax.all_to_all(values, "blk", 0, 0, tiled=True), axis=0)


def scatter_head(values):
    count, me = lax.axis_size("head"), lax.axis_index("head")
    total = lax.dynamic_index_in_dim(values, me, 0, False)
    for s in range(1, count):
        sent = lax.dynamic_index_in_dim(values, (me + s) % count, 0, False)
        total = total + lax.ppermute(sent, "head", cyclic(count, s))
    return total


def lane_low(shape):
    return lax.broadcasted_iota(jnp.int32, shape, 1) < HD


def swap_halves(tile):
    return pltpu.roll(tile, HD, 1)


def pair_up(first, second):
    low = lane_low(first.shape)
    return (
        jnp.where(low, first, swap_halves(second)),
        jnp.where(low, swap_halves(first), second),
    )


def project_kernel(slots, *refs):
    x_refs = refs[:slots]
    gain_ref, wq_ref, wk_ref, wv_ref, normed_ref, packed_ref, scale_ref = refs[slots:]
    rows = slots * SPAN

    @pl.when(pl.program_id(0) == 0)
    def _():
        for s in range(slots):
            wide = x_refs[s][...].astype(f32)
            scale = rms_scale(wide)
            normed = wide * scale * gain_ref[...]
            normed_ref[s * SPAN : (s + 1) * SPAN, :] = normed.astype(bf16)
            scale_ref[s * SPAN : (s + 1) * SPAN, :] = jnp.broadcast_to(scale, (SPAN, LANES))

    normed = normed_ref[...]
    query = dot_nn(normed, wq_ref[...])
    key = dot_nn(normed, wk_ref[...])
    value = dot_nn(normed, wv_ref[...])
    half = rows // 2
    for pair in range(query.shape[1] // LANES):
        cols = slice(pair * LANES, (pair + 1) * LANES)
        both = pair_up(value[:, cols], key[:, cols])
        queries = pair_up(query[:half, cols], query[half:, cols])
        for member in range(2):
            packed_ref[2 * pair + member, :rows, :] = both[member].astype(bf16)
            packed_ref[2 * pair + member, rows:, :] = queries[member].astype(bf16)


def project(x_slots, gain, weights):
    slots = len(x_slots)
    rows, depth = slots * SPAN, x_slots[0].shape[1]
    width = weights.shape[1] // 3
    heads = width // HD
    tile = min(width, 256)
    steps = width // tile
    whole = pl.BlockSpec((SPAN, depth), lambda j: (0, 0))

    def columns(part):
        return pl.BlockSpec((depth, tile), lambda j: (0, part * steps + j))

    return pl.pallas_call(
        functools.partial(project_kernel, slots),
        grid=(steps,),
        in_specs=[whole] * slots
        + [pl.BlockSpec((1, depth), lambda j: (0, 0)), columns(0), columns(1), columns(2)],
        out_specs=[
            pl.BlockSpec((rows, depth), lambda j: (0, 0)),
            pl.BlockSpec((tile // HD, rows + rows // 2, LANES), lambda j: (j, 0, 0)),
            pl.BlockSpec((rows, LANES), lambda j: (0, 0)),
        ],
        out_shape=[
            jax.ShapeDtypeStruct((rows, depth), bf16),
            jax.ShapeDtypeStruct((heads, rows + rows // 2, LANES), bf16),
            jax.ShapeDtypeStruct((rows, LANES), f32),
        ],
        compiler_params=pltpu.CompilerParams(vmem_limit_bytes=40 * MIB),
        cost_estimate=pl.CostEstimate(
            flops=6 * rows * depth * width, bytes_accessed=6 * depth * width, transcendentals=0
        ),
        name="project",
    )(*x_slots, gain, weights, weights, weights)


def place_of(order_ref, info_ref, source, slot, slots):
    z = info_ref[0]
    return order_ref[source * slots + lax.rem(z - slot + slots, slots)]


def dyn(start, size, multiple):
    return pl.ds(pl.multiple_of(start, multiple), size)


def fill_table(bias_ref, table_ref):
    left = OFF - SPAN
    right = left + MID_BLOCKS * SPAN
    table_ref[:left, :] = jnp.broadcast_to(bias_ref[MID_BLOCKS : MID_BLOCKS + 1, :BQ], (left, BQ))
    table_ref[right:, :] = jnp.broadcast_to(
        bias_ref[MID_BLOCKS + 1 : MID_BLOCKS + 2, :BQ], (TABLE_ROWS - right, BQ)
    )
    for c in range(MID_BLOCKS):
        spread = jnp.broadcast_to(bias_ref[c : c + 1, :], (SPAN, WIDE))
        rolled = pltpu.roll(spread, 0, 1, stride=1, stride_axis=0)
        table_ref[left + c * SPAN : left + (c + 1) * SPAN, :] = rolled[:, :BQ]


def block_range(ends_ref, q0, total):
    count = ends_ref.shape[0]
    start, end, cut = jnp.int32(0), jnp.int32(total), jnp.bool_(False)
    for n in range(count):
        edge = ends_ref[n]
        start = jnp.where(edge <= q0, edge, start)
        cut = cut | ((edge > q0) & (edge < q0 + BQ))
    for n in range(count - 1, -1, -1):
        edge = ends_ref[n]
        end = jnp.where(edge >= q0 + BQ, edge, end)
    first = lax.div(start, BK)
    last = lax.div(end + BK - 1, BK)
    whole = jnp.logical_not(cut) & (lax.rem(start, BK) == 0) & (lax.rem(end, BK) == 0)
    near = jnp.clip(lax.div(jnp.maximum(q0 - SPAN, 0), BK), first, last)
    beyond = jnp.clip(lax.div(q0 + BQ + SPAN + BK - 1, BK), first, last)
    return first, near, beyond, last, whole


def same_sequence(ends_ref, k0, q0):
    key_place = k0 + lax.broadcasted_iota(jnp.int32, (BK, 1), 0)
    query_place = q0 + lax.broadcasted_iota(jnp.int32, (1, BQ), 1)
    key_seg = jnp.zeros((BK, 1), jnp.int32)
    query_seg = jnp.zeros((1, BQ), jnp.int32)
    for n in range(ends_ref.shape[0]):
        key_seg = key_seg + jnp.where(key_place >= ends_ref[n], 1, 0)
        query_seg = query_seg + jnp.where(query_place >= ends_ref[n], 1, 0)
    return key_seg == query_seg


def table_start(k0, q0):
    return pl.multiple_of(jnp.clip(k0 - q0, -(BK + 2 * SPAN), BQ + 2 * SPAN) + OFF, SPAN)


def sort_blocks(order_ref, info_ref, x_ref, slots, keep):
    sources = x_ref.shape[0]
    half = slots // 2
    high = jnp.logical_not(lane_low((SPAN, LANES)))
    for source in range(sources):
        for pair in range(half):
            packed = x_ref[
                source, (slots + pair) * SPAN : (slots + pair + 1) * SPAN, :
            ].astype(f32)
            queries = (swap_halves(packed), packed)
            for member in range(2):
                slot = pair + member * half
                place = place_of(order_ref, info_ref, source, slot, slots) * SPAN
                both = x_ref[source, slot * SPAN : (slot + 1) * SPAN, :]
                keep(place, both, jnp.where(high, queries[member], 0.0).astype(bf16))


def attend_kernel(
    slots, order_ref, ends_ref, info_ref, x_ref, bias_ref, mixed_ref, exact_ref, lse_ref,
    both_ref, query_ref, turned_ref, table_ref, held_ref,
):
    total = both_ref.shape[0]
    parted = info_ref.shape[0] > 3

    def keep(place, both, query):
        both_ref[dyn(place, SPAN, SPAN), :] = both
        query_ref[dyn(place, SPAN, SPAN), :] = query
        turned = both.astype(f32).T
        turned_ref[:, dyn(place, SPAN, SPAN)] = turned[:HD, :].astype(bf16)

    sort_blocks(order_ref, info_ref, x_ref, slots, keep)
    fill_table(bias_ref, table_ref)
    if parted:
        held_ref[...] = jnp.zeros_like(held_ref)
        exact_ref[...] = jnp.zeros_like(exact_ref)
        lse_ref[...] = jnp.zeros_like(lse_ref)
    left_bias = bias_ref[MID_BLOCKS : MID_BLOCKS + 1, :BQ]
    right_bias = bias_ref[MID_BLOCKS + 1 : MID_BLOCKS + 2, :BQ]
    start_state = (
        jnp.full((1, BQ), masked_score, f32),
        jnp.zeros((1, BQ), f32),
        jnp.zeros((HD, BQ), f32),
    )

    def one_block(block, unused):
        q0 = block * BQ
        first, near, beyond, last, whole = block_range(ends_ref, q0, total)
        query = query_ref[dyn(q0, BQ, BQ), :]

        def step(kind, tile, state):
            peak, mass, mix = state
            k0 = tile * BK
            scores = dot_nt(both_ref[dyn(k0, BK, BK), :], query)
            constant = 0.0
            if kind in ("near", "cut"):
                scores = scores + table_ref[pl.ds(table_start(k0, q0), BK), :]
            elif kind == "left":
                constant = left_bias
            else:
                constant = right_bias
            if kind == "cut":
                same = same_sequence(ends_ref, k0, q0)
                scores = jnp.where(same, scores, masked_score)
            new_peak = jnp.maximum(peak, jnp.max(scores, axis=0, keepdims=True) + constant)
            weights = jnp.exp(scores - (new_peak - constant))
            if kind == "cut":
                weights = jnp.where(same, weights, 0.0)
            rescale = jnp.exp(peak - new_peak)
            mass = mass * rescale + jnp.sum(weights, axis=0, keepdims=True)
            turned = turned_ref[:, dyn(k0, BK, BK)]
            mix = mix * rescale + dot_nn(turned, weights.astype(bf16))
            return (new_peak, mass, mix)

        def finish(state):
            peak, mass, mix = state
            exact = mix / mass
            exact_ref[:, dyn(q0, BQ, BQ)] = exact
            lse_ref[:, dyn(q0, BQ, BQ)] = peak + jnp.log(mass)
            padded = jnp.concatenate([exact, exact], axis=0)
            held_ref[dyn(q0, BQ, BQ), :] = padded.T

        @pl.when(whole)
        def _():
            state = lax.fori_loop(first, near, functools.partial(step, "left"), start_state)
            state = lax.fori_loop(near, beyond, functools.partial(step, "near"), state)
            finish(lax.fori_loop(beyond, last, functools.partial(step, "right"), state))

        @pl.when(jnp.logical_not(whole))
        def _():
            finish(lax.fori_loop(first, last, functools.partial(step, "cut"), start_state))

        return unused

    lax.fori_loop(info_ref[1], info_ref[2], one_block, 0)
    half = slots // 2
    low = lane_low((SPAN, LANES))
    for source in range(x_ref.shape[0]):
        for pair in range(half):
            places = [
                place_of(order_ref, info_ref, source, pair + m * half, slots) * SPAN
                for m in range(2)
            ]
            tiles = [held_ref[dyn(place, SPAN, SPAN), :] for place in places]
            mixed_ref[source, pair * SPAN : (pair + 1) * SPAN, :] = jnp.where(
                low, tiles[0], tiles[1]
            ).astype(bf16)


def vmem(shape, dtype):
    return pltpu.VMEM(shape, dtype)


def smem_spec():
    return pl.BlockSpec(memory_space=pltpu.SMEM)


def vmem_spec():
    return pl.BlockSpec(memory_space=pltpu.VMEM)


def attention_vmem(total):
    return int(min(58, 16 + 44 * (total / 16384)) * MIB)


def attend(order, ends, info, swapped, bias_rows, slots):
    sources = swapped.shape[0]
    total = sources * slots * SPAN
    return pl.pallas_call(
        functools.partial(attend_kernel, slots),
        in_specs=[smem_spec()] * 3 + [vmem_spec()] * 2,
        out_specs=[vmem_spec()] * 3,
        out_shape=[
            jax.ShapeDtypeStruct((sources, slots * SPAN // 2, LANES), bf16),
            jax.ShapeDtypeStruct((HD, total), f32),
            jax.ShapeDtypeStruct((1, total), f32),
        ],
        scratch_shapes=[
            vmem((total, LANES), bf16),
            vmem((total, LANES), bf16),
            vmem((HD, total), bf16),
            vmem((TABLE_ROWS, BQ), f32),
            vmem((total, LANES), f32),
        ],
        compiler_params=pltpu.CompilerParams(vmem_limit_bytes=attention_vmem(total)),
        cost_estimate=pl.CostEstimate(
            flops=total * total * 128, bytes_accessed=total * 2048, transcendentals=total * total // 2
        ),
        name="attend",
    )(order, ends, info, swapped, bias_rows)


def unroll_rows(tile):
    row = lax.broadcasted_iota(jnp.int32, tile.shape, 0)
    bit = 1
    while bit < tile.shape[0]:
        moved = pltpu.roll(tile, tile.shape[1] - bit, 1)
        tile = jnp.where((row // bit) % 2 == 1, moved, tile)
        bit *= 2
    return tile


def attend_back_kernel(
    slots, bucket_count, order_ref, ends_ref, info_ref, x_ref, mixed_ref, exact_ref, lse_ref,
    bias_ref, bucket_ref, grad_ref,
    both_ref, query_ref, back_ref, turned_ref, table_ref, d_table_ref, d_both_ref, d_query_ref,
    far_ref,
):
    total = both_ref.shape[0]
    sources = x_ref.shape[0]
    half = slots // 2
    low = lane_low((SPAN, LANES))

    def keep(place, both, query):
        both_ref[dyn(place, SPAN, SPAN), :] = both
        query_ref[dyn(place, SPAN, SPAN), :] = query
        turned = both.astype(f32).T
        turned_ref[:HD, dyn(place, SPAN, SPAN)] = turned[HD:, :].astype(bf16)

    sort_blocks(order_ref, info_ref, x_ref, slots, keep)
    for source in range(sources):
        for pair in range(half):
            packed = mixed_ref[source, pair * SPAN : (pair + 1) * SPAN, :].astype(f32)
            for member, tile in enumerate((packed, swap_halves(packed))):
                place = place_of(order_ref, info_ref, source, pair + member * half, slots) * SPAN
                back_ref[dyn(place, SPAN, SPAN), :] = jnp.where(low, tile, 0.0).astype(bf16)
    fill_table(bias_ref, table_ref)
    tail = lax.broadcasted_iota(jnp.int32, (KT_ROWS - HD, total), 0)
    turned_ref[HD:, :] = jnp.where(tail == 0, 1.0, 0.0).astype(bf16)
    d_table_ref[...] = jnp.zeros_like(d_table_ref)
    d_both_ref[...] = jnp.zeros_like(d_both_ref)
    far_ref[...] = jnp.zeros_like(far_ref)
    if info_ref.shape[0] > 3:
        d_query_ref[...] = jnp.zeros_like(d_query_ref)
    left_bias = bias_ref[MID_BLOCKS : MID_BLOCKS + 1, :BQ]
    right_bias = bias_ref[MID_BLOCKS + 1 : MID_BLOCKS + 2, :BQ]

    def one_block(block, unused):
        q0 = block * BQ
        first, near, beyond, last, whole = block_range(ends_ref, q0, total)
        query = query_ref[dyn(q0, BQ, BQ), :]
        back = back_ref[dyn(q0, BQ, BQ), :]
        lse = lse_ref[:, dyn(q0, BQ, BQ)]
        turned_back = back.astype(f32).T[:HD, :]
        delta = jnp.sum(turned_back * exact_ref[:, dyn(q0, BQ, BQ)], axis=0, keepdims=True)

        def step(kind, tile, d_turned):
            k0 = tile * BK
            keys = dyn(k0, BK, BK)
            both = both_ref[keys, :]
            scores = dot_nt(both, query)
            if kind in ("near", "cut"):
                rows = pl.ds(table_start(k0, q0), BK)
                weights = jnp.exp(scores + table_ref[rows, :] - lse)
            elif kind == "left":
                weights = jnp.exp(scores - (lse - left_bias))
            else:
                weights = jnp.exp(scores - (lse - right_bias))
            if kind == "cut":
                weights = jnp.where(same_sequence(ends_ref, k0, q0), weights, 0.0)
            d_probs = dot_nt(both, back)
            d_scores = (weights * (d_probs - delta)).astype(bf16)
            if kind in ("near", "cut"):
                d_table_ref[rows, :] = d_table_ref[rows, :] + d_scores.astype(f32)
            d_both_ref[keys, :] = (
                d_both_ref[keys, :] + dot_nn(weights.astype(bf16), back) + dot_nn(d_scores, query)
            )
            return d_turned + dot_nn(turned_ref[:, keys], d_scores)

        def finish(d_turned):
            top = d_turned[:HD, :]
            d_query_ref[dyn(q0, BQ, BQ), :] = jnp.concatenate([top, top], axis=0).T

        zero = jnp.zeros((KT_ROWS, BQ), f32)

        @pl.when(whole)
        def _():
            at_left = lax.fori_loop(first, near, functools.partial(step, "left"), zero)
            far_ref[0:1, :] = far_ref[0:1, :] + at_left[HD : HD + 1, :]
            at_near = lax.fori_loop(near, beyond, functools.partial(step, "near"), at_left)
            at_right = lax.fori_loop(beyond, last, functools.partial(step, "right"), zero)
            far_ref[1:2, :] = far_ref[1:2, :] + at_right[HD : HD + 1, :]
            finish(at_near + at_right)

        @pl.when(jnp.logical_not(whole))
        def _():
            finish(lax.fori_loop(first, last, functools.partial(step, "cut"), zero))

        return unused

    lax.fori_loop(info_ref[1], info_ref[2], one_block, 0)

    left = OFF - SPAN
    right = left + MID_BLOCKS * SPAN
    sums = []
    for c in range(MID_BLOCKS):
        tile = d_table_ref[left + c * SPAN : left + (c + 1) * SPAN, :]
        wide = jnp.concatenate([tile, jnp.zeros((SPAN, WIDE - BQ), f32)], axis=1)
        sums.append(jnp.sum(unroll_rows(wide), axis=0, keepdims=True))
    lefts = far_ref[0:1, :] + jnp.sum(d_table_ref[:left, :], axis=0, keepdims=True)
    rights = far_ref[1:2, :] + jnp.sum(d_table_ref[right:, :], axis=0, keepdims=True)
    blank = jnp.zeros((1, WIDE - BQ), f32)
    sums.append(jnp.concatenate([lefts, blank], axis=1))
    sums.append(jnp.concatenate([rights, blank], axis=1))
    sums = jnp.concatenate(sums, axis=0)
    buckets = bucket_ref[: MID_BLOCKS + 2, :]
    per_source = bucket_count // sources
    lane = lax.broadcasted_iota(jnp.int32, (1, LANES), 1)
    row = lax.broadcasted_iota(jnp.int32, (EXTRA, LANES), 0)
    for source in range(sources):
        line = jnp.zeros((1, LANES), f32)
        for j in range(per_source):
            picked = jnp.where(buckets == source * per_source + j, sums, 0.0)
            one = jnp.sum(jnp.sum(picked, axis=0, keepdims=True), axis=1, keepdims=True)
            line = jnp.where(lane == j, one, line)
        upper = line.astype(bf16).astype(f32)
        rest = line - upper
        grad_ref[source, 3 * half * SPAN :, :] = jnp.where(
            row == 0, upper, jnp.where(row == 1, rest, 0.0)
        ).astype(bf16)

    for source in range(sources):
        for pair in range(half):
            tiles = []
            for member in range(2):
                slot = pair + member * half
                place = place_of(order_ref, info_ref, source, slot, slots) * SPAN
                grad_ref[source, slot * SPAN : (slot + 1) * SPAN, :] = d_both_ref[
                    dyn(place, SPAN, SPAN), :
                ].astype(bf16)
                tiles.append(d_query_ref[dyn(place, SPAN, SPAN), :])
            grad_ref[source, (slots + pair) * SPAN : (slots + pair + 1) * SPAN, :] = jnp.where(
                low, tiles[0], tiles[1]
            ).astype(bf16)


def attend_back(
    order, ends, info, swapped, mixed_grad, exact, lse, bias_rows, bucket_rows, slots, bucket_count
):
    sources = swapped.shape[0]
    total = sources * slots * SPAN
    return pl.pallas_call(
        functools.partial(attend_back_kernel, slots, bucket_count),
        in_specs=[smem_spec()] * 3 + [vmem_spec()] * 6,
        out_specs=vmem_spec(),
        out_shape=jax.ShapeDtypeStruct((sources, slots * SPAN * 3 // 2 + EXTRA, LANES), bf16),
        scratch_shapes=[
            vmem((total, LANES), bf16),
            vmem((total, LANES), bf16),
            vmem((total, LANES), bf16),
            vmem((KT_ROWS, total), bf16),
            vmem((TABLE_ROWS, BQ), f32),
            vmem((TABLE_ROWS, BQ), f32),
            vmem((total, LANES), f32),
            vmem((total, LANES), f32),
            vmem((8, BQ), f32),
        ],
        compiler_params=pltpu.CompilerParams(vmem_limit_bytes=attention_vmem(total)),
        cost_estimate=pl.CostEstimate(
            flops=total * total * 320, bytes_accessed=total * 3072, transcendentals=total * total // 2
        ),
        name="attend_back",
    )(order, ends, info, swapped, mixed_grad, exact, lse, bias_rows, bucket_rows)


def out_kernel(slots, packed_ref, weight_ref, mix_ref, part_ref):
    heads = packed_ref.shape[0]
    half = slots * SPAN // 2

    @pl.when(pl.program_id(0) == 0)
    def _():
        for pair in range(heads // 2):
            first = packed_ref[2 * pair].astype(f32)
            second = packed_ref[2 * pair + 1].astype(f32)
            top, bottom = pair_up(first, second)
            cols = slice(pair * LANES, (pair + 1) * LANES)
            mix_ref[:half, cols] = top.astype(bf16)
            mix_ref[half:, cols] = bottom.astype(bf16)

    part = dot_nn(mix_ref[...], weight_ref[...]).astype(bf16)
    for s in range(slots):
        part_ref[s] = part[s * SPAN : (s + 1) * SPAN]


def out_project(packed, weight, slots):
    heads = packed.shape[0]
    rows, width, depth = slots * SPAN, heads * HD, weight.shape[1]
    tile = 512
    return pl.pallas_call(
        functools.partial(out_kernel, slots),
        grid=(depth // tile,),
        in_specs=[
            pl.BlockSpec(packed.shape, lambda j: (0, 0, 0)),
            pl.BlockSpec((width, tile), lambda j: (0, j)),
        ],
        out_specs=[
            pl.BlockSpec((rows, width), lambda j: (0, 0)),
            pl.BlockSpec((slots, SPAN, tile), lambda j: (0, 0, j)),
        ],
        out_shape=[
            jax.ShapeDtypeStruct((rows, width), bf16),
            jax.ShapeDtypeStruct((slots, SPAN, depth), bf16),
        ],
        compiler_params=pltpu.CompilerParams(vmem_limit_bytes=32 * MIB),
        cost_estimate=pl.CostEstimate(
            flops=2 * rows * depth * width, bytes_accessed=4 * depth * width, transcendentals=0
        ),
        name="out_project",
    )(packed, weight)


def feed_kernel(slots, *refs):
    normed_refs, grad_refs = refs[:slots], refs[slots : 2 * slots]
    gate_ref, up_ref, down_ref, rows_ref, rows_grad_ref, active_ref, d_both_ref = refs[2 * slots :]

    @pl.when(pl.program_id(0) == 0)
    def _():
        for s in range(slots):
            rows_ref[s * SPAN : (s + 1) * SPAN, :] = normed_refs[s][...]
            rows_grad_ref[s * SPAN : (s + 1) * SPAN, :] = grad_refs[s][...]

    tile = down_ref.shape[0]
    width = d_both_ref.shape[1] // 2
    gate = dot_nn(rows_ref[...], gate_ref[...])
    up = dot_nn(rows_ref[...], up_ref[...])
    d_hidden = dot_nt(rows_grad_ref[...], down_ref[...])
    scale, cubic = 0.7978845608028654, 0.044715
    square = gate * gate
    bent = jnp.tanh(scale * (gate + cubic * square * gate))
    half = 0.5 * (1.0 + bent)
    gelu = gate * half
    slope = half + 0.5 * gate * (1.0 - bent * bent) * (scale * (1.0 + 3.0 * cubic * square))
    active_ref[...] = (gelu * up).astype(bf16)
    start = pl.program_id(0) * tile
    d_both_ref[:, dyn(start, tile, tile)] = (d_hidden * up * slope).astype(bf16)
    d_both_ref[:, dyn(width + start, tile, LANES)] = (d_hidden * gelu).astype(bf16)


def feed_tile(width):
    return 256 if width % 256 == 0 else 128


def feed(normed_slots, grad_slots, both, down):
    slots = len(normed_slots)
    rows, depth, width = slots * SPAN, both.shape[0], down.shape[0]
    tile = feed_tile(width)
    steps = width // tile
    whole = pl.BlockSpec((SPAN, depth), lambda j: (0, 0))
    rows_spec = pl.BlockSpec((rows, depth), lambda j: (0, 0))
    return pl.pallas_call(
        functools.partial(feed_kernel, slots),
        grid=(steps,),
        in_specs=[whole] * (2 * slots)
        + [
            pl.BlockSpec((depth, tile), lambda j: (0, j)),
            pl.BlockSpec((depth, tile), lambda j: (0, steps + j)),
            pl.BlockSpec((tile, depth), lambda j: (j, 0)),
        ],
        out_specs=[
            rows_spec,
            rows_spec,
            pl.BlockSpec((rows, tile), lambda j: (0, j)),
            pl.BlockSpec((rows, 2 * width), lambda j: (0, 0)),
        ],
        out_shape=[
            jax.ShapeDtypeStruct((rows, depth), bf16),
            jax.ShapeDtypeStruct((rows, depth), bf16),
            jax.ShapeDtypeStruct((rows, width), bf16),
            jax.ShapeDtypeStruct((rows, 2 * width), bf16),
        ],
        compiler_params=pltpu.CompilerParams(vmem_limit_bytes=56 * MIB),
        cost_estimate=pl.CostEstimate(
            flops=6 * rows * depth * width,
            bytes_accessed=6 * depth * width,
            transcendentals=rows * width,
        ),
        name="feed",
    )(*normed_slots, *grad_slots, both, both, down)


def mix_back_kernel(slots, *refs):
    grad_refs = refs[:slots]
    weight_ref, rows_ref, packed_ref = refs[slots:]
    half = slots * SPAN // 2

    @pl.when(pl.program_id(0) == 0)
    def _():
        for s in range(slots):
            rows_ref[s * SPAN : (s + 1) * SPAN, :] = grad_refs[s][...]

    mixed = dot_nt(rows_ref[...], weight_ref[...])
    for pair in range(mixed.shape[1] // LANES):
        cols = slice(pair * LANES, (pair + 1) * LANES)
        both = pair_up(mixed[:half, cols], mixed[half:, cols])
        for member in range(2):
            packed_ref[2 * pair + member] = both[member].astype(bf16)


def mix_back(grad_slots, weight):
    slots = len(grad_slots)
    width, depth = weight.shape
    rows = slots * SPAN
    tile = min(width, 256)
    whole = pl.BlockSpec((SPAN, depth), lambda j: (0, 0))
    return pl.pallas_call(
        functools.partial(mix_back_kernel, slots),
        grid=(width // tile,),
        in_specs=[whole] * slots + [pl.BlockSpec((tile, depth), lambda j: (j, 0))],
        out_specs=[
            pl.BlockSpec((rows, depth), lambda j: (0, 0)),
            pl.BlockSpec((tile // HD, rows // 2, LANES), lambda j: (j, 0, 0)),
        ],
        out_shape=[
            jax.ShapeDtypeStruct((rows, depth), bf16),
            jax.ShapeDtypeStruct((width // HD, rows // 2, LANES), bf16),
        ],
        compiler_params=pltpu.CompilerParams(vmem_limit_bytes=32 * MIB),
        cost_estimate=pl.CostEstimate(
            flops=2 * rows * depth * width, bytes_accessed=4 * depth * width, transcendentals=0
        ),
        name="mix_back",
    )(*grad_slots, weight)


def project_back_kernel(slots, packed_ref, weight_ref, scale_ref, *refs):
    x_refs = refs[:slots]
    grads_ref, part_ref, gain_ref = refs[slots:]
    heads = packed_ref.shape[0]
    rows = slots * SPAN
    half = rows // 2
    width = heads * HD

    @pl.when(pl.program_id(0) == 0)
    def _():
        for pair in range(heads // 2):
            start = pair * LANES
            tiles = [packed_ref[2 * pair + m].astype(f32) for m in range(2)]
            value, key = pair_up(tiles[0][:rows], tiles[1][:rows])
            top, bottom = pair_up(tiles[0][rows : rows + half], tiles[1][rows : rows + half])
            grads_ref[:half, start : start + LANES] = top.astype(bf16)
            grads_ref[half:, start : start + LANES] = bottom.astype(bf16)
            grads_ref[:, width + start : width + start + LANES] = key.astype(bf16)
            grads_ref[:, 2 * width + start : 2 * width + start + LANES] = value.astype(bf16)

    part = dot_nt(grads_ref[...], weight_ref[...])
    gain = jnp.zeros((1, part.shape[1]), f32)
    for s in range(slots):
        span = slice(s * SPAN, (s + 1) * SPAN)
        part_ref[s] = part[span].astype(bf16)
        x_hat = x_refs[s][...].astype(f32) * scale_ref[span, :1]
        gain = gain + jnp.sum(part[span] * x_hat, axis=0, keepdims=True)
    gain_ref[...] = gain


def project_back(packed, weights, scale, x_slots):
    slots = len(x_slots)
    heads = packed.shape[0]
    depth, width = weights.shape
    rows = slots * SPAN
    tile = 512
    return pl.pallas_call(
        functools.partial(project_back_kernel, slots),
        grid=(depth // tile,),
        in_specs=[
            pl.BlockSpec(packed.shape, lambda j: (0, 0, 0)),
            pl.BlockSpec((tile, width), lambda j: (j, 0)),
            pl.BlockSpec((rows, LANES), lambda j: (0, 0)),
        ]
        + [pl.BlockSpec((SPAN, tile), lambda j: (0, j))] * slots,
        out_specs=[
            pl.BlockSpec((rows, width), lambda j: (0, 0)),
            pl.BlockSpec((slots, SPAN, tile), lambda j: (0, 0, j)),
            pl.BlockSpec((1, tile), lambda j: (0, j)),
        ],
        out_shape=[
            jax.ShapeDtypeStruct((rows, width), bf16),
            jax.ShapeDtypeStruct((slots, SPAN, depth), bf16),
            jax.ShapeDtypeStruct((1, depth), f32),
        ],
        compiler_params=pltpu.CompilerParams(vmem_limit_bytes=40 * MIB),
        cost_estimate=pl.CostEstimate(
            flops=2 * rows * depth * width, bytes_accessed=2 * depth * width, transcendentals=0
        ),
        name="project_back",
    )(packed, weights, scale, *x_slots)


def bucket_lines(bucket_of):
    count = bucket_of.shape[0]
    turned = bucket_of[::-1]
    pad = 5 * WIDE // 4
    padded = jnp.concatenate(
        [
            jnp.broadcast_to(turned[:1], (pad,)),
            turned,
            jnp.broadcast_to(turned[-1:], (pad,)),
        ]
    )
    zero_at = pad + count // 2
    keep = BQ + HD
    rows = []
    for c in range(MID_BLOCKS):
        base = zero_at - (c - 1) * SPAN
        rows.append(
            jnp.concatenate([padded[base : base + keep], padded[base - (WIDE - keep) : base]])
        )
    rows.append(jnp.broadcast_to(bucket_of[:1], (WIDE,)))
    rows.append(jnp.broadcast_to(bucket_of[-1:], (WIDE,)))
    spare = 8 * ((MID_BLOCKS + 2 + 7) // 8) - (MID_BLOCKS + 2)
    return jnp.concatenate([jnp.stack(rows), jnp.full((spare, WIDE), -1, bucket_of.dtype)])


def on_device(
    tokens,
    lengths,
    block_order,
    bucket_of,
    gain_attn,
    w_query,
    w_key,
    w_value,
    w_out,
    bias_table,
    gain_ffn,
    w_gate,
    w_up,
    w_down,
    cotangent,
):
    blk_count, slots = lax.axis_size("blk"), lax.axis_size("head")
    blk_spot, head_spot = lax.axis_index("blk"), lax.axis_index("head")
    depth = tokens.shape[1]
    width = w_query.shape[1]
    heads = width // HD
    shares = blk_count // heads
    table_rows, table_heads = bias_table.shape
    bucket_count = table_rows * blk_count
    total = blk_count * slots * SPAN
    gain_size = gain_attn.shape[0]
    hidden = w_gate.shape[1]

    token_slots = gather_far(gather_near(tokens))
    small = gather_small(
        jnp.concatenate([gain_attn, gain_ffn, bias_table.astype(f32).reshape(-1)])
    )
    full_qkv = lax.all_gather(
        jnp.concatenate([w_query, w_key, w_value], axis=1), "blk", axis=0, tiled=True
    )
    full_out = lax.all_gather(w_out, "blk", axis=1, tiled=True)
    full_both = lax.all_gather(
        jnp.concatenate([w_gate, w_up], axis=1), "blk", axis=0, tiled=True
    )
    full_down = lax.all_gather(w_down, "blk", axis=1, tiled=True)
    gain_one = small[:, :, :gain_size].reshape(1, depth)
    gain_two = small[:, :, gain_size : 2 * gain_size].reshape(1, depth)

    tables = lax.dynamic_index_in_dim(small, head_spot, 1, False)[:, 2 * gain_size :]
    tables = tables.reshape(bucket_count, table_heads)
    my_head = blk_spot // shares
    my_bias = lax.dynamic_index_in_dim(tables, my_head, 1, False)
    bucket_rows = bucket_lines(bucket_of)
    bias_rows = jnp.sum(
        jnp.where(
            bucket_rows[None] == jnp.arange(bucket_count, dtype=jnp.int32)[:, None, None],
            my_bias[:, None, None],
            0.0,
        ),
        axis=0,
    )
    ends = jnp.cumsum(lengths).astype(jnp.int32)
    per_share = total // BQ // shares
    start = (blk_spot % shares) * per_share
    info = [head_spot, start, start + per_share] + ([start] if shares > 1 else [])
    info = jnp.stack([jnp.asarray(item, jnp.int32) for item in info])

    def swap(values):
        return lax.all_to_all(values, "blk", 0, 0, tiled=True)

    def to_heads(values):
        return swap(values if shares == 1 else jnp.repeat(values, shares, axis=0))

    def to_rows(values):
        values = swap(values)
        if shares == 1:
            return values
        values = values.reshape((heads, shares) + values.shape[1:])
        return jnp.sum(values.astype(f32), axis=1).astype(bf16)

    cotangent, *token_slots = together(cotangent, *token_slots)
    normed_one, packed, scale_one = project(token_slots, gain_one, full_qkv)
    grad_near = gather_near(cotangent)
    swapped, *grad_near = together(to_heads(packed), *grad_near)
    grad_slots = gather_far(grad_near)
    mixed, exact, lse = attend(block_order, ends, info, swapped, bias_rows, slots)
    mixed, *grad_slots = together(mixed, *grad_slots)
    attn_mix, out_parts = out_project(to_rows(mixed), full_out, slots)
    out_parts = [out_parts[s] for s in range(slots)]
    tokens_wide = tokens.astype(f32)
    hidden_one = tokens_wide + sum_terms(sum_near(out_parts, sum_far(out_parts)))
    rstd_two = rms_scale(hidden_one)
    normed_two = (hidden_one * rstd_two * gain_two).astype(bf16)

    normed_slots = gather_far(gather_near(normed_two))
    rows_two, rows_grad, active, d_both = feed(normed_slots, grad_slots, full_both, full_down)

    def spans(rows):
        return [rows[s * SPAN : (s + 1) * SPAN] for s in range(slots)]

    d_parts = spans(dot_nt(d_both, full_both).astype(bf16))
    d_far = sum_far(d_parts)
    grad_both, *d_far = together(dot_tn(rows_two, d_both).astype(bf16), *d_far)
    grad_both = lax.psum_scatter(grad_both, "blk", scatter_dimension=0, tiled=True)
    d_near = sum_near(d_parts, d_far)
    grad_down, *d_near = together(dot_tn(active, rows_grad).astype(bf16), *d_near)
    grad_down = lax.psum_scatter(grad_down, "blk", scatter_dimension=1, tiled=True)
    d_normed_two = sum_terms(d_near)
    d_source_two, gain_part_two = norm_back(d_normed_two, hidden_one, rstd_two, gain_two)
    d_hidden_one = cotangent.astype(f32) + d_source_two

    attn_near = gather_near(d_hidden_one.astype(bf16))
    down_parts, *attn_near = together(dot_nn(active, full_down).astype(bf16), *attn_near)
    down_parts = spans(down_parts)
    rows_attn, mix_grads = mix_back(gather_far(attn_near), full_out)
    grad_out = lax.psum_scatter(
        dot_tn(attn_mix, rows_attn).astype(bf16), "blk", scatter_dimension=1, tiled=True
    )
    down_far = sum_far(down_parts)
    mix_grads, grad_both, *down_far = together(to_heads(mix_grads), grad_both, *down_far)
    down_near = sum_near(down_parts, down_far)
    grads = attend_back(
        block_order, ends, info, swapped, mix_grads, exact, lse, bias_rows, bucket_rows,
        slots, bucket_count,
    )
    grads, grad_down, *down_near = together(grads, grad_down, *down_near)
    output = hidden_one + sum_terms(down_near)
    grads = swap(grads)
    extra = grads[:, -EXTRA : -EXTRA + 2, :table_rows].astype(f32).sum(axis=1)
    grad_table = extra.reshape(heads, shares, table_rows).sum(axis=1).T
    if shares > 1:
        grads = grads.reshape((heads, shares) + grads.shape[1:])
        grads = jnp.sum(grads.astype(f32), axis=1).astype(bf16)
    d_qkv, one_parts, gain_part_one = project_back(grads, full_qkv, scale_one, token_slots)
    one_parts = [one_parts[s] for s in range(slots)]
    one_far = sum_far(one_parts)
    gain_parts = jnp.stack(
        [part.reshape(blk_count, slots, gain_size) for part in (gain_part_one, gain_part_two)],
        axis=2,
    )
    grad_qkv, gain_parts = together(dot_tn(normed_one, d_qkv).astype(bf16), gain_parts)
    grad_qkv, gain_sums, grad_out, *one_far = together(
        grad_qkv, scatter_blk(gain_parts), grad_out, *one_far
    )
    grad_qkv = lax.psum_scatter(grad_qkv, "blk", scatter_dimension=0, tiled=True).astype(f32)
    gain_sums, *one_near = together(scatter_head(gain_sums), *sum_near(one_parts, one_far))
    d_normed_one = sum_terms(one_near)
    d_source_one, unused = norm_back(d_normed_one, tokens_wide, rms_scale(tokens_wide), gain_one)
    input_grad = d_hidden_one + d_source_one
    grad_both = grad_both.astype(f32)
    return (
        output,
        input_grad,
        gain_sums[0],
        grad_qkv[:, :width],
        grad_qkv[:, width : 2 * width],
        grad_qkv[:, 2 * width :],
        grad_out.astype(f32),
        grad_table,
        gain_sums[1],
        grad_both[:, :hidden],
        grad_both[:, hidden:],
        grad_down.astype(f32),
    )


def solution(mesh):
    rows, spread = P(("blk", "head"), None), P(("blk", "head"))
    inward, outward = P("blk", "head"), P("head", "blk")
    in_specs = (
        rows, P(), P(), P(), spread, inward, inward, inward, outward, inward, spread,
        inward, inward, outward, rows,
    )
    out_specs = (
        rows, rows, spread, inward, inward, inward, outward, inward, spread,
        inward, inward, outward,
    )
    return jax.shard_map(
        on_device, mesh=mesh, in_specs=in_specs, out_specs=out_specs, check_vma=False
    )
```

```python
import functools

import jax
import jax.numpy as jnp
import numpy as np
from jax import lax
from jax.experimental import pallas as pl
from jax.experimental.pallas import tpu as pltpu
from jax.sharding import PartitionSpec as P

HD = 64
LANES = 2 * HD
MAXDIST = 128
SPAN = 128
BQ = 512
BK = 512
OFF = BK + 2 * SPAN
TABLE_ROWS = 2 * BK + BQ + 4 * SPAN
MID_BLOCKS = BQ // SPAN + 2
WIDE = 2 * BQ
EXTRA = 16
KT_ROWS = 80
SHIFT_ROOM = 60.0
CH = 512
CB = 256

norm_eps = 1e-06
masked_score = -1e30
f32 = jnp.float32
bf16 = jnp.bfloat16
MIB = 1 << 20


def rms_scale(values):
    return lax.rsqrt(jnp.mean(values * values, axis=-1, keepdims=True) + norm_eps)


def norm_back(d_normed, source, inv_rms, gain_vec):
    scaled = d_normed * gain_vec
    x_hat = source * inv_rms
    gain_part = jnp.sum(d_normed * x_hat, axis=0)
    d_source = inv_rms * (scaled - x_hat * jnp.mean(scaled * x_hat, axis=-1, keepdims=True))
    return (d_source, gain_part)


def dot_nn(left, right):
    return jnp.dot(left, right, preferred_element_type=f32)


def dot_nt(left, right):
    return lax.dot_general(left, right, (((1,), (1,)), ((), ())), preferred_element_type=f32)


def dot_tn(left, right):
    return lax.dot_general(left, right, (((0,), (0,)), ((), ())), preferred_element_type=f32)


def cyclic(count, by):
    return [(i, (i + by) % count) for i in range(count)]


def together(*values):
    return lax.optimization_barrier(values)


def gather_near(rows):
    count = lax.axis_size("head")
    if count != 4:
        return [rows] + [lax.ppermute(rows, "head", cyclic(count, s)) for s in range(1, count)]
    return [rows, lax.ppermute(rows, "head", cyclic(4, 1)), lax.ppermute(rows, "head", cyclic(4, 3))]


def gather_far(near):
    if lax.axis_size("head") != 4:
        return near
    rows, back_one, ahead_one = near
    me = lax.axis_index("head")
    passed = jnp.where(me == 1, ahead_one, jnp.where(me == 2, back_one, rows))
    back_two = lax.ppermute(passed, "head", [(1, 0), (3, 1), (0, 2), (2, 3)])
    return [rows, back_one, back_two, ahead_one]


def gather_direct(rows):
    count = lax.axis_size("head")
    return [rows] + [lax.ppermute(rows, "head", cyclic(count, s)) for s in range(1, count)]


def sum_far(parts):
    count = lax.axis_size("head")
    if count != 4:
        return []
    return [lax.ppermute(parts[2], "head", [(0, 1), (1, 3), (2, 0), (3, 2)])]


def sum_near(parts, far, beside=()):
    count = lax.axis_size("head")
    if count != 4:
        return [parts[0]] + [
            lax.ppermute(parts[s], "head", cyclic(count, count - s)) for s in range(1, count)
        ], beside
    me = lax.axis_index("head")
    wide = far[0].astype(f32)
    to_back = jnp.where(me == 2, parts[1].astype(f32) + wide, parts[1].astype(f32)).astype(bf16)
    to_ahead = jnp.where(me == 1, parts[3].astype(f32) + wide, parts[3].astype(f32)).astype(bf16)
    to_back, to_ahead, *beside = together(to_back, to_ahead, *beside)
    from_ahead = lax.ppermute(to_back, "head", cyclic(4, 3))
    from_back = lax.ppermute(to_ahead, "head", cyclic(4, 1))
    return [parts[0], from_ahead, from_back, far[0]], beside


def sum_terms(terms):
    total = terms[0].astype(f32) + terms[1].astype(f32) + terms[2].astype(f32)
    if lax.axis_size("head") != 4:
        for term in terms[3:]:
            total = total + term.astype(f32)
        return total
    me = lax.axis_index("head")
    return total + jnp.where((me == 0) | (me == 3), terms[3].astype(f32), 0.0)


def is_power(count):
    return count & (count - 1) == 0


def gather_small(values):
    held = values[None]
    for axis in ("head", "blk"):
        count = lax.axis_size(axis)
        if not is_power(count):
            held = lax.all_gather(held, axis, axis=0, tiled=False)
        else:
            me = lax.axis_index(axis)
            held = held[None]
            bit = 1
            while bit < count:
                other = lax.ppermute(held, axis, [(i, i ^ bit) for i in range(count)])
                low = jnp.concatenate([held, other])
                high = jnp.concatenate([other, held])
                held = jnp.where((me // bit) % 2 == 0, low, high)
                bit *= 2
        if axis == "head":
            held = held.reshape(count, -1)
    return held


def exchange(parts):
    count = len(parts)
    return [parts[0]] + [
        lax.ppermute(parts[count - s], "head", cyclic(count, s)) for s in range(1, count)
    ]


def sum_direct(parts, steps):
    count = len(parts)
    return [lax.ppermute(parts[s], "head", cyclic(count, count - s)) for s in steps]


def sum_all(terms):
    total = terms[0].astype(f32)
    for term in terms[1:]:
        total = total + term.astype(f32)
    return total


def scatter_blk(values):
    return jnp.sum(lax.all_to_all(values, "blk", 0, 0, tiled=True), axis=0)


def scatter_head(values):
    count, me = lax.axis_size("head"), lax.axis_index("head")
    total = lax.dynamic_index_in_dim(values, me, 0, False)
    for s in range(1, count):
        sent = lax.dynamic_index_in_dim(values, (me + s) % count, 0, False)
        total = total + lax.ppermute(sent, "head", cyclic(count, s))
    return total


def lane_low(shape):
    return lax.broadcasted_iota(jnp.int32, shape, 1) < HD


def swap_halves(tile):
    return pltpu.roll(tile, HD, 1)


def pair_up(first, second):
    low = lane_low(first.shape)
    return (
        jnp.where(low, first, swap_halves(second)),
        jnp.where(low, swap_halves(first), second),
    )


def project_kernel(slots, *refs):
    x_refs = refs[:slots]
    gain_ref, wq_ref, wk_ref, wv_ref, normed_ref, packed_ref, scale_ref = refs[slots:]
    rows = slots * SPAN

    @pl.when(pl.program_id(0) == 0)
    def _():
        for s in range(slots):
            wide = x_refs[s][...].astype(f32)
            scale = rms_scale(wide)
            normed = wide * scale * gain_ref[...]
            normed_ref[s * SPAN : (s + 1) * SPAN, :] = normed.astype(bf16)
            scale_ref[s * SPAN : (s + 1) * SPAN, :] = jnp.broadcast_to(scale, (SPAN, LANES))

    normed = normed_ref[...]
    query = dot_nn(normed, wq_ref[...])
    key = dot_nn(normed, wk_ref[...])
    value = dot_nn(normed, wv_ref[...])
    half = rows // 2
    for pair in range(query.shape[1] // LANES):
        cols = slice(pair * LANES, (pair + 1) * LANES)
        both = pair_up(value[:, cols], key[:, cols])
        queries = pair_up(query[:half, cols], query[half:, cols])
        for member in range(2):
            packed_ref[2 * pair + member, :rows, :] = both[member].astype(bf16)
            packed_ref[2 * pair + member, rows:, :] = queries[member].astype(bf16)


def project(x_slots, gain, weights):
    slots = len(x_slots)
    rows, depth = slots * SPAN, x_slots[0].shape[1]
    width = weights.shape[1] // 3
    heads = width // HD
    tile = min(width, 256)
    steps = width // tile
    whole = pl.BlockSpec((SPAN, depth), lambda j: (0, 0))

    def columns(part):
        return pl.BlockSpec((depth, tile), lambda j: (0, part * steps + j))

    return pl.pallas_call(
        functools.partial(project_kernel, slots),
        grid=(steps,),
        in_specs=[whole] * slots
        + [pl.BlockSpec((1, depth), lambda j: (0, 0)), columns(0), columns(1), columns(2)],
        out_specs=[
            pl.BlockSpec((rows, depth), lambda j: (0, 0)),
            pl.BlockSpec((tile // HD, rows + rows // 2, LANES), lambda j: (j, 0, 0)),
            pl.BlockSpec((rows, LANES), lambda j: (0, 0)),
        ],
        out_shape=[
            jax.ShapeDtypeStruct((rows, depth), bf16),
            jax.ShapeDtypeStruct((heads, rows + rows // 2, LANES), bf16),
            jax.ShapeDtypeStruct((rows, LANES), f32),
        ],
        compiler_params=pltpu.CompilerParams(vmem_limit_bytes=40 * MIB),
        cost_estimate=pl.CostEstimate(
            flops=6 * rows * depth * width, bytes_accessed=6 * depth * width, transcendentals=0
        ),
        name="project",
    )(*x_slots, gain, weights, weights, weights)


def place_of(order_ref, info_ref, source, slot, slots):
    z = info_ref[0]
    return order_ref[source * slots + lax.rem(z - slot + slots, slots)]


def dyn(start, size, multiple):
    return pl.ds(pl.multiple_of(start, multiple), size)


def fill_table(bias_ref, table_ref):
    left = OFF - SPAN
    right = left + MID_BLOCKS * SPAN
    table_ref[:left, :] = jnp.broadcast_to(bias_ref[MID_BLOCKS : MID_BLOCKS + 1, :BQ], (left, BQ))
    table_ref[right:, :] = jnp.broadcast_to(
        bias_ref[MID_BLOCKS + 1 : MID_BLOCKS + 2, :BQ], (TABLE_ROWS - right, BQ)
    )
    for c in range(MID_BLOCKS):
        spread = jnp.broadcast_to(bias_ref[c : c + 1, :], (SPAN, WIDE))
        rolled = pltpu.roll(spread, 0, 1, stride=1, stride_axis=0)
        table_ref[left + c * SPAN : left + (c + 1) * SPAN, :] = rolled[:, :BQ]


def block_range(ends_ref, q0, total):
    count = ends_ref.shape[0]
    start, end, cut = jnp.int32(0), jnp.int32(total), jnp.bool_(False)
    for n in range(count):
        edge = ends_ref[n]
        start = jnp.where(edge <= q0, edge, start)
        cut = cut | ((edge > q0) & (edge < q0 + BQ))
    for n in range(count - 1, -1, -1):
        edge = ends_ref[n]
        end = jnp.where(edge >= q0 + BQ, edge, end)
    first = lax.div(start, BK)
    last = lax.div(end + BK - 1, BK)
    whole = jnp.logical_not(cut) & (lax.rem(start, BK) == 0) & (lax.rem(end, BK) == 0)
    near = jnp.clip(lax.div(jnp.maximum(q0 - SPAN, 0), BK), first, last)
    beyond = jnp.clip(lax.div(q0 + BQ + SPAN + BK - 1, BK), first, last)
    return first, near, beyond, last, whole


def same_sequence(ends_ref, k0, q0, size=BK):
    key_place = k0 + lax.broadcasted_iota(jnp.int32, (size, 1), 0)
    query_place = q0 + lax.broadcasted_iota(jnp.int32, (1, BQ), 1)
    key_seg = jnp.zeros((size, 1), jnp.int32)
    query_seg = jnp.zeros((1, BQ), jnp.int32)
    for n in range(ends_ref.shape[0]):
        key_seg = key_seg + jnp.where(key_place >= ends_ref[n], 1, 0)
        query_seg = query_seg + jnp.where(query_place >= ends_ref[n], 1, 0)
    return key_seg == query_seg


def table_start(k0, q0):
    return pl.multiple_of(jnp.clip(k0 - q0, -(BK + 2 * SPAN), BQ + 2 * SPAN) + OFF, SPAN)


def sort_blocks(order_ref, info_ref, x_ref, slots, keep):
    sources = x_ref.shape[0]
    half = slots // 2
    high = jnp.logical_not(lane_low((SPAN, LANES)))
    for source in range(sources):
        for pair in range(half):
            packed = x_ref[
                source, (slots + pair) * SPAN : (slots + pair + 1) * SPAN, :
            ].astype(f32)
            queries = (swap_halves(packed), packed)
            for member in range(2):
                slot = pair + member * half
                place = place_of(order_ref, info_ref, source, slot, slots) * SPAN
                both = x_ref[source, slot * SPAN : (slot + 1) * SPAN, :]
                keep(place, both, jnp.where(high, queries[member], 0.0).astype(bf16))


def attend_kernel(
    slots, order_ref, ends_ref, info_ref, x_ref, bias_ref, mixed_ref, exact_ref, lse_ref,
    both_ref, query_ref, turned_ref, table_ref, held_ref, rows_ref,
):
    total = both_ref.shape[0]
    parted = info_ref.shape[0] > 3

    def keep(place, both, query):
        both_ref[dyn(place, SPAN, SPAN), :] = both
        query_ref[dyn(place, SPAN, SPAN), :] = query
        turned = both.astype(f32).T
        turned_ref[:, dyn(place, SPAN, SPAN)] = turned[:HD, :].astype(bf16)
        turned_key, turned_query = turned[HD:, :], query.astype(f32).T[HD:, :]
        for line, product in enumerate(
            (turned_key * turned_query, turned_key * turned_key, turned_query * turned_query)
        ):
            rows_ref[line : line + 1, dyn(place, SPAN, SPAN)] = jnp.sum(
                product, axis=0, keepdims=True
            )

    sort_blocks(order_ref, info_ref, x_ref, slots, keep)
    fill_table(bias_ref, table_ref)
    if parted:
        held_ref[...] = jnp.zeros_like(held_ref)
        exact_ref[...] = jnp.zeros_like(exact_ref)
        lse_ref[...] = jnp.zeros_like(lse_ref)
    left_bias = bias_ref[MID_BLOCKS : MID_BLOCKS + 1, :BQ]
    right_bias = bias_ref[MID_BLOCKS + 1 : MID_BLOCKS + 2, :BQ]
    start_state = (
        jnp.full((1, BQ), masked_score, f32),
        jnp.zeros((1, BQ), f32),
        jnp.zeros((HD, BQ), f32),
    )
    longest_key = jnp.sqrt(jnp.max(rows_ref[1:2, :], axis=1, keepdims=True))
    most_bias = jnp.max(
        jnp.max(bias_ref[: MID_BLOCKS + 2, :], axis=0, keepdims=True), axis=1, keepdims=True
    )

    def one_block(block, unused):
        q0 = block * BQ
        first, near, beyond, last, whole = block_range(ends_ref, q0, total)
        query = query_ref[dyn(q0, BQ, BQ), :]
        own = rows_ref[0:1, dyn(q0, BQ, BQ)] + bias_ref[1:2, 0:1]
        bound = jnp.sqrt(rows_ref[2:3, dyn(q0, BQ, BQ)]) * longest_key + most_bias
        whole = whole & (jnp.max(bound - own) < SHIFT_ROOM)

        def quick_step(kind, tile, state):
            mass, mix = state
            for part in range(BK // CH):
                k0 = tile * BK + part * CH
                scores = dot_nt(both_ref[dyn(k0, CH, CH), :], query)
                if kind == "near":
                    weights = jnp.exp(scores + table_ref[pl.ds(table_start(k0, q0), CH), :] - own)
                else:
                    weights = jnp.exp(scores - (own - (left_bias if kind == "left" else right_bias)))
                mass = mass + jnp.sum(weights, axis=0, keepdims=True)
                mix = mix + dot_nn(turned_ref[:, dyn(k0, CH, CH)], weights.astype(bf16))
            return (mass, mix)

        def step(tile, state):
            peak, mass, mix = state
            k0 = tile * BK
            scores = dot_nt(both_ref[dyn(k0, BK, BK), :], query)
            same = same_sequence(ends_ref, k0, q0)
            scores = scores + table_ref[pl.ds(table_start(k0, q0), BK), :]
            scores = jnp.where(same, scores, masked_score)
            new_peak = jnp.maximum(peak, jnp.max(scores, axis=0, keepdims=True))
            weights = jnp.where(same, jnp.exp(scores - new_peak), 0.0)
            rescale = jnp.exp(peak - new_peak)
            mass = mass * rescale + jnp.sum(weights, axis=0, keepdims=True)
            turned = turned_ref[:, dyn(k0, BK, BK)]
            mix = mix * rescale + dot_nn(turned, weights.astype(bf16))
            return (new_peak, mass, mix)

        def finish(peak, mass, mix):
            exact = mix / mass
            exact_ref[:, dyn(q0, BQ, BQ)] = exact
            lse_ref[:, dyn(q0, BQ, BQ)] = peak + jnp.log(mass)
            padded = jnp.concatenate([exact, exact], axis=0)
            held_ref[dyn(q0, BQ, BQ), :] = padded.T

        @pl.when(whole)
        def _():
            state = start_state[1:]
            state = lax.fori_loop(first, near, functools.partial(quick_step, "left"), state)
            state = lax.fori_loop(near, beyond, functools.partial(quick_step, "near"), state)
            state = lax.fori_loop(beyond, last, functools.partial(quick_step, "right"), state)
            finish(own, *state)

        @pl.when(jnp.logical_not(whole))
        def _():
            finish(*lax.fori_loop(first, last, step, start_state))

        return unused

    lax.fori_loop(info_ref[1], info_ref[2], one_block, 0)
    half = slots // 2
    low = lane_low((SPAN, LANES))
    for source in range(x_ref.shape[0]):
        for pair in range(half):
            places = [
                place_of(order_ref, info_ref, source, pair + m * half, slots) * SPAN
                for m in range(2)
            ]
            tiles = [held_ref[dyn(place, SPAN, SPAN), :] for place in places]
            mixed_ref[source, pair * SPAN : (pair + 1) * SPAN, :] = jnp.where(
                low, tiles[0], tiles[1]
            ).astype(bf16)


def vmem(shape, dtype):
    return pltpu.VMEM(shape, dtype)


def smem_spec():
    return pl.BlockSpec(memory_space=pltpu.SMEM)


def vmem_spec():
    return pl.BlockSpec(memory_space=pltpu.VMEM)


def attention_vmem(total):
    return int(min(58, 16 + 44 * (total / 16384)) * MIB)


def attend(order, ends, info, swapped, bias_rows, slots):
    sources = swapped.shape[0]
    total = sources * slots * SPAN
    return pl.pallas_call(
        functools.partial(attend_kernel, slots),
        in_specs=[smem_spec()] * 3 + [vmem_spec()] * 2,
        out_specs=[vmem_spec()] * 3,
        out_shape=[
            jax.ShapeDtypeStruct((sources, slots * SPAN // 2, LANES), bf16),
            jax.ShapeDtypeStruct((HD, total), f32),
            jax.ShapeDtypeStruct((1, total), f32),
        ],
        scratch_shapes=[
            vmem((total, LANES), bf16),
            vmem((total, LANES), bf16),
            vmem((HD, total), bf16),
            vmem((TABLE_ROWS, BQ), f32),
            vmem((total, LANES), f32),
            vmem((8, total), f32),
        ],
        compiler_params=pltpu.CompilerParams(vmem_limit_bytes=attention_vmem(total)),
        cost_estimate=pl.CostEstimate(
            flops=total * total * 128, bytes_accessed=total * 2048, transcendentals=total * total // 2
        ),
        name="attend",
    )(order, ends, info, swapped, bias_rows)


def unroll_rows(tile):
    row = lax.broadcasted_iota(jnp.int32, tile.shape, 0)
    bit = 1
    while bit < tile.shape[0]:
        moved = pltpu.roll(tile, tile.shape[1] - bit, 1)
        tile = jnp.where((row // bit) % 2 == 1, moved, tile)
        bit *= 2
    return tile


def attend_back_kernel(
    slots, bucket_count, order_ref, ends_ref, info_ref, x_ref, mixed_ref, exact_ref, lse_ref,
    bias_ref, bucket_ref, grad_ref,
    both_ref, query_ref, back_ref, turned_ref, table_ref, d_table_ref, d_both_ref, d_query_ref,
    far_ref,
):
    total = both_ref.shape[0]
    sources = x_ref.shape[0]
    half = slots // 2
    low = lane_low((SPAN, LANES))

    def keep(place, both, query):
        both_ref[dyn(place, SPAN, SPAN), :] = both
        query_ref[dyn(place, SPAN, SPAN), :] = query
        turned = both.astype(f32).T
        turned_ref[:HD, dyn(place, SPAN, SPAN)] = turned[HD:, :].astype(bf16)

    sort_blocks(order_ref, info_ref, x_ref, slots, keep)
    for source in range(sources):
        for pair in range(half):
            packed = mixed_ref[source, pair * SPAN : (pair + 1) * SPAN, :].astype(f32)
            for member, tile in enumerate((packed, swap_halves(packed))):
                place = place_of(order_ref, info_ref, source, pair + member * half, slots) * SPAN
                back_ref[dyn(place, SPAN, SPAN), :] = jnp.where(low, tile, 0.0).astype(bf16)
    fill_table(bias_ref, table_ref)
    tail = lax.broadcasted_iota(jnp.int32, (KT_ROWS - HD, total), 0)
    turned_ref[HD:, :] = jnp.where(tail == 0, 1.0, 0.0).astype(bf16)
    d_table_ref[...] = jnp.zeros_like(d_table_ref)
    d_both_ref[...] = jnp.zeros_like(d_both_ref)
    far_ref[...] = jnp.zeros_like(far_ref)
    if info_ref.shape[0] > 3:
        d_query_ref[...] = jnp.zeros_like(d_query_ref)
    left_bias = bias_ref[MID_BLOCKS : MID_BLOCKS + 1, :BQ]
    right_bias = bias_ref[MID_BLOCKS + 1 : MID_BLOCKS + 2, :BQ]

    def one_block(block, unused):
        q0 = block * BQ
        first, near, beyond, last, whole = block_range(ends_ref, q0, total)
        query = query_ref[dyn(q0, BQ, BQ), :]
        back = back_ref[dyn(q0, BQ, BQ), :]
        lse = lse_ref[:, dyn(q0, BQ, BQ)]
        turned_back = back.astype(f32).T[:HD, :]
        delta = jnp.sum(turned_back * exact_ref[:, dyn(q0, BQ, BQ)], axis=0, keepdims=True)

        def step(kind, tile, d_turned):
            for part in range(BK // CB):
                k0 = tile * BK + part * CB
                keys = dyn(k0, CB, CB)
                both = both_ref[keys, :]
                scores = dot_nt(both, query)
                if kind in ("near", "cut"):
                    rows = pl.ds(table_start(k0, q0), CB)
                    weights = jnp.exp(scores + table_ref[rows, :] - lse)
                elif kind == "left":
                    weights = jnp.exp(scores - (lse - left_bias))
                else:
                    weights = jnp.exp(scores - (lse - right_bias))
                if kind == "cut":
                    weights = jnp.where(same_sequence(ends_ref, k0, q0, CB), weights, 0.0)
                d_probs = dot_nt(both, back)
                d_scores = (weights * (d_probs - delta)).astype(bf16)
                if kind in ("near", "cut"):
                    d_table_ref[rows, :] = d_table_ref[rows, :] + d_scores.astype(f32)
                d_both_ref[keys, :] = (
                    d_both_ref[keys, :] + dot_nn(weights.astype(bf16), back) + dot_nn(d_scores, query)
                )
                d_turned = d_turned + dot_nn(turned_ref[:, keys], d_scores)
            return d_turned

        def finish(d_turned):
            top = d_turned[:HD, :]
            d_query_ref[dyn(q0, BQ, BQ), :] = jnp.concatenate([top, top], axis=0).T.astype(bf16)

        zero = jnp.zeros((KT_ROWS, BQ), f32)

        @pl.when(whole)
        def _():
            at_left = lax.fori_loop(first, near, functools.partial(step, "left"), zero)
            far_ref[0:1, :] = far_ref[0:1, :] + at_left[HD : HD + 1, :]
            at_near = lax.fori_loop(near, beyond, functools.partial(step, "near"), at_left)
            at_right = lax.fori_loop(beyond, last, functools.partial(step, "right"), zero)
            far_ref[1:2, :] = far_ref[1:2, :] + at_right[HD : HD + 1, :]
            finish(at_near + at_right)

        @pl.when(jnp.logical_not(whole))
        def _():
            finish(lax.fori_loop(first, last, functools.partial(step, "cut"), zero))

        return unused

    lax.fori_loop(info_ref[1], info_ref[2], one_block, 0)

    left = OFF - SPAN
    right = left + MID_BLOCKS * SPAN
    sums = []
    for c in range(MID_BLOCKS):
        tile = d_table_ref[left + c * SPAN : left + (c + 1) * SPAN, :]
        wide = jnp.concatenate([tile, jnp.zeros((SPAN, WIDE - BQ), f32)], axis=1)
        sums.append(jnp.sum(unroll_rows(wide), axis=0, keepdims=True))
    lefts = far_ref[0:1, :] + jnp.sum(d_table_ref[:left, :], axis=0, keepdims=True)
    rights = far_ref[1:2, :] + jnp.sum(d_table_ref[right:, :], axis=0, keepdims=True)
    blank = jnp.zeros((1, WIDE - BQ), f32)
    sums.append(jnp.concatenate([lefts, blank], axis=1))
    sums.append(jnp.concatenate([rights, blank], axis=1))
    sums = jnp.concatenate(sums, axis=0)
    buckets = bucket_ref[: MID_BLOCKS + 2, :]
    per_source = bucket_count // sources
    lane = lax.broadcasted_iota(jnp.int32, (1, LANES), 1)
    row = lax.broadcasted_iota(jnp.int32, (EXTRA, LANES), 0)
    for source in range(sources):
        line = jnp.zeros((1, LANES), f32)
        for j in range(per_source):
            picked = jnp.where(buckets == source * per_source + j, sums, 0.0)
            one = jnp.sum(jnp.sum(picked, axis=0, keepdims=True), axis=1, keepdims=True)
            line = jnp.where(lane == j, one, line)
        upper = line.astype(bf16).astype(f32)
        rest = line - upper
        grad_ref[source, 3 * half * SPAN :, :] = jnp.where(
            row == 0, upper, jnp.where(row == 1, rest, 0.0)
        ).astype(bf16)

    for source in range(sources):
        for pair in range(half):
            tiles = []
            for member in range(2):
                slot = pair + member * half
                place = place_of(order_ref, info_ref, source, slot, slots) * SPAN
                grad_ref[source, slot * SPAN : (slot + 1) * SPAN, :] = d_both_ref[
                    dyn(place, SPAN, SPAN), :
                ].astype(bf16)
                tiles.append(d_query_ref[dyn(place, SPAN, SPAN), :].astype(f32))
            grad_ref[source, (slots + pair) * SPAN : (slots + pair + 1) * SPAN, :] = jnp.where(
                low, tiles[0], tiles[1]
            ).astype(bf16)


def attend_back(
    order, ends, info, swapped, mixed_grad, exact, lse, bias_rows, bucket_rows, slots, bucket_count
):
    sources = swapped.shape[0]
    total = sources * slots * SPAN
    return pl.pallas_call(
        functools.partial(attend_back_kernel, slots, bucket_count),
        in_specs=[smem_spec()] * 3 + [vmem_spec()] * 6,
        out_specs=vmem_spec(),
        out_shape=jax.ShapeDtypeStruct((sources, slots * SPAN * 3 // 2 + EXTRA, LANES), bf16),
        scratch_shapes=[
            vmem((total, LANES), bf16),
            vmem((total, LANES), bf16),
            vmem((total, LANES), bf16),
            vmem((KT_ROWS, total), bf16),
            vmem((TABLE_ROWS, BQ), f32),
            vmem((TABLE_ROWS, BQ), f32),
            vmem((total, LANES), f32),
            vmem((total, LANES), bf16),
            vmem((8, BQ), f32),
        ],
        compiler_params=pltpu.CompilerParams(vmem_limit_bytes=attention_vmem(total)),
        cost_estimate=pl.CostEstimate(
            flops=total * total * 320, bytes_accessed=total * 3072, transcendentals=total * total // 2
        ),
        name="attend_back",
    )(order, ends, info, swapped, mixed_grad, exact, lse, bias_rows, bucket_rows)


def out_kernel(slots, packed_ref, weight_ref, mix_ref, *part_refs):
    heads = packed_ref.shape[0]
    half = slots * SPAN // 2

    @pl.when(pl.program_id(0) == 0)
    def _():
        for pair in range(heads // 2):
            first = packed_ref[2 * pair].astype(f32)
            second = packed_ref[2 * pair + 1].astype(f32)
            top, bottom = pair_up(first, second)
            cols = slice(pair * LANES, (pair + 1) * LANES)
            mix_ref[:half, cols] = top.astype(bf16)
            mix_ref[half:, cols] = bottom.astype(bf16)

    part = dot_nn(mix_ref[...], weight_ref[...]).astype(bf16)
    for s in range(slots):
        part_refs[s][...] = part[s * SPAN : (s + 1) * SPAN]


def out_project(packed, weight, slots):
    heads = packed.shape[0]
    rows, width, depth = slots * SPAN, heads * HD, weight.shape[1]
    tile = 512
    return pl.pallas_call(
        functools.partial(out_kernel, slots),
        grid=(depth // tile,),
        in_specs=[
            pl.BlockSpec(packed.shape, lambda j: (0, 0, 0)),
            pl.BlockSpec((width, tile), lambda j: (0, j)),
        ],
        out_specs=[
            pl.BlockSpec((rows, width), lambda j: (0, 0)),
        ]
        + [pl.BlockSpec((SPAN, tile), lambda j: (0, j))] * slots,
        out_shape=[jax.ShapeDtypeStruct((rows, width), bf16)]
        + [jax.ShapeDtypeStruct((SPAN, depth), bf16)] * slots,
        compiler_params=pltpu.CompilerParams(vmem_limit_bytes=40 * MIB),
        cost_estimate=pl.CostEstimate(
            flops=2 * rows * depth * width, bytes_accessed=4 * depth * width, transcendentals=0
        ),
        name="out_project",
    )(packed, weight)


def feed_kernel(slots, *refs):
    normed_refs, grad_refs = refs[:slots], refs[slots : 2 * slots]
    gate_ref, up_ref, down_ref, rows_ref, rows_grad_ref, active_ref, d_both_ref = refs[2 * slots :]

    @pl.when(pl.program_id(0) == 0)
    def _():
        for s in range(slots):
            rows_ref[s * SPAN : (s + 1) * SPAN, :] = normed_refs[s][...]
            rows_grad_ref[s * SPAN : (s + 1) * SPAN, :] = grad_refs[s][...]

    tile = down_ref.shape[0]
    width = d_both_ref.shape[1] // 2
    gate = dot_nn(rows_ref[...], gate_ref[...])
    up = dot_nn(rows_ref[...], up_ref[...])
    d_hidden = dot_nt(rows_grad_ref[...], down_ref[...])
    scale, cubic = 0.7978845608028654, 0.044715
    square = gate * gate
    bent = jnp.tanh(scale * (gate + cubic * square * gate))
    half = 0.5 * (1.0 + bent)
    gelu = gate * half
    slope = half + 0.5 * gate * (1.0 - bent * bent) * (scale * (1.0 + 3.0 * cubic * square))
    active_ref[...] = (gelu * up).astype(bf16)
    start = pl.program_id(0) * tile
    d_both_ref[:, dyn(start, tile, tile)] = (d_hidden * up * slope).astype(bf16)
    d_both_ref[:, dyn(width + start, tile, LANES)] = (d_hidden * gelu).astype(bf16)


def feed_tile(width):
    return 256 if width % 256 == 0 else 128


def feed(normed_slots, grad_slots, both, down):
    slots = len(normed_slots)
    rows, depth, width = slots * SPAN, both.shape[0], both.shape[1] // 2
    tile = feed_tile(width)
    steps = width // tile
    whole = pl.BlockSpec((SPAN, depth), lambda j: (0, 0))
    rows_spec = pl.BlockSpec((rows, depth), lambda j: (0, 0))
    return pl.pallas_call(
        functools.partial(feed_kernel, slots),
        grid=(steps,),
        in_specs=[whole] * (2 * slots)
        + [
            pl.BlockSpec((depth, tile), lambda j: (0, j)),
            pl.BlockSpec((depth, tile), lambda j: (0, steps + j)),
            pl.BlockSpec((tile, depth), lambda j: (j, 0)),
        ],
        out_specs=[
            rows_spec,
            rows_spec,
            pl.BlockSpec((rows, tile), lambda j: (0, j)),
            pl.BlockSpec((rows, 2 * width), lambda j: (0, 0)),
        ],
        out_shape=[
            jax.ShapeDtypeStruct((rows, depth), bf16),
            jax.ShapeDtypeStruct((rows, depth), bf16),
            jax.ShapeDtypeStruct((rows, width), bf16),
            jax.ShapeDtypeStruct((rows, 2 * width), bf16),
        ],
        compiler_params=pltpu.CompilerParams(vmem_limit_bytes=56 * MIB),
        cost_estimate=pl.CostEstimate(
            flops=6 * rows * depth * width,
            bytes_accessed=6 * depth * width,
            transcendentals=rows * width,
        ),
        name="feed",
    )(*normed_slots, *grad_slots, both, both, down)


def pack_kernel(slots, *refs):
    packed_ref = refs[slots]
    half = slots // 2
    for pair in range(packed_ref.shape[0] // 2):
        cols = slice(pair * LANES, (pair + 1) * LANES)
        for s in range(half):
            span = slice(s * SPAN, (s + 1) * SPAN)
            first, second = (refs[s + m * half][:, cols].astype(f32) for m in range(2))
            for member, tile in enumerate(pair_up(first, second)):
                packed_ref[2 * pair + member, span, :] = tile.astype(bf16)


def pack(parts):
    slots = len(parts)
    heads = parts[0].shape[1] // HD
    return pl.pallas_call(
        functools.partial(pack_kernel, slots),
        in_specs=[vmem_spec()] * slots,
        out_specs=vmem_spec(),
        out_shape=jax.ShapeDtypeStruct((heads, slots * SPAN // 2, LANES), bf16),
        compiler_params=pltpu.CompilerParams(vmem_limit_bytes=16 * MIB),
        name="pack",
    )(*parts)


def project_back_kernel(slots, packed_ref, weight_ref, scale_ref, *refs):
    x_refs = refs[:slots]
    grads_ref, gain_ref, *part_refs = refs[slots:]
    heads = packed_ref.shape[0]
    rows = slots * SPAN
    half = rows // 2
    width = heads * HD

    @pl.when(pl.program_id(0) == 0)
    def _():
        for pair in range(heads // 2):
            start = pair * LANES
            tiles = [packed_ref[2 * pair + m].astype(f32) for m in range(2)]
            value, key = pair_up(tiles[0][:rows], tiles[1][:rows])
            top, bottom = pair_up(tiles[0][rows : rows + half], tiles[1][rows : rows + half])
            grads_ref[:half, start : start + LANES] = top.astype(bf16)
            grads_ref[half:, start : start + LANES] = bottom.astype(bf16)
            grads_ref[:, width + start : width + start + LANES] = key.astype(bf16)
            grads_ref[:, 2 * width + start : 2 * width + start + LANES] = value.astype(bf16)

    part = dot_nt(grads_ref[...], weight_ref[...])
    gain = jnp.zeros((1, part.shape[1]), f32)
    for s in range(slots):
        span = slice(s * SPAN, (s + 1) * SPAN)
        part_refs[s][...] = part[span].astype(bf16)
        x_hat = x_refs[s][...].astype(f32) * scale_ref[span, :1]
        gain = gain + jnp.sum(part[span] * x_hat, axis=0, keepdims=True)
    gain_ref[...] = gain


def project_back(packed, weights, scale, x_slots):
    slots = len(x_slots)
    heads = packed.shape[0]
    depth, width = weights.shape
    rows = slots * SPAN
    tile = 512
    return pl.pallas_call(
        functools.partial(project_back_kernel, slots),
        grid=(depth // tile,),
        in_specs=[
            pl.BlockSpec(packed.shape, lambda j: (0, 0, 0)),
            pl.BlockSpec((tile, width), lambda j: (j, 0)),
            pl.BlockSpec((rows, LANES), lambda j: (0, 0)),
        ]
        + [pl.BlockSpec((SPAN, tile), lambda j: (0, j))] * slots,
        out_specs=[
            pl.BlockSpec((rows, width), lambda j: (0, 0)),
            pl.BlockSpec((1, tile), lambda j: (0, j)),
        ]
        + [pl.BlockSpec((SPAN, tile), lambda j: (0, j))] * slots,
        out_shape=[
            jax.ShapeDtypeStruct((rows, width), bf16),
            jax.ShapeDtypeStruct((1, depth), f32),
        ]
        + [jax.ShapeDtypeStruct((SPAN, depth), bf16)] * slots,
        compiler_params=pltpu.CompilerParams(vmem_limit_bytes=40 * MIB),
        cost_estimate=pl.CostEstimate(
            flops=2 * rows * depth * width, bytes_accessed=2 * depth * width, transcendentals=0
        ),
        name="project_back",
    )(packed, weights, scale, *x_slots)


def pair_kernel(left_one_ref, right_one_ref, left_two_ref, right_two_ref, out_ref):
    cut = right_one_ref.shape[1]
    out_ref[:, :cut] = dot_tn(left_one_ref[...], right_one_ref[...]).astype(bf16)
    out_ref[:, cut:] = dot_tn(left_two_ref[...], right_two_ref[...]).astype(bf16)


def pair_product(left_one, right_one, left_two, right_two):
    rows, depth = left_one.shape
    width = right_one.shape[1] + right_two.shape[1]
    block = 256

    def left():
        return pl.BlockSpec((rows, block), lambda j: (0, j))

    def right(array):
        return pl.BlockSpec(array.shape, lambda j: (0, 0))

    return pl.pallas_call(
        pair_kernel,
        grid=(depth // block,),
        in_specs=[left(), right(right_one), left(), right(right_two)],
        out_specs=pl.BlockSpec((block, width), lambda j: (j, 0)),
        out_shape=jax.ShapeDtypeStruct((depth, width), bf16),
        compiler_params=pltpu.CompilerParams(vmem_limit_bytes=32 * MIB),
        cost_estimate=pl.CostEstimate(
            flops=2 * rows * depth * width, bytes_accessed=2 * depth * width, transcendentals=0
        ),
        name="pair_product",
    )(left_one, right_one, left_two, right_two)


def bucket_lines(bucket_of):
    count = bucket_of.shape[0]
    turned = bucket_of[::-1]
    pad = 5 * WIDE // 4
    padded = jnp.concatenate(
        [
            jnp.broadcast_to(turned[:1], (pad,)),
            turned,
            jnp.broadcast_to(turned[-1:], (pad,)),
        ]
    )
    zero_at = pad + count // 2
    keep = BQ + HD
    rows = []
    for c in range(MID_BLOCKS):
        base = zero_at - (c - 1) * SPAN
        rows.append(
            jnp.concatenate([padded[base : base + keep], padded[base - (WIDE - keep) : base]])
        )
    rows.append(jnp.broadcast_to(bucket_of[:1], (WIDE,)))
    rows.append(jnp.broadcast_to(bucket_of[-1:], (WIDE,)))
    spare = 8 * ((MID_BLOCKS + 2 + 7) // 8) - (MID_BLOCKS + 2)
    return jnp.concatenate([jnp.stack(rows), jnp.full((spare, WIDE), -1, bucket_of.dtype)])


def on_device(
    tokens,
    lengths,
    block_order,
    bucket_of,
    gain_attn,
    w_query,
    w_key,
    w_value,
    w_out,
    bias_table,
    gain_ffn,
    w_gate,
    w_up,
    w_down,
    cotangent,
):
    blk_count, slots = lax.axis_size("blk"), lax.axis_size("head")
    blk_spot, head_spot = lax.axis_index("blk"), lax.axis_index("head")
    depth = tokens.shape[1]
    width = w_query.shape[1]
    heads = width // HD
    shares = blk_count // heads
    table_rows, table_heads = bias_table.shape
    bucket_count = table_rows * blk_count
    total = blk_count * slots * SPAN
    gain_size = gain_attn.shape[0]
    hidden = w_gate.shape[1]

    token_slots = gather_far(gather_near(tokens))
    small = gather_small(
        jnp.concatenate([gain_attn, gain_ffn, bias_table.astype(f32).reshape(-1)])
    )
    full_qkv = lax.all_gather(
        jnp.concatenate([w_query, w_key, w_value], axis=1), "blk", axis=0, tiled=True
    )
    full_out = lax.all_gather(w_out, "blk", axis=1, tiled=True)
    full_both = lax.all_gather(
        jnp.concatenate([w_gate, w_up], axis=1), "blk", axis=0, tiled=True
    )
    full_down = lax.all_gather(w_down, "blk", axis=1, tiled=True)
    gain_one = small[:, :, :gain_size].reshape(1, depth)
    gain_two = small[:, :, gain_size : 2 * gain_size].reshape(1, depth)

    tables = lax.dynamic_index_in_dim(small, head_spot, 1, False)[:, 2 * gain_size :]
    tables = tables.reshape(bucket_count, table_heads)
    my_head = blk_spot // shares
    my_bias = lax.dynamic_index_in_dim(tables, my_head, 1, False)
    bucket_rows = bucket_lines(bucket_of)
    bias_rows = jnp.sum(
        jnp.where(
            bucket_rows[None] == jnp.arange(bucket_count, dtype=jnp.int32)[:, None, None],
            my_bias[:, None, None],
            0.0,
        ),
        axis=0,
    )
    ends = jnp.cumsum(lengths).astype(jnp.int32)
    per_share = total // BQ // shares
    start = (blk_spot % shares) * per_share
    info = [head_spot, start, start + per_share] + ([start] if shares > 1 else [])
    info = jnp.stack([jnp.asarray(item, jnp.int32) for item in info])

    def swap(values):
        return lax.all_to_all(values, "blk", 0, 0, tiled=True)

    def to_heads(values):
        return swap(values if shares == 1 else jnp.repeat(values, shares, axis=0))

    def to_rows(values):
        values = swap(values)
        if shares == 1:
            return values
        values = values.reshape((heads, shares) + values.shape[1:])
        return jnp.sum(values.astype(f32), axis=1).astype(bf16)

    w_out, cotangent, *token_slots = together(w_out, cotangent, *token_slots)
    normed_one, packed, scale_one = project(token_slots, gain_one, full_qkv)
    early = (ends, info, bias_rows, bucket_rows)
    swapped, ends, info, bias_rows, bucket_rows, *out_near = together(
        to_heads(packed), *early, *gather_near(w_out)
    )
    grad_near, out_slots = gather_near(cotangent), gather_far(out_near)
    mixed, exact, lse = attend(block_order, ends, info, swapped, bias_rows, slots)
    mixed, *moved = together(mixed, *grad_near, *out_slots)
    grad_near, out_slots = moved[: len(grad_near)], moved[len(grad_near) :]
    packed_mix, *moved = together(to_rows(mixed), *gather_far(grad_near), *out_slots)
    grad_slots, out_slots = moved[:slots], moved[slots:]
    full_rest = lax.all_gather(jnp.concatenate(out_slots[1:]), "blk", axis=1, tiled=True)
    attn_mix, *out_parts = out_project(packed_mix, full_out, slots)
    tokens_wide = tokens.astype(f32)
    hidden_one = tokens_wide + sum_terms(sum_near(out_parts, sum_far(out_parts))[0])
    rstd_two = rms_scale(hidden_one)
    normed_two = (hidden_one * rstd_two * gain_two).astype(bf16)

    normed_slots = gather_far(gather_near(normed_two))
    rows_two, rows_grad, active, d_both = feed(normed_slots, grad_slots, full_both, full_down)

    def spans(rows):
        return [rows[s * SPAN : (s + 1) * SPAN] for s in range(slots)]

    d_parts = spans(dot_nt(d_both, full_both).astype(bf16))
    d_far = sum_far(d_parts)
    grad_both, full_rest, *d_far = together(
        dot_tn(rows_two, d_both).astype(bf16), full_rest, *d_far
    )
    grad_both = lax.psum_scatter(grad_both, "blk", scatter_dimension=0, tiled=True)
    d_near, (active,) = sum_near(d_parts, d_far, (active,))
    grad_down, down_parts, *d_near = together(
        dot_tn(active, rows_grad).astype(bf16), dot_nn(active, full_down).astype(bf16), *d_near
    )
    grad_down = lax.psum_scatter(grad_down, "blk", scatter_dimension=1, tiled=True)
    down_parts = spans(down_parts)
    d_normed_two = sum_terms(d_near)
    d_source_two, gain_part_two = norm_back(d_normed_two, hidden_one, rstd_two, gain_two)
    d_hidden_one = cotangent.astype(f32) + d_source_two

    d_attn = d_hidden_one.astype(bf16)
    mix_parts = [dot_nt(d_attn, full_out).astype(bf16)]
    mix_rest = dot_nt(d_attn, full_rest).astype(bf16)
    mix_parts += [mix_rest[:, s * width : (s + 1) * width] for s in range(slots - 1)]
    mix_grads, d_attn = together(pack(exchange(mix_parts)), d_attn)
    middle = slots // 2
    steps = [t for t in range(1, slots) if t != middle]
    moved = (*gather_near(d_attn), *sum_direct(down_parts, steps))
    grads = attend_back(
        block_order, ends, info, swapped, to_heads(mix_grads), exact, lse, bias_rows, bucket_rows,
        slots, bucket_count,
    )
    grads, grad_both, *moved = together(grads, grad_both, *moved)
    attn_near, down_terms = moved[: 2 - slots], moved[2 - slots :]
    grads, *attn_slots = together(swap(grads), *gather_far(attn_near))
    rows_attn = jnp.concatenate(attn_slots)
    extra = grads[:, -EXTRA : -EXTRA + 2, :table_rows].astype(f32).sum(axis=1)
    grad_table = extra.reshape(heads, shares, table_rows).sum(axis=1).T
    if shares > 1:
        grads = grads.reshape((heads, shares) + grads.shape[1:])
        grads = jnp.sum(grads.astype(f32), axis=1).astype(bf16)
    d_qkv, gain_part_one, *one_parts = project_back(grads, full_qkv, scale_one, token_slots)

    one_far = sum_far(one_parts)
    gain_parts = jnp.stack(
        [part.reshape(blk_count, slots, gain_size) for part in (gain_part_one, gain_part_two)],
        axis=2,
    )
    d_qkv, grad_down = together(d_qkv, grad_down)
    grad_heads = pair_product(normed_one, d_qkv, rows_attn, attn_mix)
    grad_heads, gain_parts, *one_far = together(grad_heads, gain_parts, *one_far)
    grad_heads = lax.psum_scatter(grad_heads, "blk", scatter_dimension=0, tiled=True).astype(f32)
    one_near, unused = sum_near(one_parts, one_far)
    gain_sums = scatter_blk(gain_parts)
    gain_sums, down_parts, grad_both, grad_down, *one_near = together(
        gain_sums, down_parts, grad_both, grad_down, *one_near
    )
    gain_sums = scatter_head(gain_sums)
    grad_both = grad_both.astype(f32)
    output = hidden_one + sum_all([down_parts[0]] + down_terms + sum_direct(down_parts, [middle]))
    d_normed_one = sum_terms(one_near)
    d_source_one, unused = norm_back(d_normed_one, tokens_wide, rms_scale(tokens_wide), gain_one)
    input_grad = d_hidden_one + d_source_one
    return (
        output,
        input_grad,
        gain_sums[0],
        grad_heads[:, :width],
        grad_heads[:, width : 2 * width],
        grad_heads[:, 2 * width : 3 * width],
        grad_heads[:, 3 * width :].T,
        grad_table,
        gain_sums[1],
        grad_both[:, :hidden],
        grad_both[:, hidden:],
        grad_down.astype(f32),
    )


def solution(mesh):
    rows, spread = P(("blk", "head"), None), P(("blk", "head"))
    inward, outward = P("blk", "head"), P("head", "blk")
    in_specs = (
        rows, P(), P(), P(), spread, inward, inward, inward, outward, inward, spread,
        inward, inward, outward, rows,
    )
    out_specs = (
        rows, rows, spread, inward, inward, inward, outward, inward, spread,
        inward, inward, outward,
    )
    return jax.shard_map(
        on_device, mesh=mesh, in_specs=in_specs, out_specs=out_specs, check_vma=False
    )
```

```python
import functools

import jax
import jax.numpy as jnp
import numpy as np
from jax import lax
from jax.experimental import pallas as pl
from jax.experimental.pallas import tpu as pltpu
from jax.sharding import PartitionSpec as P

HD = 64
LANES = 2 * HD
MAXDIST = 128
SPAN = 128
BQ = 512
BK = 512
OFF = BK + 2 * SPAN
TABLE_ROWS = 2 * BK + BQ + 4 * SPAN
MID_BLOCKS = BQ // SPAN + 2
WIDE = 2 * BQ
EXTRA = 16
KT_ROWS = 80
SHIFT_ROOM = 60.0
CH = 512
CB = 256

norm_eps = 1e-06
masked_score = -1e30
f32 = jnp.float32
bf16 = jnp.bfloat16
MIB = 1 << 20
LARGE = 58 * MIB


def rms_scale(values):
    return lax.rsqrt(jnp.mean(values * values, axis=-1, keepdims=True) + norm_eps)


def norm_back(d_normed, source, inv_rms, gain_vec):
    scaled = d_normed * gain_vec
    x_hat = source * inv_rms
    gain_part = jnp.sum(d_normed * x_hat, axis=0)
    d_source = inv_rms * (scaled - x_hat * jnp.mean(scaled * x_hat, axis=-1, keepdims=True))
    return (d_source, gain_part)


def dot_nn(left, right):
    return jnp.dot(left, right, preferred_element_type=f32)


def dot_nt(left, right):
    return lax.dot_general(left, right, (((1,), (1,)), ((), ())), preferred_element_type=f32)


def dot_tn(left, right):
    return lax.dot_general(left, right, (((0,), (0,)), ((), ())), preferred_element_type=f32)


def cyclic(count, by):
    return [(i, (i + by) % count) for i in range(count)]


def together(*values):
    return lax.optimization_barrier(values)


def gather_near(rows):
    count = lax.axis_size("head")
    if count != 4:
        return [rows] + [lax.ppermute(rows, "head", cyclic(count, s)) for s in range(1, count)]
    return [rows, lax.ppermute(rows, "head", cyclic(4, 1)), lax.ppermute(rows, "head", cyclic(4, 3))]


def gather_far(near):
    if lax.axis_size("head") != 4:
        return near
    rows, back_one, ahead_one = near
    me = lax.axis_index("head")
    passed = jnp.where(me == 1, ahead_one, jnp.where(me == 2, back_one, rows))
    back_two = lax.ppermute(passed, "head", [(1, 0), (3, 1), (0, 2), (2, 3)])
    return [rows, back_one, back_two, ahead_one]


def gather_direct(rows):
    count = lax.axis_size("head")
    return [rows] + [lax.ppermute(rows, "head", cyclic(count, s)) for s in range(1, count)]


def sum_far(parts):
    count = lax.axis_size("head")
    if count != 4:
        return []
    return [lax.ppermute(parts[2], "head", [(0, 1), (1, 3), (2, 0), (3, 2)])]


def sum_near(parts, far, beside=()):
    count = lax.axis_size("head")
    if count != 4:
        return [parts[0]] + [
            lax.ppermute(parts[s], "head", cyclic(count, count - s)) for s in range(1, count)
        ], beside
    me = lax.axis_index("head")
    wide = far[0].astype(f32)
    to_back = jnp.where(me == 2, parts[1].astype(f32) + wide, parts[1].astype(f32)).astype(bf16)
    to_ahead = jnp.where(me == 1, parts[3].astype(f32) + wide, parts[3].astype(f32)).astype(bf16)
    to_back, to_ahead, *beside = together(to_back, to_ahead, *beside)
    from_ahead = lax.ppermute(to_back, "head", cyclic(4, 3))
    from_back = lax.ppermute(to_ahead, "head", cyclic(4, 1))
    return [parts[0], from_ahead, from_back, far[0]], beside


def sum_terms(terms):
    total = terms[0].astype(f32) + terms[1].astype(f32) + terms[2].astype(f32)
    if lax.axis_size("head") != 4:
        for term in terms[3:]:
            total = total + term.astype(f32)
        return total
    me = lax.axis_index("head")
    return total + jnp.where((me == 0) | (me == 3), terms[3].astype(f32), 0.0)


def is_power(count):
    return count & (count - 1) == 0


def gather_small(values):
    held = values[None]
    for axis in ("head", "blk"):
        count = lax.axis_size(axis)
        if not is_power(count):
            held = lax.all_gather(held, axis, axis=0, tiled=False)
        else:
            me = lax.axis_index(axis)
            held = held[None]
            bit = 1
            while bit < count:
                other = lax.ppermute(held, axis, [(i, i ^ bit) for i in range(count)])
                low = jnp.concatenate([held, other])
                high = jnp.concatenate([other, held])
                held = jnp.where((me // bit) % 2 == 0, low, high)
                bit *= 2
        if axis == "head":
            held = held.reshape(count, -1)
    return held


def exchange(parts):
    count = len(parts)
    return [parts[0]] + [
        lax.ppermute(parts[count - s], "head", cyclic(count, s)) for s in range(1, count)
    ]


def sum_direct(parts, steps):
    count = len(parts)
    return [lax.ppermute(parts[s], "head", cyclic(count, count - s)) for s in steps]


def sum_all(terms):
    total = terms[0].astype(f32)
    for term in terms[1:]:
        total = total + term.astype(f32)
    return total


def scatter_blk(values):
    return jnp.sum(lax.all_to_all(values, "blk", 0, 0, tiled=True), axis=0)


def scatter_head(values):
    count, me = lax.axis_size("head"), lax.axis_index("head")
    total = lax.dynamic_index_in_dim(values, me, 0, False)
    for s in range(1, count):
        sent = lax.dynamic_index_in_dim(values, (me + s) % count, 0, False)
        total = total + lax.ppermute(sent, "head", cyclic(count, s))
    return total


def lane_low(shape):
    return lax.broadcasted_iota(jnp.int32, shape, 1) < HD


def swap_halves(tile):
    return pltpu.roll(tile, HD, 1)


def pair_up(first, second):
    low = lane_low(first.shape)
    return (
        jnp.where(low, first, swap_halves(second)),
        jnp.where(low, swap_halves(first), second),
    )


def project_kernel(slots, *refs):
    x_refs = refs[:slots]
    gain_ref, wq_ref, wk_ref, wv_ref, normed_ref, packed_ref, scale_ref = refs[slots:]
    rows = slots * SPAN

    @pl.when(pl.program_id(0) == 0)
    def _():
        for s in range(slots):
            wide = x_refs[s][...].astype(f32)
            scale = rms_scale(wide)
            normed = wide * scale * gain_ref[...]
            normed_ref[s * SPAN : (s + 1) * SPAN, :] = normed.astype(bf16)
            scale_ref[s * SPAN : (s + 1) * SPAN, :] = jnp.broadcast_to(scale, (SPAN, LANES))

    normed = normed_ref[...]
    query = dot_nn(normed, wq_ref[...])
    key = dot_nn(normed, wk_ref[...])
    value = dot_nn(normed, wv_ref[...])
    half = rows // 2
    for pair in range(query.shape[1] // LANES):
        cols = slice(pair * LANES, (pair + 1) * LANES)
        both = pair_up(value[:, cols], key[:, cols])
        queries = pair_up(query[:half, cols], query[half:, cols])
        for member in range(2):
            packed_ref[2 * pair + member, :rows, :] = both[member].astype(bf16)
            packed_ref[2 * pair + member, rows:, :] = queries[member].astype(bf16)


def project(x_slots, gain, weights):
    slots = len(x_slots)
    rows, depth = slots * SPAN, x_slots[0].shape[1]
    width = weights.shape[1] // 3
    heads = width // HD
    tile = min(width, 256)
    steps = width // tile
    whole = pl.BlockSpec((SPAN, depth), lambda j: (0, 0))

    def columns(part):
        return pl.BlockSpec((depth, tile), lambda j: (0, part * steps + j))

    return pl.pallas_call(
        functools.partial(project_kernel, slots),
        grid=(steps,),
        in_specs=[whole] * slots
        + [pl.BlockSpec((1, depth), lambda j: (0, 0)), columns(0), columns(1), columns(2)],
        out_specs=[
            pl.BlockSpec((rows, depth), lambda j: (0, 0)),
            pl.BlockSpec((tile // HD, rows + rows // 2, LANES), lambda j: (j, 0, 0)),
            pl.BlockSpec((rows, LANES), lambda j: (0, 0)),
        ],
        out_shape=[
            jax.ShapeDtypeStruct((rows, depth), bf16),
            jax.ShapeDtypeStruct((heads, rows + rows // 2, LANES), bf16),
            jax.ShapeDtypeStruct((rows, LANES), f32),
        ],
        compiler_params=pltpu.CompilerParams(vmem_limit_bytes=40 * MIB),
        cost_estimate=pl.CostEstimate(
            flops=10 * rows * depth * width, bytes_accessed=6 * depth * width, transcendentals=0
        ),
        name="project",
    )(*x_slots, gain, weights, weights, weights)


def place_of(order_ref, info_ref, source, slot, slots):
    z = info_ref[0]
    return order_ref[source * slots + lax.rem(z - slot + slots, slots)]


def dyn(start, size, multiple):
    return pl.ds(pl.multiple_of(start, multiple), size)


def fill_table(bias_ref, table_ref):
    left = OFF - SPAN
    right = left + MID_BLOCKS * SPAN
    table_ref[:left, :] = jnp.broadcast_to(bias_ref[MID_BLOCKS : MID_BLOCKS + 1, :BQ], (left, BQ))
    table_ref[right:, :] = jnp.broadcast_to(
        bias_ref[MID_BLOCKS + 1 : MID_BLOCKS + 2, :BQ], (TABLE_ROWS - right, BQ)
    )
    for c in range(MID_BLOCKS):
        spread = jnp.broadcast_to(bias_ref[c : c + 1, :], (SPAN, WIDE))
        rolled = pltpu.roll(spread, 0, 1, stride=1, stride_axis=0)
        table_ref[left + c * SPAN : left + (c + 1) * SPAN, :] = rolled[:, :BQ]


def block_range(ends_ref, q0, total):
    count = ends_ref.shape[0]
    start, end, cut = jnp.int32(0), jnp.int32(total), jnp.bool_(False)
    for n in range(count):
        edge = ends_ref[n]
        start = jnp.where(edge <= q0, edge, start)
        cut = cut | ((edge > q0) & (edge < q0 + BQ))
    for n in range(count - 1, -1, -1):
        edge = ends_ref[n]
        end = jnp.where(edge >= q0 + BQ, edge, end)
    first = lax.div(start, BK)
    last = lax.div(end + BK - 1, BK)
    whole = jnp.logical_not(cut) & (lax.rem(start, BK) == 0) & (lax.rem(end, BK) == 0)
    near = jnp.clip(lax.div(jnp.maximum(q0 - SPAN, 0), BK), first, last)
    beyond = jnp.clip(lax.div(q0 + BQ + SPAN + BK - 1, BK), first, last)
    return first, near, beyond, last, whole


def same_sequence(ends_ref, k0, q0, size=BK):
    key_place = k0 + lax.broadcasted_iota(jnp.int32, (size, 1), 0)
    query_place = q0 + lax.broadcasted_iota(jnp.int32, (1, BQ), 1)
    key_seg = jnp.zeros((size, 1), jnp.int32)
    query_seg = jnp.zeros((1, BQ), jnp.int32)
    for n in range(ends_ref.shape[0]):
        key_seg = key_seg + jnp.where(key_place >= ends_ref[n], 1, 0)
        query_seg = query_seg + jnp.where(query_place >= ends_ref[n], 1, 0)
    return key_seg == query_seg


def table_start(k0, q0):
    return pl.multiple_of(jnp.clip(k0 - q0, -(BK + 2 * SPAN), BQ + 2 * SPAN) + OFF, SPAN)


def sort_blocks(order_ref, info_ref, x_ref, slots, keep):
    sources = x_ref.shape[0]
    half = slots // 2
    high = jnp.logical_not(lane_low((SPAN, LANES)))
    for source in range(sources):
        for pair in range(half):
            packed = x_ref[
                source, (slots + pair) * SPAN : (slots + pair + 1) * SPAN, :
            ].astype(f32)
            queries = (swap_halves(packed), packed)
            for member in range(2):
                slot = pair + member * half
                place = place_of(order_ref, info_ref, source, slot, slots) * SPAN
                both = x_ref[source, slot * SPAN : (slot + 1) * SPAN, :]
                keep(place, both, jnp.where(high, queries[member], 0.0).astype(bf16))


def attend_kernel(
    slots, order_ref, ends_ref, info_ref, x_ref, bias_ref, mixed_ref, exact_ref, lse_ref,
    both_ref, query_ref, turned_ref, table_ref, held_ref, rows_ref,
):
    total = both_ref.shape[0]
    parted = info_ref.shape[0] > 3

    def keep(place, both, query):
        both_ref[dyn(place, SPAN, SPAN), :] = both
        query_ref[dyn(place, SPAN, SPAN), :] = query
        turned = both.astype(f32).T
        turned_ref[:, dyn(place, SPAN, SPAN)] = turned[:HD, :].astype(bf16)
        turned_key, turned_query = turned[HD:, :], query.astype(f32).T[HD:, :]
        for line, product in enumerate(
            (turned_key * turned_query, turned_key * turned_key, turned_query * turned_query)
        ):
            rows_ref[line : line + 1, dyn(place, SPAN, SPAN)] = jnp.sum(
                product, axis=0, keepdims=True
            )

    sort_blocks(order_ref, info_ref, x_ref, slots, keep)
    fill_table(bias_ref, table_ref)
    if parted:
        held_ref[...] = jnp.zeros_like(held_ref)
        exact_ref[...] = jnp.zeros_like(exact_ref)
        lse_ref[...] = jnp.zeros_like(lse_ref)
    left_bias = bias_ref[MID_BLOCKS : MID_BLOCKS + 1, :BQ]
    right_bias = bias_ref[MID_BLOCKS + 1 : MID_BLOCKS + 2, :BQ]
    start_state = (
        jnp.full((1, BQ), masked_score, f32),
        jnp.zeros((1, BQ), f32),
        jnp.zeros((HD, BQ), f32),
    )
    longest_key = jnp.sqrt(jnp.max(rows_ref[1:2, :], axis=1, keepdims=True))
    most_bias = jnp.max(
        jnp.max(bias_ref[: MID_BLOCKS + 2, :], axis=0, keepdims=True), axis=1, keepdims=True
    )

    def one_block(block, unused):
        q0 = block * BQ
        first, near, beyond, last, whole = block_range(ends_ref, q0, total)
        query = query_ref[dyn(q0, BQ, BQ), :]
        own = rows_ref[0:1, dyn(q0, BQ, BQ)] + bias_ref[1:2, 0:1]
        bound = jnp.sqrt(rows_ref[2:3, dyn(q0, BQ, BQ)]) * longest_key + most_bias
        whole = whole & (jnp.max(bound - own) < SHIFT_ROOM)

        def quick_step(kind, tile, state):
            mass, mix = state
            for part in range(BK // CH):
                k0 = tile * BK + part * CH
                scores = dot_nt(both_ref[dyn(k0, CH, CH), :], query)
                if kind == "near":
                    weights = jnp.exp(scores + table_ref[pl.ds(table_start(k0, q0), CH), :] - own)
                else:
                    weights = jnp.exp(scores - (own - (left_bias if kind == "left" else right_bias)))
                mass = mass + jnp.sum(weights, axis=0, keepdims=True)
                mix = mix + dot_nn(turned_ref[:, dyn(k0, CH, CH)], weights.astype(bf16))
            return (mass, mix)

        def step(tile, state):
            peak, mass, mix = state
            k0 = tile * BK
            scores = dot_nt(both_ref[dyn(k0, BK, BK), :], query)
            same = same_sequence(ends_ref, k0, q0)
            scores = scores + table_ref[pl.ds(table_start(k0, q0), BK), :]
            scores = jnp.where(same, scores, masked_score)
            new_peak = jnp.maximum(peak, jnp.max(scores, axis=0, keepdims=True))
            weights = jnp.where(same, jnp.exp(scores - new_peak), 0.0)
            rescale = jnp.exp(peak - new_peak)
            mass = mass * rescale + jnp.sum(weights, axis=0, keepdims=True)
            turned = turned_ref[:, dyn(k0, BK, BK)]
            mix = mix * rescale + dot_nn(turned, weights.astype(bf16))
            return (new_peak, mass, mix)

        def finish(peak, mass, mix):
            exact = mix / mass
            exact_ref[:, dyn(q0, BQ, BQ)] = exact
            lse_ref[:, dyn(q0, BQ, BQ)] = peak + jnp.log(mass)
            padded = jnp.concatenate([exact, exact], axis=0)
            held_ref[dyn(q0, BQ, BQ), :] = padded.T

        @pl.when(whole)
        def _():
            state = start_state[1:]
            state = lax.fori_loop(first, near, functools.partial(quick_step, "left"), state)
            state = lax.fori_loop(near, beyond, functools.partial(quick_step, "near"), state)
            state = lax.fori_loop(beyond, last, functools.partial(quick_step, "right"), state)
            finish(own, *state)

        @pl.when(jnp.logical_not(whole))
        def _():
            finish(*lax.fori_loop(first, last, step, start_state))

        return unused

    lax.fori_loop(info_ref[1], info_ref[2], one_block, 0)
    half = slots // 2
    low = lane_low((SPAN, LANES))
    for source in range(x_ref.shape[0]):
        for pair in range(half):
            places = [
                place_of(order_ref, info_ref, source, pair + m * half, slots) * SPAN
                for m in range(2)
            ]
            tiles = [held_ref[dyn(place, SPAN, SPAN), :] for place in places]
            mixed_ref[source, pair * SPAN : (pair + 1) * SPAN, :] = jnp.where(
                low, tiles[0], tiles[1]
            ).astype(bf16)


def vmem(shape, dtype):
    return pltpu.VMEM(shape, dtype)


def smem_spec():
    return pl.BlockSpec(memory_space=pltpu.SMEM)


def vmem_spec():
    return pl.BlockSpec(memory_space=pltpu.VMEM)


def attention_vmem(total):
    return int(min(58, 16 + 44 * (total / 16384)) * MIB)


def attend(order, ends, info, swapped, bias_rows, slots):
    sources = swapped.shape[0]
    total = sources * slots * SPAN
    return pl.pallas_call(
        functools.partial(attend_kernel, slots),
        in_specs=[smem_spec()] * 3 + [vmem_spec()] * 2,
        out_specs=[vmem_spec()] * 3,
        out_shape=[
            jax.ShapeDtypeStruct((sources, slots * SPAN // 2, LANES), bf16),
            jax.ShapeDtypeStruct((HD, total), f32),
            jax.ShapeDtypeStruct((1, total), f32),
        ],
        scratch_shapes=[
            vmem((total, LANES), bf16),
            vmem((total, LANES), bf16),
            vmem((HD, total), bf16),
            vmem((TABLE_ROWS, BQ), f32),
            vmem((total, LANES), f32),
            vmem((8, total), f32),
        ],
        compiler_params=pltpu.CompilerParams(vmem_limit_bytes=attention_vmem(total)),
        cost_estimate=pl.CostEstimate(
            flops=total * total * 128, bytes_accessed=total * 2048, transcendentals=total * total // 2
        ),
        name="attend",
    )(order, ends, info, swapped, bias_rows)


def unroll_rows(tile):
    row = lax.broadcasted_iota(jnp.int32, tile.shape, 0)
    bit = 1
    while bit < tile.shape[0]:
        moved = pltpu.roll(tile, tile.shape[1] - bit, 1)
        tile = jnp.where((row // bit) % 2 == 1, moved, tile)
        bit *= 2
    return tile


def attend_back_kernel(
    slots, bucket_count, order_ref, ends_ref, info_ref, x_ref, mixed_ref, exact_ref, lse_ref,
    bias_ref, bucket_ref, grad_ref,
    both_ref, query_ref, back_ref, turned_ref, table_ref, d_table_ref, d_both_ref, d_query_ref,
    far_ref,
):
    total = both_ref.shape[0]
    sources = x_ref.shape[0]
    half = slots // 2
    low = lane_low((SPAN, LANES))

    def keep(place, both, query):
        both_ref[dyn(place, SPAN, SPAN), :] = both
        query_ref[dyn(place, SPAN, SPAN), :] = query
        turned = both.astype(f32).T
        turned_ref[:HD, dyn(place, SPAN, SPAN)] = turned[HD:, :].astype(bf16)

    sort_blocks(order_ref, info_ref, x_ref, slots, keep)
    for source in range(sources):
        for pair in range(half):
            packed = mixed_ref[source, pair * SPAN : (pair + 1) * SPAN, :].astype(f32)
            for member, tile in enumerate((packed, swap_halves(packed))):
                place = place_of(order_ref, info_ref, source, pair + member * half, slots) * SPAN
                back_ref[dyn(place, SPAN, SPAN), :] = jnp.where(low, tile, 0.0).astype(bf16)
    fill_table(bias_ref, table_ref)
    tail = lax.broadcasted_iota(jnp.int32, (KT_ROWS - HD, total), 0)
    turned_ref[HD:, :] = jnp.where(tail == 0, 1.0, 0.0).astype(bf16)
    d_table_ref[...] = jnp.zeros_like(d_table_ref)
    d_both_ref[...] = jnp.zeros_like(d_both_ref)
    far_ref[...] = jnp.zeros_like(far_ref)
    if info_ref.shape[0] > 3:
        d_query_ref[...] = jnp.zeros_like(d_query_ref)
    left_bias = bias_ref[MID_BLOCKS : MID_BLOCKS + 1, :BQ]
    right_bias = bias_ref[MID_BLOCKS + 1 : MID_BLOCKS + 2, :BQ]

    def one_block(block, unused):
        q0 = block * BQ
        first, near, beyond, last, whole = block_range(ends_ref, q0, total)
        query = query_ref[dyn(q0, BQ, BQ), :]
        back = back_ref[dyn(q0, BQ, BQ), :]
        lse = lse_ref[:, dyn(q0, BQ, BQ)]
        turned_back = back.astype(f32).T[:HD, :]
        delta = jnp.sum(turned_back * exact_ref[:, dyn(q0, BQ, BQ)], axis=0, keepdims=True)

        def step(kind, tile, d_turned):
            for part in range(BK // CB):
                k0 = tile * BK + part * CB
                keys = dyn(k0, CB, CB)
                both = both_ref[keys, :]
                scores = dot_nt(both, query)
                if kind in ("near", "cut"):
                    rows = pl.ds(table_start(k0, q0), CB)
                    weights = jnp.exp(scores + table_ref[rows, :] - lse)
                elif kind == "left":
                    weights = jnp.exp(scores - (lse - left_bias))
                else:
                    weights = jnp.exp(scores - (lse - right_bias))
                if kind == "cut":
                    weights = jnp.where(same_sequence(ends_ref, k0, q0, CB), weights, 0.0)
                d_probs = dot_nt(both, back)
                d_scores = (weights * (d_probs - delta)).astype(bf16)
                if kind in ("near", "cut"):
                    d_table_ref[rows, :] = d_table_ref[rows, :] + d_scores.astype(f32)
                d_both_ref[keys, :] = (
                    d_both_ref[keys, :] + dot_nn(weights.astype(bf16), back) + dot_nn(d_scores, query)
                )
                d_turned = d_turned + dot_nn(turned_ref[:, keys], d_scores)
            return d_turned

        def finish(d_turned):
            top = d_turned[:HD, :]
            d_query_ref[dyn(q0, BQ, BQ), :] = jnp.concatenate([top, top], axis=0).T.astype(bf16)

        zero = jnp.zeros((KT_ROWS, BQ), f32)

        @pl.when(whole)
        def _():
            at_left = lax.fori_loop(first, near, functools.partial(step, "left"), zero)
            far_ref[0:1, :] = far_ref[0:1, :] + at_left[HD : HD + 1, :]
            at_near = lax.fori_loop(near, beyond, functools.partial(step, "near"), at_left)
            at_right = lax.fori_loop(beyond, last, functools.partial(step, "right"), zero)
            far_ref[1:2, :] = far_ref[1:2, :] + at_right[HD : HD + 1, :]
            finish(at_near + at_right)

        @pl.when(jnp.logical_not(whole))
        def _():
            finish(lax.fori_loop(first, last, functools.partial(step, "cut"), zero))

        return unused

    lax.fori_loop(info_ref[1], info_ref[2], one_block, 0)

    left = OFF - SPAN
    right = left + MID_BLOCKS * SPAN
    sums = []
    for c in range(MID_BLOCKS):
        tile = d_table_ref[left + c * SPAN : left + (c + 1) * SPAN, :]
        wide = jnp.concatenate([tile, jnp.zeros((SPAN, WIDE - BQ), f32)], axis=1)
        sums.append(jnp.sum(unroll_rows(wide), axis=0, keepdims=True))
    lefts = far_ref[0:1, :] + jnp.sum(d_table_ref[:left, :], axis=0, keepdims=True)
    rights = far_ref[1:2, :] + jnp.sum(d_table_ref[right:, :], axis=0, keepdims=True)
    blank = jnp.zeros((1, WIDE - BQ), f32)
    sums.append(jnp.concatenate([lefts, blank], axis=1))
    sums.append(jnp.concatenate([rights, blank], axis=1))
    sums = jnp.concatenate(sums, axis=0)
    buckets = bucket_ref[: MID_BLOCKS + 2, :]
    per_source = bucket_count // sources
    lane = lax.broadcasted_iota(jnp.int32, (1, LANES), 1)
    row = lax.broadcasted_iota(jnp.int32, (EXTRA, LANES), 0)
    for source in range(sources):
        line = jnp.zeros((1, LANES), f32)
        for j in range(per_source):
            picked = jnp.where(buckets == source * per_source + j, sums, 0.0)
            one = jnp.sum(jnp.sum(picked, axis=0, keepdims=True), axis=1, keepdims=True)
            line = jnp.where(lane == j, one, line)
        upper = line.astype(bf16).astype(f32)
        rest = line - upper
        grad_ref[source, 3 * half * SPAN :, :] = jnp.where(
            row == 0, upper, jnp.where(row == 1, rest, 0.0)
        ).astype(bf16)

    for source in range(sources):
        for pair in range(half):
            tiles = []
            for member in range(2):
                slot = pair + member * half
                place = place_of(order_ref, info_ref, source, slot, slots) * SPAN
                grad_ref[source, slot * SPAN : (slot + 1) * SPAN, :] = d_both_ref[
                    dyn(place, SPAN, SPAN), :
                ].astype(bf16)
                tiles.append(d_query_ref[dyn(place, SPAN, SPAN), :].astype(f32))
            grad_ref[source, (slots + pair) * SPAN : (slots + pair + 1) * SPAN, :] = jnp.where(
                low, tiles[0], tiles[1]
            ).astype(bf16)


def attend_back(
    order, ends, info, swapped, mixed_grad, exact, lse, bias_rows, bucket_rows, slots, bucket_count
):
    sources = swapped.shape[0]
    total = sources * slots * SPAN
    return pl.pallas_call(
        functools.partial(attend_back_kernel, slots, bucket_count),
        in_specs=[smem_spec()] * 3 + [vmem_spec()] * 6,
        out_specs=vmem_spec(),
        out_shape=jax.ShapeDtypeStruct((sources, slots * SPAN * 3 // 2 + EXTRA, LANES), bf16),
        scratch_shapes=[
            vmem((total, LANES), bf16),
            vmem((total, LANES), bf16),
            vmem((total, LANES), bf16),
            vmem((KT_ROWS, total), bf16),
            vmem((TABLE_ROWS, BQ), f32),
            vmem((TABLE_ROWS, BQ), f32),
            vmem((total, LANES), f32),
            vmem((total, LANES), bf16),
            vmem((8, BQ), f32),
        ],
        compiler_params=pltpu.CompilerParams(vmem_limit_bytes=attention_vmem(total)),
        cost_estimate=pl.CostEstimate(
            flops=total * total * 320, bytes_accessed=total * 3072, transcendentals=total * total // 2
        ),
        name="attend_back",
    )(order, ends, info, swapped, mixed_grad, exact, lse, bias_rows, bucket_rows)


def out_kernel(slots, packed_ref, weight_ref, mix_ref, *part_refs):
    heads = packed_ref.shape[0]
    half = slots * SPAN // 2

    @pl.when(pl.program_id(0) == 0)
    def _():
        for pair in range(heads // 2):
            first = packed_ref[2 * pair].astype(f32)
            second = packed_ref[2 * pair + 1].astype(f32)
            top, bottom = pair_up(first, second)
            cols = slice(pair * LANES, (pair + 1) * LANES)
            mix_ref[:half, cols] = top.astype(bf16)
            mix_ref[half:, cols] = bottom.astype(bf16)

    part = dot_nn(mix_ref[...], weight_ref[...]).astype(bf16)
    for s in range(slots):
        part_refs[s][...] = part[s * SPAN : (s + 1) * SPAN]


def out_project(packed, weight, slots):
    heads = packed.shape[0]
    rows, width, depth = slots * SPAN, heads * HD, weight.shape[1]
    tile = 512
    return pl.pallas_call(
        functools.partial(out_kernel, slots),
        grid=(depth // tile,),
        in_specs=[
            pl.BlockSpec(packed.shape, lambda j: (0, 0, 0)),
            pl.BlockSpec((width, tile), lambda j: (0, j)),
        ],
        out_specs=[
            pl.BlockSpec((rows, width), lambda j: (0, 0)),
        ]
        + [pl.BlockSpec((SPAN, tile), lambda j: (0, j))] * slots,
        out_shape=[jax.ShapeDtypeStruct((rows, width), bf16)]
        + [jax.ShapeDtypeStruct((SPAN, depth), bf16)] * slots,
        compiler_params=pltpu.CompilerParams(vmem_limit_bytes=40 * MIB),
        cost_estimate=pl.CostEstimate(
            flops=2 * rows * depth * width, bytes_accessed=4 * depth * width, transcendentals=0
        ),
        name="out_project",
    )(packed, weight)


def feed_kernel(slots, *refs):
    normed_refs, grad_refs = refs[:slots], refs[slots : 2 * slots]
    gate_ref, up_ref, down_ref, rows_ref, rows_grad_ref, active_ref, d_both_ref = refs[2 * slots :]

    @pl.when(pl.program_id(0) == 0)
    def _():
        for s in range(slots):
            rows_ref[s * SPAN : (s + 1) * SPAN, :] = normed_refs[s][...]
            rows_grad_ref[s * SPAN : (s + 1) * SPAN, :] = grad_refs[s][...]

    tile = down_ref.shape[0]
    width = d_both_ref.shape[1] // 2
    gate = dot_nn(rows_ref[...], gate_ref[...])
    up = dot_nn(rows_ref[...], up_ref[...])
    d_hidden = dot_nt(rows_grad_ref[...], down_ref[...])
    scale, cubic = 0.7978845608028654, 0.044715
    square = gate * gate
    bent = jnp.tanh(scale * (gate + cubic * square * gate))
    half = 0.5 * (1.0 + bent)
    gelu = gate * half
    slope = half + 0.5 * gate * (1.0 - bent * bent) * (scale * (1.0 + 3.0 * cubic * square))
    active_ref[...] = (gelu * up).astype(bf16)
    start = pl.program_id(0) * tile
    d_both_ref[:, dyn(start, tile, tile)] = (d_hidden * up * slope).astype(bf16)
    d_both_ref[:, dyn(width + start, tile, LANES)] = (d_hidden * gelu).astype(bf16)


def feed_tile(width):
    return 256 if width % 256 == 0 else 128


def feed(normed_slots, grad_slots, both, down):
    slots = len(normed_slots)
    rows, depth, width = slots * SPAN, both.shape[0], both.shape[1] // 2
    tile = feed_tile(width)
    steps = width // tile
    whole = pl.BlockSpec((SPAN, depth), lambda j: (0, 0))
    rows_spec = pl.BlockSpec((rows, depth), lambda j: (0, 0))
    return pl.pallas_call(
        functools.partial(feed_kernel, slots),
        grid=(steps,),
        in_specs=[whole] * (2 * slots)
        + [
            pl.BlockSpec((depth, tile), lambda j: (0, j)),
            pl.BlockSpec((depth, tile), lambda j: (0, steps + j)),
            pl.BlockSpec((tile, depth), lambda j: (j, 0)),
        ],
        out_specs=[
            rows_spec,
            rows_spec,
            pl.BlockSpec((rows, tile), lambda j: (0, j)),
            pl.BlockSpec((rows, 2 * width), lambda j: (0, 0)),
        ],
        out_shape=[
            jax.ShapeDtypeStruct((rows, depth), bf16),
            jax.ShapeDtypeStruct((rows, depth), bf16),
            jax.ShapeDtypeStruct((rows, width), bf16),
            jax.ShapeDtypeStruct((rows, 2 * width), bf16),
        ],
        compiler_params=pltpu.CompilerParams(vmem_limit_bytes=56 * MIB),
        cost_estimate=pl.CostEstimate(
            flops=6 * rows * depth * width,
            bytes_accessed=6 * depth * width,
            transcendentals=rows * width,
        ),
        name="feed",
    )(*normed_slots, *grad_slots, both, both, down)


def pack_kernel(slots, *refs):
    packed_ref = refs[slots]
    half = slots // 2
    for pair in range(packed_ref.shape[0] // 2):
        cols = slice(pair * LANES, (pair + 1) * LANES)
        for s in range(half):
            span = slice(s * SPAN, (s + 1) * SPAN)
            first, second = (refs[s + m * half][:, cols].astype(f32) for m in range(2))
            for member, tile in enumerate(pair_up(first, second)):
                packed_ref[2 * pair + member, span, :] = tile.astype(bf16)


def pack(parts):
    slots = len(parts)
    heads = parts[0].shape[1] // HD
    return pl.pallas_call(
        functools.partial(pack_kernel, slots),
        in_specs=[vmem_spec()] * slots,
        out_specs=vmem_spec(),
        out_shape=jax.ShapeDtypeStruct((heads, slots * SPAN // 2, LANES), bf16),
        compiler_params=pltpu.CompilerParams(vmem_limit_bytes=16 * MIB),
        name="pack",
    )(*parts)


def project_back_kernel(slots, packed_ref, weight_ref, scale_ref, mix_ref, left_ref, *refs):
    x_refs, attn_refs = refs[:slots], refs[slots : 2 * slots]
    product_ref, gain_ref = refs[2 * slots : 2 * slots + 2]
    part_refs, grads_ref = refs[2 * slots + 2 : -1], refs[-1]
    heads = packed_ref.shape[0]
    rows = slots * SPAN
    half = rows // 2
    width = heads * HD

    @pl.when(pl.program_id(0) == 0)
    def _():
        for pair in range(heads // 2):
            start = pair * LANES
            tiles = [packed_ref[2 * pair + m].astype(f32) for m in range(2)]
            value, key = pair_up(tiles[0][:rows], tiles[1][:rows])
            top, bottom = pair_up(tiles[0][rows : rows + half], tiles[1][rows : rows + half])
            grads_ref[:half, start : start + LANES] = top.astype(bf16)
            grads_ref[half:, start : start + LANES] = bottom.astype(bf16)
            grads_ref[:, width + start : width + start + LANES] = key.astype(bf16)
            grads_ref[:, 2 * width + start : 2 * width + start + LANES] = value.astype(bf16)

    part = dot_nt(grads_ref[...], weight_ref[...])
    gain = jnp.zeros((1, part.shape[1]), f32)
    for s in range(slots):
        span = slice(s * SPAN, (s + 1) * SPAN)
        part_refs[s][...] = part[span].astype(bf16)
        x_hat = x_refs[s][...].astype(f32) * scale_ref[span, :1]
        gain = gain + jnp.sum(part[span] * x_hat, axis=0, keepdims=True)
    gain_ref[...] = gain
    product_ref[:, : 3 * width] = dot_tn(left_ref[...], grads_ref[...]).astype(bf16)
    attn = jnp.concatenate([ref[...] for ref in attn_refs], axis=0)
    product_ref[:, 3 * width :] = dot_tn(attn, mix_ref[...]).astype(bf16)


def project_back(packed, weights, scale, mix, left, x_slots, attn_slots):
    slots = len(x_slots)
    depth, width = weights.shape
    rows = slots * SPAN
    tile = 256
    spans = [pl.BlockSpec((SPAN, tile), lambda j: (0, j))] * slots
    total = width + mix.shape[1]
    return pl.pallas_call(
        functools.partial(project_back_kernel, slots),
        grid=(depth // tile,),
        in_specs=[
            pl.BlockSpec(packed.shape, lambda j: (0, 0, 0)),
            pl.BlockSpec((tile, width), lambda j: (j, 0)),
            pl.BlockSpec((rows, LANES), lambda j: (0, 0)),
            pl.BlockSpec(mix.shape, lambda j: (0, 0)),
            pl.BlockSpec((rows, tile), lambda j: (0, j)),
        ]
        + spans
        + spans,
        out_specs=[
            pl.BlockSpec((tile, total), lambda j: (j, 0)),
            pl.BlockSpec((1, tile), lambda j: (0, j)),
        ]
        + spans,
        out_shape=[
            jax.ShapeDtypeStruct((depth, total), bf16),
            jax.ShapeDtypeStruct((1, depth), f32),
        ]
        + [jax.ShapeDtypeStruct((SPAN, depth), bf16)] * slots,
        scratch_shapes=[vmem((rows, width), bf16)],
        compiler_params=pltpu.CompilerParams(vmem_limit_bytes=LARGE),
        cost_estimate=pl.CostEstimate(
            flops=4 * rows * depth * total, bytes_accessed=4 * depth * total, transcendentals=0
        ),
        name="project_back",
    )(packed, weights, scale, mix, left, *x_slots, *attn_slots)


def pair_kernel(left_one_ref, right_one_ref, left_two_ref, right_two_ref, out_ref):
    cut = right_one_ref.shape[1]
    out_ref[:, :cut] = dot_tn(left_one_ref[...], right_one_ref[...]).astype(bf16)
    out_ref[:, cut:] = dot_tn(left_two_ref[...], right_two_ref[...]).astype(bf16)


def pair_product(left_one, right_one, left_two, right_two):
    rows, depth = left_one.shape
    width = right_one.shape[1] + right_two.shape[1]
    block = 256

    def left():
        return pl.BlockSpec((rows, block), lambda j: (0, j))

    def right(array):
        return pl.BlockSpec(array.shape, lambda j: (0, 0))

    return pl.pallas_call(
        pair_kernel,
        grid=(depth // block,),
        in_specs=[left(), right(right_one), left(), right(right_two)],
        out_specs=pl.BlockSpec((block, width), lambda j: (j, 0)),
        out_shape=jax.ShapeDtypeStruct((depth, width), bf16),
        compiler_params=pltpu.CompilerParams(vmem_limit_bytes=32 * MIB),
        cost_estimate=pl.CostEstimate(
            flops=2 * rows * depth * width, bytes_accessed=2 * depth * width, transcendentals=0
        ),
        name="pair_product",
    )(left_one, right_one, left_two, right_two)


def bucket_lines(bucket_of):
    count = bucket_of.shape[0]
    turned = bucket_of[::-1]
    pad = 5 * WIDE // 4
    padded = jnp.concatenate(
        [
            jnp.broadcast_to(turned[:1], (pad,)),
            turned,
            jnp.broadcast_to(turned[-1:], (pad,)),
        ]
    )
    zero_at = pad + count // 2
    keep = BQ + HD
    rows = []
    for c in range(MID_BLOCKS):
        base = zero_at - (c - 1) * SPAN
        rows.append(
            jnp.concatenate([padded[base : base + keep], padded[base - (WIDE - keep) : base]])
        )
    rows.append(jnp.broadcast_to(bucket_of[:1], (WIDE,)))
    rows.append(jnp.broadcast_to(bucket_of[-1:], (WIDE,)))
    spare = 8 * ((MID_BLOCKS + 2 + 7) // 8) - (MID_BLOCKS + 2)
    return jnp.concatenate([jnp.stack(rows), jnp.full((spare, WIDE), -1, bucket_of.dtype)])


def on_device(
    tokens,
    lengths,
    block_order,
    bucket_of,
    gain_attn,
    w_query,
    w_key,
    w_value,
    w_out,
    bias_table,
    gain_ffn,
    w_gate,
    w_up,
    w_down,
    cotangent,
):
    blk_count, slots = lax.axis_size("blk"), lax.axis_size("head")
    blk_spot, head_spot = lax.axis_index("blk"), lax.axis_index("head")
    depth = tokens.shape[1]
    width = w_query.shape[1]
    heads = width // HD
    shares = blk_count // heads
    table_rows, table_heads = bias_table.shape
    bucket_count = table_rows * blk_count
    total = blk_count * slots * SPAN
    gain_size = gain_attn.shape[0]
    hidden = w_gate.shape[1]

    token_slots = gather_far(gather_near(tokens))
    small = gather_small(
        jnp.concatenate([gain_attn, gain_ffn, bias_table.astype(f32).reshape(-1)])
    )
    full_qkv = lax.all_gather(
        jnp.concatenate([w_query, w_key, w_value], axis=1), "blk", axis=0, tiled=True
    )
    full_out = lax.all_gather(w_out, "blk", axis=1, tiled=True)
    full_both = lax.all_gather(
        jnp.concatenate([w_gate, w_up], axis=1), "blk", axis=0, tiled=True
    )
    full_down = lax.all_gather(w_down, "blk", axis=1, tiled=True)
    gain_one = small[:, :, :gain_size].reshape(1, depth)
    gain_two = small[:, :, gain_size : 2 * gain_size].reshape(1, depth)

    tables = lax.dynamic_index_in_dim(small, head_spot, 1, False)[:, 2 * gain_size :]
    tables = tables.reshape(bucket_count, table_heads)
    my_head = blk_spot // shares
    my_bias = lax.dynamic_index_in_dim(tables, my_head, 1, False)
    bucket_rows = bucket_lines(bucket_of)
    bias_rows = jnp.sum(
        jnp.where(
            bucket_rows[None] == jnp.arange(bucket_count, dtype=jnp.int32)[:, None, None],
            my_bias[:, None, None],
            0.0,
        ),
        axis=0,
    )
    ends = jnp.cumsum(lengths).astype(jnp.int32)
    per_share = total // BQ // shares
    start = (blk_spot % shares) * per_share
    info = [head_spot, start, start + per_share] + ([start] if shares > 1 else [])
    info = jnp.stack([jnp.asarray(item, jnp.int32) for item in info])

    def swap(values):
        return lax.all_to_all(values, "blk", 0, 0, tiled=True)

    def to_heads(values):
        return swap(values if shares == 1 else jnp.repeat(values, shares, axis=0))

    def to_rows(values):
        values = swap(values)
        if shares == 1:
            return values
        values = values.reshape((heads, shares) + values.shape[1:])
        return jnp.sum(values.astype(f32), axis=1).astype(bf16)

    w_out, cotangent, *token_slots = together(w_out, cotangent, *token_slots)
    normed_one, packed, scale_one = project(token_slots, gain_one, full_qkv)
    early = (ends, info, bias_rows, bucket_rows)
    swapped, ends, info, bias_rows, bucket_rows, *out_near = together(
        to_heads(packed), *early, *gather_near(w_out)
    )
    grad_near, out_slots = gather_near(cotangent), gather_far(out_near)
    mixed, exact, lse = attend(block_order, ends, info, swapped, bias_rows, slots)
    mixed, *moved = together(mixed, *grad_near, *out_slots)
    grad_near, out_slots = moved[: len(grad_near)], moved[len(grad_near) :]
    packed_mix, *grad_slots = together(to_rows(mixed), *gather_far(grad_near))
    attn_mix, *out_parts = out_project(packed_mix, full_out, slots)
    out_parts, out_slots = together(out_parts, out_slots)
    full_rest = lax.all_gather(jnp.concatenate(out_slots[1:]), "blk", axis=1, tiled=True)
    tokens_wide = tokens.astype(f32)
    hidden_one = tokens_wide + sum_terms(sum_near(out_parts, sum_far(out_parts))[0])
    rstd_two = rms_scale(hidden_one)
    normed_two = (hidden_one * rstd_two * gain_two).astype(bf16)

    normed_slots = gather_far(gather_near(normed_two))
    rows_two, rows_grad, active, d_both = feed(normed_slots, grad_slots, full_both, full_down)

    def spans(rows):
        return [rows[s * SPAN : (s + 1) * SPAN] for s in range(slots)]

    d_parts = spans(dot_nt(d_both, full_both).astype(bf16))
    d_far = sum_far(d_parts)
    grad_hidden, full_rest, *d_far = together(
        pair_product(rows_two, d_both, rows_grad, active), full_rest, *d_far
    )
    grad_hidden = lax.psum_scatter(grad_hidden, "blk", scatter_dimension=0, tiled=True)
    d_near, (active,) = sum_near(d_parts, d_far, (active,))
    down_parts, *d_near = together(dot_nn(active, full_down).astype(bf16), *d_near)
    down_parts = spans(down_parts)
    d_normed_two = sum_terms(d_near)
    d_source_two, gain_part_two = norm_back(d_normed_two, hidden_one, rstd_two, gain_two)
    d_hidden_one = cotangent.astype(f32) + d_source_two

    d_attn = d_hidden_one.astype(bf16)
    mix_parts = [dot_nt(d_attn, full_out).astype(bf16)]
    mix_rest = dot_nt(d_attn, full_rest).astype(bf16)
    mix_parts += [mix_rest[:, s * width : (s + 1) * width] for s in range(slots - 1)]
    mix_grads, d_attn = together(pack(exchange(mix_parts)), d_attn)
    middle = slots // 2
    steps = [t for t in range(1, slots) if t != middle]
    moved = (*gather_near(d_attn), *sum_direct(down_parts, steps))
    grads = attend_back(
        block_order, ends, info, swapped, to_heads(mix_grads), exact, lse, bias_rows, bucket_rows,
        slots, bucket_count,
    )
    grads, *moved = together(grads, *moved)
    attn_near, down_terms = moved[: 2 - slots], moved[2 - slots :]
    grads, *attn_slots = together(swap(grads), *gather_far(attn_near))
    extra = grads[:, -EXTRA : -EXTRA + 2, :table_rows].astype(f32).sum(axis=1)
    grad_table = extra.reshape(heads, shares, table_rows).sum(axis=1).T
    if shares > 1:
        grads = grads.reshape((heads, shares) + grads.shape[1:])
        grads = jnp.sum(grads.astype(f32), axis=1).astype(bf16)
    grad_heads, gain_part_one, *one_parts = project_back(
        grads, full_qkv, scale_one, attn_mix, normed_one, token_slots, attn_slots
    )

    one_far = sum_far(one_parts)
    gain_parts = jnp.stack(
        [part.reshape(blk_count, slots, gain_size) for part in (gain_part_one, gain_part_two)],
        axis=2,
    )
    grad_heads, grad_hidden = together(grad_heads, grad_hidden)
    gain_parts, *one_far = together(gain_parts, *one_far)
    grad_heads = lax.psum_scatter(grad_heads, "blk", scatter_dimension=0, tiled=True).astype(f32)
    one_near, unused = sum_near(one_parts, one_far)
    gain_sums = scatter_blk(gain_parts)
    gain_sums, down_parts, grad_hidden, *one_near = together(
        gain_sums, down_parts, grad_hidden, *one_near
    )
    gain_sums = scatter_head(gain_sums)
    grad_hidden = grad_hidden.astype(f32)
    output = hidden_one + sum_all([down_parts[0]] + down_terms + sum_direct(down_parts, [middle]))
    d_normed_one = sum_terms(one_near)
    d_source_one, unused = norm_back(d_normed_one, tokens_wide, rms_scale(tokens_wide), gain_one)
    input_grad = d_hidden_one + d_source_one
    return (
        output,
        input_grad,
        gain_sums[0],
        grad_heads[:, :width],
        grad_heads[:, width : 2 * width],
        grad_heads[:, 2 * width : 3 * width],
        grad_heads[:, 3 * width :].T,
        grad_table,
        gain_sums[1],
        grad_hidden[:, :hidden],
        grad_hidden[:, hidden : 2 * hidden],
        grad_hidden[:, 2 * hidden :].T,
    )


def solution(mesh):
    rows, spread = P(("blk", "head"), None), P(("blk", "head"))
    inward, outward = P("blk", "head"), P("head", "blk")
    in_specs = (
        rows, P(), P(), P(), spread, inward, inward, inward, outward, inward, spread,
        inward, inward, outward, rows,
    )
    out_specs = (
        rows, rows, spread, inward, inward, inward, outward, inward, spread,
        inward, inward, outward,
    )
    return jax.shard_map(
        on_device, mesh=mesh, in_specs=in_specs, out_specs=out_specs, check_vma=False
    )
```

```python
import functools

import jax
import jax.numpy as jnp
import numpy as np
from jax import lax
from jax.experimental import pallas as pl
from jax.experimental.pallas import tpu as pltpu
from jax.sharding import PartitionSpec as P

HD = 64
LANES = 2 * HD
MAXDIST = 128
SPAN = 128
BQ = 512
BK = BQ
NEAR = 3
WIDE = 2 * SPAN
EXTRA = 16
KT_ROWS = 80
SHIFT_ROOM = 60.0

norm_eps = 1e-06
masked_score = -1e30
f32 = jnp.float32
bf16 = jnp.bfloat16
MIB = 1 << 20
LARGE = 58 * MIB


def rms_scale(values):
    return lax.rsqrt(jnp.mean(values * values, axis=-1, keepdims=True) + norm_eps)


def norm_back(d_normed, source, inv_rms, gain_vec):
    scaled = d_normed * gain_vec
    x_hat = source * inv_rms
    gain_part = jnp.sum(d_normed * x_hat, axis=0)
    d_source = inv_rms * (scaled - x_hat * jnp.mean(scaled * x_hat, axis=-1, keepdims=True))
    return (d_source, gain_part)


def dot_nn(left, right):
    return jnp.dot(left, right, preferred_element_type=f32)


def dot_nt(left, right):
    return lax.dot_general(left, right, (((1,), (1,)), ((), ())), preferred_element_type=f32)


def dot_tn(left, right):
    return lax.dot_general(left, right, (((0,), (0,)), ((), ())), preferred_element_type=f32)


def cyclic(count, by):
    return [(i, (i + by) % count) for i in range(count)]


def together(*values):
    return lax.optimization_barrier(values)


def gather_near(rows):
    count = lax.axis_size("head")
    if count != 4:
        return [rows] + [lax.ppermute(rows, "head", cyclic(count, s)) for s in range(1, count)]
    return [rows, lax.ppermute(rows, "head", cyclic(4, 1)), lax.ppermute(rows, "head", cyclic(4, 3))]


def gather_far(near):
    if lax.axis_size("head") != 4:
        return near
    rows, back_one, ahead_one = near
    me = lax.axis_index("head")
    passed = jnp.where(me == 1, ahead_one, jnp.where(me == 2, back_one, rows))
    back_two = lax.ppermute(passed, "head", [(1, 0), (3, 1), (0, 2), (2, 3)])
    return [rows, back_one, back_two, ahead_one]


def gather_direct(rows):
    count = lax.axis_size("head")
    return [rows] + [lax.ppermute(rows, "head", cyclic(count, s)) for s in range(1, count)]


def sum_far(parts):
    count = lax.axis_size("head")
    if count != 4:
        return []
    return [lax.ppermute(parts[2], "head", [(0, 1), (1, 3), (2, 0), (3, 2)])]


def sum_near(parts, far, beside=()):
    count = lax.axis_size("head")
    if count != 4:
        return [parts[0]] + [
            lax.ppermute(parts[s], "head", cyclic(count, count - s)) for s in range(1, count)
        ], beside
    me = lax.axis_index("head")
    wide = far[0].astype(f32)
    to_back = jnp.where(me == 2, parts[1].astype(f32) + wide, parts[1].astype(f32)).astype(bf16)
    to_ahead = jnp.where(me == 1, parts[3].astype(f32) + wide, parts[3].astype(f32)).astype(bf16)
    to_back, to_ahead, *beside = together(to_back, to_ahead, *beside)
    from_ahead = lax.ppermute(to_back, "head", cyclic(4, 3))
    from_back = lax.ppermute(to_ahead, "head", cyclic(4, 1))
    return [parts[0], from_ahead, from_back, far[0]], beside


def sum_terms(terms):
    total = terms[0].astype(f32) + terms[1].astype(f32) + terms[2].astype(f32)
    if lax.axis_size("head") != 4:
        for term in terms[3:]:
            total = total + term.astype(f32)
        return total
    me = lax.axis_index("head")
    return total + jnp.where((me == 0) | (me == 3), terms[3].astype(f32), 0.0)


def is_power(count):
    return count & (count - 1) == 0


def gather_small(values):
    held = values[None]
    for axis in ("head", "blk"):
        count = lax.axis_size(axis)
        if not is_power(count):
            held = lax.all_gather(held, axis, axis=0, tiled=False)
        else:
            me = lax.axis_index(axis)
            held = held[None]
            bit = 1
            while bit < count:
                other = lax.ppermute(held, axis, [(i, i ^ bit) for i in range(count)])
                low = jnp.concatenate([held, other])
                high = jnp.concatenate([other, held])
                held = jnp.where((me // bit) % 2 == 0, low, high)
                bit *= 2
        if axis == "head":
            held = held.reshape(count, -1)
    return held


def sum_direct(parts, steps):
    count = len(parts)
    return [lax.ppermute(parts[s], "head", cyclic(count, count - s)) for s in steps]


def sum_all(terms):
    total = terms[0].astype(f32)
    for term in terms[1:]:
        total = total + term.astype(f32)
    return total


def scatter_blk(values):
    return jnp.sum(lax.all_to_all(values, "blk", 0, 0, tiled=True), axis=0)


def scatter_head(values):
    count, me = lax.axis_size("head"), lax.axis_index("head")
    total = lax.dynamic_index_in_dim(values, me, 0, False)
    for s in range(1, count):
        sent = lax.dynamic_index_in_dim(values, (me + s) % count, 0, False)
        total = total + lax.ppermute(sent, "head", cyclic(count, s))
    return total


def lane_low(shape):
    return lax.broadcasted_iota(jnp.int32, shape, 1) < HD


def swap_halves(tile):
    return pltpu.roll(tile, HD, 1)


def pair_up(first, second):
    low = lane_low(first.shape)
    return (
        jnp.where(low, first, swap_halves(second)),
        jnp.where(low, swap_halves(first), second),
    )


def project_kernel(slots, *refs):
    x_refs = refs[:slots]
    gain_ref, wq_ref, wk_ref, wv_ref, normed_ref, packed_ref, scale_ref = refs[slots:]
    rows = slots * SPAN

    @pl.when(pl.program_id(0) == 0)
    def _():
        for s in range(slots):
            wide = x_refs[s][...].astype(f32)
            scale = rms_scale(wide)
            normed = wide * scale * gain_ref[...]
            normed_ref[s * SPAN : (s + 1) * SPAN, :] = normed.astype(bf16)
            scale_ref[s * SPAN : (s + 1) * SPAN, :] = jnp.broadcast_to(scale, (SPAN, LANES))

    normed = normed_ref[...]
    query = dot_nn(normed, wq_ref[...])
    key = dot_nn(normed, wk_ref[...])
    value = dot_nn(normed, wv_ref[...])
    half = rows // 2
    for pair in range(query.shape[1] // LANES):
        cols = slice(pair * LANES, (pair + 1) * LANES)
        both = pair_up(value[:, cols], key[:, cols])
        queries = pair_up(query[:half, cols], query[half:, cols])
        for member in range(2):
            packed_ref[2 * pair + member, :rows, :] = both[member].astype(bf16)
            packed_ref[2 * pair + member, rows:, :] = queries[member].astype(bf16)


def project(x_slots, gain, weights):
    slots = len(x_slots)
    rows, depth = slots * SPAN, x_slots[0].shape[1]
    width = weights.shape[1] // 3
    heads = width // HD
    tile = min(width, 256)
    steps = width // tile
    whole = pl.BlockSpec((SPAN, depth), lambda j: (0, 0))

    def columns(part):
        return pl.BlockSpec((depth, tile), lambda j: (0, part * steps + j))

    return pl.pallas_call(
        functools.partial(project_kernel, slots),
        grid=(steps,),
        in_specs=[whole] * slots
        + [pl.BlockSpec((1, depth), lambda j: (0, 0)), columns(0), columns(1), columns(2)],
        out_specs=[
            pl.BlockSpec((rows, depth), lambda j: (0, 0)),
            pl.BlockSpec((tile // HD, rows + rows // 2, LANES), lambda j: (j, 0, 0)),
            pl.BlockSpec((rows, LANES), lambda j: (0, 0)),
        ],
        out_shape=[
            jax.ShapeDtypeStruct((rows, depth), bf16),
            jax.ShapeDtypeStruct((heads, rows + rows // 2, LANES), bf16),
            jax.ShapeDtypeStruct((rows, LANES), f32),
        ],
        compiler_params=pltpu.CompilerParams(vmem_limit_bytes=40 * MIB),
        cost_estimate=pl.CostEstimate(
            flops=10 * rows * depth * width, bytes_accessed=6 * depth * width, transcendentals=0
        ),
        name="project",
    )(*x_slots, gain, weights, weights, weights)


def place_of(order_ref, info_ref, source, slot, slots):
    z = info_ref[0]
    return order_ref[source * slots + lax.rem(z - slot + slots, slots)]


def dyn(start, size, multiple):
    return pl.ds(pl.multiple_of(start, multiple), size)


def near_blocks(bias_ref):
    tiles = []
    for c in range(NEAR):
        spread = jnp.broadcast_to(bias_ref[c : c + 1, :], (SPAN, WIDE))
        tiles.append(pltpu.roll(spread, 0, 1, stride=1, stride_axis=0)[:, :SPAN])
    return tiles


def block_step(a, b):
    return a - b + 1 if abs(a - b) <= 1 else 3 if a < b else 4


def fill_tables(bias_ref, table_ref, corner_ref):
    tiles = near_blocks(bias_ref)
    far = [jnp.broadcast_to(bias_ref[NEAR + m : NEAR + m + 1, :SPAN], (SPAN, SPAN)) for m in range(2)]
    every = tiles + far
    for a in range(BK // SPAN):
        for b in range(BQ // SPAN):
            table_ref[a * SPAN : (a + 1) * SPAN, b * SPAN : (b + 1) * SPAN] = every[block_step(a, b)]
    corner_ref[0] = tiles[0] - far[0]
    corner_ref[1] = tiles[2] - far[1]


def with_corner(tile, kind, corner):
    if kind == "prev":
        upper, lower = tile[: BK - SPAN], tile[BK - SPAN :]
        lower = jnp.concatenate([lower[:, :SPAN] + corner, lower[:, SPAN:]], axis=1)
    else:
        upper, lower = tile[:SPAN], tile[SPAN:]
        upper = jnp.concatenate([upper[:, : BQ - SPAN], upper[:, BQ - SPAN :] + corner], axis=1)
    return jnp.concatenate([upper, lower], axis=0)


def corner_of(tile, kind):
    return tile[BK - SPAN :, :SPAN] if kind == "prev" else tile[:SPAN, BQ - SPAN :]


def any_bias(bias_ref, table_ref, corner_ref, tile, block):
    left = jnp.broadcast_to(bias_ref[NEAR : NEAR + 1, 0:1], (BK, BQ))
    right = jnp.broadcast_to(bias_ref[NEAR + 1 : NEAR + 2, 0:1], (BK, BQ))
    left = with_corner(left, "prev", jnp.where(tile + 1 == block, corner_ref[0], 0.0))
    right = with_corner(right, "next", jnp.where(tile == block + 1, corner_ref[1], 0.0))
    return jnp.where(tile == block, table_ref[...], jnp.where(tile < block, left, right))


def block_range(ends_ref, q0, total):
    count = ends_ref.shape[0]
    start, end, cut = jnp.int32(0), jnp.int32(total), jnp.bool_(False)
    for n in range(count):
        edge = ends_ref[n]
        start = jnp.where(edge <= q0, edge, start)
        cut = cut | ((edge > q0) & (edge < q0 + BQ))
    for n in range(count - 1, -1, -1):
        edge = ends_ref[n]
        end = jnp.where(edge >= q0 + BQ, edge, end)
    first = lax.div(start, BK)
    last = lax.div(end + BK - 1, BK)
    whole = jnp.logical_not(cut) & (lax.rem(start, BK) == 0) & (lax.rem(end, BK) == 0)
    return first, last, whole


def row_of_tiles(first, last, block, step, left, middle, right):
    before, after = jnp.maximum(block - 1, first), jnp.minimum(block + 2, last)
    left = lax.fori_loop(first, before, functools.partial(step, "left"), left)
    left = lax.fori_loop(before, block, functools.partial(step, "prev"), left)
    middle = step("diagonal", block, left if middle is None else middle)
    right = middle if right is None else right
    right = lax.fori_loop(block + 1, after, functools.partial(step, "next"), right)
    right = lax.fori_loop(after, last, functools.partial(step, "right"), right)
    return left, middle, right


def same_sequence(ends_ref, k0, q0):
    key_place = k0 + lax.broadcasted_iota(jnp.int32, (BK, 1), 0)
    query_place = q0 + lax.broadcasted_iota(jnp.int32, (1, BQ), 1)
    key_seg = jnp.zeros((BK, 1), jnp.int32)
    query_seg = jnp.zeros((1, BQ), jnp.int32)
    for n in range(ends_ref.shape[0]):
        key_seg = key_seg + jnp.where(key_place >= ends_ref[n], 1, 0)
        query_seg = query_seg + jnp.where(query_place >= ends_ref[n], 1, 0)
    return key_seg == query_seg


def sort_blocks(order_ref, info_ref, x_ref, slots, keep):
    sources = x_ref.shape[0]
    half = slots // 2
    high = jnp.logical_not(lane_low((SPAN, LANES)))
    for source in range(sources):
        for pair in range(half):
            packed = x_ref[
                source, (slots + pair) * SPAN : (slots + pair + 1) * SPAN, :
            ].astype(f32)
            queries = (swap_halves(packed), packed)
            for member in range(2):
                slot = pair + member * half
                place = place_of(order_ref, info_ref, source, slot, slots) * SPAN
                both = x_ref[source, slot * SPAN : (slot + 1) * SPAN, :]
                keep(place, both, jnp.where(high, queries[member], 0.0).astype(bf16))


def attend_kernel(
    slots, order_ref, ends_ref, info_ref, x_ref, bias_ref, mixed_ref, exact_ref, lse_ref,
    both_ref, query_ref, turned_ref, table_ref, corner_ref, held_ref, rows_ref,
):
    total = both_ref.shape[0]
    parted = info_ref.shape[0] > 3

    def keep(place, both, query):
        both_ref[dyn(place, SPAN, SPAN), :] = both
        query_ref[dyn(place, SPAN, SPAN), :] = query
        turned = both.astype(f32).T
        turned_ref[:, dyn(place, SPAN, SPAN)] = turned[:HD, :].astype(bf16)
        turned_key, turned_query = turned[HD:, :], query.astype(f32).T[HD:, :]
        for line, product in enumerate(
            (turned_key * turned_query, turned_key * turned_key, turned_query * turned_query)
        ):
            rows_ref[line : line + 1, dyn(place, SPAN, SPAN)] = jnp.sum(
                product, axis=0, keepdims=True
            )

    sort_blocks(order_ref, info_ref, x_ref, slots, keep)
    fill_tables(bias_ref, table_ref, corner_ref)
    if parted:
        held_ref[...] = jnp.zeros_like(held_ref)
        exact_ref[...] = jnp.zeros_like(exact_ref)
        lse_ref[...] = jnp.zeros_like(lse_ref)
    left_bias = bias_ref[NEAR : NEAR + 1, 0:1]
    right_bias = bias_ref[NEAR + 1 : NEAR + 2, 0:1]
    start_state = (
        jnp.full((1, BQ), masked_score, f32),
        jnp.zeros((1, BQ), f32),
        jnp.zeros((HD, BQ), f32),
    )
    longest_key = jnp.sqrt(jnp.max(rows_ref[1:2, :], axis=1, keepdims=True))
    most_bias = jnp.max(
        jnp.max(bias_ref[: NEAR + 2, :], axis=0, keepdims=True), axis=1, keepdims=True
    )

    def one_block(block, unused):
        q0 = block * BQ
        first, last, whole = block_range(ends_ref, q0, total)
        query = query_ref[dyn(q0, BQ, BQ), :]
        own = rows_ref[0:1, dyn(q0, BQ, BQ)] + bias_ref[1:2, 0:1]
        bound = jnp.sqrt(rows_ref[2:3, dyn(q0, BQ, BQ)]) * longest_key + most_bias
        whole = whole & (jnp.max(bound - own) < SHIFT_ROOM)

        def quick_step(kind, tile, state):
            mass, mix = state
            k0 = tile * BK
            scores = dot_nt(both_ref[dyn(k0, BK, BK), :], query)
            if kind == "diagonal":
                weights = jnp.exp(scores + table_ref[...] - own)
            else:
                if kind in ("prev", "next"):
                    scores = with_corner(scores, kind, corner_ref[0 if kind == "prev" else 1])
                weights = jnp.exp(scores - (own - (left_bias if kind in ("left", "prev") else right_bias)))
            mass = mass + jnp.sum(weights, axis=0, keepdims=True)
            return (mass, mix + dot_nn(turned_ref[:, dyn(k0, BK, BK)], weights.astype(bf16)))

        def step(tile, state):
            peak, mass, mix = state
            k0 = tile * BK
            scores = dot_nt(both_ref[dyn(k0, BK, BK), :], query)
            same = same_sequence(ends_ref, k0, q0)
            scores = scores + any_bias(bias_ref, table_ref, corner_ref, tile, block)
            scores = jnp.where(same, scores, masked_score)
            new_peak = jnp.maximum(peak, jnp.max(scores, axis=0, keepdims=True))
            weights = jnp.where(same, jnp.exp(scores - new_peak), 0.0)
            rescale = jnp.exp(peak - new_peak)
            mass = mass * rescale + jnp.sum(weights, axis=0, keepdims=True)
            turned = turned_ref[:, dyn(k0, BK, BK)]
            mix = mix * rescale + dot_nn(turned, weights.astype(bf16))
            return (new_peak, mass, mix)

        def finish(peak, mass, mix):
            exact = mix / mass
            exact_ref[:, dyn(q0, BQ, BQ)] = exact
            lse_ref[:, dyn(q0, BQ, BQ)] = peak + jnp.log(mass)
            padded = jnp.concatenate([exact, exact], axis=0)
            held_ref[dyn(q0, BQ, BQ), :] = padded.T

        @pl.when(whole)
        def _():
            *unused, state = row_of_tiles(
                first, last, block, quick_step, start_state[1:], None, None
            )
            finish(own, *state)

        @pl.when(jnp.logical_not(whole))
        def _():
            finish(*lax.fori_loop(first, last, step, start_state))

        return unused

    lax.fori_loop(info_ref[1], info_ref[2], one_block, 0)
    half = slots // 2
    low = lane_low((SPAN, LANES))
    for source in range(x_ref.shape[0]):
        for pair in range(half):
            places = [
                place_of(order_ref, info_ref, source, pair + m * half, slots) * SPAN
                for m in range(2)
            ]
            tiles = [held_ref[dyn(place, SPAN, SPAN), :] for place in places]
            mixed_ref[source, pair * SPAN : (pair + 1) * SPAN, :] = jnp.where(
                low, tiles[0], tiles[1]
            ).astype(bf16)


def vmem(shape, dtype):
    return pltpu.VMEM(shape, dtype)


def smem_spec():
    return pl.BlockSpec(memory_space=pltpu.SMEM)


def vmem_spec():
    return pl.BlockSpec(memory_space=pltpu.VMEM)


def attention_vmem(total):
    return int(min(58, 16 + 44 * (total / 16384)) * MIB)


def attend(order, ends, info, swapped, bias_rows, slots):
    sources = swapped.shape[0]
    total = sources * slots * SPAN
    return pl.pallas_call(
        functools.partial(attend_kernel, slots),
        in_specs=[smem_spec()] * 3 + [vmem_spec()] * 2,
        out_specs=[vmem_spec()] * 3,
        out_shape=[
            jax.ShapeDtypeStruct((sources, slots * SPAN // 2, LANES), bf16),
            jax.ShapeDtypeStruct((HD, total), f32),
            jax.ShapeDtypeStruct((1, total), f32),
        ],
        scratch_shapes=[
            vmem((total, LANES), bf16),
            vmem((total, LANES), bf16),
            vmem((HD, total), bf16),
            vmem((BK, BQ), f32),
            vmem((2, SPAN, SPAN), f32),
            vmem((total, LANES), f32),
            vmem((8, total), f32),
        ],
        compiler_params=pltpu.CompilerParams(vmem_limit_bytes=attention_vmem(total)),
        cost_estimate=pl.CostEstimate(
            flops=total * total * 128, bytes_accessed=total * 2048, transcendentals=total * total // 2
        ),
        name="attend",
    )(order, ends, info, swapped, bias_rows)


def unroll_rows(tile):
    row = lax.broadcasted_iota(jnp.int32, tile.shape, 0)
    bit = 1
    while bit < tile.shape[0]:
        moved = pltpu.roll(tile, tile.shape[1] - bit, 1)
        tile = jnp.where((row // bit) % 2 == 1, moved, tile)
        bit *= 2
    return tile


def attend_back_kernel(
    slots, bucket_count, order_ref, ends_ref, info_ref, x_ref, mixed_ref, exact_ref, lse_ref,
    bias_ref, bucket_ref, grad_ref,
    both_ref, query_ref, back_ref, turned_ref, table_ref, corner_ref, d_block_ref, d_corner_ref,
    d_both_ref, d_query_ref, far_ref,
):
    total = both_ref.shape[0]
    sources = x_ref.shape[0]
    half = slots // 2
    low = lane_low((SPAN, LANES))

    def keep(place, both, query):
        both_ref[dyn(place, SPAN, SPAN), :] = both
        query_ref[dyn(place, SPAN, SPAN), :] = query
        turned = both.astype(f32).T
        turned_ref[:HD, dyn(place, SPAN, SPAN)] = turned[HD:, :].astype(bf16)

    sort_blocks(order_ref, info_ref, x_ref, slots, keep)
    low_half = lane_low((SPAN // 2, LANES))
    for block in range(mixed_ref.shape[0]):
        packed = mixed_ref[block].astype(f32)
        for part, tile in enumerate((packed, swap_halves(packed))):
            start = order_ref[block] * SPAN + part * (SPAN // 2)
            back_ref[dyn(start, SPAN // 2, SPAN // 2), :] = jnp.where(low_half, tile, 0.0).astype(bf16)
    fill_tables(bias_ref, table_ref, corner_ref)
    tail = lax.broadcasted_iota(jnp.int32, (KT_ROWS - HD, total), 0)
    turned_ref[HD:, :] = jnp.where(tail == 0, 1.0, 0.0).astype(bf16)
    d_block_ref[...] = jnp.zeros_like(d_block_ref)
    d_corner_ref[...] = jnp.zeros_like(d_corner_ref)
    d_both_ref[...] = jnp.zeros_like(d_both_ref)
    far_ref[...] = jnp.zeros_like(far_ref)
    if info_ref.shape[0] > 3:
        d_query_ref[...] = jnp.zeros_like(d_query_ref)
    left_bias = bias_ref[NEAR : NEAR + 1, 0:1]
    right_bias = bias_ref[NEAR + 1 : NEAR + 2, 0:1]

    def one_block(block, unused):
        q0 = block * BQ
        first, last, whole = block_range(ends_ref, q0, total)
        query = query_ref[dyn(q0, BQ, BQ), :]
        back = back_ref[dyn(q0, BQ, BQ), :]
        lse = lse_ref[:, dyn(q0, BQ, BQ)]
        turned_back = back.astype(f32).T[:HD, :]
        delta = jnp.sum(turned_back * exact_ref[:, dyn(q0, BQ, BQ)], axis=0, keepdims=True)

        def step(kind, tile, d_turned):
            k0 = tile * BK
            keys = dyn(k0, BK, BK)
            both = both_ref[keys, :]
            scores = dot_nt(both, query)
            if kind == "diagonal":
                weights = jnp.exp(scores + table_ref[...] - lse)
            elif kind == "cut":
                bias = any_bias(bias_ref, table_ref, corner_ref, tile, block)
                weights = jnp.exp(jnp.where(same_sequence(ends_ref, k0, q0), scores + bias - lse, masked_score))
            else:
                if kind in ("prev", "next"):
                    scores = with_corner(scores, kind, corner_ref[0 if kind == "prev" else 1])
                weights = jnp.exp(scores - (lse - (left_bias if kind in ("left", "prev") else right_bias)))
            d_probs = dot_nt(both, back)
            d_scores = (weights * (d_probs - delta)).astype(bf16)
            if kind == "diagonal":
                add_blocks(d_scores.astype(f32))
            elif kind in ("prev", "next"):
                m = 0 if kind == "prev" else 1
                d_corner_ref[m] = d_corner_ref[m] + corner_of(d_scores, kind).astype(f32)
            elif kind == "cut":
                wide = d_scores.astype(f32)
                sums = jnp.sum(wide, axis=0, keepdims=True)

                @pl.when(tile == block)
                def _():
                    add_blocks(wide)

                for m, (there, corner) in enumerate(
                    ((tile < block, tile + 1 == block), (tile > block, tile == block + 1))
                ):
                    far_ref[m : m + 1, :] = far_ref[m : m + 1, :] + jnp.where(there, sums, 0.0)
                    piece = corner_of(wide, ("prev", "next")[m])
                    d_corner_ref[m] = d_corner_ref[m] + jnp.where(corner, piece, 0.0)
            d_both_ref[keys, :] = (
                d_both_ref[keys, :] + dot_nn(weights.astype(bf16), back) + dot_nn(d_scores, query)
            )
            return d_turned + dot_nn(turned_ref[:, keys], d_scores)

        def add_blocks(wide):
            sums = [None] * (NEAR + 2)
            for a in range(BK // SPAN):
                for b in range(BQ // SPAN):
                    piece = wide[a * SPAN : (a + 1) * SPAN, b * SPAN : (b + 1) * SPAN]
                    at = block_step(a, b)
                    sums[at] = piece if sums[at] is None else sums[at] + piece
            for at, item in enumerate(sums):
                d_block_ref[at] = d_block_ref[at] + item

        def finish(d_turned):
            top = d_turned[:HD, :]
            d_query_ref[dyn(q0, BQ, BQ), :] = jnp.concatenate([top, top], axis=0).T.astype(bf16)

        zero = jnp.zeros((KT_ROWS, BQ), f32)

        @pl.when(whole)
        def _():
            parts = row_of_tiles(first, last, block, step, zero, zero, zero)
            for m in range(2):
                far_ref[m : m + 1, :] = far_ref[m : m + 1, :] + parts[2 * m][HD : HD + 1, :]
            finish(parts[0] + parts[1] + parts[2])

        @pl.when(jnp.logical_not(whole))
        def _():
            finish(lax.fori_loop(first, last, functools.partial(step, "cut"), zero))

        return unused

    lax.fori_loop(info_ref[1], info_ref[2], one_block, 0)

    d_blocks = [d_block_ref[0] + d_corner_ref[0], d_block_ref[1], d_block_ref[2] + d_corner_ref[1]]
    blank = jnp.zeros((SPAN, WIDE - SPAN), f32)
    sums = [
        jnp.sum(unroll_rows(jnp.concatenate([tile, blank], axis=1)), axis=0, keepdims=True)
        for tile in d_blocks
    ]
    for m in range(2):
        line = jnp.sum(d_block_ref[NEAR + m] - d_corner_ref[m], axis=0, keepdims=True)
        for b in range(BQ // SPAN):
            line = line + far_ref[m : m + 1, b * SPAN : (b + 1) * SPAN]
        sums.append(jnp.concatenate([line, blank[:1]], axis=1))
    sums = jnp.concatenate(sums, axis=0)
    buckets = bucket_ref[: NEAR + 2, :]
    by_bucket = jnp.concatenate(
        [
            jnp.sum(jnp.where(buckets == bucket, sums, 0.0), axis=0, keepdims=True)
            for bucket in range(bucket_count)
        ],
        axis=0,
    )
    totals = jnp.broadcast_to(jnp.sum(by_bucket, axis=1, keepdims=True), (bucket_count, LANES))
    upper = totals.astype(bf16).astype(f32)
    rest = totals - upper
    per_source = bucket_count // sources
    spare = jnp.zeros((EXTRA // 2 - per_source, LANES), f32)
    for source in range(sources):
        span = slice(source * per_source, (source + 1) * per_source)
        grad_ref[source, 3 * half * SPAN :, :] = jnp.concatenate(
            [upper[span], spare, rest[span], spare], axis=0
        ).astype(bf16)

    for source in range(sources):
        for pair in range(half):
            tiles = []
            for member in range(2):
                slot = pair + member * half
                place = place_of(order_ref, info_ref, source, slot, slots) * SPAN
                grad_ref[source, slot * SPAN : (slot + 1) * SPAN, :] = d_both_ref[
                    dyn(place, SPAN, SPAN), :
                ].astype(bf16)
                tiles.append(d_query_ref[dyn(place, SPAN, SPAN), :].astype(f32))
            grad_ref[source, (slots + pair) * SPAN : (slots + pair + 1) * SPAN, :] = jnp.where(
                low, tiles[0], tiles[1]
            ).astype(bf16)


def attend_back(
    order, ends, info, swapped, mixed_grad, exact, lse, bias_rows, bucket_rows, slots, bucket_count
):
    sources = swapped.shape[0]
    total = sources * slots * SPAN
    return pl.pallas_call(
        functools.partial(attend_back_kernel, slots, bucket_count),
        in_specs=[smem_spec()] * 3 + [vmem_spec()] * 6,
        out_specs=vmem_spec(),
        out_shape=jax.ShapeDtypeStruct((sources, slots * SPAN * 3 // 2 + EXTRA, LANES), bf16),
        scratch_shapes=[
            vmem((total, LANES), bf16),
            vmem((total, LANES), bf16),
            vmem((total, LANES), bf16),
            vmem((KT_ROWS, total), bf16),
            vmem((BK, BQ), f32),
            vmem((2, SPAN, SPAN), f32),
            vmem((NEAR + 2, SPAN, SPAN), f32),
            vmem((2, SPAN, SPAN), f32),
            vmem((total, LANES), f32),
            vmem((total, LANES), bf16),
            vmem((8, BQ), f32),
        ],
        compiler_params=pltpu.CompilerParams(vmem_limit_bytes=attention_vmem(total)),
        cost_estimate=pl.CostEstimate(
            flops=total * total * 320, bytes_accessed=total * 3072, transcendentals=total * total // 2
        ),
        name="attend_back",
    )(order, ends, info, swapped, mixed_grad, exact, lse, bias_rows, bucket_rows)


def out_kernel(slots, packed_ref, weight_ref, mix_ref, *part_refs):
    heads = packed_ref.shape[0]
    half = slots * SPAN // 2

    @pl.when(pl.program_id(0) == 0)
    def _():
        for pair in range(heads // 2):
            first = packed_ref[2 * pair].astype(f32)
            second = packed_ref[2 * pair + 1].astype(f32)
            top, bottom = pair_up(first, second)
            cols = slice(pair * LANES, (pair + 1) * LANES)
            mix_ref[:half, cols] = top.astype(bf16)
            mix_ref[half:, cols] = bottom.astype(bf16)

    part = dot_nn(mix_ref[...], weight_ref[...]).astype(bf16)
    for s in range(slots):
        part_refs[s][...] = part[s * SPAN : (s + 1) * SPAN]


def out_project(packed, weight, slots):
    heads = packed.shape[0]
    rows, width, depth = slots * SPAN, heads * HD, weight.shape[1]
    tile = 512
    return pl.pallas_call(
        functools.partial(out_kernel, slots),
        grid=(depth // tile,),
        in_specs=[
            pl.BlockSpec(packed.shape, lambda j: (0, 0, 0)),
            pl.BlockSpec((width, tile), lambda j: (0, j)),
        ],
        out_specs=[
            pl.BlockSpec((rows, width), lambda j: (0, 0)),
        ]
        + [pl.BlockSpec((SPAN, tile), lambda j: (0, j))] * slots,
        out_shape=[jax.ShapeDtypeStruct((rows, width), bf16)]
        + [jax.ShapeDtypeStruct((SPAN, depth), bf16)] * slots,
        compiler_params=pltpu.CompilerParams(vmem_limit_bytes=40 * MIB),
        cost_estimate=pl.CostEstimate(
            flops=2 * rows * depth * width, bytes_accessed=4 * depth * width, transcendentals=0
        ),
        name="out_project",
    )(packed, weight)


def feed_kernel(slots, *refs):
    normed_refs, grad_refs = refs[:slots], refs[slots : 2 * slots]
    gate_ref, up_ref, down_ref, active_ref, d_both_ref, rows_ref, rows_grad_ref = refs[2 * slots :]

    @pl.when(pl.program_id(0) == 0)
    def _():
        for s in range(slots):
            rows_ref[s * SPAN : (s + 1) * SPAN, :] = normed_refs[s][...]
            rows_grad_ref[s * SPAN : (s + 1) * SPAN, :] = grad_refs[s][...]

    tile = down_ref.shape[1]
    width = d_both_ref.shape[1] // 2
    gate = dot_nn(rows_ref[...], gate_ref[...])
    up = dot_nn(rows_ref[...], up_ref[...])
    d_hidden = dot_nn(rows_grad_ref[...], down_ref[...])
    scale, cubic = 0.7978845608028654, 0.044715
    square = gate * gate
    bent = jnp.tanh(scale * (gate + cubic * square * gate))
    half = 0.5 * (1.0 + bent)
    gelu = gate * half
    slope = half + 0.5 * gate * (1.0 - bent * bent) * (scale * (1.0 + 3.0 * cubic * square))
    active_ref[...] = (gelu * up).astype(bf16)
    start = pl.program_id(0) * tile
    d_both_ref[:, dyn(start, tile, tile)] = (d_hidden * up * slope).astype(bf16)
    d_both_ref[:, dyn(width + start, tile, LANES)] = (d_hidden * gelu).astype(bf16)


def feed_tile(width):
    return 256 if width % 256 == 0 else 128


def feed(normed_slots, grad_slots, weights):
    slots = len(normed_slots)
    rows, depth, width = slots * SPAN, weights.shape[0], weights.shape[1] // 3
    tile = feed_tile(width)
    steps = width // tile
    whole = pl.BlockSpec((SPAN, depth), lambda j: (0, 0))

    def columns(part):
        return pl.BlockSpec((depth, tile), lambda j: (0, part * steps + j))

    return pl.pallas_call(
        functools.partial(feed_kernel, slots),
        grid=(steps,),
        in_specs=[whole] * (2 * slots) + [columns(0), columns(1), columns(2)],
        out_specs=[
            pl.BlockSpec((rows, tile), lambda j: (0, j)),
            pl.BlockSpec((rows, 2 * width), lambda j: (0, 0)),
        ],
        out_shape=[
            jax.ShapeDtypeStruct((rows, width), bf16),
            jax.ShapeDtypeStruct((rows, 2 * width), bf16),
        ],
        scratch_shapes=[vmem((rows, depth), bf16), vmem((rows, depth), bf16)],
        compiler_params=pltpu.CompilerParams(vmem_limit_bytes=56 * MIB),
        cost_estimate=pl.CostEstimate(
            flops=6 * rows * depth * width,
            bytes_accessed=6 * depth * width,
            transcendentals=rows * width,
        ),
        name="feed",
    )(*normed_slots, *grad_slots, weights, weights, weights)


def pack_kernel(slots, shares, spot_ref, mine_ref, rest_ref, packed_ref):
    width = mine_ref.shape[1]
    half = SPAN // 2
    for s in range(slots):
        there = lax.rem(spot_ref[0] - s + slots, slots)
        for pair in range(width // LANES):
            if s == 0:
                tile = mine_ref[:, pair * LANES : (pair + 1) * LANES].astype(f32)
            else:
                start = (s - 1) * width + pair * LANES
                tile = rest_ref[:, start : start + LANES].astype(f32)
            for member, piece in enumerate(pair_up(tile[:half], tile[half:])):
                for share in range(shares):
                    packed_ref[(2 * pair + member) * shares + share, there] = piece.astype(bf16)


def pack(spot, mine, rest, shares):
    width = mine.shape[1]
    slots = 1 + rest.shape[1] // width
    return pl.pallas_call(
        functools.partial(pack_kernel, slots, shares),
        in_specs=[smem_spec(), vmem_spec(), vmem_spec()],
        out_specs=vmem_spec(),
        out_shape=jax.ShapeDtypeStruct((width // HD * shares, slots, SPAN // 2, LANES), bf16),
        compiler_params=pltpu.CompilerParams(vmem_limit_bytes=16 * MIB),
        name="pack",
    )(spot, mine, rest)


def project_back_kernel(slots, packed_ref, weight_ref, scale_ref, mix_ref, left_ref, *refs):
    x_refs, attn_refs = refs[:slots], refs[slots : 2 * slots]
    product_ref, gain_ref = refs[2 * slots : 2 * slots + 2]
    part_refs, grads_ref = refs[2 * slots + 2 : -1], refs[-1]
    heads = packed_ref.shape[0]
    rows = slots * SPAN
    half = rows // 2
    width = heads * HD

    @pl.when(pl.program_id(0) == 0)
    def _():
        for pair in range(heads // 2):
            start = pair * LANES
            tiles = [packed_ref[2 * pair + m].astype(f32) for m in range(2)]
            value, key = pair_up(tiles[0][:rows], tiles[1][:rows])
            top, bottom = pair_up(tiles[0][rows : rows + half], tiles[1][rows : rows + half])
            grads_ref[:half, start : start + LANES] = top.astype(bf16)
            grads_ref[half:, start : start + LANES] = bottom.astype(bf16)
            grads_ref[:, width + start : width + start + LANES] = key.astype(bf16)
            grads_ref[:, 2 * width + start : 2 * width + start + LANES] = value.astype(bf16)

    part = dot_nt(grads_ref[...], weight_ref[...])
    gain = jnp.zeros((1, part.shape[1]), f32)
    for s in range(slots):
        span = slice(s * SPAN, (s + 1) * SPAN)
        part_refs[s][...] = part[span].astype(bf16)
        x_hat = x_refs[s][...].astype(f32) * scale_ref[span, :1]
        gain = gain + jnp.sum(part[span] * x_hat, axis=0, keepdims=True)
    gain_ref[...] = gain
    product_ref[:, : 3 * width] = dot_tn(left_ref[...], grads_ref[...]).astype(bf16)
    attn = jnp.concatenate([ref[...] for ref in attn_refs], axis=0)
    product_ref[:, 3 * width :] = dot_tn(attn, mix_ref[...]).astype(bf16)


def project_back(packed, weights, scale, mix, left, x_slots, attn_slots):
    slots = len(x_slots)
    depth, width = weights.shape
    rows = slots * SPAN
    tile = 256
    spans = [pl.BlockSpec((SPAN, tile), lambda j: (0, j))] * slots
    total = width + mix.shape[1]
    return pl.pallas_call(
        functools.partial(project_back_kernel, slots),
        grid=(depth // tile,),
        in_specs=[
            pl.BlockSpec(packed.shape, lambda j: (0, 0, 0)),
            pl.BlockSpec((tile, width), lambda j: (j, 0)),
            pl.BlockSpec((rows, LANES), lambda j: (0, 0)),
            pl.BlockSpec(mix.shape, lambda j: (0, 0)),
            pl.BlockSpec((rows, tile), lambda j: (0, j)),
        ]
        + spans
        + spans,
        out_specs=[
            pl.BlockSpec((tile, total), lambda j: (j, 0)),
            pl.BlockSpec((1, tile), lambda j: (0, j)),
        ]
        + spans,
        out_shape=[
            jax.ShapeDtypeStruct((depth, total), bf16),
            jax.ShapeDtypeStruct((1, depth), f32),
        ]
        + [jax.ShapeDtypeStruct((SPAN, depth), bf16)] * slots,
        scratch_shapes=[vmem((rows, width), bf16)],
        compiler_params=pltpu.CompilerParams(vmem_limit_bytes=LARGE),
        cost_estimate=pl.CostEstimate(
            flops=4 * rows * depth * total, bytes_accessed=4 * depth * total, transcendentals=0
        ),
        name="project_back",
    )(packed, weights, scale, mix, left, *x_slots, *attn_slots)


def pair_kernel(slots, groups, *refs):
    left_one, left_two = refs[:slots], refs[slots : 2 * slots]
    right_one = refs[2 * slots : 2 * slots + groups]
    right_two = refs[2 * slots + groups : 2 * slots + 2 * groups]
    out_ref, right_ref = refs[-2:]
    cut = right_one[0].shape[1]

    @pl.when(pl.program_id(0) == 0)
    def _():
        start = 0
        for one, two in zip(right_one, right_two, strict=True):
            span = slice(start, start + one.shape[0])
            right_ref[span, :cut] = one[...]
            right_ref[span, cut:] = two[...]
            start += one.shape[0]

    one = jnp.concatenate([ref[...] for ref in left_one], axis=0)
    two = jnp.concatenate([ref[...] for ref in left_two], axis=0)
    out_ref[:, :cut] = dot_tn(one, right_ref[:, :cut]).astype(bf16)
    out_ref[:, cut:] = dot_tn(two, right_ref[:, cut:]).astype(bf16)


def pair_product(left_one, right_one, left_two, right_two):
    slots, groups = len(left_one), len(right_one)
    rows, depth = slots * SPAN, left_one[0].shape[1]
    width = right_one[0].shape[1] + right_two[0].shape[1]
    block = 256

    def whole(array):
        return pl.BlockSpec(array.shape, lambda j: (0, 0))

    return pl.pallas_call(
        functools.partial(pair_kernel, slots, groups),
        grid=(depth // block,),
        in_specs=[pl.BlockSpec((SPAN, block), lambda j: (0, j))] * (2 * slots)
        + [whole(piece) for piece in (*right_one, *right_two)],
        out_specs=pl.BlockSpec((block, width), lambda j: (j, 0)),
        out_shape=jax.ShapeDtypeStruct((depth, width), bf16),
        scratch_shapes=[vmem((rows, width), bf16)],
        compiler_params=pltpu.CompilerParams(vmem_limit_bytes=32 * MIB),
        cost_estimate=pl.CostEstimate(
            flops=2 * rows * depth * width, bytes_accessed=2 * depth * width, transcendentals=0
        ),
        name="pair_product",
    )(*left_one, *left_two, *right_one, *right_two)


def bucket_lines(bucket_of):
    count = bucket_of.shape[0]
    turned = bucket_of[::-1]
    ends = [jnp.broadcast_to(end, (2 * SPAN,)) for end in (turned[:1], turned[-1:])]
    padded = jnp.concatenate([ends[0], turned, ends[1]])
    zero_at = 2 * SPAN + count // 2
    rows = []
    for c in range(NEAR):
        base = zero_at - (c - 1) * SPAN
        rows.append(jnp.concatenate([padded[base : base + SPAN], padded[base - SPAN : base]]))
    rows.append(jnp.broadcast_to(bucket_of[:1], (WIDE,)))
    rows.append(jnp.broadcast_to(bucket_of[-1:], (WIDE,)))
    spare = 8 - (NEAR + 2)
    return jnp.concatenate([jnp.stack(rows), jnp.full((spare, WIDE), -1, bucket_of.dtype)])


def on_device(
    tokens,
    lengths,
    block_order,
    bucket_of,
    gain_attn,
    w_query,
    w_key,
    w_value,
    w_out,
    bias_table,
    gain_ffn,
    w_gate,
    w_up,
    w_down,
    cotangent,
):
    blk_count, slots = lax.axis_size("blk"), lax.axis_size("head")
    blk_spot, head_spot = lax.axis_index("blk"), lax.axis_index("head")
    depth = tokens.shape[1]
    width = w_query.shape[1]
    heads = width // HD
    shares = blk_count // heads
    table_rows, table_heads = bias_table.shape
    bucket_count = table_rows * blk_count
    total = blk_count * slots * SPAN
    gain_size = gain_attn.shape[0]
    hidden = w_gate.shape[1]

    token_slots = gather_far(gather_near(tokens))
    small = gather_small(
        jnp.concatenate([gain_attn, gain_ffn, bias_table.astype(f32).reshape(-1)])
    )
    full_qkv = lax.all_gather(
        jnp.concatenate([w_query, w_key, w_value], axis=1), "blk", axis=0, tiled=True
    )
    full_out = lax.all_gather(w_out, "blk", axis=1, tiled=True)
    full_ffn = lax.all_gather(
        jnp.concatenate([w_gate, w_up, w_down.T], axis=1), "blk", axis=0, tiled=True
    )
    gain_one = small[:, :, :gain_size].reshape(1, depth)
    gain_two = small[:, :, gain_size : 2 * gain_size].reshape(1, depth)

    tables = lax.dynamic_index_in_dim(small, head_spot, 1, False)[:, 2 * gain_size :]
    tables = tables.reshape(bucket_count, table_heads)
    my_head = blk_spot // shares
    my_bias = lax.dynamic_index_in_dim(tables, my_head, 1, False)
    bucket_rows = bucket_lines(bucket_of)
    bias_rows = jnp.sum(
        jnp.where(
            bucket_rows[None] == jnp.arange(bucket_count, dtype=jnp.int32)[:, None, None],
            my_bias[:, None, None],
            0.0,
        ),
        axis=0,
    )
    ends = jnp.cumsum(lengths).astype(jnp.int32)
    per_share = total // BQ // shares
    start = (blk_spot % shares) * per_share
    info = [head_spot, start, start + per_share] + ([start] if shares > 1 else [])
    info = jnp.stack([jnp.asarray(item, jnp.int32) for item in info])

    def swap(values):
        return lax.all_to_all(values, "blk", 0, 0, tiled=True)

    def to_all(values):
        values = values.reshape((blk_count * slots,) + values.shape[2:])
        return lax.all_to_all(values, ("blk", "head"), 0, 0, tiled=True)

    def to_heads(values):
        return swap(values if shares == 1 else jnp.repeat(values, shares, axis=0))

    def to_rows(values):
        values = swap(values)
        if shares == 1:
            return values
        values = values.reshape((heads, shares) + values.shape[1:])
        return jnp.sum(values.astype(f32), axis=1).astype(bf16)

    w_out, cotangent, *token_slots = together(w_out, cotangent, *token_slots)
    normed_one, packed, scale_one = project(token_slots, gain_one, full_qkv)
    early = (ends, info, bias_rows, bucket_rows)
    swapped, ends, info, bias_rows, bucket_rows, *out_near = together(
        to_heads(packed), *early, *gather_near(w_out)
    )
    grad_near, out_slots = gather_near(cotangent), gather_far(out_near)
    mixed, exact, lse = attend(block_order, ends, info, swapped, bias_rows, slots)
    mixed, *moved = together(mixed, *grad_near, *out_slots)
    grad_near, out_slots = moved[: len(grad_near)], moved[len(grad_near) :]
    packed_mix, *grad_slots = together(to_rows(mixed), *gather_far(grad_near))
    attn_mix, *out_parts = out_project(packed_mix, full_out, slots)
    out_parts, out_slots = together(out_parts, out_slots)
    full_rest = lax.all_gather(jnp.concatenate(out_slots[1:]), "blk", axis=1, tiled=True)
    tokens_wide = tokens.astype(f32)
    hidden_one = tokens_wide + sum_terms(sum_near(out_parts, sum_far(out_parts))[0])
    rstd_two = rms_scale(hidden_one)
    normed_two = (hidden_one * rstd_two * gain_two).astype(bf16)

    normed_slots = gather_far(gather_near(normed_two))
    active, d_both = feed(normed_slots, grad_slots, full_ffn)

    def spans(rows):
        return [rows[s * SPAN : (s + 1) * SPAN] for s in range(rows.shape[0] // SPAN)]

    d_parts = spans(dot_nt(d_both, full_ffn[:, : 2 * hidden]).astype(bf16))
    d_far = sum_far(d_parts)
    grad_hidden, *d_far = together(
        pair_product(normed_slots, [d_both], grad_slots, [active]), *d_far
    )
    grad_hidden = lax.psum_scatter(grad_hidden, "blk", scatter_dimension=0, tiled=True)
    d_near, (active,) = sum_near(d_parts, d_far, (active,))
    down_rows = dot_nt(active, full_ffn[:, 2 * hidden :]).astype(bf16)
    down_rows, full_rest, *d_near = together(down_rows, full_rest, *d_near)
    down_parts = spans(down_rows)
    d_normed_two = sum_terms(d_near)
    d_source_two, gain_part_two = norm_back(d_normed_two, hidden_one, rstd_two, gain_two)
    d_hidden_one = cotangent.astype(f32) + d_source_two

    d_attn = d_hidden_one.astype(bf16)
    mix_grads = pack(
        jnp.reshape(head_spot, (1,)).astype(jnp.int32),
        dot_nt(d_attn, full_out).astype(bf16),
        dot_nt(d_attn, full_rest).astype(bf16),
        shares,
    )
    mix_grads, d_attn = together(mix_grads, d_attn)
    middle = slots // 2
    steps = [t for t in range(1, slots) if t != middle]
    moved = (*gather_near(d_attn), *sum_direct(down_parts, steps))
    grads = attend_back(
        block_order, ends, info, swapped, to_all(mix_grads), exact, lse, bias_rows, bucket_rows,
        slots, bucket_count,
    )
    grads, *moved = together(grads, *moved)
    attn_near, down_terms = moved[: 2 - slots], moved[2 - slots :]
    grads, *attn_slots = together(swap(grads), *gather_far(attn_near))
    extra = grads[:, -EXTRA:, 0].astype(f32).reshape(blk_count, 2, -1).sum(axis=1)
    grad_table = extra[:, :table_rows].reshape(heads, shares, table_rows).sum(axis=1).T
    if shares > 1:
        grads = grads.reshape((heads, shares) + grads.shape[1:])
        grads = jnp.sum(grads.astype(f32), axis=1).astype(bf16)
    grad_heads, gain_part_one, *one_parts = project_back(
        grads, full_qkv, scale_one, attn_mix, normed_one, token_slots, attn_slots
    )

    one_far = sum_far(one_parts)
    gain_parts = jnp.stack(
        [part.reshape(blk_count, slots, gain_size) for part in (gain_part_one, gain_part_two)],
        axis=2,
    )
    grad_heads, grad_hidden = together(grad_heads, grad_hidden)
    gain_parts, *one_far = together(gain_parts, *one_far)
    grad_heads = lax.psum_scatter(grad_heads, "blk", scatter_dimension=0, tiled=True).astype(f32)
    one_near, unused = sum_near(one_parts, one_far)
    gain_sums = scatter_blk(gain_parts)
    gain_sums, down_parts, grad_hidden, *one_near = together(
        gain_sums, down_parts, grad_hidden, *one_near
    )
    gain_sums = scatter_head(gain_sums)
    grad_hidden = grad_hidden.astype(f32)
    output = hidden_one + sum_all([down_parts[0]] + down_terms + sum_direct(down_parts, [middle]))
    d_normed_one = sum_terms(one_near)
    d_source_one, unused = norm_back(d_normed_one, tokens_wide, rms_scale(tokens_wide), gain_one)
    input_grad = d_hidden_one + d_source_one
    return (
        output,
        input_grad,
        gain_sums[0],
        grad_heads[:, :width],
        grad_heads[:, width : 2 * width],
        grad_heads[:, 2 * width : 3 * width],
        grad_heads[:, 3 * width :].T,
        grad_table,
        gain_sums[1],
        grad_hidden[:, :hidden],
        grad_hidden[:, hidden : 2 * hidden],
        grad_hidden[:, 2 * hidden :].T,
    )


def solution(mesh):
    rows, spread = P(("blk", "head"), None), P(("blk", "head"))
    inward, outward = P("blk", "head"), P("head", "blk")
    in_specs = (
        rows, P(), P(), P(), spread, inward, inward, inward, outward, inward, spread,
        inward, inward, outward, rows,
    )
    out_specs = (
        rows, rows, spread, inward, inward, inward, outward, inward, spread,
        inward, inward, outward,
    )
    return jax.shard_map(
        on_device, mesh=mesh, in_specs=in_specs, out_specs=out_specs, check_vma=False
    )
```

```python
import functools

import jax
import jax.numpy as jnp
from jax import lax
from jax.experimental import pallas as pl
from jax.experimental.pallas import tpu as pltpu
from jax.sharding import PartitionSpec as P

HD = 64
LANES = 2 * HD
MAXDIST = 128
SPAN = 128
BQ = 512
BK = BQ
NEAR = 3
WIDE = 2 * SPAN
EXTRA = 16
KT_ROWS = 80
SHIFT_ROOM = 60.0

norm_eps = 1e-06
masked_score = -1e30
f32 = jnp.float32
bf16 = jnp.bfloat16
MIB = 1 << 20
LARGE = 58 * MIB


def rms_scale(values):
    return lax.rsqrt(jnp.mean(values * values, axis=-1, keepdims=True) + norm_eps)


def norm_back(d_normed, source, inv_rms, gain_vec):
    scaled = d_normed * gain_vec
    x_hat = source * inv_rms
    gain_part = jnp.sum(d_normed * x_hat, axis=0)
    d_source = inv_rms * (scaled - x_hat * jnp.mean(scaled * x_hat, axis=-1, keepdims=True))
    return (d_source, gain_part)


def dot_nn(left, right):
    return jnp.dot(left, right, preferred_element_type=f32)


def dot_nt(left, right):
    return lax.dot_general(left, right, (((1,), (1,)), ((), ())), preferred_element_type=f32)


def dot_tn(left, right):
    return lax.dot_general(left, right, (((0,), (0,)), ((), ())), preferred_element_type=f32)


def cyclic(count, by):
    return [(i, (i + by) % count) for i in range(count)]


def together(*values):
    return lax.optimization_barrier(values)


def gather_near(rows):
    count = lax.axis_size("head")
    if count != 4:
        return [rows] + [lax.ppermute(rows, "head", cyclic(count, s)) for s in range(1, count)]
    return [rows, lax.ppermute(rows, "head", cyclic(4, 1)), lax.ppermute(rows, "head", cyclic(4, 3))]


def gather_far(near):
    if lax.axis_size("head") != 4:
        return near
    rows, back_one, ahead_one = near
    me = lax.axis_index("head")
    passed = jnp.where(me == 1, ahead_one, jnp.where(me == 2, back_one, rows))
    back_two = lax.ppermute(passed, "head", [(1, 0), (3, 1), (0, 2), (2, 3)])
    return [rows, back_one, back_two, ahead_one]


def gather_direct(rows):
    count = lax.axis_size("head")
    return [rows] + [lax.ppermute(rows, "head", cyclic(count, s)) for s in range(1, count)]


def sum_far(parts):
    count = lax.axis_size("head")
    if count != 4:
        return []
    return [lax.ppermute(parts[2], "head", [(0, 1), (1, 3), (2, 0), (3, 2)])]


def sum_near(parts, far, beside=()):
    count = lax.axis_size("head")
    if count != 4:
        return [parts[0]] + [
            lax.ppermute(parts[s], "head", cyclic(count, count - s)) for s in range(1, count)
        ], beside
    me = lax.axis_index("head")
    wide = far[0].astype(f32)
    to_back = jnp.where(me == 2, parts[1].astype(f32) + wide, parts[1].astype(f32)).astype(bf16)
    to_ahead = jnp.where(me == 1, parts[3].astype(f32) + wide, parts[3].astype(f32)).astype(bf16)
    to_back, to_ahead, *beside = together(to_back, to_ahead, *beside)
    from_ahead = lax.ppermute(to_back, "head", cyclic(4, 3))
    from_back = lax.ppermute(to_ahead, "head", cyclic(4, 1))
    return [parts[0], from_ahead, from_back, far[0]], beside


def sum_terms(terms):
    total = terms[0].astype(f32) + terms[1].astype(f32) + terms[2].astype(f32)
    if lax.axis_size("head") != 4:
        for term in terms[3:]:
            total = total + term.astype(f32)
        return total
    me = lax.axis_index("head")
    return total + jnp.where((me == 0) | (me == 3), terms[3].astype(f32), 0.0)


def is_power(count):
    return count & (count - 1) == 0


def gather_small(values):
    held = values[None]
    for axis in ("head", "blk"):
        count = lax.axis_size(axis)
        if not is_power(count):
            held = lax.all_gather(held, axis, axis=0, tiled=False)
        else:
            me = lax.axis_index(axis)
            held = held[None]
            bit = 1
            while bit < count:
                other = lax.ppermute(held, axis, [(i, i ^ bit) for i in range(count)])
                low = jnp.concatenate([held, other])
                high = jnp.concatenate([other, held])
                held = jnp.where((me // bit) % 2 == 0, low, high)
                bit *= 2
        if axis == "head":
            held = held.reshape(count, -1)
    return held


def sum_direct(parts, steps):
    count = len(parts)
    return [lax.ppermute(parts[s], "head", cyclic(count, count - s)) for s in steps]


def sum_all(terms):
    total = terms[0].astype(f32)
    for term in terms[1:]:
        total = total + term.astype(f32)
    return total


def scatter_blk(values):
    return jnp.sum(lax.all_to_all(values, "blk", 0, 0, tiled=True), axis=0)


def scatter_head(values):
    count, me = lax.axis_size("head"), lax.axis_index("head")
    total = lax.dynamic_index_in_dim(values, me, 0, False)
    for s in range(1, count):
        sent = lax.dynamic_index_in_dim(values, (me + s) % count, 0, False)
        total = total + lax.ppermute(sent, "head", cyclic(count, s))
    return total


def lane_low(shape):
    return lax.broadcasted_iota(jnp.int32, shape, 1) < HD


def swap_halves(tile):
    return pltpu.roll(tile, HD, 1)


def pair_up(first, second):
    low = lane_low(first.shape)
    return (
        jnp.where(low, first, swap_halves(second)),
        jnp.where(low, swap_halves(first), second),
    )


def project_kernel(slots, *refs):
    x_refs = refs[:slots]
    gain_ref, wq_ref, wk_ref, wv_ref, normed_ref, packed_ref, scale_ref = refs[slots:]
    rows = slots * SPAN

    @pl.when(pl.program_id(0) == 0)
    def _():
        for s in range(slots):
            wide = x_refs[s][...].astype(f32)
            scale = rms_scale(wide)
            normed = wide * scale * gain_ref[...]
            normed_ref[s * SPAN : (s + 1) * SPAN, :] = normed.astype(bf16)
            scale_ref[s * SPAN : (s + 1) * SPAN, :] = jnp.broadcast_to(scale, (SPAN, LANES))

    normed = normed_ref[...]
    query = dot_nn(normed, wq_ref[...])
    key = dot_nn(normed, wk_ref[...])
    value = dot_nn(normed, wv_ref[...])
    half = rows // 2
    for pair in range(query.shape[1] // LANES):
        cols = slice(pair * LANES, (pair + 1) * LANES)
        both = pair_up(value[:, cols], key[:, cols])
        queries = pair_up(query[:half, cols], query[half:, cols])
        for member in range(2):
            packed_ref[2 * pair + member, :rows, :] = both[member].astype(bf16)
            packed_ref[2 * pair + member, rows:, :] = queries[member].astype(bf16)


def project(x_slots, gain, weights):
    slots = len(x_slots)
    rows, depth = slots * SPAN, x_slots[0].shape[1]
    width = weights.shape[1] // 3
    heads = width // HD
    tile = min(width, 256)
    steps = width // tile
    whole = pl.BlockSpec((SPAN, depth), lambda j: (0, 0))

    def columns(part):
        return pl.BlockSpec((depth, tile), lambda j: (0, part * steps + j))

    return pl.pallas_call(
        functools.partial(project_kernel, slots),
        grid=(steps,),
        in_specs=[whole] * slots
        + [pl.BlockSpec((1, depth), lambda j: (0, 0)), columns(0), columns(1), columns(2)],
        out_specs=[
            pl.BlockSpec((rows, depth), lambda j: (0, 0)),
            pl.BlockSpec((tile // HD, rows + rows // 2, LANES), lambda j: (j, 0, 0)),
            pl.BlockSpec((rows, LANES), lambda j: (0, 0)),
        ],
        out_shape=[
            jax.ShapeDtypeStruct((rows, depth), bf16),
            jax.ShapeDtypeStruct((heads, rows + rows // 2, LANES), bf16),
            jax.ShapeDtypeStruct((rows, LANES), f32),
        ],
        compiler_params=pltpu.CompilerParams(vmem_limit_bytes=40 * MIB),
        cost_estimate=pl.CostEstimate(
            flops=10 * rows * depth * width, bytes_accessed=6 * depth * width, transcendentals=0
        ),
        name="project",
    )(*x_slots, gain, weights, weights, weights)


def place_of(order_ref, info_ref, source, slot, slots):
    z = info_ref[0]
    return order_ref[source * slots + lax.rem(z - slot + slots, slots)]


def dyn(start, size, multiple):
    return pl.ds(pl.multiple_of(start, multiple), size)


def near_blocks(bias_ref):
    tiles = []
    for c in range(NEAR):
        spread = jnp.broadcast_to(bias_ref[c : c + 1, :], (SPAN, WIDE))
        tiles.append(pltpu.roll(spread, 0, 1, stride=1, stride_axis=0)[:, :SPAN])
    return tiles


def block_step(a, b):
    return a - b + 1 if abs(a - b) <= 1 else 3 if a < b else 4


def fill_tables(bias_ref, table_ref, corner_ref):
    tiles = near_blocks(bias_ref)
    far = [jnp.broadcast_to(bias_ref[NEAR + m : NEAR + m + 1, :SPAN], (SPAN, SPAN)) for m in range(2)]
    every = tiles + far
    for a in range(BK // SPAN):
        for b in range(BQ // SPAN):
            table_ref[a * SPAN : (a + 1) * SPAN, b * SPAN : (b + 1) * SPAN] = every[block_step(a, b)]
    corner_ref[0] = tiles[0] - far[0]
    corner_ref[1] = tiles[2] - far[1]


def with_corner(tile, kind, corner):
    if kind == "prev":
        upper, lower = tile[: BK - SPAN], tile[BK - SPAN :]
        lower = jnp.concatenate([lower[:, :SPAN] + corner, lower[:, SPAN:]], axis=1)
    else:
        upper, lower = tile[:SPAN], tile[SPAN:]
        upper = jnp.concatenate([upper[:, : BQ - SPAN], upper[:, BQ - SPAN :] + corner], axis=1)
    return jnp.concatenate([upper, lower], axis=0)


def corner_of(tile, kind):
    return tile[BK - SPAN :, :SPAN] if kind == "prev" else tile[:SPAN, BQ - SPAN :]


def any_bias(bias_ref, table_ref, corner_ref, tile, block):
    left = jnp.broadcast_to(bias_ref[NEAR : NEAR + 1, 0:1], (BK, BQ))
    right = jnp.broadcast_to(bias_ref[NEAR + 1 : NEAR + 2, 0:1], (BK, BQ))
    left = with_corner(left, "prev", jnp.where(tile + 1 == block, corner_ref[0], 0.0))
    right = with_corner(right, "next", jnp.where(tile == block + 1, corner_ref[1], 0.0))
    return jnp.where(tile == block, table_ref[...], jnp.where(tile < block, left, right))


def block_range(ends_ref, q0, total):
    count = ends_ref.shape[0]
    start, end, cut = jnp.int32(0), jnp.int32(total), jnp.bool_(False)
    for n in range(count):
        edge = ends_ref[n]
        start = jnp.where(edge <= q0, edge, start)
        cut = cut | ((edge > q0) & (edge < q0 + BQ))
    for n in range(count - 1, -1, -1):
        edge = ends_ref[n]
        end = jnp.where(edge >= q0 + BQ, edge, end)
    first = lax.div(start, BK)
    last = lax.div(end + BK - 1, BK)
    whole = jnp.logical_not(cut) & (lax.rem(start, BK) == 0) & (lax.rem(end, BK) == 0)
    return first, last, whole


def row_of_tiles(first, last, block, step, left, middle, right):
    before, after = jnp.maximum(block - 1, first), jnp.minimum(block + 2, last)
    left = lax.fori_loop(first, before, functools.partial(step, "left"), left)
    left = lax.fori_loop(before, block, functools.partial(step, "prev"), left)
    middle = step("diagonal", block, left if middle is None else middle)
    right = middle if right is None else right
    right = lax.fori_loop(block + 1, after, functools.partial(step, "next"), right)
    right = lax.fori_loop(after, last, functools.partial(step, "right"), right)
    return left, middle, right


def same_sequence(ends_ref, k0, q0):
    key_place = k0 + lax.broadcasted_iota(jnp.int32, (BK, 1), 0)
    query_place = q0 + lax.broadcasted_iota(jnp.int32, (1, BQ), 1)
    key_seg = jnp.zeros((BK, 1), jnp.int32)
    query_seg = jnp.zeros((1, BQ), jnp.int32)
    for n in range(ends_ref.shape[0]):
        key_seg = key_seg + jnp.where(key_place >= ends_ref[n], 1, 0)
        query_seg = query_seg + jnp.where(query_place >= ends_ref[n], 1, 0)
    return key_seg == query_seg


def sort_blocks(order_ref, info_ref, x_ref, slots, keep):
    sources = x_ref.shape[0]
    half = slots // 2
    high = jnp.logical_not(lane_low((SPAN, LANES)))
    for source in range(sources):
        for pair in range(half):
            packed = x_ref[
                source, (slots + pair) * SPAN : (slots + pair + 1) * SPAN, :
            ].astype(f32)
            queries = (swap_halves(packed), packed)
            for member in range(2):
                slot = pair + member * half
                place = place_of(order_ref, info_ref, source, slot, slots) * SPAN
                both = x_ref[source, slot * SPAN : (slot + 1) * SPAN, :]
                keep(place, both, jnp.where(high, queries[member], 0.0).astype(bf16))


def attend_kernel(
    slots, order_ref, ends_ref, info_ref, x_ref, bias_ref, mixed_ref, exact_ref, lse_ref,
    both_ref, query_ref, turned_ref, table_ref, corner_ref, held_ref, rows_ref,
):
    total = both_ref.shape[0]
    parted = info_ref.shape[0] > 3

    def keep(place, both, query):
        both_ref[dyn(place, SPAN, SPAN), :] = both
        query_ref[dyn(place, SPAN, SPAN), :] = query
        turned = both.astype(f32).T
        turned_ref[:, dyn(place, SPAN, SPAN)] = turned[:HD, :].astype(bf16)
        turned_key, turned_query = turned[HD:, :], query.astype(f32).T[HD:, :]
        for line, product in enumerate(
            (turned_key * turned_query, turned_key * turned_key, turned_query * turned_query)
        ):
            rows_ref[line : line + 1, dyn(place, SPAN, SPAN)] = jnp.sum(
                product, axis=0, keepdims=True
            )

    sort_blocks(order_ref, info_ref, x_ref, slots, keep)
    fill_tables(bias_ref, table_ref, corner_ref)
    if parted:
        held_ref[...] = jnp.zeros_like(held_ref)
        exact_ref[...] = jnp.zeros_like(exact_ref)
        lse_ref[...] = jnp.zeros_like(lse_ref)
    left_bias = bias_ref[NEAR : NEAR + 1, 0:1]
    right_bias = bias_ref[NEAR + 1 : NEAR + 2, 0:1]
    start_state = (
        jnp.full((1, BQ), masked_score, f32),
        jnp.zeros((1, BQ), f32),
        jnp.zeros((HD, BQ), f32),
    )
    longest_key = jnp.sqrt(jnp.max(rows_ref[1:2, :], axis=1, keepdims=True))
    most_bias = jnp.max(
        jnp.max(bias_ref[: NEAR + 2, :], axis=0, keepdims=True), axis=1, keepdims=True
    )

    def one_block(block, unused):
        q0 = block * BQ
        first, last, whole = block_range(ends_ref, q0, total)
        query = query_ref[dyn(q0, BQ, BQ), :]
        own = rows_ref[0:1, dyn(q0, BQ, BQ)] + bias_ref[1:2, 0:1]
        bound = jnp.sqrt(rows_ref[2:3, dyn(q0, BQ, BQ)]) * longest_key + most_bias
        whole = whole & (jnp.max(bound - own) < SHIFT_ROOM)

        def quick_step(kind, tile, state):
            mass, mix = state
            k0 = tile * BK
            scores = dot_nt(both_ref[dyn(k0, BK, BK), :], query)
            if kind == "diagonal":
                weights = jnp.exp(scores + table_ref[...] - own)
            else:
                if kind in ("prev", "next"):
                    scores = with_corner(scores, kind, corner_ref[0 if kind == "prev" else 1])
                weights = jnp.exp(scores - (own - (left_bias if kind in ("left", "prev") else right_bias)))
            mass = mass + jnp.sum(weights, axis=0, keepdims=True)
            return (mass, mix + dot_nn(turned_ref[:, dyn(k0, BK, BK)], weights.astype(bf16)))

        def step(tile, state):
            peak, mass, mix = state
            k0 = tile * BK
            scores = dot_nt(both_ref[dyn(k0, BK, BK), :], query)
            same = same_sequence(ends_ref, k0, q0)
            scores = scores + any_bias(bias_ref, table_ref, corner_ref, tile, block)
            scores = jnp.where(same, scores, masked_score)
            new_peak = jnp.maximum(peak, jnp.max(scores, axis=0, keepdims=True))
            weights = jnp.where(same, jnp.exp(scores - new_peak), 0.0)
            rescale = jnp.exp(peak - new_peak)
            mass = mass * rescale + jnp.sum(weights, axis=0, keepdims=True)
            turned = turned_ref[:, dyn(k0, BK, BK)]
            mix = mix * rescale + dot_nn(turned, weights.astype(bf16))
            return (new_peak, mass, mix)

        def finish(peak, mass, mix):
            exact = mix / mass
            exact_ref[:, dyn(q0, BQ, BQ)] = exact
            lse_ref[:, dyn(q0, BQ, BQ)] = peak + jnp.log(mass)
            padded = jnp.concatenate([exact, exact], axis=0)
            held_ref[dyn(q0, BQ, BQ), :] = padded.T

        @pl.when(whole)
        def _():
            *unused, state = row_of_tiles(
                first, last, block, quick_step, start_state[1:], None, None
            )
            finish(own, *state)

        @pl.when(jnp.logical_not(whole))
        def _():
            finish(*lax.fori_loop(first, last, step, start_state))

        return unused

    lax.fori_loop(info_ref[1], info_ref[2], one_block, 0)
    half = slots // 2
    low = lane_low((SPAN, LANES))
    for source in range(x_ref.shape[0]):
        for pair in range(half):
            places = [
                place_of(order_ref, info_ref, source, pair + m * half, slots) * SPAN
                for m in range(2)
            ]
            tiles = [held_ref[dyn(place, SPAN, SPAN), :] for place in places]
            mixed_ref[source, pair * SPAN : (pair + 1) * SPAN, :] = jnp.where(
                low, tiles[0], tiles[1]
            ).astype(bf16)


def vmem(shape, dtype):
    return pltpu.VMEM(shape, dtype)


def smem_spec():
    return pl.BlockSpec(memory_space=pltpu.SMEM)


def vmem_spec():
    return pl.BlockSpec(memory_space=pltpu.VMEM)


def attention_vmem(total):
    return int(min(58, 16 + 44 * (total / 16384)) * MIB)


def attend(order, ends, info, swapped, bias_rows, slots):
    sources = swapped.shape[0]
    total = sources * slots * SPAN
    return pl.pallas_call(
        functools.partial(attend_kernel, slots),
        in_specs=[smem_spec()] * 3 + [vmem_spec()] * 2,
        out_specs=[vmem_spec()] * 3,
        out_shape=[
            jax.ShapeDtypeStruct((sources, slots * SPAN // 2, LANES), bf16),
            jax.ShapeDtypeStruct((HD, total), f32),
            jax.ShapeDtypeStruct((1, total), f32),
        ],
        scratch_shapes=[
            vmem((total, LANES), bf16),
            vmem((total, LANES), bf16),
            vmem((HD, total), bf16),
            vmem((BK, BQ), f32),
            vmem((2, SPAN, SPAN), f32),
            vmem((total, LANES), f32),
            vmem((8, total), f32),
        ],
        compiler_params=pltpu.CompilerParams(vmem_limit_bytes=attention_vmem(total)),
        cost_estimate=pl.CostEstimate(
            flops=total * total * 128, bytes_accessed=total * 2048, transcendentals=total * total // 2
        ),
        name="attend",
    )(order, ends, info, swapped, bias_rows)


def unroll_rows(tile):
    row = lax.broadcasted_iota(jnp.int32, tile.shape, 0)
    bit = 1
    while bit < tile.shape[0]:
        moved = pltpu.roll(tile, tile.shape[1] - bit, 1)
        tile = jnp.where((row // bit) % 2 == 1, moved, tile)
        bit *= 2
    return tile


def attend_back_kernel(
    slots, bucket_count, order_ref, ends_ref, info_ref, x_ref, mixed_ref, exact_ref, lse_ref,
    bias_ref, bucket_ref, grad_ref,
    both_ref, query_ref, back_ref, turned_ref, table_ref, corner_ref, d_block_ref, d_corner_ref,
    d_both_ref, d_query_ref, far_ref,
):
    total = both_ref.shape[0]
    sources = x_ref.shape[0]
    half = slots // 2
    low = lane_low((SPAN, LANES))

    def keep(place, both, query):
        both_ref[dyn(place, SPAN, SPAN), :] = both
        query_ref[dyn(place, SPAN, SPAN), :] = query
        turned = both.astype(f32).T
        turned_ref[:HD, dyn(place, SPAN, SPAN)] = turned[HD:, :].astype(bf16)

    sort_blocks(order_ref, info_ref, x_ref, slots, keep)
    low_half = lane_low((SPAN // 2, LANES))
    for block in range(mixed_ref.shape[0]):
        packed = mixed_ref[block].astype(f32)
        for part, tile in enumerate((packed, swap_halves(packed))):
            start = order_ref[block] * SPAN + part * (SPAN // 2)
            back_ref[dyn(start, SPAN // 2, SPAN // 2), :] = jnp.where(low_half, tile, 0.0).astype(bf16)
    fill_tables(bias_ref, table_ref, corner_ref)
    tail = lax.broadcasted_iota(jnp.int32, (KT_ROWS - HD, total), 0)
    turned_ref[HD:, :] = jnp.where(tail == 0, 1.0, 0.0).astype(bf16)
    d_block_ref[...] = jnp.zeros_like(d_block_ref)
    d_corner_ref[...] = jnp.zeros_like(d_corner_ref)
    d_both_ref[...] = jnp.zeros_like(d_both_ref)
    far_ref[...] = jnp.zeros_like(far_ref)
    if info_ref.shape[0] > 3:
        d_query_ref[...] = jnp.zeros_like(d_query_ref)
    left_bias = bias_ref[NEAR : NEAR + 1, 0:1]
    right_bias = bias_ref[NEAR + 1 : NEAR + 2, 0:1]

    def one_block(block, unused):
        q0 = block * BQ
        first, last, whole = block_range(ends_ref, q0, total)
        query = query_ref[dyn(q0, BQ, BQ), :]
        back = back_ref[dyn(q0, BQ, BQ), :]
        lse = lse_ref[:, dyn(q0, BQ, BQ)]
        turned_back = back.astype(f32).T[:HD, :]
        delta = jnp.sum(turned_back * exact_ref[:, dyn(q0, BQ, BQ)], axis=0, keepdims=True)

        def step(kind, tile, d_turned):
            k0 = tile * BK
            keys = dyn(k0, BK, BK)
            both = both_ref[keys, :]
            scores = dot_nt(both, query)
            if kind == "diagonal":
                weights = jnp.exp(scores + table_ref[...] - lse)
            elif kind == "cut":
                bias = any_bias(bias_ref, table_ref, corner_ref, tile, block)
                weights = jnp.exp(jnp.where(same_sequence(ends_ref, k0, q0), scores + bias - lse, masked_score))
            else:
                if kind in ("prev", "next"):
                    scores = with_corner(scores, kind, corner_ref[0 if kind == "prev" else 1])
                weights = jnp.exp(scores - (lse - (left_bias if kind in ("left", "prev") else right_bias)))
            d_probs = dot_nt(both, back)
            d_scores = (weights * (d_probs - delta)).astype(bf16)
            if kind == "diagonal":
                add_blocks(d_scores.astype(f32))
            elif kind in ("prev", "next"):
                m = 0 if kind == "prev" else 1
                d_corner_ref[m] = d_corner_ref[m] + corner_of(d_scores, kind).astype(f32)
            elif kind == "cut":
                wide = d_scores.astype(f32)
                sums = jnp.sum(wide, axis=0, keepdims=True)

                @pl.when(tile == block)
                def _():
                    add_blocks(wide)

                for m, (there, corner) in enumerate(
                    ((tile < block, tile + 1 == block), (tile > block, tile == block + 1))
                ):
                    far_ref[m : m + 1, :] = far_ref[m : m + 1, :] + jnp.where(there, sums, 0.0)
                    piece = corner_of(wide, ("prev", "next")[m])
                    d_corner_ref[m] = d_corner_ref[m] + jnp.where(corner, piece, 0.0)
            d_both_ref[keys, :] = (
                d_both_ref[keys, :] + dot_nn(weights.astype(bf16), back) + dot_nn(d_scores, query)
            )
            return d_turned + dot_nn(turned_ref[:, keys], d_scores)

        def add_blocks(wide):
            sums = [None] * (NEAR + 2)
            for a in range(BK // SPAN):
                for b in range(BQ // SPAN):
                    piece = wide[a * SPAN : (a + 1) * SPAN, b * SPAN : (b + 1) * SPAN]
                    at = block_step(a, b)
                    sums[at] = piece if sums[at] is None else sums[at] + piece
            for at, item in enumerate(sums):
                d_block_ref[at] = d_block_ref[at] + item

        def finish(d_turned):
            top = d_turned[:HD, :]
            d_query_ref[dyn(q0, BQ, BQ), :] = jnp.concatenate([top, top], axis=0).T.astype(bf16)

        zero = jnp.zeros((KT_ROWS, BQ), f32)

        @pl.when(whole)
        def _():
            parts = row_of_tiles(first, last, block, step, zero, zero, zero)
            for m in range(2):
                far_ref[m : m + 1, :] = far_ref[m : m + 1, :] + parts[2 * m][HD : HD + 1, :]
            finish(parts[0] + parts[1] + parts[2])

        @pl.when(jnp.logical_not(whole))
        def _():
            finish(lax.fori_loop(first, last, functools.partial(step, "cut"), zero))

        return unused

    lax.fori_loop(info_ref[1], info_ref[2], one_block, 0)

    d_blocks = [d_block_ref[0] + d_corner_ref[0], d_block_ref[1], d_block_ref[2] + d_corner_ref[1]]
    blank = jnp.zeros((SPAN, WIDE - SPAN), f32)
    sums = [
        jnp.sum(unroll_rows(jnp.concatenate([tile, blank], axis=1)), axis=0, keepdims=True)
        for tile in d_blocks
    ]
    for m in range(2):
        line = jnp.sum(d_block_ref[NEAR + m] - d_corner_ref[m], axis=0, keepdims=True)
        for b in range(BQ // SPAN):
            line = line + far_ref[m : m + 1, b * SPAN : (b + 1) * SPAN]
        sums.append(jnp.concatenate([line, blank[:1]], axis=1))
    sums = jnp.concatenate(sums, axis=0)
    buckets = bucket_ref[: NEAR + 2, :]
    by_bucket = jnp.concatenate(
        [
            jnp.sum(jnp.where(buckets == bucket, sums, 0.0), axis=0, keepdims=True)
            for bucket in range(bucket_count)
        ],
        axis=0,
    )
    totals = jnp.broadcast_to(jnp.sum(by_bucket, axis=1, keepdims=True), (bucket_count, LANES))
    upper = totals.astype(bf16).astype(f32)
    rest = totals - upper
    per_source = bucket_count // sources
    spare = jnp.zeros((EXTRA // 2 - per_source, LANES), f32)
    for source in range(sources):
        span = slice(source * per_source, (source + 1) * per_source)
        grad_ref[source, 3 * half * SPAN :, :] = jnp.concatenate(
            [upper[span], spare, rest[span], spare], axis=0
        ).astype(bf16)

    for source in range(sources):
        for pair in range(half):
            tiles = []
            for member in range(2):
                slot = pair + member * half
                place = place_of(order_ref, info_ref, source, slot, slots) * SPAN
                grad_ref[source, slot * SPAN : (slot + 1) * SPAN, :] = d_both_ref[
                    dyn(place, SPAN, SPAN), :
                ].astype(bf16)
                tiles.append(d_query_ref[dyn(place, SPAN, SPAN), :].astype(f32))
            grad_ref[source, (slots + pair) * SPAN : (slots + pair + 1) * SPAN, :] = jnp.where(
                low, tiles[0], tiles[1]
            ).astype(bf16)


def attend_back(
    order, ends, info, swapped, mixed_grad, exact, lse, bias_rows, bucket_rows, slots, bucket_count
):
    sources = swapped.shape[0]
    total = sources * slots * SPAN
    return pl.pallas_call(
        functools.partial(attend_back_kernel, slots, bucket_count),
        in_specs=[smem_spec()] * 3 + [vmem_spec()] * 6,
        out_specs=vmem_spec(),
        out_shape=jax.ShapeDtypeStruct((sources, slots * SPAN * 3 // 2 + EXTRA, LANES), bf16),
        scratch_shapes=[
            vmem((total, LANES), bf16),
            vmem((total, LANES), bf16),
            vmem((total, LANES), bf16),
            vmem((KT_ROWS, total), bf16),
            vmem((BK, BQ), f32),
            vmem((2, SPAN, SPAN), f32),
            vmem((NEAR + 2, SPAN, SPAN), f32),
            vmem((2, SPAN, SPAN), f32),
            vmem((total, LANES), f32),
            vmem((total, LANES), bf16),
            vmem((8, BQ), f32),
        ],
        compiler_params=pltpu.CompilerParams(vmem_limit_bytes=attention_vmem(total)),
        cost_estimate=pl.CostEstimate(
            flops=total * total * 320, bytes_accessed=total * 3072, transcendentals=total * total // 2
        ),
        name="attend_back",
    )(order, ends, info, swapped, mixed_grad, exact, lse, bias_rows, bucket_rows)


def out_kernel(slots, packed_ref, weight_ref, mix_ref, *part_refs):
    heads = packed_ref.shape[0]
    half = slots * SPAN // 2

    @pl.when(pl.program_id(0) == 0)
    def _():
        for pair in range(heads // 2):
            first = packed_ref[2 * pair].astype(f32)
            second = packed_ref[2 * pair + 1].astype(f32)
            top, bottom = pair_up(first, second)
            cols = slice(pair * LANES, (pair + 1) * LANES)
            mix_ref[:half, cols] = top.astype(bf16)
            mix_ref[half:, cols] = bottom.astype(bf16)

    part = dot_nn(mix_ref[...], weight_ref[...]).astype(bf16)
    for s in range(slots):
        part_refs[s][...] = part[s * SPAN : (s + 1) * SPAN]


def out_project(packed, weight, slots):
    heads = packed.shape[0]
    rows, width, depth = slots * SPAN, heads * HD, weight.shape[1]
    tile = 512
    return pl.pallas_call(
        functools.partial(out_kernel, slots),
        grid=(depth // tile,),
        in_specs=[
            pl.BlockSpec(packed.shape, lambda j: (0, 0, 0)),
            pl.BlockSpec((width, tile), lambda j: (0, j)),
        ],
        out_specs=[
            pl.BlockSpec((rows, width), lambda j: (0, 0)),
        ]
        + [pl.BlockSpec((SPAN, tile), lambda j: (0, j))] * slots,
        out_shape=[jax.ShapeDtypeStruct((rows, width), bf16)]
        + [jax.ShapeDtypeStruct((SPAN, depth), bf16)] * slots,
        compiler_params=pltpu.CompilerParams(vmem_limit_bytes=40 * MIB),
        cost_estimate=pl.CostEstimate(
            flops=2 * rows * depth * width, bytes_accessed=4 * depth * width, transcendentals=0
        ),
        name="out_project",
    )(packed, weight)


def feed_kernel(slots, *refs):
    normed_refs, grad_refs = refs[:slots], refs[slots : 2 * slots]
    gate_ref, up_ref, down_ref, active_ref, d_both_ref, rows_ref, rows_grad_ref = refs[2 * slots :]

    @pl.when(pl.program_id(0) == 0)
    def _():
        for s in range(slots):
            rows_ref[s * SPAN : (s + 1) * SPAN, :] = normed_refs[s][...]
            rows_grad_ref[s * SPAN : (s + 1) * SPAN, :] = grad_refs[s][...]

    tile = down_ref.shape[1]
    width = d_both_ref.shape[1] // 2
    gate = dot_nn(rows_ref[...], gate_ref[...])
    up = dot_nn(rows_ref[...], up_ref[...])
    d_hidden = dot_nn(rows_grad_ref[...], down_ref[...])
    scale, cubic = 0.7978845608028654, 0.044715
    square = gate * gate
    bent = jnp.tanh(scale * (gate + cubic * square * gate))
    half = 0.5 * (1.0 + bent)
    gelu = gate * half
    slope = half + 0.5 * gate * (1.0 - bent * bent) * (scale * (1.0 + 3.0 * cubic * square))
    active_ref[...] = (gelu * up).astype(bf16)
    start = pl.program_id(0) * tile
    d_both_ref[:, dyn(start, tile, tile)] = (d_hidden * up * slope).astype(bf16)
    d_both_ref[:, dyn(width + start, tile, LANES)] = (d_hidden * gelu).astype(bf16)


def feed_tile(width):
    return 256 if width % 256 == 0 else 128


def feed(normed_slots, grad_slots, weights):
    slots = len(normed_slots)
    rows, depth, width = slots * SPAN, weights.shape[0], weights.shape[1] // 3
    tile = feed_tile(width)
    steps = width // tile
    whole = pl.BlockSpec((SPAN, depth), lambda j: (0, 0))

    def columns(part):
        return pl.BlockSpec((depth, tile), lambda j: (0, part * steps + j))

    return pl.pallas_call(
        functools.partial(feed_kernel, slots),
        grid=(steps,),
        in_specs=[whole] * (2 * slots) + [columns(0), columns(1), columns(2)],
        out_specs=[
            pl.BlockSpec((rows, tile), lambda j: (0, j)),
            pl.BlockSpec((rows, 2 * width), lambda j: (0, 0)),
        ],
        out_shape=[
            jax.ShapeDtypeStruct((rows, width), bf16),
            jax.ShapeDtypeStruct((rows, 2 * width), bf16),
        ],
        scratch_shapes=[vmem((rows, depth), bf16), vmem((rows, depth), bf16)],
        compiler_params=pltpu.CompilerParams(vmem_limit_bytes=56 * MIB),
        cost_estimate=pl.CostEstimate(
            flops=6 * rows * depth * width,
            bytes_accessed=6 * depth * width,
            transcendentals=rows * width,
        ),
        name="feed",
    )(*normed_slots, *grad_slots, weights, weights, weights)


def pack_kernel(slots, shares, spot_ref, mine_ref, rest_ref, packed_ref):
    width = mine_ref.shape[1]
    half = SPAN // 2
    for s in range(slots):
        there = lax.rem(spot_ref[0] - s + slots, slots)
        for pair in range(width // LANES):
            if s == 0:
                tile = mine_ref[:, pair * LANES : (pair + 1) * LANES].astype(f32)
            else:
                start = (s - 1) * width + pair * LANES
                tile = rest_ref[:, start : start + LANES].astype(f32)
            for member, piece in enumerate(pair_up(tile[:half], tile[half:])):
                for share in range(shares):
                    packed_ref[(2 * pair + member) * shares + share, there] = piece.astype(bf16)


def pack(spot, mine, rest, shares):
    width = mine.shape[1]
    slots = 1 + rest.shape[1] // width
    return pl.pallas_call(
        functools.partial(pack_kernel, slots, shares),
        in_specs=[smem_spec(), vmem_spec(), vmem_spec()],
        out_specs=vmem_spec(),
        out_shape=jax.ShapeDtypeStruct((width // HD * shares, slots, SPAN // 2, LANES), bf16),
        compiler_params=pltpu.CompilerParams(vmem_limit_bytes=16 * MIB),
        name="pack",
    )(spot, mine, rest)


def weigh_kernel(slots, packed_ref, mix_ref, left_ref, *refs):
    attn_refs = refs[:slots]
    product_ref, grads_ref = refs[slots:]
    heads = packed_ref.shape[0]
    rows = slots * SPAN
    half = rows // 2
    width = heads * HD

    @pl.when(pl.program_id(0) == 0)
    def _():
        for pair in range(heads // 2):
            start = pair * LANES
            tiles = [packed_ref[2 * pair + m].astype(f32) for m in range(2)]
            value, key = pair_up(tiles[0][:rows], tiles[1][:rows])
            top, bottom = pair_up(tiles[0][rows : rows + half], tiles[1][rows : rows + half])
            grads_ref[:half, start : start + LANES] = top.astype(bf16)
            grads_ref[half:, start : start + LANES] = bottom.astype(bf16)
            grads_ref[:, width + start : width + start + LANES] = key.astype(bf16)
            grads_ref[:, 2 * width + start : 2 * width + start + LANES] = value.astype(bf16)

    product_ref[:, : 3 * width] = dot_tn(left_ref[...], grads_ref[...]).astype(bf16)
    attn = jnp.concatenate([ref[...] for ref in attn_refs], axis=0)
    product_ref[:, 3 * width :] = dot_tn(attn, mix_ref[...]).astype(bf16)


def weigh(packed, mix, left, attn_slots):
    slots = len(attn_slots)
    heads = packed.shape[0]
    rows, depth = left.shape
    width = 3 * heads * HD
    total = width + mix.shape[1]
    tile = 512
    return pl.pallas_call(
        functools.partial(weigh_kernel, slots),
        grid=(depth // tile,),
        in_specs=[
            pl.BlockSpec(packed.shape, lambda j: (0, 0, 0)),
            pl.BlockSpec(mix.shape, lambda j: (0, 0)),
            pl.BlockSpec((rows, tile), lambda j: (0, j)),
        ]
        + [pl.BlockSpec((SPAN, tile), lambda j: (0, j))] * slots,
        out_specs=[
            pl.BlockSpec((tile, total), lambda j: (j, 0)),
            pl.BlockSpec((rows, width), lambda j: (0, 0)),
        ],
        out_shape=[
            jax.ShapeDtypeStruct((depth, total), bf16),
            jax.ShapeDtypeStruct((rows, width), bf16),
        ],
        compiler_params=pltpu.CompilerParams(vmem_limit_bytes=LARGE),
        cost_estimate=pl.CostEstimate(
            flops=2 * rows * depth * total, bytes_accessed=4 * depth * total, transcendentals=0
        ),
        name="weigh",
    )(packed, mix, left, *attn_slots)


def project_back_kernel(slots, grads_ref, weight_ref, scale_ref, *refs):
    x_refs = refs[:slots]
    gain_ref, *part_refs = refs[slots:]
    part = dot_nt(grads_ref[...], weight_ref[...])
    gain = jnp.zeros((1, part.shape[1]), f32)
    for s in range(slots):
        span = slice(s * SPAN, (s + 1) * SPAN)
        part_refs[s][...] = part[span].astype(bf16)
        x_hat = x_refs[s][...].astype(f32) * scale_ref[span, :1]
        gain = gain + jnp.sum(part[span] * x_hat, axis=0, keepdims=True)
    gain_ref[...] = gain


def project_back(grads, weights, scale, x_slots):
    slots = len(x_slots)
    depth, width = weights.shape
    rows = slots * SPAN
    tile = 512
    spans = [pl.BlockSpec((SPAN, tile), lambda j: (0, j))] * slots
    return pl.pallas_call(
        functools.partial(project_back_kernel, slots),
        grid=(depth // tile,),
        in_specs=[
            pl.BlockSpec((rows, width), lambda j: (0, 0)),
            pl.BlockSpec((tile, width), lambda j: (j, 0)),
            pl.BlockSpec((rows, LANES), lambda j: (0, 0)),
        ]
        + spans,
        out_specs=[pl.BlockSpec((1, tile), lambda j: (0, j))] + spans,
        out_shape=[jax.ShapeDtypeStruct((1, depth), f32)]
        + [jax.ShapeDtypeStruct((SPAN, depth), bf16)] * slots,
        compiler_params=pltpu.CompilerParams(vmem_limit_bytes=LARGE),
        cost_estimate=pl.CostEstimate(
            flops=2 * rows * depth * width, bytes_accessed=4 * depth * width, transcendentals=0
        ),
        name="project_back",
    )(grads, weights, scale, *x_slots)


def pair_kernel(slots, groups, *refs):
    left_one, left_two = refs[:slots], refs[slots : 2 * slots]
    right_one = refs[2 * slots : 2 * slots + groups]
    right_two = refs[2 * slots + groups : 2 * slots + 2 * groups]
    out_ref, right_ref = refs[-2:]
    cut = right_one[0].shape[1]

    @pl.when(pl.program_id(0) == 0)
    def _():
        start = 0
        for one, two in zip(right_one, right_two, strict=True):
            span = slice(start, start + one.shape[0])
            right_ref[span, :cut] = one[...]
            right_ref[span, cut:] = two[...]
            start += one.shape[0]

    one = jnp.concatenate([ref[...] for ref in left_one], axis=0)
    two = jnp.concatenate([ref[...] for ref in left_two], axis=0)
    out_ref[:, :cut] = dot_tn(one, right_ref[:, :cut]).astype(bf16)
    out_ref[:, cut:] = dot_tn(two, right_ref[:, cut:]).astype(bf16)


def pair_product(left_one, right_one, left_two, right_two):
    slots, groups = len(left_one), len(right_one)
    rows, depth = slots * SPAN, left_one[0].shape[1]
    width = right_one[0].shape[1] + right_two[0].shape[1]
    block = 512

    def whole(array):
        return pl.BlockSpec(array.shape, lambda j: (0, 0))

    return pl.pallas_call(
        functools.partial(pair_kernel, slots, groups),
        grid=(depth // block,),
        in_specs=[pl.BlockSpec((SPAN, block), lambda j: (0, j))] * (2 * slots)
        + [whole(piece) for piece in (*right_one, *right_two)],
        out_specs=pl.BlockSpec((block, width), lambda j: (j, 0)),
        out_shape=jax.ShapeDtypeStruct((depth, width), bf16),
        scratch_shapes=[vmem((rows, width), bf16)],
        compiler_params=pltpu.CompilerParams(vmem_limit_bytes=32 * MIB),
        cost_estimate=pl.CostEstimate(
            flops=2 * rows * depth * width, bytes_accessed=2 * depth * width, transcendentals=0
        ),
        name="pair_product",
    )(*left_one, *left_two, *right_one, *right_two)


def bucket_lines(bucket_of):
    count = bucket_of.shape[0]
    turned = bucket_of[::-1]
    ends = [jnp.broadcast_to(end, (2 * SPAN,)) for end in (turned[:1], turned[-1:])]
    padded = jnp.concatenate([ends[0], turned, ends[1]])
    zero_at = 2 * SPAN + count // 2
    rows = []
    for c in range(NEAR):
        base = zero_at - (c - 1) * SPAN
        rows.append(jnp.concatenate([padded[base : base + SPAN], padded[base - SPAN : base]]))
    rows.append(jnp.broadcast_to(bucket_of[:1], (WIDE,)))
    rows.append(jnp.broadcast_to(bucket_of[-1:], (WIDE,)))
    spare = 8 - (NEAR + 2)
    return jnp.concatenate([jnp.stack(rows), jnp.full((spare, WIDE), -1, bucket_of.dtype)])


def on_device(
    tokens,
    lengths,
    block_order,
    bucket_of,
    gain_attn,
    w_query,
    w_key,
    w_value,
    w_out,
    bias_table,
    gain_ffn,
    w_gate,
    w_up,
    w_down,
    cotangent,
):
    blk_count, slots = lax.axis_size("blk"), lax.axis_size("head")
    blk_spot, head_spot = lax.axis_index("blk"), lax.axis_index("head")
    depth = tokens.shape[1]
    width = w_query.shape[1]
    heads = width // HD
    shares = blk_count // heads
    table_rows, table_heads = bias_table.shape
    bucket_count = table_rows * blk_count
    total = blk_count * slots * SPAN
    gain_size = gain_attn.shape[0]
    hidden = w_gate.shape[1]

    token_slots = gather_far(gather_near(tokens))
    small = gather_small(
        jnp.concatenate([gain_attn, gain_ffn, bias_table.astype(f32).reshape(-1)])
    )
    full_qkv = lax.all_gather(
        jnp.concatenate([w_query, w_key, w_value], axis=1), "blk", axis=0, tiled=True
    )
    full_out = lax.all_gather(w_out, "blk", axis=1, tiled=True)
    full_ffn = lax.all_gather(
        jnp.concatenate([w_gate, w_up, w_down.T], axis=1), "blk", axis=0, tiled=True
    )
    gain_one = small[:, :, :gain_size].reshape(1, depth)
    gain_two = small[:, :, gain_size : 2 * gain_size].reshape(1, depth)

    tables = lax.dynamic_index_in_dim(small, head_spot, 1, False)[:, 2 * gain_size :]
    tables = tables.reshape(bucket_count, table_heads)
    my_head = blk_spot // shares
    my_bias = lax.dynamic_index_in_dim(tables, my_head, 1, False)
    bucket_rows = bucket_lines(bucket_of)
    bias_rows = jnp.sum(
        jnp.where(
            bucket_rows[None] == jnp.arange(bucket_count, dtype=jnp.int32)[:, None, None],
            my_bias[:, None, None],
            0.0,
        ),
        axis=0,
    )
    ends = jnp.cumsum(lengths).astype(jnp.int32)
    per_share = total // BQ // shares
    start = (blk_spot % shares) * per_share
    info = [head_spot, start, start + per_share] + ([start] if shares > 1 else [])
    info = jnp.stack([jnp.asarray(item, jnp.int32) for item in info])

    def swap(values):
        return lax.all_to_all(values, "blk", 0, 0, tiled=True)

    def to_all(values):
        values = values.reshape((blk_count * slots,) + values.shape[2:])
        return lax.all_to_all(values, ("blk", "head"), 0, 0, tiled=True)

    def to_heads(values):
        return swap(values if shares == 1 else jnp.repeat(values, shares, axis=0))

    def to_rows(values):
        values = swap(values)
        if shares == 1:
            return values
        values = values.reshape((heads, shares) + values.shape[1:])
        return jnp.sum(values.astype(f32), axis=1).astype(bf16)

    w_out, cotangent, *token_slots = together(w_out, cotangent, *token_slots)
    normed_one, packed, scale_one = project(token_slots, gain_one, full_qkv)
    early = (ends, info, bias_rows, bucket_rows)
    swapped, ends, info, bias_rows, bucket_rows, *out_near = together(
        to_heads(packed), *early, *gather_near(w_out)
    )
    grad_near, out_slots = gather_near(cotangent), gather_far(out_near)
    mixed, exact, lse = attend(block_order, ends, info, swapped, bias_rows, slots)
    mixed, *moved = together(mixed, *grad_near, *out_slots)
    grad_near, out_slots = moved[: len(grad_near)], moved[len(grad_near) :]
    packed_mix, *grad_slots = together(to_rows(mixed), *gather_far(grad_near))
    attn_mix, *out_parts = out_project(packed_mix, full_out, slots)
    tokens_wide = tokens.astype(f32)
    hidden_one = tokens_wide + sum_terms(sum_near(out_parts, sum_far(out_parts))[0])
    rstd_two = rms_scale(hidden_one)
    normed_two = (hidden_one * rstd_two * gain_two).astype(bf16)

    normed_two, out_slots = together(normed_two, out_slots)
    full_rest = lax.all_gather(jnp.concatenate(out_slots[1:]), "blk", axis=1, tiled=True)
    normed_slots = gather_far(gather_near(normed_two))
    active, d_both = feed(normed_slots, grad_slots, full_ffn)

    def spans(rows):
        return [rows[s * SPAN : (s + 1) * SPAN] for s in range(rows.shape[0] // SPAN)]

    d_parts = spans(dot_nt(d_both, full_ffn[:, : 2 * hidden]).astype(bf16))
    d_far = sum_far(d_parts)
    grad_hidden, *d_far = together(
        pair_product(normed_slots, [d_both], grad_slots, [active]), *d_far
    )
    grad_hidden = lax.psum_scatter(grad_hidden, "blk", scatter_dimension=0, tiled=True)
    d_near, (active,) = sum_near(d_parts, d_far, (active,))
    down_rows = dot_nt(active, full_ffn[:, 2 * hidden :]).astype(bf16)
    down_rows, full_rest, *d_near = together(down_rows, full_rest, *d_near)
    down_parts = spans(down_rows)
    d_normed_two = sum_terms(d_near)
    d_source_two, gain_part_two = norm_back(d_normed_two, hidden_one, rstd_two, gain_two)
    d_hidden_one = cotangent.astype(f32) + d_source_two

    d_attn = d_hidden_one.astype(bf16)
    mix_grads = pack(
        jnp.reshape(head_spot, (1,)).astype(jnp.int32),
        dot_nt(d_attn, full_out).astype(bf16),
        dot_nt(d_attn, full_rest).astype(bf16),
        shares,
    )
    mix_grads, d_attn = together(mix_grads, d_attn)
    middle = slots // 2
    steps = [t for t in range(1, slots) if t != middle]
    moved = (*gather_near(d_attn), *sum_direct(down_parts, steps))
    grads = attend_back(
        block_order, ends, info, swapped, to_all(mix_grads), exact, lse, bias_rows, bucket_rows,
        slots, bucket_count,
    )
    grads, down_parts, *moved = together(grads, down_parts, *moved)
    attn_near, down_terms = moved[: 2 - slots], moved[2 - slots :]
    grads, *attn_slots = together(swap(grads), *gather_far(attn_near))
    extra = grads[:, -EXTRA:, 0].astype(f32).reshape(blk_count, 2, -1).sum(axis=1)
    grad_table = extra[:, :table_rows].reshape(heads, shares, table_rows).sum(axis=1).T
    if shares > 1:
        grads = grads.reshape((heads, shares) + grads.shape[1:])
        grads = jnp.sum(grads.astype(f32), axis=1).astype(bf16)
    grad_heads, d_qkv = weigh(grads, attn_mix, normed_one, attn_slots)
    grad_heads, grad_hidden = together(grad_heads, grad_hidden)
    gain_part_one, *one_parts = project_back(d_qkv, full_qkv, scale_one, token_slots)

    one_far = sum_far(one_parts)
    gain_parts = jnp.stack(
        [part.reshape(blk_count, slots, gain_size) for part in (gain_part_one, gain_part_two)],
        axis=2,
    )
    gain_parts, *one_far = together(gain_parts, *one_far)
    grad_heads = lax.psum_scatter(grad_heads, "blk", scatter_dimension=0, tiled=True).astype(f32)
    one_near, unused = sum_near(one_parts, one_far)
    gain_sums = scatter_blk(gain_parts)
    gain_sums, down_parts, grad_hidden, *one_near = together(
        gain_sums, down_parts, grad_hidden, *one_near
    )
    far_term = sum_direct(down_parts, [middle])
    gain_sums = scatter_head(gain_sums)
    grad_hidden = grad_hidden.astype(f32)
    output = hidden_one + sum_all([down_parts[0]] + down_terms + far_term)
    d_normed_one = sum_terms(one_near)
    d_source_one, unused = norm_back(d_normed_one, tokens_wide, rms_scale(tokens_wide), gain_one)
    input_grad = d_hidden_one + d_source_one
    return (
        output,
        input_grad,
        gain_sums[0],
        grad_heads[:, :width],
        grad_heads[:, width : 2 * width],
        grad_heads[:, 2 * width : 3 * width],
        grad_heads[:, 3 * width :].T,
        grad_table,
        gain_sums[1],
        grad_hidden[:, :hidden],
        grad_hidden[:, hidden : 2 * hidden],
        grad_hidden[:, 2 * hidden :].T,
    )


def solution(mesh):
    rows, spread = P(("blk", "head"), None), P(("blk", "head"))
    inward, outward = P("blk", "head"), P("head", "blk")
    in_specs = (
        rows, P(), P(), P(), spread, inward, inward, inward, outward, inward, spread,
        inward, inward, outward, rows,
    )
    out_specs = (
        rows, rows, spread, inward, inward, inward, outward, inward, spread,
        inward, inward, outward,
    )
    return jax.shard_map(
        on_device, mesh=mesh, in_specs=in_specs, out_specs=out_specs, check_vma=False
    )
```

```python
import functools

import jax
import jax.numpy as jnp
from jax import lax
from jax.experimental import pallas as pl
from jax.experimental.pallas import tpu as pltpu
from jax.sharding import PartitionSpec as P

HD = 64
LANES = 2 * HD
MAXDIST = 128
SPAN = 128
BQ = 512
BK = BQ
NEAR = 3
WIDE = 2 * SPAN
EXTRA = 16
KT_ROWS = 80
SHIFT_ROOM = 60.0

norm_eps = 1e-06
masked_score = -1e30
f32 = jnp.float32
bf16 = jnp.bfloat16
MIB = 1 << 20
LARGE = 58 * MIB


def rms_scale(values):
    return lax.rsqrt(jnp.mean(values * values, axis=-1, keepdims=True) + norm_eps)


def norm_back(d_normed, source, inv_rms, gain_vec):
    scaled = d_normed * gain_vec
    x_hat = source * inv_rms
    gain_part = jnp.sum(d_normed * x_hat, axis=0)
    d_source = inv_rms * (scaled - x_hat * jnp.mean(scaled * x_hat, axis=-1, keepdims=True))
    return (d_source, gain_part)


def dot_nn(left, right):
    return jnp.dot(left, right, preferred_element_type=f32)


def dot_nt(left, right):
    return lax.dot_general(left, right, (((1,), (1,)), ((), ())), preferred_element_type=f32)


def dot_tn(left, right):
    return lax.dot_general(left, right, (((0,), (0,)), ((), ())), preferred_element_type=f32)


def cyclic(count, by):
    return [(i, (i + by) % count) for i in range(count)]


def together(*values):
    return lax.optimization_barrier(values)


def gather_near(rows):
    count = lax.axis_size("head")
    if count != 4:
        return [rows] + [lax.ppermute(rows, "head", cyclic(count, s)) for s in range(1, count)]
    return [rows, lax.ppermute(rows, "head", cyclic(4, 1)), lax.ppermute(rows, "head", cyclic(4, 3))]


def gather_far(near):
    if lax.axis_size("head") != 4:
        return near
    rows, back_one, ahead_one = near
    me = lax.axis_index("head")
    passed = jnp.where(me == 1, ahead_one, jnp.where(me == 2, back_one, rows))
    back_two = lax.ppermute(passed, "head", [(1, 0), (3, 1), (0, 2), (2, 3)])
    return [rows, back_one, back_two, ahead_one]


def gather_direct(rows):
    count = lax.axis_size("head")
    return [rows] + [lax.ppermute(rows, "head", cyclic(count, s)) for s in range(1, count)]


def sum_far(parts):
    count = lax.axis_size("head")
    if count != 4:
        return []
    return [lax.ppermute(parts[2], "head", [(0, 1), (1, 3), (2, 0), (3, 2)])]


def sum_near(parts, far, beside=()):
    count = lax.axis_size("head")
    if count != 4:
        return [parts[0]] + [
            lax.ppermute(parts[s], "head", cyclic(count, count - s)) for s in range(1, count)
        ], beside
    me = lax.axis_index("head")
    wide = far[0].astype(f32)
    to_back = jnp.where(me == 2, parts[1].astype(f32) + wide, parts[1].astype(f32)).astype(bf16)
    to_ahead = jnp.where(me == 1, parts[3].astype(f32) + wide, parts[3].astype(f32)).astype(bf16)
    to_back, to_ahead, *beside = together(to_back, to_ahead, *beside)
    from_ahead = lax.ppermute(to_back, "head", cyclic(4, 3))
    from_back = lax.ppermute(to_ahead, "head", cyclic(4, 1))
    return [parts[0], from_ahead, from_back, far[0]], beside


def sum_terms(terms):
    total = terms[0].astype(f32) + terms[1].astype(f32) + terms[2].astype(f32)
    if lax.axis_size("head") != 4:
        for term in terms[3:]:
            total = total + term.astype(f32)
        return total
    me = lax.axis_index("head")
    return total + jnp.where((me == 0) | (me == 3), terms[3].astype(f32), 0.0)


def is_power(count):
    return count & (count - 1) == 0


def gather_small(values):
    held = values[None]
    for axis in ("head", "blk"):
        count = lax.axis_size(axis)
        if not is_power(count):
            held = lax.all_gather(held, axis, axis=0, tiled=False)
        else:
            me = lax.axis_index(axis)
            held = held[None]
            bit = 1
            while bit < count:
                other = lax.ppermute(held, axis, [(i, i ^ bit) for i in range(count)])
                low = jnp.concatenate([held, other])
                high = jnp.concatenate([other, held])
                held = jnp.where((me // bit) % 2 == 0, low, high)
                bit *= 2
        if axis == "head":
            held = held.reshape(count, -1)
    return held


def sum_direct(parts, steps):
    count = len(parts)
    return [lax.ppermute(parts[s], "head", cyclic(count, count - s)) for s in steps]


def sum_all(terms):
    total = terms[0].astype(f32)
    for term in terms[1:]:
        total = total + term.astype(f32)
    return total


def scatter_blk(values):
    return jnp.sum(lax.all_to_all(values, "blk", 0, 0, tiled=True), axis=0)


def scatter_head(values):
    count, me = lax.axis_size("head"), lax.axis_index("head")
    total = lax.dynamic_index_in_dim(values, me, 0, False)
    for s in range(1, count):
        sent = lax.dynamic_index_in_dim(values, (me + s) % count, 0, False)
        total = total + lax.ppermute(sent, "head", cyclic(count, s))
    return total


def lane_low(shape):
    return lax.broadcasted_iota(jnp.int32, shape, 1) < HD


def swap_halves(tile):
    return pltpu.roll(tile, HD, 1)


def pair_up(first, second):
    low = lane_low(first.shape)
    return (
        jnp.where(low, first, swap_halves(second)),
        jnp.where(low, swap_halves(first), second),
    )


def project_kernel(slots, *refs):
    x_refs = refs[:slots]
    gain_ref, wq_ref, wk_ref, wv_ref, normed_ref, packed_ref, scale_ref = refs[slots:]
    rows = slots * SPAN

    @pl.when(pl.program_id(0) == 0)
    def _():
        for s in range(slots):
            wide = x_refs[s][...].astype(f32)
            scale = rms_scale(wide)
            normed = wide * scale * gain_ref[...]
            normed_ref[s * SPAN : (s + 1) * SPAN, :] = normed.astype(bf16)
            scale_ref[s * SPAN : (s + 1) * SPAN, :] = jnp.broadcast_to(scale, (SPAN, LANES))

    normed = normed_ref[...]
    query = dot_nn(normed, wq_ref[...])
    key = dot_nn(normed, wk_ref[...])
    value = dot_nn(normed, wv_ref[...])
    half = rows // 2
    for pair in range(query.shape[1] // LANES):
        cols = slice(pair * LANES, (pair + 1) * LANES)
        both = pair_up(value[:, cols], key[:, cols])
        queries = pair_up(query[:half, cols], query[half:, cols])
        for member in range(2):
            packed_ref[2 * pair + member, :rows, :] = both[member].astype(bf16)
            packed_ref[2 * pair + member, rows:, :] = queries[member].astype(bf16)


def project(x_slots, gain, weights):
    slots = len(x_slots)
    rows, depth = slots * SPAN, x_slots[0].shape[1]
    width = weights.shape[1] // 3
    heads = width // HD
    tile = min(width, 256)
    steps = width // tile
    whole = pl.BlockSpec((SPAN, depth), lambda j: (0, 0))

    def columns(part):
        return pl.BlockSpec((depth, tile), lambda j: (0, part * steps + j))

    return pl.pallas_call(
        functools.partial(project_kernel, slots),
        grid=(steps,),
        in_specs=[whole] * slots
        + [pl.BlockSpec((1, depth), lambda j: (0, 0)), columns(0), columns(1), columns(2)],
        out_specs=[
            pl.BlockSpec((rows, depth), lambda j: (0, 0)),
            pl.BlockSpec((tile // HD, rows + rows // 2, LANES), lambda j: (j, 0, 0)),
            pl.BlockSpec((rows, LANES), lambda j: (0, 0)),
        ],
        out_shape=[
            jax.ShapeDtypeStruct((rows, depth), bf16),
            jax.ShapeDtypeStruct((heads, rows + rows // 2, LANES), bf16),
            jax.ShapeDtypeStruct((rows, LANES), f32),
        ],
        compiler_params=pltpu.CompilerParams(vmem_limit_bytes=40 * MIB),
        cost_estimate=pl.CostEstimate(
            flops=10 * rows * depth * width, bytes_accessed=6 * depth * width, transcendentals=0
        ),
        name="project",
    )(*x_slots, gain, weights, weights, weights)


def place_of(order_ref, info_ref, source, slot, slots):
    z = info_ref[0]
    return order_ref[source * slots + lax.rem(z - slot + slots, slots)]


def dyn(start, size, multiple):
    return pl.ds(pl.multiple_of(start, multiple), size)


def near_blocks(bias_ref):
    tiles = []
    for c in range(NEAR):
        spread = jnp.broadcast_to(bias_ref[c : c + 1, :], (SPAN, WIDE))
        tiles.append(pltpu.roll(spread, 0, 1, stride=1, stride_axis=0)[:, :SPAN])
    return tiles


def block_step(a, b):
    return a - b + 1 if abs(a - b) <= 1 else 3 if a < b else 4


def fill_tables(bias_ref, table_ref, corner_ref):
    tiles = near_blocks(bias_ref)
    far = [jnp.broadcast_to(bias_ref[NEAR + m : NEAR + m + 1, :SPAN], (SPAN, SPAN)) for m in range(2)]
    every = tiles + far
    for a in range(BK // SPAN):
        for b in range(BQ // SPAN):
            table_ref[a * SPAN : (a + 1) * SPAN, b * SPAN : (b + 1) * SPAN] = every[block_step(a, b)]
    corner_ref[0] = tiles[0] - far[0]
    corner_ref[1] = tiles[2] - far[1]


def with_corner(tile, kind, corner):
    if kind == "prev":
        upper, lower = tile[: BK - SPAN], tile[BK - SPAN :]
        lower = jnp.concatenate([lower[:, :SPAN] + corner, lower[:, SPAN:]], axis=1)
    else:
        upper, lower = tile[:SPAN], tile[SPAN:]
        upper = jnp.concatenate([upper[:, : BQ - SPAN], upper[:, BQ - SPAN :] + corner], axis=1)
    return jnp.concatenate([upper, lower], axis=0)


def corner_of(tile, kind):
    return tile[BK - SPAN :, :SPAN] if kind == "prev" else tile[:SPAN, BQ - SPAN :]


def any_bias(bias_ref, table_ref, corner_ref, tile, block):
    left = jnp.broadcast_to(bias_ref[NEAR : NEAR + 1, 0:1], (BK, BQ))
    right = jnp.broadcast_to(bias_ref[NEAR + 1 : NEAR + 2, 0:1], (BK, BQ))
    left = with_corner(left, "prev", jnp.where(tile + 1 == block, corner_ref[0], 0.0))
    right = with_corner(right, "next", jnp.where(tile == block + 1, corner_ref[1], 0.0))
    return jnp.where(tile == block, table_ref[...], jnp.where(tile < block, left, right))


def block_range(ends_ref, q0, total):
    count = ends_ref.shape[0]
    start, end, cut = jnp.int32(0), jnp.int32(total), jnp.bool_(False)
    for n in range(count):
        edge = ends_ref[n]
        start = jnp.where(edge <= q0, edge, start)
        cut = cut | ((edge > q0) & (edge < q0 + BQ))
    for n in range(count - 1, -1, -1):
        edge = ends_ref[n]
        end = jnp.where(edge >= q0 + BQ, edge, end)
    first = lax.div(start, BK)
    last = lax.div(end + BK - 1, BK)
    whole = jnp.logical_not(cut) & (lax.rem(start, BK) == 0) & (lax.rem(end, BK) == 0)
    return first, last, whole


def row_of_tiles(first, last, block, step, left, middle, right):
    before, after = jnp.maximum(block - 1, first), jnp.minimum(block + 2, last)
    left = lax.fori_loop(first, before, functools.partial(step, "left"), left)
    left = lax.fori_loop(before, block, functools.partial(step, "prev"), left)
    middle = step("diagonal", block, left if middle is None else middle)
    right = middle if right is None else right
    right = lax.fori_loop(block + 1, after, functools.partial(step, "next"), right)
    right = lax.fori_loop(after, last, functools.partial(step, "right"), right)
    return left, middle, right


def same_sequence(ends_ref, k0, q0):
    key_place = k0 + lax.broadcasted_iota(jnp.int32, (BK, 1), 0)
    query_place = q0 + lax.broadcasted_iota(jnp.int32, (1, BQ), 1)
    key_seg = jnp.zeros((BK, 1), jnp.int32)
    query_seg = jnp.zeros((1, BQ), jnp.int32)
    for n in range(ends_ref.shape[0]):
        key_seg = key_seg + jnp.where(key_place >= ends_ref[n], 1, 0)
        query_seg = query_seg + jnp.where(query_place >= ends_ref[n], 1, 0)
    return key_seg == query_seg


def sort_blocks(order_ref, info_ref, x_ref, slots, keep):
    sources = x_ref.shape[0]
    half = slots // 2
    high = jnp.logical_not(lane_low((SPAN, LANES)))
    for source in range(sources):
        for pair in range(half):
            packed = x_ref[
                source, (slots + pair) * SPAN : (slots + pair + 1) * SPAN, :
            ].astype(f32)
            queries = (swap_halves(packed), packed)
            for member in range(2):
                slot = pair + member * half
                place = place_of(order_ref, info_ref, source, slot, slots) * SPAN
                both = x_ref[source, slot * SPAN : (slot + 1) * SPAN, :]
                keep(place, both, jnp.where(high, queries[member], 0.0).astype(bf16))


def attend_kernel(
    slots, order_ref, ends_ref, info_ref, x_ref, bias_ref, mixed_ref, exact_ref, lse_ref,
    both_ref, query_ref, turned_ref, table_ref, corner_ref, held_ref, rows_ref,
):
    total = both_ref.shape[0]
    parted = info_ref.shape[0] > 3

    def keep(place, both, query):
        both_ref[dyn(place, SPAN, SPAN), :] = both
        query_ref[dyn(place, SPAN, SPAN), :] = query
        turned = both.astype(f32).T
        turned_ref[:, dyn(place, SPAN, SPAN)] = turned[:HD, :].astype(bf16)
        turned_key, turned_query = turned[HD:, :], query.astype(f32).T[HD:, :]
        for line, product in enumerate(
            (turned_key * turned_query, turned_key * turned_key, turned_query * turned_query)
        ):
            rows_ref[line : line + 1, dyn(place, SPAN, SPAN)] = jnp.sum(
                product, axis=0, keepdims=True
            )

    sort_blocks(order_ref, info_ref, x_ref, slots, keep)
    fill_tables(bias_ref, table_ref, corner_ref)
    if parted:
        held_ref[...] = jnp.zeros_like(held_ref)
        exact_ref[...] = jnp.zeros_like(exact_ref)
        lse_ref[...] = jnp.zeros_like(lse_ref)
    left_bias = bias_ref[NEAR : NEAR + 1, 0:1]
    right_bias = bias_ref[NEAR + 1 : NEAR + 2, 0:1]
    start_state = (
        jnp.full((1, BQ), masked_score, f32),
        jnp.zeros((1, BQ), f32),
        jnp.zeros((HD, BQ), f32),
    )
    longest_key = jnp.sqrt(jnp.max(rows_ref[1:2, :], axis=1, keepdims=True))
    most_bias = jnp.max(
        jnp.max(bias_ref[: NEAR + 2, :], axis=0, keepdims=True), axis=1, keepdims=True
    )

    def one_block(block, unused):
        q0 = block * BQ
        first, last, whole = block_range(ends_ref, q0, total)
        query = query_ref[dyn(q0, BQ, BQ), :]
        own = rows_ref[0:1, dyn(q0, BQ, BQ)] + bias_ref[1:2, 0:1]
        bound = jnp.sqrt(rows_ref[2:3, dyn(q0, BQ, BQ)]) * longest_key + most_bias
        whole = whole & (jnp.max(bound - own) < SHIFT_ROOM)

        def quick_step(kind, tile, state):
            mass, mix = state
            k0 = tile * BK
            scores = dot_nt(both_ref[dyn(k0, BK, BK), :], query)
            if kind == "diagonal":
                weights = jnp.exp(scores + table_ref[...] - own)
            else:
                if kind in ("prev", "next"):
                    scores = with_corner(scores, kind, corner_ref[0 if kind == "prev" else 1])
                weights = jnp.exp(scores - (own - (left_bias if kind in ("left", "prev") else right_bias)))
            mass = mass + jnp.sum(weights, axis=0, keepdims=True)
            return (mass, mix + dot_nn(turned_ref[:, dyn(k0, BK, BK)], weights.astype(bf16)))

        def step(tile, state):
            peak, mass, mix = state
            k0 = tile * BK
            scores = dot_nt(both_ref[dyn(k0, BK, BK), :], query)
            same = same_sequence(ends_ref, k0, q0)
            scores = scores + any_bias(bias_ref, table_ref, corner_ref, tile, block)
            scores = jnp.where(same, scores, masked_score)
            new_peak = jnp.maximum(peak, jnp.max(scores, axis=0, keepdims=True))
            weights = jnp.where(same, jnp.exp(scores - new_peak), 0.0)
            rescale = jnp.exp(peak - new_peak)
            mass = mass * rescale + jnp.sum(weights, axis=0, keepdims=True)
            turned = turned_ref[:, dyn(k0, BK, BK)]
            mix = mix * rescale + dot_nn(turned, weights.astype(bf16))
            return (new_peak, mass, mix)

        def finish(peak, mass, mix):
            exact = mix / mass
            exact_ref[:, dyn(q0, BQ, BQ)] = exact
            lse_ref[:, dyn(q0, BQ, BQ)] = peak + jnp.log(mass)
            padded = jnp.concatenate([exact, exact], axis=0)
            held_ref[dyn(q0, BQ, BQ), :] = padded.T

        @pl.when(whole)
        def _():
            *unused, state = row_of_tiles(
                first, last, block, quick_step, start_state[1:], None, None
            )
            finish(own, *state)

        @pl.when(jnp.logical_not(whole))
        def _():
            finish(*lax.fori_loop(first, last, step, start_state))

        return unused

    lax.fori_loop(info_ref[1], info_ref[2], one_block, 0)
    half = slots // 2
    low = lane_low((SPAN, LANES))
    for source in range(x_ref.shape[0]):
        for pair in range(half):
            places = [
                place_of(order_ref, info_ref, source, pair + m * half, slots) * SPAN
                for m in range(2)
            ]
            tiles = [held_ref[dyn(place, SPAN, SPAN), :] for place in places]
            mixed_ref[source, pair * SPAN : (pair + 1) * SPAN, :] = jnp.where(
                low, tiles[0], tiles[1]
            ).astype(bf16)


def vmem(shape, dtype):
    return pltpu.VMEM(shape, dtype)


def smem_spec():
    return pl.BlockSpec(memory_space=pltpu.SMEM)


def vmem_spec():
    return pl.BlockSpec(memory_space=pltpu.VMEM)


def attention_vmem(total):
    return int(min(58, 16 + 44 * (total / 16384)) * MIB)


def attend(order, ends, info, swapped, bias_rows, slots):
    sources = swapped.shape[0]
    total = sources * slots * SPAN
    return pl.pallas_call(
        functools.partial(attend_kernel, slots),
        in_specs=[smem_spec()] * 3 + [vmem_spec()] * 2,
        out_specs=[vmem_spec()] * 3,
        out_shape=[
            jax.ShapeDtypeStruct((sources, slots * SPAN // 2, LANES), bf16),
            jax.ShapeDtypeStruct((HD, total), f32),
            jax.ShapeDtypeStruct((1, total), f32),
        ],
        scratch_shapes=[
            vmem((total, LANES), bf16),
            vmem((total, LANES), bf16),
            vmem((HD, total), bf16),
            vmem((BK, BQ), f32),
            vmem((2, SPAN, SPAN), f32),
            vmem((total, LANES), f32),
            vmem((8, total), f32),
        ],
        compiler_params=pltpu.CompilerParams(vmem_limit_bytes=attention_vmem(total)),
        cost_estimate=pl.CostEstimate(
            flops=total * total * 128, bytes_accessed=total * 2048, transcendentals=total * total // 2
        ),
        name="attend",
    )(order, ends, info, swapped, bias_rows)


def unroll_rows(tile):
    row = lax.broadcasted_iota(jnp.int32, tile.shape, 0)
    bit = 1
    while bit < tile.shape[0]:
        moved = pltpu.roll(tile, tile.shape[1] - bit, 1)
        tile = jnp.where((row // bit) % 2 == 1, moved, tile)
        bit *= 2
    return tile


def attend_back_kernel(
    slots, bucket_count, order_ref, ends_ref, info_ref, x_ref, mixed_ref, exact_ref, lse_ref,
    bias_ref, bucket_ref, grad_ref,
    both_ref, query_ref, back_ref, turned_ref, table_ref, corner_ref, d_block_ref, d_corner_ref,
    d_both_ref, d_query_ref, far_ref,
):
    total = both_ref.shape[0]
    sources = x_ref.shape[0]
    half = slots // 2
    low = lane_low((SPAN, LANES))

    def keep(place, both, query):
        both_ref[dyn(place, SPAN, SPAN), :] = both
        query_ref[dyn(place, SPAN, SPAN), :] = query
        turned = both.astype(f32).T
        turned_ref[:HD, dyn(place, SPAN, SPAN)] = turned[HD:, :].astype(bf16)

    sort_blocks(order_ref, info_ref, x_ref, slots, keep)
    low_half = lane_low((SPAN // 2, LANES))
    for block in range(mixed_ref.shape[0]):
        packed = mixed_ref[block].astype(f32)
        for part, tile in enumerate((packed, swap_halves(packed))):
            start = order_ref[block] * SPAN + part * (SPAN // 2)
            back_ref[dyn(start, SPAN // 2, SPAN // 2), :] = jnp.where(low_half, tile, 0.0).astype(bf16)
    fill_tables(bias_ref, table_ref, corner_ref)
    tail = lax.broadcasted_iota(jnp.int32, (KT_ROWS - HD, total), 0)
    turned_ref[HD:, :] = jnp.where(tail == 0, 1.0, 0.0).astype(bf16)
    d_block_ref[...] = jnp.zeros_like(d_block_ref)
    d_corner_ref[...] = jnp.zeros_like(d_corner_ref)
    d_both_ref[...] = jnp.zeros_like(d_both_ref)
    far_ref[...] = jnp.zeros_like(far_ref)
    if info_ref.shape[0] > 3:
        d_query_ref[...] = jnp.zeros_like(d_query_ref)
    left_bias = bias_ref[NEAR : NEAR + 1, 0:1]
    right_bias = bias_ref[NEAR + 1 : NEAR + 2, 0:1]

    def one_block(block, unused):
        q0 = block * BQ
        first, last, whole = block_range(ends_ref, q0, total)
        query = query_ref[dyn(q0, BQ, BQ), :]
        back = back_ref[dyn(q0, BQ, BQ), :]
        lse = lse_ref[:, dyn(q0, BQ, BQ)]
        turned_back = back.astype(f32).T[:HD, :]
        delta = jnp.sum(turned_back * exact_ref[:, dyn(q0, BQ, BQ)], axis=0, keepdims=True)

        def step(kind, tile, d_turned):
            k0 = tile * BK
            keys = dyn(k0, BK, BK)
            both = both_ref[keys, :]
            scores = dot_nt(both, query)
            if kind == "diagonal":
                weights = jnp.exp(scores + table_ref[...] - lse)
            elif kind == "cut":
                bias = any_bias(bias_ref, table_ref, corner_ref, tile, block)
                weights = jnp.exp(jnp.where(same_sequence(ends_ref, k0, q0), scores + bias - lse, masked_score))
            else:
                if kind in ("prev", "next"):
                    scores = with_corner(scores, kind, corner_ref[0 if kind == "prev" else 1])
                weights = jnp.exp(scores - (lse - (left_bias if kind in ("left", "prev") else right_bias)))
            d_probs = dot_nt(both, back)
            d_scores = (weights * (d_probs - delta)).astype(bf16)
            if kind == "diagonal":
                add_blocks(d_scores.astype(f32))
            elif kind in ("prev", "next"):
                m = 0 if kind == "prev" else 1
                d_corner_ref[m] = d_corner_ref[m] + corner_of(d_scores, kind).astype(f32)
            elif kind == "cut":
                wide = d_scores.astype(f32)
                sums = jnp.sum(wide, axis=0, keepdims=True)

                @pl.when(tile == block)
                def _():
                    add_blocks(wide)

                for m, (there, corner) in enumerate(
                    ((tile < block, tile + 1 == block), (tile > block, tile == block + 1))
                ):
                    far_ref[m : m + 1, :] = far_ref[m : m + 1, :] + jnp.where(there, sums, 0.0)
                    piece = corner_of(wide, ("prev", "next")[m])
                    d_corner_ref[m] = d_corner_ref[m] + jnp.where(corner, piece, 0.0)
            d_both_ref[keys, :] = (
                d_both_ref[keys, :] + dot_nn(weights.astype(bf16), back) + dot_nn(d_scores, query)
            )
            return d_turned + dot_nn(turned_ref[:, keys], d_scores)

        def add_blocks(wide):
            sums = [None] * (NEAR + 2)
            for a in range(BK // SPAN):
                for b in range(BQ // SPAN):
                    piece = wide[a * SPAN : (a + 1) * SPAN, b * SPAN : (b + 1) * SPAN]
                    at = block_step(a, b)
                    sums[at] = piece if sums[at] is None else sums[at] + piece
            for at, item in enumerate(sums):
                d_block_ref[at] = d_block_ref[at] + item

        def finish(d_turned):
            top = d_turned[:HD, :]
            d_query_ref[dyn(q0, BQ, BQ), :] = jnp.concatenate([top, top], axis=0).T.astype(bf16)

        zero = jnp.zeros((KT_ROWS, BQ), f32)

        @pl.when(whole)
        def _():
            parts = row_of_tiles(first, last, block, step, zero, zero, zero)
            for m in range(2):
                far_ref[m : m + 1, :] = far_ref[m : m + 1, :] + parts[2 * m][HD : HD + 1, :]
            finish(parts[0] + parts[1] + parts[2])

        @pl.when(jnp.logical_not(whole))
        def _():
            finish(lax.fori_loop(first, last, functools.partial(step, "cut"), zero))

        return unused

    lax.fori_loop(info_ref[1], info_ref[2], one_block, 0)

    d_blocks = [d_block_ref[0] + d_corner_ref[0], d_block_ref[1], d_block_ref[2] + d_corner_ref[1]]
    blank = jnp.zeros((SPAN, WIDE - SPAN), f32)
    sums = [
        jnp.sum(unroll_rows(jnp.concatenate([tile, blank], axis=1)), axis=0, keepdims=True)
        for tile in d_blocks
    ]
    for m in range(2):
        line = jnp.sum(d_block_ref[NEAR + m] - d_corner_ref[m], axis=0, keepdims=True)
        for b in range(BQ // SPAN):
            line = line + far_ref[m : m + 1, b * SPAN : (b + 1) * SPAN]
        sums.append(jnp.concatenate([line, blank[:1]], axis=1))
    sums = jnp.concatenate(sums, axis=0)
    buckets = bucket_ref[: NEAR + 2, :]
    by_bucket = jnp.concatenate(
        [
            jnp.sum(jnp.where(buckets == bucket, sums, 0.0), axis=0, keepdims=True)
            for bucket in range(bucket_count)
        ],
        axis=0,
    )
    totals = jnp.broadcast_to(jnp.sum(by_bucket, axis=1, keepdims=True), (bucket_count, LANES))
    upper = totals.astype(bf16).astype(f32)
    rest = totals - upper
    per_source = bucket_count // sources
    spare = jnp.zeros((EXTRA // 2 - per_source, LANES), f32)
    for source in range(sources):
        span = slice(source * per_source, (source + 1) * per_source)
        grad_ref[source, 3 * half * SPAN :, :] = jnp.concatenate(
            [upper[span], spare, rest[span], spare], axis=0
        ).astype(bf16)

    for source in range(sources):
        for pair in range(half):
            tiles = []
            for member in range(2):
                slot = pair + member * half
                place = place_of(order_ref, info_ref, source, slot, slots) * SPAN
                grad_ref[source, slot * SPAN : (slot + 1) * SPAN, :] = d_both_ref[
                    dyn(place, SPAN, SPAN), :
                ].astype(bf16)
                tiles.append(d_query_ref[dyn(place, SPAN, SPAN), :].astype(f32))
            grad_ref[source, (slots + pair) * SPAN : (slots + pair + 1) * SPAN, :] = jnp.where(
                low, tiles[0], tiles[1]
            ).astype(bf16)


def attend_back(
    order, ends, info, swapped, mixed_grad, exact, lse, bias_rows, bucket_rows, slots, bucket_count
):
    sources = swapped.shape[0]
    total = sources * slots * SPAN
    return pl.pallas_call(
        functools.partial(attend_back_kernel, slots, bucket_count),
        in_specs=[smem_spec()] * 3 + [vmem_spec()] * 6,
        out_specs=vmem_spec(),
        out_shape=jax.ShapeDtypeStruct((sources, slots * SPAN * 3 // 2 + EXTRA, LANES), bf16),
        scratch_shapes=[
            vmem((total, LANES), bf16),
            vmem((total, LANES), bf16),
            vmem((total, LANES), bf16),
            vmem((KT_ROWS, total), bf16),
            vmem((BK, BQ), f32),
            vmem((2, SPAN, SPAN), f32),
            vmem((NEAR + 2, SPAN, SPAN), f32),
            vmem((2, SPAN, SPAN), f32),
            vmem((total, LANES), f32),
            vmem((total, LANES), bf16),
            vmem((8, BQ), f32),
        ],
        compiler_params=pltpu.CompilerParams(vmem_limit_bytes=attention_vmem(total)),
        cost_estimate=pl.CostEstimate(
            flops=total * total * 320, bytes_accessed=total * 3072, transcendentals=total * total // 2
        ),
        name="attend_back",
    )(order, ends, info, swapped, mixed_grad, exact, lse, bias_rows, bucket_rows)


def out_kernel(slots, packed_ref, weight_ref, mix_ref, *part_refs):
    heads = packed_ref.shape[0]
    half = slots * SPAN // 2

    @pl.when(pl.program_id(0) == 0)
    def _():
        for pair in range(heads // 2):
            first = packed_ref[2 * pair].astype(f32)
            second = packed_ref[2 * pair + 1].astype(f32)
            top, bottom = pair_up(first, second)
            cols = slice(pair * LANES, (pair + 1) * LANES)
            mix_ref[:half, cols] = top.astype(bf16)
            mix_ref[half:, cols] = bottom.astype(bf16)

    part = dot_nn(mix_ref[...], weight_ref[...]).astype(bf16)
    for s in range(slots):
        part_refs[s][...] = part[s * SPAN : (s + 1) * SPAN]


def out_project(packed, weight, slots):
    heads = packed.shape[0]
    rows, width, depth = slots * SPAN, heads * HD, weight.shape[1]
    tile = 512
    return pl.pallas_call(
        functools.partial(out_kernel, slots),
        grid=(depth // tile,),
        in_specs=[
            pl.BlockSpec(packed.shape, lambda j: (0, 0, 0)),
            pl.BlockSpec((width, tile), lambda j: (0, j)),
        ],
        out_specs=[
            pl.BlockSpec((rows, width), lambda j: (0, 0)),
        ]
        + [pl.BlockSpec((SPAN, tile), lambda j: (0, j))] * slots,
        out_shape=[jax.ShapeDtypeStruct((rows, width), bf16)]
        + [jax.ShapeDtypeStruct((SPAN, depth), bf16)] * slots,
        compiler_params=pltpu.CompilerParams(vmem_limit_bytes=40 * MIB),
        cost_estimate=pl.CostEstimate(
            flops=2 * rows * depth * width, bytes_accessed=4 * depth * width, transcendentals=0
        ),
        name="out_project",
    )(packed, weight)


def feed_kernel(slots, *refs):
    normed_refs, grad_refs = refs[:slots], refs[slots : 2 * slots]
    gate_ref, up_ref, down_ref, active_ref, d_both_ref, rows_ref, rows_grad_ref = refs[2 * slots :]

    @pl.when(pl.program_id(0) == 0)
    def _():
        for s in range(slots):
            rows_ref[s * SPAN : (s + 1) * SPAN, :] = normed_refs[s][...]
            rows_grad_ref[s * SPAN : (s + 1) * SPAN, :] = grad_refs[s][...]

    tile = down_ref.shape[1]
    width = d_both_ref.shape[1] // 2
    gate = dot_nn(rows_ref[...], gate_ref[...])
    up = dot_nn(rows_ref[...], up_ref[...])
    d_hidden = dot_nn(rows_grad_ref[...], down_ref[...])
    scale, cubic = 0.7978845608028654, 0.044715
    square = gate * gate
    bent = jnp.tanh(scale * (gate + cubic * square * gate))
    half = 0.5 * (1.0 + bent)
    gelu = gate * half
    slope = half + 0.5 * gate * (1.0 - bent * bent) * (scale * (1.0 + 3.0 * cubic * square))
    active_ref[...] = (gelu * up).astype(bf16)
    start = pl.program_id(0) * tile
    d_both_ref[:, dyn(start, tile, tile)] = (d_hidden * up * slope).astype(bf16)
    d_both_ref[:, dyn(width + start, tile, LANES)] = (d_hidden * gelu).astype(bf16)


def feed_tile(width):
    return 256 if width % 256 == 0 else 128


def feed(normed_slots, grad_slots, weights):
    slots = len(normed_slots)
    rows, depth, width = slots * SPAN, weights.shape[0], weights.shape[1] // 3
    tile = feed_tile(width)
    steps = width // tile
    whole = pl.BlockSpec((SPAN, depth), lambda j: (0, 0))

    def columns(part):
        return pl.BlockSpec((depth, tile), lambda j: (0, part * steps + j))

    return pl.pallas_call(
        functools.partial(feed_kernel, slots),
        grid=(steps,),
        in_specs=[whole] * (2 * slots) + [columns(0), columns(1), columns(2)],
        out_specs=[
            pl.BlockSpec((rows, tile), lambda j: (0, j)),
            pl.BlockSpec((rows, 2 * width), lambda j: (0, 0)),
        ],
        out_shape=[
            jax.ShapeDtypeStruct((rows, width), bf16),
            jax.ShapeDtypeStruct((rows, 2 * width), bf16),
        ],
        scratch_shapes=[vmem((rows, depth), bf16), vmem((rows, depth), bf16)],
        compiler_params=pltpu.CompilerParams(vmem_limit_bytes=56 * MIB),
        cost_estimate=pl.CostEstimate(
            flops=6 * rows * depth * width,
            bytes_accessed=6 * depth * width,
            transcendentals=rows * width,
        ),
        name="feed",
    )(*normed_slots, *grad_slots, weights, weights, weights)


def pack_kernel(slots, shares, spot_ref, mine_ref, rest_ref, packed_ref):
    width = mine_ref.shape[1]
    half = SPAN // 2
    for s in range(slots):
        there = lax.rem(spot_ref[0] - s + slots, slots)
        for pair in range(width // LANES):
            if s == 0:
                tile = mine_ref[:, pair * LANES : (pair + 1) * LANES].astype(f32)
            else:
                start = (s - 1) * width + pair * LANES
                tile = rest_ref[:, start : start + LANES].astype(f32)
            for member, piece in enumerate(pair_up(tile[:half], tile[half:])):
                for share in range(shares):
                    packed_ref[(2 * pair + member) * shares + share, there] = piece.astype(bf16)


def pack(spot, mine, rest, shares):
    width = mine.shape[1]
    slots = 1 + rest.shape[1] // width
    return pl.pallas_call(
        functools.partial(pack_kernel, slots, shares),
        in_specs=[smem_spec(), vmem_spec(), vmem_spec()],
        out_specs=vmem_spec(),
        out_shape=jax.ShapeDtypeStruct((width // HD * shares, slots, SPAN // 2, LANES), bf16),
        compiler_params=pltpu.CompilerParams(vmem_limit_bytes=16 * MIB),
        name="pack",
    )(spot, mine, rest)


def weigh_kernel(slots, packed_ref, mix_ref, left_ref, *refs):
    attn_refs = refs[:slots]
    product_ref, grads_ref = refs[slots:]
    heads = packed_ref.shape[0]
    rows = slots * SPAN
    half = rows // 2
    width = heads * HD

    @pl.when(pl.program_id(0) == 0)
    def _():
        for pair in range(heads // 2):
            start = pair * LANES
            tiles = [packed_ref[2 * pair + m].astype(f32) for m in range(2)]
            value, key = pair_up(tiles[0][:rows], tiles[1][:rows])
            top, bottom = pair_up(tiles[0][rows : rows + half], tiles[1][rows : rows + half])
            grads_ref[:half, start : start + LANES] = top.astype(bf16)
            grads_ref[half:, start : start + LANES] = bottom.astype(bf16)
            grads_ref[:, width + start : width + start + LANES] = key.astype(bf16)
            grads_ref[:, 2 * width + start : 2 * width + start + LANES] = value.astype(bf16)

    product_ref[:, : 3 * width] = dot_tn(left_ref[...], grads_ref[...]).astype(bf16)
    attn = jnp.concatenate([ref[...] for ref in attn_refs], axis=0)
    product_ref[:, 3 * width :] = dot_tn(attn, mix_ref[...]).astype(bf16)


def weigh(packed, mix, left, attn_slots):
    slots = len(attn_slots)
    heads = packed.shape[0]
    rows, depth = left.shape
    width = 3 * heads * HD
    total = width + mix.shape[1]
    tile = 512
    return pl.pallas_call(
        functools.partial(weigh_kernel, slots),
        grid=(depth // tile,),
        in_specs=[
            pl.BlockSpec(packed.shape, lambda j: (0, 0, 0)),
            pl.BlockSpec(mix.shape, lambda j: (0, 0)),
            pl.BlockSpec((rows, tile), lambda j: (0, j)),
        ]
        + [pl.BlockSpec((SPAN, tile), lambda j: (0, j))] * slots,
        out_specs=[
            pl.BlockSpec((tile, total), lambda j: (j, 0)),
            pl.BlockSpec((rows, width), lambda j: (0, 0)),
        ],
        out_shape=[
            jax.ShapeDtypeStruct((depth, total), bf16),
            jax.ShapeDtypeStruct((rows, width), bf16),
        ],
        compiler_params=pltpu.CompilerParams(vmem_limit_bytes=LARGE),
        cost_estimate=pl.CostEstimate(
            flops=2 * rows * depth * total, bytes_accessed=4 * depth * total, transcendentals=0
        ),
        name="weigh",
    )(packed, mix, left, *attn_slots)


def project_back_kernel(which, grads_ref, weight_ref, scale_ref, *refs):
    x_refs = refs[: len(which)]
    gain_ref, *part_refs = refs[len(which) :]
    part = dot_nt(grads_ref[...], weight_ref[...])
    gain = jnp.zeros((1, part.shape[1]), f32)
    for s, x_ref, part_ref in zip(which, x_refs, part_refs, strict=True):
        start = s * SPAN if len(which) > 1 else 0
        piece = part[start : start + SPAN]
        part_ref[...] = piece.astype(bf16)
        x_hat = x_ref[...].astype(f32) * scale_ref[start : start + SPAN, :1]
        gain = gain + jnp.sum(piece * x_hat, axis=0, keepdims=True)
    gain_ref[...] = gain


def project_back(grads, weights, scale, x_slots, which):
    depth, width = weights.shape
    single = len(which) == 1
    rows, at = (SPAN, which[0]) if single else (grads.shape[0], 0)
    tile = 512
    spans = [pl.BlockSpec((SPAN, tile), lambda j: (0, j))] * len(which)
    return pl.pallas_call(
        functools.partial(project_back_kernel, which),
        grid=(depth // tile,),
        in_specs=[
            pl.BlockSpec((rows, width), lambda j: (at, 0)),
            pl.BlockSpec((tile, width), lambda j: (j, 0)),
            pl.BlockSpec((rows, LANES), lambda j: (at, 0)),
        ]
        + spans,
        out_specs=[pl.BlockSpec((1, tile), lambda j: (0, j))] + spans,
        out_shape=[jax.ShapeDtypeStruct((1, depth), f32)]
        + [jax.ShapeDtypeStruct((SPAN, depth), bf16)] * len(which),
        compiler_params=pltpu.CompilerParams(vmem_limit_bytes=LARGE),
        cost_estimate=pl.CostEstimate(
            flops=2 * rows * depth * width, bytes_accessed=4 * depth * width, transcendentals=0
        ),
        name="project_back",
    )(grads, weights, scale, *[x_slots[s] for s in which])


def pair_kernel(slots, groups, *refs):
    left_one, left_two = refs[:slots], refs[slots : 2 * slots]
    right_one = refs[2 * slots : 2 * slots + groups]
    right_two = refs[2 * slots + groups : 2 * slots + 2 * groups]
    out_ref, right_ref = refs[-2:]
    cut = right_one[0].shape[1]

    @pl.when(pl.program_id(0) == 0)
    def _():
        start = 0
        for one, two in zip(right_one, right_two, strict=True):
            span = slice(start, start + one.shape[0])
            right_ref[span, :cut] = one[...]
            right_ref[span, cut:] = two[...]
            start += one.shape[0]

    one = jnp.concatenate([ref[...] for ref in left_one], axis=0)
    two = jnp.concatenate([ref[...] for ref in left_two], axis=0)
    out_ref[:, :cut] = dot_tn(one, right_ref[:, :cut]).astype(bf16)
    out_ref[:, cut:] = dot_tn(two, right_ref[:, cut:]).astype(bf16)


def pair_product(left_one, right_one, left_two, right_two):
    slots, groups = len(left_one), len(right_one)
    rows, depth = slots * SPAN, left_one[0].shape[1]
    width = right_one[0].shape[1] + right_two[0].shape[1]
    block = 512

    def whole(array):
        return pl.BlockSpec(array.shape, lambda j: (0, 0))

    return pl.pallas_call(
        functools.partial(pair_kernel, slots, groups),
        grid=(depth // block,),
        in_specs=[pl.BlockSpec((SPAN, block), lambda j: (0, j))] * (2 * slots)
        + [whole(piece) for piece in (*right_one, *right_two)],
        out_specs=pl.BlockSpec((block, width), lambda j: (j, 0)),
        out_shape=jax.ShapeDtypeStruct((depth, width), bf16),
        scratch_shapes=[vmem((rows, width), bf16)],
        compiler_params=pltpu.CompilerParams(vmem_limit_bytes=32 * MIB),
        cost_estimate=pl.CostEstimate(
            flops=2 * rows * depth * width, bytes_accessed=2 * depth * width, transcendentals=0
        ),
        name="pair_product",
    )(*left_one, *left_two, *right_one, *right_two)


def bucket_lines(bucket_of):
    count = bucket_of.shape[0]
    turned = bucket_of[::-1]
    ends = [jnp.broadcast_to(end, (2 * SPAN,)) for end in (turned[:1], turned[-1:])]
    padded = jnp.concatenate([ends[0], turned, ends[1]])
    zero_at = 2 * SPAN + count // 2
    rows = []
    for c in range(NEAR):
        base = zero_at - (c - 1) * SPAN
        rows.append(jnp.concatenate([padded[base : base + SPAN], padded[base - SPAN : base]]))
    rows.append(jnp.broadcast_to(bucket_of[:1], (WIDE,)))
    rows.append(jnp.broadcast_to(bucket_of[-1:], (WIDE,)))
    spare = 8 - (NEAR + 2)
    return jnp.concatenate([jnp.stack(rows), jnp.full((spare, WIDE), -1, bucket_of.dtype)])


def on_device(
    tokens,
    lengths,
    block_order,
    bucket_of,
    gain_attn,
    w_query,
    w_key,
    w_value,
    w_out,
    bias_table,
    gain_ffn,
    w_gate,
    w_up,
    w_down,
    cotangent,
):
    blk_count, slots = lax.axis_size("blk"), lax.axis_size("head")
    blk_spot, head_spot = lax.axis_index("blk"), lax.axis_index("head")
    depth = tokens.shape[1]
    width = w_query.shape[1]
    heads = width // HD
    shares = blk_count // heads
    table_rows, table_heads = bias_table.shape
    bucket_count = table_rows * blk_count
    total = blk_count * slots * SPAN
    gain_size = gain_attn.shape[0]
    hidden = w_gate.shape[1]

    token_slots = gather_far(gather_near(tokens))
    small = gather_small(
        jnp.concatenate([gain_attn, gain_ffn, bias_table.astype(f32).reshape(-1)])
    )
    full_qkv = lax.all_gather(
        jnp.concatenate([w_query, w_key, w_value], axis=1), "blk", axis=0, tiled=True
    )
    full_out = lax.all_gather(w_out, "blk", axis=1, tiled=True)
    full_ffn = lax.all_gather(
        jnp.concatenate([w_gate, w_up, w_down.T], axis=1), "blk", axis=0, tiled=True
    )
    gain_one = small[:, :, :gain_size].reshape(1, depth)
    gain_two = small[:, :, gain_size : 2 * gain_size].reshape(1, depth)

    tables = lax.dynamic_index_in_dim(small, head_spot, 1, False)[:, 2 * gain_size :]
    tables = tables.reshape(bucket_count, table_heads)
    my_head = blk_spot // shares
    my_bias = lax.dynamic_index_in_dim(tables, my_head, 1, False)
    bucket_rows = bucket_lines(bucket_of)
    bias_rows = jnp.sum(
        jnp.where(
            bucket_rows[None] == jnp.arange(bucket_count, dtype=jnp.int32)[:, None, None],
            my_bias[:, None, None],
            0.0,
        ),
        axis=0,
    )
    ends = jnp.cumsum(lengths).astype(jnp.int32)
    per_share = total // BQ // shares
    start = (blk_spot % shares) * per_share
    info = [head_spot, start, start + per_share] + ([start] if shares > 1 else [])
    info = jnp.stack([jnp.asarray(item, jnp.int32) for item in info])

    def swap(values):
        return lax.all_to_all(values, "blk", 0, 0, tiled=True)

    def to_all(values):
        values = values.reshape((blk_count * slots,) + values.shape[2:])
        return lax.all_to_all(values, ("blk", "head"), 0, 0, tiled=True)

    def to_heads(values):
        return swap(values if shares == 1 else jnp.repeat(values, shares, axis=0))

    def to_rows(values):
        values = swap(values)
        if shares == 1:
            return values
        values = values.reshape((heads, shares) + values.shape[1:])
        return jnp.sum(values.astype(f32), axis=1).astype(bf16)

    w_out, cotangent, *token_slots = together(w_out, cotangent, *token_slots)
    normed_one, packed, scale_one = project(token_slots, gain_one, full_qkv)
    early = (ends, info, bias_rows, bucket_rows)
    swapped, ends, info, bias_rows, bucket_rows, *out_near = together(
        to_heads(packed), *early, *gather_near(w_out)
    )
    grad_near, out_slots = gather_near(cotangent), gather_far(out_near)
    mixed, exact, lse = attend(block_order, ends, info, swapped, bias_rows, slots)
    mixed, *moved = together(mixed, *grad_near, *out_slots)
    grad_near, out_slots = moved[: len(grad_near)], moved[len(grad_near) :]
    packed_mix, *grad_slots = together(to_rows(mixed), *gather_far(grad_near))
    attn_mix, *out_parts = out_project(packed_mix, full_out, slots)
    tokens_wide = tokens.astype(f32)
    hidden_one = tokens_wide + sum_terms(sum_near(out_parts, sum_far(out_parts))[0])
    rstd_two = rms_scale(hidden_one)
    normed_two = (hidden_one * rstd_two * gain_two).astype(bf16)

    normed_two, out_slots = together(normed_two, out_slots)
    full_rest = lax.all_gather(jnp.concatenate(out_slots[1:]), "blk", axis=1, tiled=True)
    normed_slots = gather_far(gather_near(normed_two))
    active, d_both = feed(normed_slots, grad_slots, full_ffn)

    def spans(rows):
        return [rows[s * SPAN : (s + 1) * SPAN] for s in range(rows.shape[0] // SPAN)]

    d_parts = spans(dot_nt(d_both, full_ffn[:, : 2 * hidden]).astype(bf16))
    d_far = sum_far(d_parts)
    grad_hidden, *d_far = together(
        pair_product(normed_slots, [d_both], grad_slots, [active]), *d_far
    )
    grad_hidden = lax.psum_scatter(grad_hidden, "blk", scatter_dimension=0, tiled=True)
    d_near, (active,) = sum_near(d_parts, d_far, (active,))
    down_rows = dot_nt(active, full_ffn[:, 2 * hidden :]).astype(bf16)
    down_rows, full_rest, *d_near = together(down_rows, full_rest, *d_near)
    down_parts = spans(down_rows)
    d_normed_two = sum_terms(d_near)
    d_source_two, gain_part_two = norm_back(d_normed_two, hidden_one, rstd_two, gain_two)
    d_hidden_one = cotangent.astype(f32) + d_source_two

    d_attn = d_hidden_one.astype(bf16)
    mix_grads = pack(
        jnp.reshape(head_spot, (1,)).astype(jnp.int32),
        dot_nt(d_attn, full_out).astype(bf16),
        dot_nt(d_attn, full_rest).astype(bf16),
        shares,
    )
    mix_grads, d_attn = together(mix_grads, d_attn)
    middle = slots // 2
    steps = [t for t in range(1, slots) if t != middle]
    moved = (*gather_near(d_attn), *sum_direct(down_parts, steps))
    grads = attend_back(
        block_order, ends, info, swapped, to_all(mix_grads), exact, lse, bias_rows, bucket_rows,
        slots, bucket_count,
    )
    grads, down_parts, *moved = together(grads, down_parts, *moved)
    attn_near, down_terms = moved[: 2 - slots], moved[2 - slots :]
    grads, *attn_slots = together(swap(grads), *gather_far(attn_near))
    extra = grads[:, -EXTRA:, 0].astype(f32).reshape(blk_count, 2, -1).sum(axis=1)
    grad_table = extra[:, :table_rows].reshape(heads, shares, table_rows).sum(axis=1).T
    if shares > 1:
        grads = grads.reshape((heads, shares) + grads.shape[1:])
        grads = jnp.sum(grads.astype(f32), axis=1).astype(bf16)
    grad_heads, d_qkv = weigh(grads, attn_mix, normed_one, attn_slots)
    grad_heads, grad_hidden = together(grad_heads, grad_hidden)
    if slots == 4:
        gain_part_one, far_part = project_back(d_qkv, full_qkv, scale_one, token_slots, [2])
        one_far = sum_far([None, None, far_part, None])
        d_qkv, far_part = together(d_qkv, far_part)
        gain_rest, *one_parts = project_back(d_qkv, full_qkv, scale_one, token_slots, [0, 1, 3])
        gain_part_one = gain_part_one + gain_rest
        one_parts.insert(2, far_part)
    else:
        gain_part_one, *one_parts = project_back(
            d_qkv, full_qkv, scale_one, token_slots, list(range(slots))
        )
        one_far = []

    gain_parts = jnp.stack(
        [part.reshape(blk_count, slots, gain_size) for part in (gain_part_one, gain_part_two)],
        axis=2,
    )
    gain_parts, *one_far = together(gain_parts, *one_far)
    grad_heads = lax.psum_scatter(grad_heads, "blk", scatter_dimension=0, tiled=True).astype(f32)
    one_near, unused = sum_near(one_parts, one_far)
    gain_sums = scatter_blk(gain_parts)
    gain_sums, down_parts, grad_hidden, *one_near = together(
        gain_sums, down_parts, grad_hidden, *one_near
    )
    far_term = sum_direct(down_parts, [middle])
    gain_sums = scatter_head(gain_sums)
    grad_hidden = grad_hidden.astype(f32)
    d_normed_one = sum_terms(one_near)
    d_source_one, unused = norm_back(d_normed_one, tokens_wide, rms_scale(tokens_wide), gain_one)
    input_grad = d_hidden_one + d_source_one
    input_grad, hidden_one = together(input_grad, hidden_one)
    output = hidden_one + sum_all([down_parts[0]] + down_terms + far_term)
    return (
        output,
        input_grad,
        gain_sums[0],
        grad_heads[:, :width],
        grad_heads[:, width : 2 * width],
        grad_heads[:, 2 * width : 3 * width],
        grad_heads[:, 3 * width :].T,
        grad_table,
        gain_sums[1],
        grad_hidden[:, :hidden],
        grad_hidden[:, hidden : 2 * hidden],
        grad_hidden[:, 2 * hidden :].T,
    )


def solution(mesh):
    rows, spread = P(("blk", "head"), None), P(("blk", "head"))
    inward, outward = P("blk", "head"), P("head", "blk")
    in_specs = (
        rows, P(), P(), P(), spread, inward, inward, inward, outward, inward, spread,
        inward, inward, outward, rows,
    )
    out_specs = (
        rows, rows, spread, inward, inward, inward, outward, inward, spread,
        inward, inward, outward,
    )
    return jax.shard_map(
        on_device, mesh=mesh, in_specs=in_specs, out_specs=out_specs, check_vma=False
    )
```

```python
import functools

import jax
import jax.numpy as jnp
from jax import lax
from jax.experimental import pallas as pl
from jax.experimental.pallas import tpu as pltpu
from jax.sharding import PartitionSpec as P

HD = 64
LANES = 2 * HD
MAXDIST = 128
SPAN = 128
BQ = 512
BK = BQ
NEAR = 3
WIDE = 2 * SPAN
EXTRA = 16
KT_ROWS = 80
SHIFT_ROOM = 60.0

norm_eps = 1e-06
masked_score = -1e30
f32 = jnp.float32
bf16 = jnp.bfloat16
MIB = 1 << 20
LARGE = 58 * MIB


def rms_scale(values):
    return lax.rsqrt(jnp.mean(values * values, axis=-1, keepdims=True) + norm_eps)


def norm_back(d_normed, source, inv_rms, gain_vec):
    scaled = d_normed * gain_vec
    x_hat = source * inv_rms
    gain_part = jnp.sum(d_normed * x_hat, axis=0)
    d_source = inv_rms * (scaled - x_hat * jnp.mean(scaled * x_hat, axis=-1, keepdims=True))
    return (d_source, gain_part)


def dot_nn(left, right):
    return jnp.dot(left, right, preferred_element_type=f32)


def dot_nt(left, right):
    return lax.dot_general(left, right, (((1,), (1,)), ((), ())), preferred_element_type=f32)


def dot_tn(left, right):
    return lax.dot_general(left, right, (((0,), (0,)), ((), ())), preferred_element_type=f32)


def cyclic(count, by):
    return [(i, (i + by) % count) for i in range(count)]


def together(*values):
    return lax.optimization_barrier(values)


def gather_near(rows):
    count = lax.axis_size("head")
    if count != 4:
        return [rows] + [lax.ppermute(rows, "head", cyclic(count, s)) for s in range(1, count)]
    return [rows, lax.ppermute(rows, "head", cyclic(4, 1)), lax.ppermute(rows, "head", cyclic(4, 3))]


def gather_far(near):
    if lax.axis_size("head") != 4:
        return near
    rows, back_one, ahead_one = near
    me = lax.axis_index("head")
    passed = jnp.where(me == 1, ahead_one, jnp.where(me == 2, back_one, rows))
    back_two = lax.ppermute(passed, "head", [(1, 0), (3, 1), (0, 2), (2, 3)])
    return [rows, back_one, back_two, ahead_one]


def gather_direct(rows):
    count = lax.axis_size("head")
    return [rows] + [lax.ppermute(rows, "head", cyclic(count, s)) for s in range(1, count)]


def sum_far(parts):
    count = lax.axis_size("head")
    if count != 4:
        return []
    return [lax.ppermute(parts[2], "head", [(0, 1), (1, 3), (2, 0), (3, 2)])]


def sum_near(parts, far, beside=()):
    count = lax.axis_size("head")
    if count != 4:
        return [parts[0]] + [
            lax.ppermute(parts[s], "head", cyclic(count, count - s)) for s in range(1, count)
        ], beside
    me = lax.axis_index("head")
    wide = far[0].astype(f32)
    to_back = jnp.where(me == 2, parts[1].astype(f32) + wide, parts[1].astype(f32)).astype(bf16)
    to_ahead = jnp.where(me == 1, parts[3].astype(f32) + wide, parts[3].astype(f32)).astype(bf16)
    to_back, to_ahead, *beside = together(to_back, to_ahead, *beside)
    from_ahead = lax.ppermute(to_back, "head", cyclic(4, 3))
    from_back = lax.ppermute(to_ahead, "head", cyclic(4, 1))
    return [parts[0], from_ahead, from_back, far[0]], beside


def sum_terms(terms):
    total = terms[0].astype(f32) + terms[1].astype(f32) + terms[2].astype(f32)
    if lax.axis_size("head") != 4:
        for term in terms[3:]:
            total = total + term.astype(f32)
        return total
    me = lax.axis_index("head")
    return total + jnp.where((me == 0) | (me == 3), terms[3].astype(f32), 0.0)


def is_power(count):
    return count & (count - 1) == 0


def gather_small(values):
    held = values[None]
    for axis in ("head", "blk"):
        count = lax.axis_size(axis)
        if not is_power(count):
            held = lax.all_gather(held, axis, axis=0, tiled=False)
        else:
            me = lax.axis_index(axis)
            held = held[None]
            bit = 1
            while bit < count:
                other = lax.ppermute(held, axis, [(i, i ^ bit) for i in range(count)])
                low = jnp.concatenate([held, other])
                high = jnp.concatenate([other, held])
                held = jnp.where((me // bit) % 2 == 0, low, high)
                bit *= 2
        if axis == "head":
            held = held.reshape(count, -1)
    return held


def send_back(rows, places):
    count = lax.axis_size("head")
    return lax.ppermute(rows, "head", cyclic(count, count - places))


def sum_direct(parts, steps):
    count = len(parts)
    return [lax.ppermute(parts[s], "head", cyclic(count, count - s)) for s in steps]


def sum_all(terms):
    total = terms[0].astype(f32)
    for term in terms[1:]:
        total = total + term.astype(f32)
    return total


def scatter_blk(values):
    return jnp.sum(lax.all_to_all(values, "blk", 0, 0, tiled=True), axis=0)


def scatter_head(values):
    count, me = lax.axis_size("head"), lax.axis_index("head")
    total = lax.dynamic_index_in_dim(values, me, 0, False)
    for s in range(1, count):
        sent = lax.dynamic_index_in_dim(values, (me + s) % count, 0, False)
        total = total + lax.ppermute(sent, "head", cyclic(count, s))
    return total


def lane_low(shape):
    return lax.broadcasted_iota(jnp.int32, shape, 1) < HD


def swap_halves(tile):
    return pltpu.roll(tile, HD, 1)


def pair_up(first, second):
    low = lane_low(first.shape)
    return (
        jnp.where(low, first, swap_halves(second)),
        jnp.where(low, swap_halves(first), second),
    )


def project_kernel(slots, *refs):
    x_refs = refs[:slots]
    gain_ref, wq_ref, wk_ref, wv_ref, normed_ref, packed_ref, scale_ref = refs[slots:]
    rows = slots * SPAN

    @pl.when(pl.program_id(0) == 0)
    def _():
        for s in range(slots):
            wide = x_refs[s][...].astype(f32)
            scale = rms_scale(wide)
            normed = wide * scale * gain_ref[...]
            normed_ref[s * SPAN : (s + 1) * SPAN, :] = normed.astype(bf16)
            scale_ref[s * SPAN : (s + 1) * SPAN, :] = jnp.broadcast_to(scale, (SPAN, LANES))

    normed = normed_ref[...]
    query = dot_nn(normed, wq_ref[...])
    key = dot_nn(normed, wk_ref[...])
    value = dot_nn(normed, wv_ref[...])
    half = rows // 2
    for pair in range(query.shape[1] // LANES):
        cols = slice(pair * LANES, (pair + 1) * LANES)
        both = pair_up(value[:, cols], key[:, cols])
        queries = pair_up(query[:half, cols], query[half:, cols])
        for member in range(2):
            packed_ref[2 * pair + member, :rows, :] = both[member].astype(bf16)
            packed_ref[2 * pair + member, rows:, :] = queries[member].astype(bf16)


def project(x_slots, gain, weights):
    slots = len(x_slots)
    rows, depth = slots * SPAN, x_slots[0].shape[1]
    width = weights.shape[1] // 3
    heads = width // HD
    tile = min(width, 256)
    steps = width // tile
    whole = pl.BlockSpec((SPAN, depth), lambda j: (0, 0))

    def columns(part):
        return pl.BlockSpec((depth, tile), lambda j: (0, part * steps + j))

    return pl.pallas_call(
        functools.partial(project_kernel, slots),
        grid=(steps,),
        in_specs=[whole] * slots
        + [pl.BlockSpec((1, depth), lambda j: (0, 0)), columns(0), columns(1), columns(2)],
        out_specs=[
            pl.BlockSpec((rows, depth), lambda j: (0, 0)),
            pl.BlockSpec((tile // HD, rows + rows // 2, LANES), lambda j: (j, 0, 0)),
            pl.BlockSpec((rows, LANES), lambda j: (0, 0)),
        ],
        out_shape=[
            jax.ShapeDtypeStruct((rows, depth), bf16),
            jax.ShapeDtypeStruct((heads, rows + rows // 2, LANES), bf16),
            jax.ShapeDtypeStruct((rows, LANES), f32),
        ],
        compiler_params=pltpu.CompilerParams(vmem_limit_bytes=40 * MIB),
        cost_estimate=pl.CostEstimate(
            flops=10 * rows * depth * width, bytes_accessed=6 * depth * width, transcendentals=0
        ),
        name="project",
    )(*x_slots, gain, weights, weights, weights)


def place_of(order_ref, info_ref, source, slot, slots):
    z = info_ref[0]
    return order_ref[source * slots + lax.rem(z - slot + slots, slots)]


def dyn(start, size, multiple):
    return pl.ds(pl.multiple_of(start, multiple), size)


def near_blocks(bias_ref):
    tiles = []
    for c in range(NEAR):
        spread = jnp.broadcast_to(bias_ref[c : c + 1, :], (SPAN, WIDE))
        tiles.append(pltpu.roll(spread, 0, 1, stride=1, stride_axis=0)[:, :SPAN])
    return tiles


def block_step(a, b):
    return a - b + 1 if abs(a - b) <= 1 else 3 if a < b else 4


def fill_tables(bias_ref, table_ref, corner_ref):
    tiles = near_blocks(bias_ref)
    far = [jnp.broadcast_to(bias_ref[NEAR + m : NEAR + m + 1, :SPAN], (SPAN, SPAN)) for m in range(2)]
    every = tiles + far
    for a in range(BK // SPAN):
        for b in range(BQ // SPAN):
            table_ref[a * SPAN : (a + 1) * SPAN, b * SPAN : (b + 1) * SPAN] = every[block_step(a, b)]
    corner_ref[0] = tiles[0] - far[0]
    corner_ref[1] = tiles[2] - far[1]


def with_corner(tile, kind, corner):
    if kind == "prev":
        upper, lower = tile[: BK - SPAN], tile[BK - SPAN :]
        lower = jnp.concatenate([lower[:, :SPAN] + corner, lower[:, SPAN:]], axis=1)
    else:
        upper, lower = tile[:SPAN], tile[SPAN:]
        upper = jnp.concatenate([upper[:, : BQ - SPAN], upper[:, BQ - SPAN :] + corner], axis=1)
    return jnp.concatenate([upper, lower], axis=0)


def corner_of(tile, kind):
    return tile[BK - SPAN :, :SPAN] if kind == "prev" else tile[:SPAN, BQ - SPAN :]


def any_bias(bias_ref, table_ref, corner_ref, tile, block):
    left = jnp.broadcast_to(bias_ref[NEAR : NEAR + 1, 0:1], (BK, BQ))
    right = jnp.broadcast_to(bias_ref[NEAR + 1 : NEAR + 2, 0:1], (BK, BQ))
    left = with_corner(left, "prev", jnp.where(tile + 1 == block, corner_ref[0], 0.0))
    right = with_corner(right, "next", jnp.where(tile == block + 1, corner_ref[1], 0.0))
    return jnp.where(tile == block, table_ref[...], jnp.where(tile < block, left, right))


def block_range(ends_ref, q0, total):
    count = ends_ref.shape[0]
    start, end, cut = jnp.int32(0), jnp.int32(total), jnp.bool_(False)
    for n in range(count):
        edge = ends_ref[n]
        start = jnp.where(edge <= q0, edge, start)
        cut = cut | ((edge > q0) & (edge < q0 + BQ))
    for n in range(count - 1, -1, -1):
        edge = ends_ref[n]
        end = jnp.where(edge >= q0 + BQ, edge, end)
    first = lax.div(start, BK)
    last = lax.div(end + BK - 1, BK)
    whole = jnp.logical_not(cut) & (lax.rem(start, BK) == 0) & (lax.rem(end, BK) == 0)
    return first, last, whole


def row_of_tiles(first, last, block, step, left, middle, right):
    before, after = jnp.maximum(block - 1, first), jnp.minimum(block + 2, last)
    left = lax.fori_loop(first, before, functools.partial(step, "left"), left)
    left = lax.fori_loop(before, block, functools.partial(step, "prev"), left)
    middle = step("diagonal", block, left if middle is None else middle)
    right = middle if right is None else right
    right = lax.fori_loop(block + 1, after, functools.partial(step, "next"), right)
    right = lax.fori_loop(after, last, functools.partial(step, "right"), right)
    return left, middle, right


def same_sequence(ends_ref, k0, q0):
    key_place = k0 + lax.broadcasted_iota(jnp.int32, (BK, 1), 0)
    query_place = q0 + lax.broadcasted_iota(jnp.int32, (1, BQ), 1)
    key_seg = jnp.zeros((BK, 1), jnp.int32)
    query_seg = jnp.zeros((1, BQ), jnp.int32)
    for n in range(ends_ref.shape[0]):
        key_seg = key_seg + jnp.where(key_place >= ends_ref[n], 1, 0)
        query_seg = query_seg + jnp.where(query_place >= ends_ref[n], 1, 0)
    return key_seg == query_seg


def sort_blocks(order_ref, info_ref, x_ref, slots, keep):
    sources = x_ref.shape[0]
    half = slots // 2
    high = jnp.logical_not(lane_low((SPAN, LANES)))
    for source in range(sources):
        for pair in range(half):
            packed = x_ref[
                source, (slots + pair) * SPAN : (slots + pair + 1) * SPAN, :
            ].astype(f32)
            queries = (swap_halves(packed), packed)
            for member in range(2):
                slot = pair + member * half
                place = place_of(order_ref, info_ref, source, slot, slots) * SPAN
                both = x_ref[source, slot * SPAN : (slot + 1) * SPAN, :]
                keep(place, both, jnp.where(high, queries[member], 0.0).astype(bf16))


def attend_kernel(
    slots, order_ref, ends_ref, info_ref, x_ref, bias_ref, mixed_ref, exact_ref, lse_ref,
    both_ref, query_ref, turned_ref, table_ref, corner_ref, held_ref, rows_ref,
):
    total = both_ref.shape[0]
    parted = info_ref.shape[0] > 3

    def keep(place, both, query):
        both_ref[dyn(place, SPAN, SPAN), :] = both
        query_ref[dyn(place, SPAN, SPAN), :] = query
        turned = both.astype(f32).T
        turned_ref[:, dyn(place, SPAN, SPAN)] = turned[:HD, :].astype(bf16)
        turned_key, turned_query = turned[HD:, :], query.astype(f32).T[HD:, :]
        for line, product in enumerate(
            (turned_key * turned_query, turned_key * turned_key, turned_query * turned_query)
        ):
            rows_ref[line : line + 1, dyn(place, SPAN, SPAN)] = jnp.sum(
                product, axis=0, keepdims=True
            )

    sort_blocks(order_ref, info_ref, x_ref, slots, keep)
    fill_tables(bias_ref, table_ref, corner_ref)
    if parted:
        held_ref[...] = jnp.zeros_like(held_ref)
        exact_ref[...] = jnp.zeros_like(exact_ref)
        lse_ref[...] = jnp.zeros_like(lse_ref)
    left_bias = bias_ref[NEAR : NEAR + 1, 0:1]
    right_bias = bias_ref[NEAR + 1 : NEAR + 2, 0:1]
    start_state = (
        jnp.full((1, BQ), masked_score, f32),
        jnp.zeros((1, BQ), f32),
        jnp.zeros((HD, BQ), f32),
    )
    longest_key = jnp.sqrt(jnp.max(rows_ref[1:2, :], axis=1, keepdims=True))
    most_bias = jnp.max(
        jnp.max(bias_ref[: NEAR + 2, :], axis=0, keepdims=True), axis=1, keepdims=True
    )

    def one_block(block, unused):
        q0 = block * BQ
        first, last, whole = block_range(ends_ref, q0, total)
        query = query_ref[dyn(q0, BQ, BQ), :]
        own = rows_ref[0:1, dyn(q0, BQ, BQ)] + bias_ref[1:2, 0:1]
        bound = jnp.sqrt(rows_ref[2:3, dyn(q0, BQ, BQ)]) * longest_key + most_bias
        whole = whole & (jnp.max(bound - own) < SHIFT_ROOM)

        def quick_step(kind, tile, state):
            mass, mix = state
            k0 = tile * BK
            scores = dot_nt(both_ref[dyn(k0, BK, BK), :], query)
            if kind == "diagonal":
                weights = jnp.exp(scores + table_ref[...] - own)
            else:
                if kind in ("prev", "next"):
                    scores = with_corner(scores, kind, corner_ref[0 if kind == "prev" else 1])
                weights = jnp.exp(scores - (own - (left_bias if kind in ("left", "prev") else right_bias)))
            mass = mass + jnp.sum(weights, axis=0, keepdims=True)
            return (mass, mix + dot_nn(turned_ref[:, dyn(k0, BK, BK)], weights.astype(bf16)))

        def step(tile, state):
            peak, mass, mix = state
            k0 = tile * BK
            scores = dot_nt(both_ref[dyn(k0, BK, BK), :], query)
            same = same_sequence(ends_ref, k0, q0)
            scores = scores + any_bias(bias_ref, table_ref, corner_ref, tile, block)
            scores = jnp.where(same, scores, masked_score)
            new_peak = jnp.maximum(peak, jnp.max(scores, axis=0, keepdims=True))
            weights = jnp.where(same, jnp.exp(scores - new_peak), 0.0)
            rescale = jnp.exp(peak - new_peak)
            mass = mass * rescale + jnp.sum(weights, axis=0, keepdims=True)
            turned = turned_ref[:, dyn(k0, BK, BK)]
            mix = mix * rescale + dot_nn(turned, weights.astype(bf16))
            return (new_peak, mass, mix)

        def finish(peak, mass, mix):
            exact = mix / mass
            exact_ref[:, dyn(q0, BQ, BQ)] = exact
            lse_ref[:, dyn(q0, BQ, BQ)] = peak + jnp.log(mass)
            padded = jnp.concatenate([exact, exact], axis=0)
            held_ref[dyn(q0, BQ, BQ), :] = padded.T

        @pl.when(whole)
        def _():
            *unused, state = row_of_tiles(
                first, last, block, quick_step, start_state[1:], None, None
            )
            finish(own, *state)

        @pl.when(jnp.logical_not(whole))
        def _():
            finish(*lax.fori_loop(first, last, step, start_state))

        return unused

    lax.fori_loop(info_ref[1], info_ref[2], one_block, 0)
    half = slots // 2
    low = lane_low((SPAN, LANES))
    for source in range(x_ref.shape[0]):
        for pair in range(half):
            places = [
                place_of(order_ref, info_ref, source, pair + m * half, slots) * SPAN
                for m in range(2)
            ]
            tiles = [held_ref[dyn(place, SPAN, SPAN), :] for place in places]
            mixed_ref[source, pair * SPAN : (pair + 1) * SPAN, :] = jnp.where(
                low, tiles[0], tiles[1]
            ).astype(bf16)


def vmem(shape, dtype):
    return pltpu.VMEM(shape, dtype)


def smem_spec():
    return pl.BlockSpec(memory_space=pltpu.SMEM)


def vmem_spec():
    return pl.BlockSpec(memory_space=pltpu.VMEM)


def attention_vmem(total):
    return int(min(58, 16 + 44 * (total / 16384)) * MIB)


def attend(order, ends, info, swapped, bias_rows, slots):
    sources = swapped.shape[0]
    total = sources * slots * SPAN
    return pl.pallas_call(
        functools.partial(attend_kernel, slots),
        in_specs=[smem_spec()] * 3 + [vmem_spec()] * 2,
        out_specs=[vmem_spec()] * 3,
        out_shape=[
            jax.ShapeDtypeStruct((sources, slots * SPAN // 2, LANES), bf16),
            jax.ShapeDtypeStruct((HD, total), f32),
            jax.ShapeDtypeStruct((1, total), f32),
        ],
        scratch_shapes=[
            vmem((total, LANES), bf16),
            vmem((total, LANES), bf16),
            vmem((HD, total), bf16),
            vmem((BK, BQ), f32),
            vmem((2, SPAN, SPAN), f32),
            vmem((total, LANES), f32),
            vmem((8, total), f32),
        ],
        compiler_params=pltpu.CompilerParams(vmem_limit_bytes=attention_vmem(total)),
        cost_estimate=pl.CostEstimate(
            flops=total * total * 128, bytes_accessed=total * 2048, transcendentals=total * total // 2
        ),
        name="attend",
    )(order, ends, info, swapped, bias_rows)


def unroll_rows(tile):
    row = lax.broadcasted_iota(jnp.int32, tile.shape, 0)
    bit = 1
    while bit < tile.shape[0]:
        moved = pltpu.roll(tile, tile.shape[1] - bit, 1)
        tile = jnp.where((row // bit) % 2 == 1, moved, tile)
        bit *= 2
    return tile


def attend_back_kernel(
    slots, bucket_count, order_ref, ends_ref, info_ref, x_ref, mixed_ref, exact_ref, lse_ref,
    bias_ref, bucket_ref, grad_ref,
    both_ref, query_ref, back_ref, turned_ref, table_ref, corner_ref, d_block_ref, d_corner_ref,
    d_both_ref, d_query_ref, far_ref,
):
    total = both_ref.shape[0]
    sources = x_ref.shape[0]
    half = slots // 2
    low = lane_low((SPAN, LANES))

    def keep(place, both, query):
        both_ref[dyn(place, SPAN, SPAN), :] = both
        query_ref[dyn(place, SPAN, SPAN), :] = query
        turned = both.astype(f32).T
        turned_ref[:HD, dyn(place, SPAN, SPAN)] = turned[HD:, :].astype(bf16)

    sort_blocks(order_ref, info_ref, x_ref, slots, keep)
    low_half = lane_low((SPAN // 2, LANES))
    for block in range(mixed_ref.shape[0]):
        packed = mixed_ref[block].astype(f32)
        for part, tile in enumerate((packed, swap_halves(packed))):
            start = order_ref[block] * SPAN + part * (SPAN // 2)
            back_ref[dyn(start, SPAN // 2, SPAN // 2), :] = jnp.where(low_half, tile, 0.0).astype(bf16)
    fill_tables(bias_ref, table_ref, corner_ref)
    tail = lax.broadcasted_iota(jnp.int32, (KT_ROWS - HD, total), 0)
    turned_ref[HD:, :] = jnp.where(tail == 0, 1.0, 0.0).astype(bf16)
    d_block_ref[...] = jnp.zeros_like(d_block_ref)
    d_corner_ref[...] = jnp.zeros_like(d_corner_ref)
    d_both_ref[...] = jnp.zeros_like(d_both_ref)
    far_ref[...] = jnp.zeros_like(far_ref)
    if info_ref.shape[0] > 3:
        d_query_ref[...] = jnp.zeros_like(d_query_ref)
    left_bias = bias_ref[NEAR : NEAR + 1, 0:1]
    right_bias = bias_ref[NEAR + 1 : NEAR + 2, 0:1]

    def one_block(block, unused):
        q0 = block * BQ
        first, last, whole = block_range(ends_ref, q0, total)
        query = query_ref[dyn(q0, BQ, BQ), :]
        back = back_ref[dyn(q0, BQ, BQ), :]
        lse = lse_ref[:, dyn(q0, BQ, BQ)]
        turned_back = back.astype(f32).T[:HD, :]
        delta = jnp.sum(turned_back * exact_ref[:, dyn(q0, BQ, BQ)], axis=0, keepdims=True)

        def step(kind, tile, d_turned):
            k0 = tile * BK
            keys = dyn(k0, BK, BK)
            both = both_ref[keys, :]
            scores = dot_nt(both, query)
            if kind == "diagonal":
                weights = jnp.exp(scores + table_ref[...] - lse)
            elif kind == "cut":
                bias = any_bias(bias_ref, table_ref, corner_ref, tile, block)
                weights = jnp.exp(jnp.where(same_sequence(ends_ref, k0, q0), scores + bias - lse, masked_score))
            else:
                if kind in ("prev", "next"):
                    scores = with_corner(scores, kind, corner_ref[0 if kind == "prev" else 1])
                weights = jnp.exp(scores - (lse - (left_bias if kind in ("left", "prev") else right_bias)))
            d_probs = dot_nt(both, back)
            d_scores = (weights * (d_probs - delta)).astype(bf16)
            if kind == "diagonal":
                add_blocks(d_scores.astype(f32))
            elif kind in ("prev", "next"):
                m = 0 if kind == "prev" else 1
                d_corner_ref[m] = d_corner_ref[m] + corner_of(d_scores, kind).astype(f32)
            elif kind == "cut":
                wide = d_scores.astype(f32)
                sums = jnp.sum(wide, axis=0, keepdims=True)

                @pl.when(tile == block)
                def _():
                    add_blocks(wide)

                for m, (there, corner) in enumerate(
                    ((tile < block, tile + 1 == block), (tile > block, tile == block + 1))
                ):
                    far_ref[m : m + 1, :] = far_ref[m : m + 1, :] + jnp.where(there, sums, 0.0)
                    piece = corner_of(wide, ("prev", "next")[m])
                    d_corner_ref[m] = d_corner_ref[m] + jnp.where(corner, piece, 0.0)
            d_both_ref[keys, :] = (
                d_both_ref[keys, :] + dot_nn(weights.astype(bf16), back) + dot_nn(d_scores, query)
            )
            return d_turned + dot_nn(turned_ref[:, keys], d_scores)

        def add_blocks(wide):
            sums = [None] * (NEAR + 2)
            for a in range(BK // SPAN):
                for b in range(BQ // SPAN):
                    piece = wide[a * SPAN : (a + 1) * SPAN, b * SPAN : (b + 1) * SPAN]
                    at = block_step(a, b)
                    sums[at] = piece if sums[at] is None else sums[at] + piece
            for at, item in enumerate(sums):
                d_block_ref[at] = d_block_ref[at] + item

        def finish(d_turned):
            top = d_turned[:HD, :]
            d_query_ref[dyn(q0, BQ, BQ), :] = jnp.concatenate([top, top], axis=0).T.astype(bf16)

        zero = jnp.zeros((KT_ROWS, BQ), f32)

        @pl.when(whole)
        def _():
            parts = row_of_tiles(first, last, block, step, zero, zero, zero)
            for m in range(2):
                far_ref[m : m + 1, :] = far_ref[m : m + 1, :] + parts[2 * m][HD : HD + 1, :]
            finish(parts[0] + parts[1] + parts[2])

        @pl.when(jnp.logical_not(whole))
        def _():
            finish(lax.fori_loop(first, last, functools.partial(step, "cut"), zero))

        return unused

    lax.fori_loop(info_ref[1], info_ref[2], one_block, 0)

    d_blocks = [d_block_ref[0] + d_corner_ref[0], d_block_ref[1], d_block_ref[2] + d_corner_ref[1]]
    blank = jnp.zeros((SPAN, WIDE - SPAN), f32)
    sums = [
        jnp.sum(unroll_rows(jnp.concatenate([tile, blank], axis=1)), axis=0, keepdims=True)
        for tile in d_blocks
    ]
    for m in range(2):
        line = jnp.sum(d_block_ref[NEAR + m] - d_corner_ref[m], axis=0, keepdims=True)
        for b in range(BQ // SPAN):
            line = line + far_ref[m : m + 1, b * SPAN : (b + 1) * SPAN]
        sums.append(jnp.concatenate([line, blank[:1]], axis=1))
    sums = jnp.concatenate(sums, axis=0)
    buckets = bucket_ref[: NEAR + 2, :]
    by_bucket = jnp.concatenate(
        [
            jnp.sum(jnp.where(buckets == bucket, sums, 0.0), axis=0, keepdims=True)
            for bucket in range(bucket_count)
        ],
        axis=0,
    )
    totals = jnp.broadcast_to(jnp.sum(by_bucket, axis=1, keepdims=True), (bucket_count, LANES))
    upper = totals.astype(bf16).astype(f32)
    rest = totals - upper
    per_source = bucket_count // sources
    spare = jnp.zeros((EXTRA // 2 - per_source, LANES), f32)
    for source in range(sources):
        span = slice(source * per_source, (source + 1) * per_source)
        grad_ref[source, 3 * half * SPAN :, :] = jnp.concatenate(
            [upper[span], spare, rest[span], spare], axis=0
        ).astype(bf16)

    for source in range(sources):
        for pair in range(half):
            tiles = []
            for member in range(2):
                slot = pair + member * half
                place = place_of(order_ref, info_ref, source, slot, slots) * SPAN
                grad_ref[source, slot * SPAN : (slot + 1) * SPAN, :] = d_both_ref[
                    dyn(place, SPAN, SPAN), :
                ].astype(bf16)
                tiles.append(d_query_ref[dyn(place, SPAN, SPAN), :].astype(f32))
            grad_ref[source, (slots + pair) * SPAN : (slots + pair + 1) * SPAN, :] = jnp.where(
                low, tiles[0], tiles[1]
            ).astype(bf16)


def attend_back(
    order, ends, info, swapped, mixed_grad, exact, lse, bias_rows, bucket_rows, slots, bucket_count
):
    sources = swapped.shape[0]
    total = sources * slots * SPAN
    return pl.pallas_call(
        functools.partial(attend_back_kernel, slots, bucket_count),
        in_specs=[smem_spec()] * 3 + [vmem_spec()] * 6,
        out_specs=vmem_spec(),
        out_shape=jax.ShapeDtypeStruct((sources, slots * SPAN * 3 // 2 + EXTRA, LANES), bf16),
        scratch_shapes=[
            vmem((total, LANES), bf16),
            vmem((total, LANES), bf16),
            vmem((total, LANES), bf16),
            vmem((KT_ROWS, total), bf16),
            vmem((BK, BQ), f32),
            vmem((2, SPAN, SPAN), f32),
            vmem((NEAR + 2, SPAN, SPAN), f32),
            vmem((2, SPAN, SPAN), f32),
            vmem((total, LANES), f32),
            vmem((total, LANES), bf16),
            vmem((8, BQ), f32),
        ],
        compiler_params=pltpu.CompilerParams(vmem_limit_bytes=attention_vmem(total)),
        cost_estimate=pl.CostEstimate(
            flops=total * total * 320, bytes_accessed=total * 3072, transcendentals=total * total // 2
        ),
        name="attend_back",
    )(order, ends, info, swapped, mixed_grad, exact, lse, bias_rows, bucket_rows)


def out_kernel(slots, packed_ref, weight_ref, mix_ref, *part_refs):
    heads = packed_ref.shape[0]
    half = slots * SPAN // 2

    @pl.when(pl.program_id(0) == 0)
    def _():
        for pair in range(heads // 2):
            first = packed_ref[2 * pair].astype(f32)
            second = packed_ref[2 * pair + 1].astype(f32)
            top, bottom = pair_up(first, second)
            cols = slice(pair * LANES, (pair + 1) * LANES)
            mix_ref[:half, cols] = top.astype(bf16)
            mix_ref[half:, cols] = bottom.astype(bf16)

    part = dot_nn(mix_ref[...], weight_ref[...]).astype(bf16)
    for s in range(slots):
        part_refs[s][...] = part[s * SPAN : (s + 1) * SPAN]


def out_project(packed, weight, slots):
    heads = packed.shape[0]
    rows, width, depth = slots * SPAN, heads * HD, weight.shape[1]
    tile = 512
    return pl.pallas_call(
        functools.partial(out_kernel, slots),
        grid=(depth // tile,),
        in_specs=[
            pl.BlockSpec(packed.shape, lambda j: (0, 0, 0)),
            pl.BlockSpec((width, tile), lambda j: (0, j)),
        ],
        out_specs=[
            pl.BlockSpec((rows, width), lambda j: (0, 0)),
        ]
        + [pl.BlockSpec((SPAN, tile), lambda j: (0, j))] * slots,
        out_shape=[jax.ShapeDtypeStruct((rows, width), bf16)]
        + [jax.ShapeDtypeStruct((SPAN, depth), bf16)] * slots,
        compiler_params=pltpu.CompilerParams(vmem_limit_bytes=40 * MIB),
        cost_estimate=pl.CostEstimate(
            flops=2 * rows * depth * width, bytes_accessed=4 * depth * width, transcendentals=0
        ),
        name="out_project",
    )(packed, weight)


def feed_kernel(slots, *refs):
    normed_refs, grad_refs = refs[:slots], refs[slots : 2 * slots]
    gate_ref, up_ref, down_ref, active_ref, d_both_ref, rows_ref, rows_grad_ref = refs[2 * slots :]

    @pl.when(pl.program_id(0) == 0)
    def _():
        for s in range(slots):
            rows_ref[s * SPAN : (s + 1) * SPAN, :] = normed_refs[s][...]
            rows_grad_ref[s * SPAN : (s + 1) * SPAN, :] = grad_refs[s][...]

    tile = down_ref.shape[1]
    width = d_both_ref.shape[1] // 2
    gate = dot_nn(rows_ref[...], gate_ref[...])
    up = dot_nn(rows_ref[...], up_ref[...])
    d_hidden = dot_nn(rows_grad_ref[...], down_ref[...])
    scale, cubic = 0.7978845608028654, 0.044715
    square = gate * gate
    bent = jnp.tanh(scale * (gate + cubic * square * gate))
    half = 0.5 * (1.0 + bent)
    gelu = gate * half
    slope = half + 0.5 * gate * (1.0 - bent * bent) * (scale * (1.0 + 3.0 * cubic * square))
    active_ref[...] = (gelu * up).astype(bf16)
    start = pl.program_id(0) * tile
    d_both_ref[:, dyn(start, tile, tile)] = (d_hidden * up * slope).astype(bf16)
    d_both_ref[:, dyn(width + start, tile, LANES)] = (d_hidden * gelu).astype(bf16)


def feed_tile(width):
    return 256 if width % 256 == 0 else 128


def feed(normed_slots, grad_slots, weights):
    slots = len(normed_slots)
    rows, depth, width = slots * SPAN, weights.shape[0], weights.shape[1] // 3
    tile = feed_tile(width)
    steps = width // tile
    whole = pl.BlockSpec((SPAN, depth), lambda j: (0, 0))

    def columns(part):
        return pl.BlockSpec((depth, tile), lambda j: (0, part * steps + j))

    return pl.pallas_call(
        functools.partial(feed_kernel, slots),
        grid=(steps,),
        in_specs=[whole] * (2 * slots) + [columns(0), columns(1), columns(2)],
        out_specs=[
            pl.BlockSpec((rows, tile), lambda j: (0, j)),
            pl.BlockSpec((rows, 2 * width), lambda j: (0, 0)),
        ],
        out_shape=[
            jax.ShapeDtypeStruct((rows, width), bf16),
            jax.ShapeDtypeStruct((rows, 2 * width), bf16),
        ],
        scratch_shapes=[vmem((rows, depth), bf16), vmem((rows, depth), bf16)],
        compiler_params=pltpu.CompilerParams(vmem_limit_bytes=56 * MIB),
        cost_estimate=pl.CostEstimate(
            flops=6 * rows * depth * width,
            bytes_accessed=6 * depth * width,
            transcendentals=rows * width,
        ),
        name="feed",
    )(*normed_slots, *grad_slots, weights, weights, weights)


def pack_kernel(slots, shares, spot_ref, mine_ref, rest_ref, packed_ref):
    width = mine_ref.shape[1]
    half = SPAN // 2
    for s in range(slots):
        there = lax.rem(spot_ref[0] - s + slots, slots)
        for pair in range(width // LANES):
            if s == 0:
                tile = mine_ref[:, pair * LANES : (pair + 1) * LANES].astype(f32)
            else:
                start = (s - 1) * width + pair * LANES
                tile = rest_ref[:, start : start + LANES].astype(f32)
            for member, piece in enumerate(pair_up(tile[:half], tile[half:])):
                for share in range(shares):
                    packed_ref[(2 * pair + member) * shares + share, there] = piece.astype(bf16)


def pack(spot, mine, rest, shares):
    width = mine.shape[1]
    slots = 1 + rest.shape[1] // width
    return pl.pallas_call(
        functools.partial(pack_kernel, slots, shares),
        in_specs=[smem_spec(), vmem_spec(), vmem_spec()],
        out_specs=vmem_spec(),
        out_shape=jax.ShapeDtypeStruct((width // HD * shares, slots, SPAN // 2, LANES), bf16),
        compiler_params=pltpu.CompilerParams(vmem_limit_bytes=16 * MIB),
        name="pack",
    )(spot, mine, rest)


def weigh_kernel(slots, packed_ref, mix_ref, left_ref, *refs):
    attn_refs = refs[:slots]
    product_ref, grads_ref = refs[slots:]
    heads = packed_ref.shape[0]
    rows = slots * SPAN
    half = rows // 2
    width = heads * HD

    @pl.when(pl.program_id(0) == 0)
    def _():
        for pair in range(heads // 2):
            start = pair * LANES
            tiles = [packed_ref[2 * pair + m].astype(f32) for m in range(2)]
            value, key = pair_up(tiles[0][:rows], tiles[1][:rows])
            top, bottom = pair_up(tiles[0][rows : rows + half], tiles[1][rows : rows + half])
            grads_ref[:half, start : start + LANES] = top.astype(bf16)
            grads_ref[half:, start : start + LANES] = bottom.astype(bf16)
            grads_ref[:, width + start : width + start + LANES] = key.astype(bf16)
            grads_ref[:, 2 * width + start : 2 * width + start + LANES] = value.astype(bf16)

    product_ref[:, : 3 * width] = dot_tn(left_ref[...], grads_ref[...]).astype(bf16)
    attn = jnp.concatenate([ref[...] for ref in attn_refs], axis=0)
    product_ref[:, 3 * width :] = dot_tn(attn, mix_ref[...]).astype(bf16)


def weigh(packed, mix, left, attn_slots):
    slots = len(attn_slots)
    heads = packed.shape[0]
    rows, depth = left.shape
    width = 3 * heads * HD
    total = width + mix.shape[1]
    tile = 512
    return pl.pallas_call(
        functools.partial(weigh_kernel, slots),
        grid=(depth // tile,),
        in_specs=[
            pl.BlockSpec(packed.shape, lambda j: (0, 0, 0)),
            pl.BlockSpec(mix.shape, lambda j: (0, 0)),
            pl.BlockSpec((rows, tile), lambda j: (0, j)),
        ]
        + [pl.BlockSpec((SPAN, tile), lambda j: (0, j))] * slots,
        out_specs=[
            pl.BlockSpec((tile, total), lambda j: (j, 0)),
            pl.BlockSpec((rows, width), lambda j: (0, 0)),
        ],
        out_shape=[
            jax.ShapeDtypeStruct((depth, total), bf16),
            jax.ShapeDtypeStruct((rows, width), bf16),
        ],
        compiler_params=pltpu.CompilerParams(vmem_limit_bytes=LARGE),
        cost_estimate=pl.CostEstimate(
            flops=2 * rows * depth * total, bytes_accessed=4 * depth * total, transcendentals=0
        ),
        name="weigh",
    )(packed, mix, left, *attn_slots)


def project_back_kernel(which, grads_ref, weight_ref, scale_ref, *refs):
    x_refs = refs[: len(which)]
    gain_ref, *part_refs = refs[len(which) :]
    part = dot_nt(grads_ref[...], weight_ref[...])
    gain = jnp.zeros((1, part.shape[1]), f32)
    for s, x_ref, part_ref in zip(which, x_refs, part_refs, strict=True):
        start = s * SPAN if len(which) > 1 else 0
        piece = part[start : start + SPAN]
        part_ref[...] = piece.astype(bf16)
        x_hat = x_ref[...].astype(f32) * scale_ref[start : start + SPAN, :1]
        gain = gain + jnp.sum(piece * x_hat, axis=0, keepdims=True)
    gain_ref[...] = gain


def project_back(grads, weights, scale, x_slots, which):
    depth, width = weights.shape
    single = len(which) == 1
    rows, at = (SPAN, which[0]) if single else (grads.shape[0], 0)
    tile = 512
    spans = [pl.BlockSpec((SPAN, tile), lambda j: (0, j))] * len(which)
    return pl.pallas_call(
        functools.partial(project_back_kernel, which),
        grid=(depth // tile,),
        in_specs=[
            pl.BlockSpec((rows, width), lambda j: (at, 0)),
            pl.BlockSpec((tile, width), lambda j: (j, 0)),
            pl.BlockSpec((rows, LANES), lambda j: (at, 0)),
        ]
        + spans,
        out_specs=[pl.BlockSpec((1, tile), lambda j: (0, j))] + spans,
        out_shape=[jax.ShapeDtypeStruct((1, depth), f32)]
        + [jax.ShapeDtypeStruct((SPAN, depth), bf16)] * len(which),
        compiler_params=pltpu.CompilerParams(vmem_limit_bytes=LARGE),
        cost_estimate=pl.CostEstimate(
            flops=2 * rows * depth * width, bytes_accessed=4 * depth * width, transcendentals=0
        ),
        name="project_back",
    )(grads, weights, scale, *[x_slots[s] for s in which])


def spread_kernel(shard_ref, query_ref, key_ref, value_ref, out_ref):
    width = query_ref.shape[1]
    for at, ref in enumerate((query_ref, key_ref, value_ref)):
        ref[...] = shard_ref[:, at * width : (at + 1) * width].astype(f32)
    out_ref[...] = shard_ref[:, 3 * width :].astype(f32).T


def spread(shard, width):
    rows = shard.shape[0]
    return pl.pallas_call(
        spread_kernel,
        in_specs=[vmem_spec()],
        out_specs=[vmem_spec()] * 4,
        out_shape=[jax.ShapeDtypeStruct((rows, width), f32)] * 3
        + [jax.ShapeDtypeStruct((width, rows), f32)],
        compiler_params=pltpu.CompilerParams(vmem_limit_bytes=16 * MIB),
        name="spread",
    )(shard)


def pair_kernel(slots, groups, *refs):
    left_one, left_two = refs[:slots], refs[slots : 2 * slots]
    right_one = refs[2 * slots : 2 * slots + groups]
    right_two = refs[2 * slots + groups : 2 * slots + 2 * groups]
    out_ref, right_ref = refs[-2:]
    cut = right_one[0].shape[1]

    @pl.when(pl.program_id(0) == 0)
    def _():
        start = 0
        for one, two in zip(right_one, right_two, strict=True):
            span = slice(start, start + one.shape[0])
            right_ref[span, :cut] = one[...]
            right_ref[span, cut:] = two[...]
            start += one.shape[0]

    one = jnp.concatenate([ref[...] for ref in left_one], axis=0)
    two = jnp.concatenate([ref[...] for ref in left_two], axis=0)
    out_ref[:, :cut] = dot_tn(one, right_ref[:, :cut]).astype(bf16)
    out_ref[:, cut:] = dot_tn(two, right_ref[:, cut:]).astype(bf16)


def pair_product(left_one, right_one, left_two, right_two):
    slots, groups = len(left_one), len(right_one)
    rows, depth = slots * SPAN, left_one[0].shape[1]
    width = right_one[0].shape[1] + right_two[0].shape[1]
    block = 512

    def whole(array):
        return pl.BlockSpec(array.shape, lambda j: (0, 0))

    return pl.pallas_call(
        functools.partial(pair_kernel, slots, groups),
        grid=(depth // block,),
        in_specs=[pl.BlockSpec((SPAN, block), lambda j: (0, j))] * (2 * slots)
        + [whole(piece) for piece in (*right_one, *right_two)],
        out_specs=pl.BlockSpec((block, width), lambda j: (j, 0)),
        out_shape=jax.ShapeDtypeStruct((depth, width), bf16),
        scratch_shapes=[vmem((rows, width), bf16)],
        compiler_params=pltpu.CompilerParams(vmem_limit_bytes=32 * MIB),
        cost_estimate=pl.CostEstimate(
            flops=2 * rows * depth * width, bytes_accessed=2 * depth * width, transcendentals=0
        ),
        name="pair_product",
    )(*left_one, *left_two, *right_one, *right_two)


def bucket_lines(bucket_of):
    count = bucket_of.shape[0]
    turned = bucket_of[::-1]
    ends = [jnp.broadcast_to(end, (2 * SPAN,)) for end in (turned[:1], turned[-1:])]
    padded = jnp.concatenate([ends[0], turned, ends[1]])
    zero_at = 2 * SPAN + count // 2
    rows = []
    for c in range(NEAR):
        base = zero_at - (c - 1) * SPAN
        rows.append(jnp.concatenate([padded[base : base + SPAN], padded[base - SPAN : base]]))
    rows.append(jnp.broadcast_to(bucket_of[:1], (WIDE,)))
    rows.append(jnp.broadcast_to(bucket_of[-1:], (WIDE,)))
    spare = 8 - (NEAR + 2)
    return jnp.concatenate([jnp.stack(rows), jnp.full((spare, WIDE), -1, bucket_of.dtype)])


def on_device(
    tokens,
    lengths,
    block_order,
    bucket_of,
    gain_attn,
    w_query,
    w_key,
    w_value,
    w_out,
    bias_table,
    gain_ffn,
    w_gate,
    w_up,
    w_down,
    cotangent,
):
    blk_count, slots = lax.axis_size("blk"), lax.axis_size("head")
    blk_spot, head_spot = lax.axis_index("blk"), lax.axis_index("head")
    depth = tokens.shape[1]
    width = w_query.shape[1]
    heads = width // HD
    shares = blk_count // heads
    table_rows, table_heads = bias_table.shape
    bucket_count = table_rows * blk_count
    total = blk_count * slots * SPAN
    gain_size = gain_attn.shape[0]
    hidden = w_gate.shape[1]

    token_slots = gather_far(gather_near(tokens))
    small = gather_small(
        jnp.concatenate([gain_attn, gain_ffn, bias_table.astype(f32).reshape(-1)])
    )
    full_qkv = lax.all_gather(
        jnp.concatenate([w_query, w_key, w_value], axis=1), "blk", axis=0, tiled=True
    )
    full_out = lax.all_gather(w_out, "blk", axis=1, tiled=True)
    full_ffn = lax.all_gather(
        jnp.concatenate([w_gate, w_up, w_down.T], axis=1), "blk", axis=0, tiled=True
    )
    gain_one = small[:, :, :gain_size].reshape(1, depth)
    gain_two = small[:, :, gain_size : 2 * gain_size].reshape(1, depth)

    tables = lax.dynamic_index_in_dim(small, head_spot, 1, False)[:, 2 * gain_size :]
    tables = tables.reshape(bucket_count, table_heads)
    my_head = blk_spot // shares
    my_bias = lax.dynamic_index_in_dim(tables, my_head, 1, False)
    bucket_rows = bucket_lines(bucket_of)
    bias_rows = jnp.sum(
        jnp.where(
            bucket_rows[None] == jnp.arange(bucket_count, dtype=jnp.int32)[:, None, None],
            my_bias[:, None, None],
            0.0,
        ),
        axis=0,
    )
    ends = jnp.cumsum(lengths).astype(jnp.int32)
    per_share = total // BQ // shares
    start = (blk_spot % shares) * per_share
    info = [head_spot, start, start + per_share] + ([start] if shares > 1 else [])
    info = jnp.stack([jnp.asarray(item, jnp.int32) for item in info])

    def swap(values):
        return lax.all_to_all(values, "blk", 0, 0, tiled=True)

    def to_all(values):
        values = values.reshape((blk_count * slots,) + values.shape[2:])
        return lax.all_to_all(values, ("blk", "head"), 0, 0, tiled=True)

    def to_heads(values):
        return swap(values if shares == 1 else jnp.repeat(values, shares, axis=0))

    def to_rows(values):
        values = swap(values)
        if shares == 1:
            return values
        values = values.reshape((heads, shares) + values.shape[1:])
        return jnp.sum(values.astype(f32), axis=1).astype(bf16)

    w_out, cotangent, *token_slots = together(w_out, cotangent, *token_slots)
    normed_one, packed, scale_one = project(token_slots, gain_one, full_qkv)
    early = (ends, info, bias_rows, bucket_rows)
    swapped, ends, info, bias_rows, bucket_rows, *out_near = together(
        to_heads(packed), *early, *gather_near(w_out)
    )
    grad_near, out_slots = gather_near(cotangent), gather_far(out_near)
    mixed, exact, lse = attend(block_order, ends, info, swapped, bias_rows, slots)
    mixed, *moved = together(mixed, *grad_near, *out_slots)
    grad_near, out_slots = moved[: len(grad_near)], moved[len(grad_near) :]
    packed_mix, *grad_slots = together(to_rows(mixed), *gather_far(grad_near))
    attn_mix, *out_parts = out_project(packed_mix, full_out, slots)
    tokens_wide = tokens.astype(f32)
    hidden_one = tokens_wide + sum_terms(sum_near(out_parts, sum_far(out_parts))[0])
    rstd_two = rms_scale(hidden_one)
    normed_two = (hidden_one * rstd_two * gain_two).astype(bf16)

    normed_two, out_slots = together(normed_two, out_slots)
    full_rest = lax.all_gather(jnp.concatenate(out_slots[1:]), "blk", axis=1, tiled=True)
    normed_slots = gather_far(gather_near(normed_two))
    active, d_both = feed(normed_slots, grad_slots, full_ffn)

    def spans(rows):
        return [rows[s * SPAN : (s + 1) * SPAN] for s in range(rows.shape[0] // SPAN)]

    d_parts = spans(dot_nt(d_both, full_ffn[:, : 2 * hidden]).astype(bf16))
    d_far = sum_far(d_parts)
    grad_hidden, *d_far = together(
        pair_product(normed_slots, [d_both], grad_slots, [active]), *d_far
    )
    grad_hidden = lax.psum_scatter(grad_hidden, "blk", scatter_dimension=0, tiled=True)
    d_near, (active,) = sum_near(d_parts, d_far, (active,))
    down_rows = dot_nt(active, full_ffn[:, 2 * hidden :]).astype(bf16)
    down_rows, full_rest, *d_near = together(down_rows, full_rest, *d_near)
    down_parts = spans(down_rows)
    d_normed_two = sum_terms(d_near)
    d_source_two, gain_part_two = norm_back(d_normed_two, hidden_one, rstd_two, gain_two)
    d_hidden_one = cotangent.astype(f32) + d_source_two

    d_attn = d_hidden_one.astype(bf16)
    mix_grads = pack(
        jnp.reshape(head_spot, (1,)).astype(jnp.int32),
        dot_nt(d_attn, full_out).astype(bf16),
        dot_nt(d_attn, full_rest).astype(bf16),
        shares,
    )
    mix_grads, d_attn = together(mix_grads, d_attn)
    middle = slots // 2
    steps = [t for t in range(1, slots) if t != middle]
    upper, lower = (down_parts[middle][h * SPAN // 2 : (h + 1) * SPAN // 2] for h in range(2))
    moved = (*gather_near(d_attn), *sum_direct(down_parts, steps))
    grads = attend_back(
        block_order, ends, info, swapped, to_all(mix_grads), exact, lse, bias_rows, bucket_rows,
        slots, bucket_count,
    )
    grads, upper, *moved = together(grads, upper, *moved)
    attn_near, down_terms = moved[: 2 - slots], moved[2 - slots :]
    grads, *attn_slots = together(swap(grads), *gather_far(attn_near))
    extra = grads[:, -EXTRA:, 0].astype(f32).reshape(blk_count, 2, -1).sum(axis=1)
    grad_table = extra[:, :table_rows].reshape(heads, shares, table_rows).sum(axis=1).T
    if shares > 1:
        grads = grads.reshape((heads, shares) + grads.shape[1:])
        grads = jnp.sum(grads.astype(f32), axis=1).astype(bf16)
    grad_heads, d_qkv = weigh(grads, attn_mix, normed_one, attn_slots)
    grad_heads, grad_hidden, upper = together(grad_heads, grad_hidden, send_back(upper, middle))
    if slots == 4:
        gain_part_one, far_part = project_back(d_qkv, full_qkv, scale_one, token_slots, [2])
        one_far = sum_far([None, None, far_part, None])
        d_qkv, far_part = together(d_qkv, far_part)
        gain_rest, *one_parts = project_back(d_qkv, full_qkv, scale_one, token_slots, [0, 1, 3])
        gain_part_one = gain_part_one + gain_rest
        one_parts.insert(2, far_part)
    else:
        gain_part_one, *one_parts = project_back(
            d_qkv, full_qkv, scale_one, token_slots, list(range(slots))
        )
        one_far = []

    gain_parts = jnp.stack(
        [part.reshape(blk_count, slots, gain_size) for part in (gain_part_one, gain_part_two)],
        axis=2,
    )
    gain_parts, *one_far = together(gain_parts, *one_far)
    grad_heads = lax.psum_scatter(grad_heads, "blk", scatter_dimension=0, tiled=True)
    one_near, unused = sum_near(one_parts, one_far)
    gain_sums = scatter_blk(gain_parts)
    gain_sums, lower, grad_hidden, *one_near = together(
        gain_sums, lower, grad_hidden, *one_near
    )
    far_term = [jnp.concatenate([upper, send_back(lower, middle)])]
    gain_sums = scatter_head(gain_sums)
    grad_hidden = grad_hidden.astype(f32)
    d_normed_one = sum_terms(one_near)
    d_source_one, unused = norm_back(d_normed_one, tokens_wide, rms_scale(tokens_wide), gain_one)
    input_grad = d_hidden_one + d_source_one
    input_grad, hidden_one = together(input_grad, hidden_one)
    output = hidden_one + sum_all([down_parts[0]] + down_terms + far_term)
    return (
        output,
        input_grad,
        gain_sums[0],
        *spread(grad_heads, width),
        grad_table,
        gain_sums[1],
        grad_hidden[:, :hidden],
        grad_hidden[:, hidden : 2 * hidden],
        grad_hidden[:, 2 * hidden :].T,
    )


def solution(mesh):
    rows, spread = P(("blk", "head"), None), P(("blk", "head"))
    inward, outward = P("blk", "head"), P("head", "blk")
    in_specs = (
        rows, P(), P(), P(), spread, inward, inward, inward, outward, inward, spread,
        inward, inward, outward, rows,
    )
    out_specs = (
        rows, rows, spread, inward, inward, inward, outward, inward, spread,
        inward, inward, outward,
    )
    return jax.shard_map(
        on_device, mesh=mesh, in_specs=in_specs, out_specs=out_specs, check_vma=False
    )
```

```python
import functools

import jax
import jax.numpy as jnp
from jax import lax
from jax.experimental import pallas as pl
from jax.experimental.pallas import tpu as pltpu
from jax.sharding import PartitionSpec as P

HD = 64
LANES = 2 * HD
MAXDIST = 128
SPAN = 128
BQ = 512
BK = BQ
NEAR = 3
WIDE = 2 * SPAN
EXTRA = 16
KT_ROWS = 80
SHIFT_ROOM = 60.0

norm_eps = 1e-06
masked_score = -1e30
f32 = jnp.float32
bf16 = jnp.bfloat16
MIB = 1 << 20
LARGE = 58 * MIB


def rms_scale(values):
    return lax.rsqrt(jnp.mean(values * values, axis=-1, keepdims=True) + norm_eps)


def norm_back(d_normed, source, inv_rms, gain_vec):
    scaled = d_normed * gain_vec
    x_hat = source * inv_rms
    gain_part = jnp.sum(d_normed * x_hat, axis=0)
    d_source = inv_rms * (scaled - x_hat * jnp.mean(scaled * x_hat, axis=-1, keepdims=True))
    return (d_source, gain_part)


def dot_nn(left, right):
    return jnp.dot(left, right, preferred_element_type=f32)


def dot_nt(left, right):
    return lax.dot_general(left, right, (((1,), (1,)), ((), ())), preferred_element_type=f32)


def dot_tn(left, right):
    return lax.dot_general(left, right, (((0,), (0,)), ((), ())), preferred_element_type=f32)


def cyclic(count, by):
    return [(i, (i + by) % count) for i in range(count)]


def together(*values):
    return lax.optimization_barrier(values)


def gather_near(rows):
    count = lax.axis_size("head")
    if count != 4:
        return [rows] + [lax.ppermute(rows, "head", cyclic(count, s)) for s in range(1, count)]
    return [rows, lax.ppermute(rows, "head", cyclic(4, 1)), lax.ppermute(rows, "head", cyclic(4, 3))]


def gather_far(near):
    if lax.axis_size("head") != 4:
        return near
    rows, back_one, ahead_one = near
    me = lax.axis_index("head")
    passed = jnp.where(me == 1, ahead_one, jnp.where(me == 2, back_one, rows))
    back_two = lax.ppermute(passed, "head", [(1, 0), (3, 1), (0, 2), (2, 3)])
    return [rows, back_one, back_two, ahead_one]


def gather_direct(rows):
    count = lax.axis_size("head")
    return [rows] + [lax.ppermute(rows, "head", cyclic(count, s)) for s in range(1, count)]


def sum_far(parts):
    count = lax.axis_size("head")
    if count != 4:
        return []
    return [lax.ppermute(parts[2], "head", [(0, 1), (1, 3), (2, 0), (3, 2)])]


def sum_near(parts, far, beside=()):
    count = lax.axis_size("head")
    if count != 4:
        return [parts[0]] + [
            lax.ppermute(parts[s], "head", cyclic(count, count - s)) for s in range(1, count)
        ], beside
    me = lax.axis_index("head")
    wide = far[0].astype(f32)
    to_back = jnp.where(me == 2, parts[1].astype(f32) + wide, parts[1].astype(f32)).astype(bf16)
    to_ahead = jnp.where(me == 1, parts[3].astype(f32) + wide, parts[3].astype(f32)).astype(bf16)
    to_back, to_ahead, *beside = together(to_back, to_ahead, *beside)
    from_ahead = lax.ppermute(to_back, "head", cyclic(4, 3))
    from_back = lax.ppermute(to_ahead, "head", cyclic(4, 1))
    return [parts[0], from_ahead, from_back, far[0]], beside


def sum_terms(terms):
    total = terms[0].astype(f32) + terms[1].astype(f32) + terms[2].astype(f32)
    if lax.axis_size("head") != 4:
        for term in terms[3:]:
            total = total + term.astype(f32)
        return total
    me = lax.axis_index("head")
    return total + jnp.where((me == 0) | (me == 3), terms[3].astype(f32), 0.0)


def is_power(count):
    return count & (count - 1) == 0


def gather_small(values):
    held = values[None]
    for axis in ("head", "blk"):
        count = lax.axis_size(axis)
        if not is_power(count):
            held = lax.all_gather(held, axis, axis=0, tiled=False)
        else:
            me = lax.axis_index(axis)
            held = held[None]
            bit = 1
            while bit < count:
                other = lax.ppermute(held, axis, [(i, i ^ bit) for i in range(count)])
                low = jnp.concatenate([held, other])
                high = jnp.concatenate([other, held])
                held = jnp.where((me // bit) % 2 == 0, low, high)
                bit *= 2
        if axis == "head":
            held = held.reshape(count, -1)
    return held


def send_back(rows, places):
    count = lax.axis_size("head")
    return lax.ppermute(rows, "head", cyclic(count, count - places))


def sum_direct(parts, steps):
    count = len(parts)
    return [lax.ppermute(parts[s], "head", cyclic(count, count - s)) for s in steps]


def sum_all(terms):
    total = terms[0].astype(f32)
    for term in terms[1:]:
        total = total + term.astype(f32)
    return total


def scatter_blk(values):
    return jnp.sum(lax.all_to_all(values, "blk", 0, 0, tiled=True), axis=0)


def scatter_head(values):
    count, me = lax.axis_size("head"), lax.axis_index("head")
    total = lax.dynamic_index_in_dim(values, me, 0, False)
    for s in range(1, count):
        sent = lax.dynamic_index_in_dim(values, (me + s) % count, 0, False)
        total = total + lax.ppermute(sent, "head", cyclic(count, s))
    return total


def lane_low(shape):
    return lax.broadcasted_iota(jnp.int32, shape, 1) < HD


def swap_halves(tile):
    return pltpu.roll(tile, HD, 1)


def pair_up(first, second):
    low = lane_low(first.shape)
    return (
        jnp.where(low, first, swap_halves(second)),
        jnp.where(low, swap_halves(first), second),
    )


def project_kernel(slots, *refs):
    x_refs = refs[:slots]
    gain_ref, wq_ref, wk_ref, wv_ref, normed_ref, packed_ref, scale_ref = refs[slots:]
    rows = slots * SPAN

    @pl.when(pl.program_id(0) == 0)
    def _():
        for s in range(slots):
            wide = x_refs[s][...].astype(f32)
            scale = rms_scale(wide)
            normed = wide * scale * gain_ref[...]
            normed_ref[s * SPAN : (s + 1) * SPAN, :] = normed.astype(bf16)
            scale_ref[s * SPAN : (s + 1) * SPAN, :] = jnp.broadcast_to(scale, (SPAN, LANES))

    normed = normed_ref[...]
    query = dot_nn(normed, wq_ref[...])
    key = dot_nn(normed, wk_ref[...])
    value = dot_nn(normed, wv_ref[...])
    half = rows // 2
    for pair in range(query.shape[1] // LANES):
        cols = slice(pair * LANES, (pair + 1) * LANES)
        both = pair_up(value[:, cols], key[:, cols])
        queries = pair_up(query[:half, cols], query[half:, cols])
        for member in range(2):
            packed_ref[2 * pair + member, :rows, :] = both[member].astype(bf16)
            packed_ref[2 * pair + member, rows:, :] = queries[member].astype(bf16)


def project(x_slots, gain, weights):
    slots = len(x_slots)
    rows, depth = slots * SPAN, x_slots[0].shape[1]
    width = weights.shape[1] // 3
    heads = width // HD
    tile = min(width, 256)
    steps = width // tile
    whole = pl.BlockSpec((SPAN, depth), lambda j: (0, 0))

    def columns(part):
        return pl.BlockSpec((depth, tile), lambda j: (0, part * steps + j))

    return pl.pallas_call(
        functools.partial(project_kernel, slots),
        grid=(steps,),
        in_specs=[whole] * slots
        + [pl.BlockSpec((1, depth), lambda j: (0, 0)), columns(0), columns(1), columns(2)],
        out_specs=[
            pl.BlockSpec((rows, depth), lambda j: (0, 0)),
            pl.BlockSpec((tile // HD, rows + rows // 2, LANES), lambda j: (j, 0, 0)),
            pl.BlockSpec((rows, LANES), lambda j: (0, 0)),
        ],
        out_shape=[
            jax.ShapeDtypeStruct((rows, depth), bf16),
            jax.ShapeDtypeStruct((heads, rows + rows // 2, LANES), bf16),
            jax.ShapeDtypeStruct((rows, LANES), f32),
        ],
        compiler_params=pltpu.CompilerParams(vmem_limit_bytes=40 * MIB),
        cost_estimate=pl.CostEstimate(
            flops=10 * rows * depth * width, bytes_accessed=6 * depth * width, transcendentals=0
        ),
        name="project",
    )(*x_slots, gain, weights, weights, weights)


def place_of(order_ref, info_ref, source, slot, slots):
    z = info_ref[0]
    return order_ref[source * slots + lax.rem(z - slot + slots, slots)]


def dyn(start, size, multiple):
    return pl.ds(pl.multiple_of(start, multiple), size)


def near_blocks(bias_ref):
    tiles = []
    for c in range(NEAR):
        spread = jnp.broadcast_to(bias_ref[c : c + 1, :], (SPAN, WIDE))
        tiles.append(pltpu.roll(spread, 0, 1, stride=1, stride_axis=0)[:, :SPAN])
    return tiles


def block_step(a, b):
    return a - b + 1 if abs(a - b) <= 1 else 3 if a < b else 4


def fill_tables(bias_ref, table_ref, corner_ref):
    tiles = near_blocks(bias_ref)
    far = [jnp.broadcast_to(bias_ref[NEAR + m : NEAR + m + 1, :SPAN], (SPAN, SPAN)) for m in range(2)]
    every = tiles + far
    for a in range(BK // SPAN):
        for b in range(BQ // SPAN):
            table_ref[a * SPAN : (a + 1) * SPAN, b * SPAN : (b + 1) * SPAN] = every[block_step(a, b)]
    corner_ref[0] = tiles[0] - far[0]
    corner_ref[1] = tiles[2] - far[1]


def with_corner(tile, kind, corner):
    if kind == "prev":
        upper, lower = tile[: BK - SPAN], tile[BK - SPAN :]
        lower = jnp.concatenate([lower[:, :SPAN] + corner, lower[:, SPAN:]], axis=1)
    else:
        upper, lower = tile[:SPAN], tile[SPAN:]
        upper = jnp.concatenate([upper[:, : BQ - SPAN], upper[:, BQ - SPAN :] + corner], axis=1)
    return jnp.concatenate([upper, lower], axis=0)


def corner_of(tile, kind):
    return tile[BK - SPAN :, :SPAN] if kind == "prev" else tile[:SPAN, BQ - SPAN :]


def any_bias(bias_ref, table_ref, corner_ref, tile, block):
    left = jnp.broadcast_to(bias_ref[NEAR : NEAR + 1, 0:1], (BK, BQ))
    right = jnp.broadcast_to(bias_ref[NEAR + 1 : NEAR + 2, 0:1], (BK, BQ))
    left = with_corner(left, "prev", jnp.where(tile + 1 == block, corner_ref[0], 0.0))
    right = with_corner(right, "next", jnp.where(tile == block + 1, corner_ref[1], 0.0))
    return jnp.where(tile == block, table_ref[...], jnp.where(tile < block, left, right))


def block_range(ends_ref, q0, total):
    count = ends_ref.shape[0]
    start, end, cut = jnp.int32(0), jnp.int32(total), jnp.bool_(False)
    for n in range(count):
        edge = ends_ref[n]
        start = jnp.where(edge <= q0, edge, start)
        cut = cut | ((edge > q0) & (edge < q0 + BQ))
    for n in range(count - 1, -1, -1):
        edge = ends_ref[n]
        end = jnp.where(edge >= q0 + BQ, edge, end)
    first = lax.div(start, BK)
    last = lax.div(end + BK - 1, BK)
    whole = jnp.logical_not(cut) & (lax.rem(start, BK) == 0) & (lax.rem(end, BK) == 0)
    return first, last, whole


def row_of_tiles(first, last, block, step, left, middle, right):
    before, after = jnp.maximum(block - 1, first), jnp.minimum(block + 2, last)
    left = lax.fori_loop(first, before, functools.partial(step, "left"), left)
    left = lax.fori_loop(before, block, functools.partial(step, "prev"), left)
    middle = step("diagonal", block, left if middle is None else middle)
    right = middle if right is None else right
    right = lax.fori_loop(block + 1, after, functools.partial(step, "next"), right)
    right = lax.fori_loop(after, last, functools.partial(step, "right"), right)
    return left, middle, right


def same_sequence(ends_ref, k0, q0):
    key_place = k0 + lax.broadcasted_iota(jnp.int32, (BK, 1), 0)
    query_place = q0 + lax.broadcasted_iota(jnp.int32, (1, BQ), 1)
    key_seg = jnp.zeros((BK, 1), jnp.int32)
    query_seg = jnp.zeros((1, BQ), jnp.int32)
    for n in range(ends_ref.shape[0]):
        key_seg = key_seg + jnp.where(key_place >= ends_ref[n], 1, 0)
        query_seg = query_seg + jnp.where(query_place >= ends_ref[n], 1, 0)
    return key_seg == query_seg


def sort_blocks(order_ref, info_ref, x_ref, slots, keep):
    sources = x_ref.shape[0]
    half = slots // 2
    high = jnp.logical_not(lane_low((SPAN, LANES)))
    for source in range(sources):
        for pair in range(half):
            packed = x_ref[
                source, (slots + pair) * SPAN : (slots + pair + 1) * SPAN, :
            ].astype(f32)
            queries = (swap_halves(packed), packed)
            for member in range(2):
                slot = pair + member * half
                place = place_of(order_ref, info_ref, source, slot, slots) * SPAN
                both = x_ref[source, slot * SPAN : (slot + 1) * SPAN, :]
                keep(place, both, jnp.where(high, queries[member], 0.0).astype(bf16))


def attend_kernel(
    slots, order_ref, ends_ref, info_ref, x_ref, bias_ref, mixed_ref, exact_ref, lse_ref,
    both_ref, query_ref, turned_ref, table_ref, corner_ref, held_ref, rows_ref,
):
    total = both_ref.shape[0]
    parted = info_ref.shape[0] > 3

    def keep(place, both, query):
        both_ref[dyn(place, SPAN, SPAN), :] = both
        query_ref[dyn(place, SPAN, SPAN), :] = query
        turned = both.astype(f32).T
        turned_ref[:, dyn(place, SPAN, SPAN)] = turned[:HD, :].astype(bf16)
        turned_key, turned_query = turned[HD:, :], query.astype(f32).T[HD:, :]
        for line, product in enumerate(
            (turned_key * turned_query, turned_key * turned_key, turned_query * turned_query)
        ):
            rows_ref[line : line + 1, dyn(place, SPAN, SPAN)] = jnp.sum(
                product, axis=0, keepdims=True
            )

    sort_blocks(order_ref, info_ref, x_ref, slots, keep)
    fill_tables(bias_ref, table_ref, corner_ref)
    if parted:
        held_ref[...] = jnp.zeros_like(held_ref)
        exact_ref[...] = jnp.zeros_like(exact_ref)
        lse_ref[...] = jnp.zeros_like(lse_ref)
    left_bias = bias_ref[NEAR : NEAR + 1, 0:1]
    right_bias = bias_ref[NEAR + 1 : NEAR + 2, 0:1]
    start_state = (
        jnp.full((1, BQ), masked_score, f32),
        jnp.zeros((1, BQ), f32),
        jnp.zeros((HD, BQ), f32),
    )
    longest_key = jnp.sqrt(jnp.max(rows_ref[1:2, :], axis=1, keepdims=True))
    most_bias = jnp.max(
        jnp.max(bias_ref[: NEAR + 2, :], axis=0, keepdims=True), axis=1, keepdims=True
    )

    def one_block(block, unused):
        q0 = block * BQ
        first, last, whole = block_range(ends_ref, q0, total)
        query = query_ref[dyn(q0, BQ, BQ), :]
        own = rows_ref[0:1, dyn(q0, BQ, BQ)] + bias_ref[1:2, 0:1]
        bound = jnp.sqrt(rows_ref[2:3, dyn(q0, BQ, BQ)]) * longest_key + most_bias
        whole = whole & (jnp.max(bound - own) < SHIFT_ROOM)

        def quick_step(kind, tile, state):
            mass, mix = state
            k0 = tile * BK
            scores = dot_nt(both_ref[dyn(k0, BK, BK), :], query)
            if kind == "diagonal":
                weights = jnp.exp(scores + table_ref[...] - own)
            else:
                if kind in ("prev", "next"):
                    scores = with_corner(scores, kind, corner_ref[0 if kind == "prev" else 1])
                weights = jnp.exp(scores - (own - (left_bias if kind in ("left", "prev") else right_bias)))
            mass = mass + jnp.sum(weights, axis=0, keepdims=True)
            return (mass, mix + dot_nn(turned_ref[:, dyn(k0, BK, BK)], weights.astype(bf16)))

        def step(tile, state):
            peak, mass, mix = state
            k0 = tile * BK
            scores = dot_nt(both_ref[dyn(k0, BK, BK), :], query)
            same = same_sequence(ends_ref, k0, q0)
            scores = scores + any_bias(bias_ref, table_ref, corner_ref, tile, block)
            scores = jnp.where(same, scores, masked_score)
            new_peak = jnp.maximum(peak, jnp.max(scores, axis=0, keepdims=True))
            weights = jnp.where(same, jnp.exp(scores - new_peak), 0.0)
            rescale = jnp.exp(peak - new_peak)
            mass = mass * rescale + jnp.sum(weights, axis=0, keepdims=True)
            turned = turned_ref[:, dyn(k0, BK, BK)]
            mix = mix * rescale + dot_nn(turned, weights.astype(bf16))
            return (new_peak, mass, mix)

        def finish(peak, mass, mix):
            exact = mix / mass
            exact_ref[:, dyn(q0, BQ, BQ)] = exact
            lse_ref[:, dyn(q0, BQ, BQ)] = peak + jnp.log(mass)
            padded = jnp.concatenate([exact, exact], axis=0)
            held_ref[dyn(q0, BQ, BQ), :] = padded.T

        @pl.when(whole)
        def _():
            *unused, state = row_of_tiles(
                first, last, block, quick_step, start_state[1:], None, None
            )
            finish(own, *state)

        @pl.when(jnp.logical_not(whole))
        def _():
            finish(*lax.fori_loop(first, last, step, start_state))

        return unused

    lax.fori_loop(info_ref[1], info_ref[2], one_block, 0)
    half = slots // 2
    low = lane_low((SPAN, LANES))
    for source in range(x_ref.shape[0]):
        for pair in range(half):
            places = [
                place_of(order_ref, info_ref, source, pair + m * half, slots) * SPAN
                for m in range(2)
            ]
            tiles = [held_ref[dyn(place, SPAN, SPAN), :] for place in places]
            mixed_ref[source, pair * SPAN : (pair + 1) * SPAN, :] = jnp.where(
                low, tiles[0], tiles[1]
            ).astype(bf16)


def vmem(shape, dtype):
    return pltpu.VMEM(shape, dtype)


def smem_spec():
    return pl.BlockSpec(memory_space=pltpu.SMEM)


def vmem_spec():
    return pl.BlockSpec(memory_space=pltpu.VMEM)


def attention_vmem(total):
    return int(min(58, 16 + 44 * (total / 16384)) * MIB)


def attend(order, ends, info, swapped, bias_rows, slots):
    sources = swapped.shape[0]
    total = sources * slots * SPAN
    return pl.pallas_call(
        functools.partial(attend_kernel, slots),
        in_specs=[smem_spec()] * 3 + [vmem_spec()] * 2,
        out_specs=[vmem_spec()] * 3,
        out_shape=[
            jax.ShapeDtypeStruct((sources, slots * SPAN // 2, LANES), bf16),
            jax.ShapeDtypeStruct((HD, total), f32),
            jax.ShapeDtypeStruct((1, total), f32),
        ],
        scratch_shapes=[
            vmem((total, LANES), bf16),
            vmem((total, LANES), bf16),
            vmem((HD, total), bf16),
            vmem((BK, BQ), f32),
            vmem((2, SPAN, SPAN), f32),
            vmem((total, LANES), f32),
            vmem((8, total), f32),
        ],
        compiler_params=pltpu.CompilerParams(vmem_limit_bytes=attention_vmem(total)),
        cost_estimate=pl.CostEstimate(
            flops=total * total * 128, bytes_accessed=total * 2048, transcendentals=total * total // 2
        ),
        name="attend",
    )(order, ends, info, swapped, bias_rows)


def unroll_rows(tile):
    row = lax.broadcasted_iota(jnp.int32, tile.shape, 0)
    bit = 1
    while bit < tile.shape[0]:
        moved = pltpu.roll(tile, tile.shape[1] - bit, 1)
        tile = jnp.where((row // bit) % 2 == 1, moved, tile)
        bit *= 2
    return tile


def attend_back_kernel(
    slots, bucket_count, order_ref, ends_ref, info_ref, x_ref, mixed_ref, exact_ref, lse_ref,
    bias_ref, bucket_ref, grad_ref,
    both_ref, query_ref, back_ref, turned_ref, table_ref, corner_ref, d_block_ref, d_corner_ref,
    d_both_ref, d_query_ref, far_ref,
):
    total = both_ref.shape[0]
    sources = x_ref.shape[0]
    half = slots // 2
    low = lane_low((SPAN, LANES))

    def keep(place, both, query):
        both_ref[dyn(place, SPAN, SPAN), :] = both
        query_ref[dyn(place, SPAN, SPAN), :] = query
        turned = both.astype(f32).T
        turned_ref[:HD, dyn(place, SPAN, SPAN)] = turned[HD:, :].astype(bf16)

    sort_blocks(order_ref, info_ref, x_ref, slots, keep)
    low_half = lane_low((SPAN // 2, LANES))
    for block in range(mixed_ref.shape[0]):
        packed = mixed_ref[block].astype(f32)
        for part, tile in enumerate((packed, swap_halves(packed))):
            start = order_ref[block] * SPAN + part * (SPAN // 2)
            back_ref[dyn(start, SPAN // 2, SPAN // 2), :] = jnp.where(low_half, tile, 0.0).astype(bf16)
    fill_tables(bias_ref, table_ref, corner_ref)
    tail = lax.broadcasted_iota(jnp.int32, (KT_ROWS - HD, total), 0)
    turned_ref[HD:, :] = jnp.where(tail == 0, 1.0, 0.0).astype(bf16)
    d_block_ref[...] = jnp.zeros_like(d_block_ref)
    d_corner_ref[...] = jnp.zeros_like(d_corner_ref)
    d_both_ref[...] = jnp.zeros_like(d_both_ref)
    far_ref[...] = jnp.zeros_like(far_ref)
    if info_ref.shape[0] > 3:
        d_query_ref[...] = jnp.zeros_like(d_query_ref)
    left_bias = bias_ref[NEAR : NEAR + 1, 0:1]
    right_bias = bias_ref[NEAR + 1 : NEAR + 2, 0:1]

    def one_block(block, unused):
        q0 = block * BQ
        first, last, whole = block_range(ends_ref, q0, total)
        query = query_ref[dyn(q0, BQ, BQ), :]
        back = back_ref[dyn(q0, BQ, BQ), :]
        lse = lse_ref[:, dyn(q0, BQ, BQ)]
        turned_back = back.astype(f32).T[:HD, :]
        delta = jnp.sum(turned_back * exact_ref[:, dyn(q0, BQ, BQ)], axis=0, keepdims=True)

        def step(kind, tile, d_turned):
            k0 = tile * BK
            keys = dyn(k0, BK, BK)
            both = both_ref[keys, :]
            scores = dot_nt(both, query)
            if kind == "diagonal":
                weights = jnp.exp(scores + table_ref[...] - lse)
            elif kind == "cut":
                bias = any_bias(bias_ref, table_ref, corner_ref, tile, block)
                weights = jnp.exp(jnp.where(same_sequence(ends_ref, k0, q0), scores + bias - lse, masked_score))
            else:
                if kind in ("prev", "next"):
                    scores = with_corner(scores, kind, corner_ref[0 if kind == "prev" else 1])
                weights = jnp.exp(scores - (lse - (left_bias if kind in ("left", "prev") else right_bias)))
            d_probs = dot_nt(both, back)
            d_scores = (weights * (d_probs - delta)).astype(bf16)
            if kind == "diagonal":
                add_blocks(d_scores.astype(f32))
            elif kind in ("prev", "next"):
                m = 0 if kind == "prev" else 1
                d_corner_ref[m] = d_corner_ref[m] + corner_of(d_scores, kind).astype(f32)
            elif kind == "cut":
                wide = d_scores.astype(f32)
                sums = jnp.sum(wide, axis=0, keepdims=True)

                @pl.when(tile == block)
                def _():
                    add_blocks(wide)

                for m, (there, corner) in enumerate(
                    ((tile < block, tile + 1 == block), (tile > block, tile == block + 1))
                ):
                    far_ref[m : m + 1, :] = far_ref[m : m + 1, :] + jnp.where(there, sums, 0.0)
                    piece = corner_of(wide, ("prev", "next")[m])
                    d_corner_ref[m] = d_corner_ref[m] + jnp.where(corner, piece, 0.0)
            d_both_ref[keys, :] = (
                d_both_ref[keys, :] + dot_nn(weights.astype(bf16), back) + dot_nn(d_scores, query)
            )
            return d_turned + dot_nn(turned_ref[:, keys], d_scores)

        def add_blocks(wide):
            sums = [None] * (NEAR + 2)
            for a in range(BK // SPAN):
                for b in range(BQ // SPAN):
                    piece = wide[a * SPAN : (a + 1) * SPAN, b * SPAN : (b + 1) * SPAN]
                    at = block_step(a, b)
                    sums[at] = piece if sums[at] is None else sums[at] + piece
            for at, item in enumerate(sums):
                d_block_ref[at] = d_block_ref[at] + item

        def finish(d_turned):
            top = d_turned[:HD, :]
            d_query_ref[dyn(q0, BQ, BQ), :] = jnp.concatenate([top, top], axis=0).T.astype(bf16)

        zero = jnp.zeros((KT_ROWS, BQ), f32)

        @pl.when(whole)
        def _():
            parts = row_of_tiles(first, last, block, step, zero, zero, zero)
            for m in range(2):
                far_ref[m : m + 1, :] = far_ref[m : m + 1, :] + parts[2 * m][HD : HD + 1, :]
            finish(parts[0] + parts[1] + parts[2])

        @pl.when(jnp.logical_not(whole))
        def _():
            finish(lax.fori_loop(first, last, functools.partial(step, "cut"), zero))

        return unused

    lax.fori_loop(info_ref[1], info_ref[2], one_block, 0)

    d_blocks = [d_block_ref[0] + d_corner_ref[0], d_block_ref[1], d_block_ref[2] + d_corner_ref[1]]
    blank = jnp.zeros((SPAN, WIDE - SPAN), f32)
    sums = [
        jnp.sum(unroll_rows(jnp.concatenate([tile, blank], axis=1)), axis=0, keepdims=True)
        for tile in d_blocks
    ]
    for m in range(2):
        line = jnp.sum(d_block_ref[NEAR + m] - d_corner_ref[m], axis=0, keepdims=True)
        for b in range(BQ // SPAN):
            line = line + far_ref[m : m + 1, b * SPAN : (b + 1) * SPAN]
        sums.append(jnp.concatenate([line, blank[:1]], axis=1))
    sums = jnp.concatenate(sums, axis=0)
    buckets = bucket_ref[: NEAR + 2, :]
    by_bucket = jnp.concatenate(
        [
            jnp.sum(jnp.where(buckets == bucket, sums, 0.0), axis=0, keepdims=True)
            for bucket in range(bucket_count)
        ],
        axis=0,
    )
    totals = jnp.broadcast_to(jnp.sum(by_bucket, axis=1, keepdims=True), (bucket_count, LANES))
    upper = totals.astype(bf16).astype(f32)
    rest = totals - upper
    per_source = bucket_count // sources
    spare = jnp.zeros((EXTRA // 2 - per_source, LANES), f32)
    for source in range(sources):
        span = slice(source * per_source, (source + 1) * per_source)
        grad_ref[source, 3 * half * SPAN :, :] = jnp.concatenate(
            [upper[span], spare, rest[span], spare], axis=0
        ).astype(bf16)

    for source in range(sources):
        for pair in range(half):
            tiles = []
            for member in range(2):
                slot = pair + member * half
                place = place_of(order_ref, info_ref, source, slot, slots) * SPAN
                grad_ref[source, slot * SPAN : (slot + 1) * SPAN, :] = d_both_ref[
                    dyn(place, SPAN, SPAN), :
                ].astype(bf16)
                tiles.append(d_query_ref[dyn(place, SPAN, SPAN), :].astype(f32))
            grad_ref[source, (slots + pair) * SPAN : (slots + pair + 1) * SPAN, :] = jnp.where(
                low, tiles[0], tiles[1]
            ).astype(bf16)


def attend_back(
    order, ends, info, swapped, mixed_grad, exact, lse, bias_rows, bucket_rows, slots, bucket_count
):
    sources = swapped.shape[0]
    total = sources * slots * SPAN
    return pl.pallas_call(
        functools.partial(attend_back_kernel, slots, bucket_count),
        in_specs=[smem_spec()] * 3 + [vmem_spec()] * 6,
        out_specs=vmem_spec(),
        out_shape=jax.ShapeDtypeStruct((sources, slots * SPAN * 3 // 2 + EXTRA, LANES), bf16),
        scratch_shapes=[
            vmem((total, LANES), bf16),
            vmem((total, LANES), bf16),
            vmem((total, LANES), bf16),
            vmem((KT_ROWS, total), bf16),
            vmem((BK, BQ), f32),
            vmem((2, SPAN, SPAN), f32),
            vmem((NEAR + 2, SPAN, SPAN), f32),
            vmem((2, SPAN, SPAN), f32),
            vmem((total, LANES), f32),
            vmem((total, LANES), bf16),
            vmem((8, BQ), f32),
        ],
        compiler_params=pltpu.CompilerParams(vmem_limit_bytes=attention_vmem(total)),
        cost_estimate=pl.CostEstimate(
            flops=total * total * 320, bytes_accessed=total * 3072, transcendentals=total * total // 2
        ),
        name="attend_back",
    )(order, ends, info, swapped, mixed_grad, exact, lse, bias_rows, bucket_rows)


def out_kernel(slots, packed_ref, weight_ref, mix_ref, *part_refs):
    heads = packed_ref.shape[0]
    half = slots * SPAN // 2

    @pl.when(pl.program_id(0) == 0)
    def _():
        for pair in range(heads // 2):
            first = packed_ref[2 * pair].astype(f32)
            second = packed_ref[2 * pair + 1].astype(f32)
            top, bottom = pair_up(first, second)
            cols = slice(pair * LANES, (pair + 1) * LANES)
            mix_ref[:half, cols] = top.astype(bf16)
            mix_ref[half:, cols] = bottom.astype(bf16)

    part = dot_nn(mix_ref[...], weight_ref[...]).astype(bf16)
    for s in range(slots):
        part_refs[s][...] = part[s * SPAN : (s + 1) * SPAN]


def out_project(packed, weight, slots):
    heads = packed.shape[0]
    rows, width, depth = slots * SPAN, heads * HD, weight.shape[1]
    tile = 512
    return pl.pallas_call(
        functools.partial(out_kernel, slots),
        grid=(depth // tile,),
        in_specs=[
            pl.BlockSpec(packed.shape, lambda j: (0, 0, 0)),
            pl.BlockSpec((width, tile), lambda j: (0, j)),
        ],
        out_specs=[
            pl.BlockSpec((rows, width), lambda j: (0, 0)),
        ]
        + [pl.BlockSpec((SPAN, tile), lambda j: (0, j))] * slots,
        out_shape=[jax.ShapeDtypeStruct((rows, width), bf16)]
        + [jax.ShapeDtypeStruct((SPAN, depth), bf16)] * slots,
        compiler_params=pltpu.CompilerParams(vmem_limit_bytes=40 * MIB),
        cost_estimate=pl.CostEstimate(
            flops=2 * rows * depth * width, bytes_accessed=4 * depth * width, transcendentals=0
        ),
        name="out_project",
    )(packed, weight)


def feed_kernel(slots, *refs):
    normed_refs, grad_refs = refs[:slots], refs[slots : 2 * slots]
    gate_ref, up_ref, down_ref, active_ref, d_both_ref, rows_ref, rows_grad_ref = refs[2 * slots :]

    @pl.when(pl.program_id(0) == 0)
    def _():
        for s in range(slots):
            rows_ref[s * SPAN : (s + 1) * SPAN, :] = normed_refs[s][...]
            rows_grad_ref[s * SPAN : (s + 1) * SPAN, :] = grad_refs[s][...]

    tile = down_ref.shape[1]
    width = d_both_ref.shape[1] // 2
    gate = dot_nn(rows_ref[...], gate_ref[...])
    up = dot_nn(rows_ref[...], up_ref[...])
    d_hidden = dot_nn(rows_grad_ref[...], down_ref[...])
    scale, cubic = 0.7978845608028654, 0.044715
    square = gate * gate
    bent = jnp.tanh(scale * (gate + cubic * square * gate))
    half = 0.5 * (1.0 + bent)
    gelu = gate * half
    slope = half + 0.5 * gate * (1.0 - bent * bent) * (scale * (1.0 + 3.0 * cubic * square))
    active_ref[...] = (gelu * up).astype(bf16)
    start = pl.program_id(0) * tile
    d_both_ref[:, dyn(start, tile, tile)] = (d_hidden * up * slope).astype(bf16)
    d_both_ref[:, dyn(width + start, tile, LANES)] = (d_hidden * gelu).astype(bf16)


def feed_tile(width):
    return 256 if width % 256 == 0 else 128


def feed(normed_slots, grad_slots, weights):
    slots = len(normed_slots)
    rows, depth, width = slots * SPAN, weights.shape[0], weights.shape[1] // 3
    tile = feed_tile(width)
    steps = width // tile
    whole = pl.BlockSpec((SPAN, depth), lambda j: (0, 0))

    def columns(part):
        return pl.BlockSpec((depth, tile), lambda j: (0, part * steps + j))

    return pl.pallas_call(
        functools.partial(feed_kernel, slots),
        grid=(steps,),
        in_specs=[whole] * (2 * slots) + [columns(0), columns(1), columns(2)],
        out_specs=[
            pl.BlockSpec((rows, tile), lambda j: (0, j)),
            pl.BlockSpec((rows, 2 * width), lambda j: (0, 0)),
        ],
        out_shape=[
            jax.ShapeDtypeStruct((rows, width), bf16),
            jax.ShapeDtypeStruct((rows, 2 * width), bf16),
        ],
        scratch_shapes=[vmem((rows, depth), bf16), vmem((rows, depth), bf16)],
        compiler_params=pltpu.CompilerParams(vmem_limit_bytes=56 * MIB),
        cost_estimate=pl.CostEstimate(
            flops=6 * rows * depth * width,
            bytes_accessed=6 * depth * width,
            transcendentals=rows * width,
        ),
        name="feed",
    )(*normed_slots, *grad_slots, weights, weights, weights)


def pack_kernel(slots, shares, spot_ref, mine_ref, rest_ref, packed_ref):
    width = mine_ref.shape[1]
    half = SPAN // 2
    for s in range(slots):
        there = lax.rem(spot_ref[0] - s + slots, slots)
        for pair in range(width // LANES):
            if s == 0:
                tile = mine_ref[:, pair * LANES : (pair + 1) * LANES].astype(f32)
            else:
                start = (s - 1) * width + pair * LANES
                tile = rest_ref[:, start : start + LANES].astype(f32)
            for member, piece in enumerate(pair_up(tile[:half], tile[half:])):
                for share in range(shares):
                    packed_ref[(2 * pair + member) * shares + share, there] = piece.astype(bf16)


def pack(spot, mine, rest, shares):
    width = mine.shape[1]
    slots = 1 + rest.shape[1] // width
    return pl.pallas_call(
        functools.partial(pack_kernel, slots, shares),
        in_specs=[smem_spec(), vmem_spec(), vmem_spec()],
        out_specs=vmem_spec(),
        out_shape=jax.ShapeDtypeStruct((width // HD * shares, slots, SPAN // 2, LANES), bf16),
        compiler_params=pltpu.CompilerParams(vmem_limit_bytes=16 * MIB),
        name="pack",
    )(spot, mine, rest)


def weigh_kernel(slots, packed_ref, mix_ref, left_ref, *refs):
    attn_refs = refs[:slots]
    product_ref, grads_ref = refs[slots:]
    heads = packed_ref.shape[0]
    rows = slots * SPAN
    half = rows // 2
    width = heads * HD

    @pl.when(pl.program_id(0) == 0)
    def _():
        for pair in range(heads // 2):
            start = pair * LANES
            tiles = [packed_ref[2 * pair + m].astype(f32) for m in range(2)]
            value, key = pair_up(tiles[0][:rows], tiles[1][:rows])
            top, bottom = pair_up(tiles[0][rows : rows + half], tiles[1][rows : rows + half])
            grads_ref[:half, start : start + LANES] = top.astype(bf16)
            grads_ref[half:, start : start + LANES] = bottom.astype(bf16)
            grads_ref[:, width + start : width + start + LANES] = key.astype(bf16)
            grads_ref[:, 2 * width + start : 2 * width + start + LANES] = value.astype(bf16)

    product_ref[:, : 3 * width] = dot_tn(left_ref[...], grads_ref[...]).astype(bf16)
    attn = jnp.concatenate([ref[...] for ref in attn_refs], axis=0)
    product_ref[:, 3 * width :] = dot_tn(attn, mix_ref[...]).astype(bf16)


def weigh(packed, mix, left, attn_slots):
    slots = len(attn_slots)
    heads = packed.shape[0]
    rows, depth = left.shape
    width = 3 * heads * HD
    total = width + mix.shape[1]
    tile = 512
    return pl.pallas_call(
        functools.partial(weigh_kernel, slots),
        grid=(depth // tile,),
        in_specs=[
            pl.BlockSpec(packed.shape, lambda j: (0, 0, 0)),
            pl.BlockSpec(mix.shape, lambda j: (0, 0)),
            pl.BlockSpec((rows, tile), lambda j: (0, j)),
        ]
        + [pl.BlockSpec((SPAN, tile), lambda j: (0, j))] * slots,
        out_specs=[
            pl.BlockSpec((tile, total), lambda j: (j, 0)),
            pl.BlockSpec((rows, width), lambda j: (0, 0)),
        ],
        out_shape=[
            jax.ShapeDtypeStruct((depth, total), bf16),
            jax.ShapeDtypeStruct((rows, width), bf16),
        ],
        compiler_params=pltpu.CompilerParams(vmem_limit_bytes=LARGE),
        cost_estimate=pl.CostEstimate(
            flops=2 * rows * depth * total, bytes_accessed=4 * depth * total, transcendentals=0
        ),
        name="weigh",
    )(packed, mix, left, *attn_slots)


def project_back_kernel(which, grads_ref, weight_ref, scale_ref, *refs):
    x_refs = refs[: len(which)]
    gain_ref, *part_refs = refs[len(which) :]
    part = dot_nt(grads_ref[...], weight_ref[...])
    gain = jnp.zeros((1, part.shape[1]), f32)
    for s, x_ref, part_ref in zip(which, x_refs, part_refs, strict=True):
        start = s * SPAN if len(which) > 1 else 0
        piece = part[start : start + SPAN]
        part_ref[...] = piece.astype(bf16)
        x_hat = x_ref[...].astype(f32) * scale_ref[start : start + SPAN, :1]
        gain = gain + jnp.sum(piece * x_hat, axis=0, keepdims=True)
    gain_ref[...] = gain


def project_back(grads, weights, scale, x_slots, which):
    depth, width = weights.shape
    single = len(which) == 1
    rows, at = (SPAN, which[0]) if single else (grads.shape[0], 0)
    tile = 512
    spans = [pl.BlockSpec((SPAN, tile), lambda j: (0, j))] * len(which)
    return pl.pallas_call(
        functools.partial(project_back_kernel, which),
        grid=(depth // tile,),
        in_specs=[
            pl.BlockSpec((rows, width), lambda j: (at, 0)),
            pl.BlockSpec((tile, width), lambda j: (j, 0)),
            pl.BlockSpec((rows, LANES), lambda j: (at, 0)),
        ]
        + spans,
        out_specs=[pl.BlockSpec((1, tile), lambda j: (0, j))] + spans,
        out_shape=[jax.ShapeDtypeStruct((1, depth), f32)]
        + [jax.ShapeDtypeStruct((SPAN, depth), bf16)] * len(which),
        compiler_params=pltpu.CompilerParams(vmem_limit_bytes=LARGE),
        cost_estimate=pl.CostEstimate(
            flops=2 * rows * depth * width, bytes_accessed=4 * depth * width, transcendentals=0
        ),
        name="project_back",
    )(grads, weights, scale, *[x_slots[s] for s in which])


def spread_kernel(shard_ref, query_ref, key_ref, value_ref, out_ref):
    width = query_ref.shape[1]
    for at, ref in enumerate((query_ref, key_ref, value_ref)):
        ref[...] = shard_ref[:, at * width : (at + 1) * width].astype(f32)
    out_ref[...] = shard_ref[:, 3 * width :].astype(f32).T


def spread(shard, width):
    rows = shard.shape[0]
    return pl.pallas_call(
        spread_kernel,
        in_specs=[vmem_spec()],
        out_specs=[vmem_spec()] * 4,
        out_shape=[jax.ShapeDtypeStruct((rows, width), f32)] * 3
        + [jax.ShapeDtypeStruct((width, rows), f32)],
        compiler_params=pltpu.CompilerParams(vmem_limit_bytes=LARGE),
        name="spread",
    )(shard)


def pair_kernel(slots, groups, *refs):
    left_one, left_two = refs[:slots], refs[slots : 2 * slots]
    right_one = refs[2 * slots : 2 * slots + groups]
    right_two = refs[2 * slots + groups : 2 * slots + 2 * groups]
    out_ref, right_ref = refs[-2:]
    cut = right_one[0].shape[1]

    @pl.when(pl.program_id(0) == 0)
    def _():
        start = 0
        for one, two in zip(right_one, right_two, strict=True):
            span = slice(start, start + one.shape[0])
            right_ref[span, :cut] = one[...]
            right_ref[span, cut:] = two[...]
            start += one.shape[0]

    one = jnp.concatenate([ref[...] for ref in left_one], axis=0)
    two = jnp.concatenate([ref[...] for ref in left_two], axis=0)
    out_ref[:, :cut] = dot_tn(one, right_ref[:, :cut]).astype(bf16)
    out_ref[:, cut:] = dot_tn(two, right_ref[:, cut:]).astype(bf16)


def pair_product(left_one, right_one, left_two, right_two):
    slots, groups = len(left_one), len(right_one)
    rows, depth = slots * SPAN, left_one[0].shape[1]
    width = right_one[0].shape[1] + right_two[0].shape[1]
    block = 512

    def whole(array):
        return pl.BlockSpec(array.shape, lambda j: (0, 0))

    return pl.pallas_call(
        functools.partial(pair_kernel, slots, groups),
        grid=(depth // block,),
        in_specs=[pl.BlockSpec((SPAN, block), lambda j: (0, j))] * (2 * slots)
        + [whole(piece) for piece in (*right_one, *right_two)],
        out_specs=pl.BlockSpec((block, width), lambda j: (j, 0)),
        out_shape=jax.ShapeDtypeStruct((depth, width), bf16),
        scratch_shapes=[vmem((rows, width), bf16)],
        compiler_params=pltpu.CompilerParams(vmem_limit_bytes=32 * MIB),
        cost_estimate=pl.CostEstimate(
            flops=2 * rows * depth * width, bytes_accessed=2 * depth * width, transcendentals=0
        ),
        name="pair_product",
    )(*left_one, *left_two, *right_one, *right_two)


def bucket_lines(bucket_of):
    count = bucket_of.shape[0]
    turned = bucket_of[::-1]
    ends = [jnp.broadcast_to(end, (2 * SPAN,)) for end in (turned[:1], turned[-1:])]
    padded = jnp.concatenate([ends[0], turned, ends[1]])
    zero_at = 2 * SPAN + count // 2
    rows = []
    for c in range(NEAR):
        base = zero_at - (c - 1) * SPAN
        rows.append(jnp.concatenate([padded[base : base + SPAN], padded[base - SPAN : base]]))
    rows.append(jnp.broadcast_to(bucket_of[:1], (WIDE,)))
    rows.append(jnp.broadcast_to(bucket_of[-1:], (WIDE,)))
    spare = 8 - (NEAR + 2)
    return jnp.concatenate([jnp.stack(rows), jnp.full((spare, WIDE), -1, bucket_of.dtype)])


def on_device(
    tokens,
    lengths,
    block_order,
    bucket_of,
    gain_attn,
    w_query,
    w_key,
    w_value,
    w_out,
    bias_table,
    gain_ffn,
    w_gate,
    w_up,
    w_down,
    cotangent,
):
    blk_count, slots = lax.axis_size("blk"), lax.axis_size("head")
    blk_spot, head_spot = lax.axis_index("blk"), lax.axis_index("head")
    depth = tokens.shape[1]
    width = w_query.shape[1]
    heads = width // HD
    shares = blk_count // heads
    table_rows, table_heads = bias_table.shape
    bucket_count = table_rows * blk_count
    total = blk_count * slots * SPAN
    gain_size = gain_attn.shape[0]
    hidden = w_gate.shape[1]

    token_slots = gather_far(gather_near(tokens))
    small = gather_small(
        jnp.concatenate([gain_attn, gain_ffn, bias_table.astype(f32).reshape(-1)])
    )
    full_qkv = lax.all_gather(
        jnp.concatenate([w_query, w_key, w_value], axis=1), "blk", axis=0, tiled=True
    )
    full_out = lax.all_gather(w_out, "blk", axis=1, tiled=True)
    full_ffn = lax.all_gather(
        jnp.concatenate([w_gate, w_up, w_down.T], axis=1), "blk", axis=0, tiled=True
    )
    gain_one = small[:, :, :gain_size].reshape(1, depth)
    gain_two = small[:, :, gain_size : 2 * gain_size].reshape(1, depth)

    tables = lax.dynamic_index_in_dim(small, head_spot, 1, False)[:, 2 * gain_size :]
    tables = tables.reshape(bucket_count, table_heads)
    my_head = blk_spot // shares
    my_bias = lax.dynamic_index_in_dim(tables, my_head, 1, False)
    bucket_rows = bucket_lines(bucket_of)
    bias_rows = jnp.sum(
        jnp.where(
            bucket_rows[None] == jnp.arange(bucket_count, dtype=jnp.int32)[:, None, None],
            my_bias[:, None, None],
            0.0,
        ),
        axis=0,
    )
    ends = jnp.cumsum(lengths).astype(jnp.int32)
    per_share = total // BQ // shares
    start = (blk_spot % shares) * per_share
    info = [head_spot, start, start + per_share] + ([start] if shares > 1 else [])
    info = jnp.stack([jnp.asarray(item, jnp.int32) for item in info])

    def swap(values):
        return lax.all_to_all(values, "blk", 0, 0, tiled=True)

    def to_all(values):
        values = values.reshape((blk_count * slots,) + values.shape[2:])
        return lax.all_to_all(values, ("blk", "head"), 0, 0, tiled=True)

    def to_heads(values):
        return swap(values if shares == 1 else jnp.repeat(values, shares, axis=0))

    def to_rows(values):
        values = swap(values)
        if shares == 1:
            return values
        values = values.reshape((heads, shares) + values.shape[1:])
        return jnp.sum(values.astype(f32), axis=1).astype(bf16)

    w_out, cotangent, *token_slots = together(w_out, cotangent, *token_slots)
    normed_one, packed, scale_one = project(token_slots, gain_one, full_qkv)
    early = (ends, info, bias_rows, bucket_rows)
    swapped, ends, info, bias_rows, bucket_rows, *out_near = together(
        to_heads(packed), *early, *gather_near(w_out)
    )
    grad_near, out_slots = gather_near(cotangent), gather_far(out_near)
    mixed, exact, lse = attend(block_order, ends, info, swapped, bias_rows, slots)
    mixed, *moved = together(mixed, *grad_near, *out_slots)
    grad_near, out_slots = moved[: len(grad_near)], moved[len(grad_near) :]
    packed_mix, *grad_slots = together(to_rows(mixed), *gather_far(grad_near))
    attn_mix, *out_parts = out_project(packed_mix, full_out, slots)
    tokens_wide = tokens.astype(f32)
    hidden_one = tokens_wide + sum_terms(sum_near(out_parts, sum_far(out_parts))[0])
    rstd_two = rms_scale(hidden_one)
    normed_two = (hidden_one * rstd_two * gain_two).astype(bf16)

    normed_two, out_slots = together(normed_two, out_slots)
    full_rest = lax.all_gather(jnp.concatenate(out_slots[1:]), "blk", axis=1, tiled=True)
    normed_slots = gather_far(gather_near(normed_two))
    active, d_both = feed(normed_slots, grad_slots, full_ffn)

    def spans(rows):
        return [rows[s * SPAN : (s + 1) * SPAN] for s in range(rows.shape[0] // SPAN)]

    d_parts = spans(dot_nt(d_both, full_ffn[:, : 2 * hidden]).astype(bf16))
    d_far = sum_far(d_parts)
    grad_hidden, *d_far = together(
        pair_product(normed_slots, [d_both], grad_slots, [active]), *d_far
    )
    grad_hidden = lax.psum_scatter(grad_hidden, "blk", scatter_dimension=0, tiled=True)
    d_near, (active,) = sum_near(d_parts, d_far, (active,))
    down_rows = dot_nt(active, full_ffn[:, 2 * hidden :]).astype(bf16)
    down_rows, full_rest, *d_near = together(down_rows, full_rest, *d_near)
    down_parts = spans(down_rows)
    d_normed_two = sum_terms(d_near)
    d_source_two, gain_part_two = norm_back(d_normed_two, hidden_one, rstd_two, gain_two)
    d_hidden_one = cotangent.astype(f32) + d_source_two

    d_attn = d_hidden_one.astype(bf16)
    mix_grads = pack(
        jnp.reshape(head_spot, (1,)).astype(jnp.int32),
        dot_nt(d_attn, full_out).astype(bf16),
        dot_nt(d_attn, full_rest).astype(bf16),
        shares,
    )
    mix_grads, d_attn = together(mix_grads, d_attn)
    middle = slots // 2
    steps = [t for t in range(1, slots) if t != middle]
    upper, lower = (down_parts[middle][h * SPAN // 2 : (h + 1) * SPAN // 2] for h in range(2))
    moved = (*gather_near(d_attn), *sum_direct(down_parts, steps))
    grads = attend_back(
        block_order, ends, info, swapped, to_all(mix_grads), exact, lse, bias_rows, bucket_rows,
        slots, bucket_count,
    )
    grads, upper, *moved = together(grads, upper, *moved)
    attn_near, down_terms = moved[: 2 - slots], moved[2 - slots :]
    grads, *attn_slots = together(swap(grads), *gather_far(attn_near))
    extra = grads[:, -EXTRA:, 0].astype(f32).reshape(blk_count, 2, -1).sum(axis=1)
    grad_table = extra[:, :table_rows].reshape(heads, shares, table_rows).sum(axis=1).T
    if shares > 1:
        grads = grads.reshape((heads, shares) + grads.shape[1:])
        grads = jnp.sum(grads.astype(f32), axis=1).astype(bf16)
    grad_heads, d_qkv = weigh(grads, attn_mix, normed_one, attn_slots)
    grad_heads, grad_hidden, upper = together(grad_heads, grad_hidden, send_back(upper, middle))
    if slots == 4:
        gain_part_one, far_part = project_back(d_qkv, full_qkv, scale_one, token_slots, [2])
        one_far = sum_far([None, None, far_part, None])
        d_qkv, far_part = together(d_qkv, far_part)
        gain_rest, *one_parts = project_back(d_qkv, full_qkv, scale_one, token_slots, [0, 1, 3])
        gain_part_one = gain_part_one + gain_rest
        one_parts.insert(2, far_part)
    else:
        gain_part_one, *one_parts = project_back(
            d_qkv, full_qkv, scale_one, token_slots, list(range(slots))
        )
        one_far = []

    grad_heads = lax.psum_scatter(grad_heads, "blk", scatter_dimension=0, tiled=True)
    one_near, gain_parts = sum_near(one_parts, one_far, (gain_part_one, gain_part_two))
    gain_parts = jnp.stack(
        [part.reshape(blk_count, slots, gain_size) for part in gain_parts], axis=2
    )
    gain_sums = scatter_blk(gain_parts)
    gain_sums, lower, grad_hidden, *one_near = together(
        gain_sums, lower, grad_hidden, *one_near
    )
    far_term = [jnp.concatenate([upper, send_back(lower, middle)])]
    gain_sums = scatter_head(gain_sums)
    grad_hidden = grad_hidden.astype(f32)
    d_normed_one = sum_terms(one_near)
    d_source_one, unused = norm_back(d_normed_one, tokens_wide, rms_scale(tokens_wide), gain_one)
    input_grad = d_hidden_one + d_source_one
    input_grad, hidden_one = together(input_grad, hidden_one)
    output = hidden_one + sum_all([down_parts[0]] + down_terms + far_term)
    return (
        output,
        input_grad,
        gain_sums[0],
        *spread(grad_heads, width),
        grad_table,
        gain_sums[1],
        grad_hidden[:, :hidden],
        grad_hidden[:, hidden : 2 * hidden],
        grad_hidden[:, 2 * hidden :].T,
    )


def solution(mesh):
    rows, spread = P(("blk", "head"), None), P(("blk", "head"))
    inward, outward = P("blk", "head"), P("head", "blk")
    in_specs = (
        rows, P(), P(), P(), spread, inward, inward, inward, outward, inward, spread,
        inward, inward, outward, rows,
    )
    out_specs = (
        rows, rows, spread, inward, inward, inward, outward, inward, spread,
        inward, inward, outward,
    )
    return jax.shard_map(
        on_device, mesh=mesh, in_specs=in_specs, out_specs=out_specs, check_vma=False
    )
```
